32 devices in a mesh: seq: 4 (over y, x), rep: 8 (over z, core).
Axes of the slice: x: 2, y: 2, z: 4, core: 2. Of those that a mesh axis runs over, the one named last changes fastest.
Arguments:
- inputs: bfloat16 [8, 4096, 768], P('rep', 'seq'), may hold values from -6 to 6
- trunk_grad: bfloat16 [8, 2048, 1536], P('rep', None, 'seq'), may hold values from -6 to 6
- weights: bfloat16 [5, 768, 1536], P(None, 'rep', 'seq'), may hold values from -0.09375 to 0.09375
Outputs:
- input_grad: bfloat16 [8, 4096, 768], P('rep', 'seq')
- weight_grad: float32 [5, 768, 1536], P(None, 'rep', 'seq')
The draws below stay inside these ranges and needn't reach their ends.
All inputs are finite; a program needn't handle non-finite values.
Results may differ from the reference program's by a relative error of at most 0.0027.
Values may be sent and summed in bfloat16 or wider, within the bound.
No kernel may reach another device: no remote copies, remote signals or barrier semaphores. Data moves between devices by JAX's collectives and lax.ppermute only.
A program may use at most 192 MiB of HBM per device.

```python
import jax
import jax.numpy as jnp
from jax import lax

CIN = 768
COUT = 1536
KW = 5
FINE = 4096
COARSE = 2048
SEQS = 8
NF = 32768


def shard_levels(stream_key, dims, split, smallest, top_value):
    def one(dim, shards_of):
        steps = jax.random.uniform(jax.random.fold_in(jax.random.fold_in(stream_key, 6), dim), (shards_of,), jnp.float32, smallest / len(split), top_value / len(split))
        return jnp.repeat(jnp.exp(steps), dims[dim] // shards_of).reshape((-1,) + (1,) * (len(dims) - dim - 1))

    gain = one(*split[0])
    for cut in split[1:]:
        gain = gain * one(*cut)
    return gain


def gaussian(own_key, shape, deviation, most, cuts=(), kind=jnp.bfloat16):
    result = jax.random.normal(own_key, shape, jnp.float32) * deviation
    if len(cuts) > 0:
        result = shard_levels(own_key, shape, cuts, -0.22, 0.18) * result
    return jnp.clip(result, min=-most, max=most).astype(kind)


def setup_inputs(seed: int = 0) -> dict:
    splits = jax.random.split(jax.random.key(seed), 4)
    return {
        "inputs": gaussian(splits[0], (SEQS, FINE, CIN), 1.0, 6.0, ((0, 8), (1, 4))),
        "trunk_grad": gaussian(splits[1], (SEQS, COARSE, COUT), 1.0, 6.0, ((0, 8), (2, 4))),
        "weights": gaussian(splits[2], (KW, CIN, COUT), (KW * CIN) ** -0.5, 0.09375, ((1, 8), (2, 4))),
    }


def one_sequence(weights, total, pair):
    seq_in, seq_grad = pair
    grad_up = jnp.repeat(seq_grad.astype(jnp.float32) * 0.5, 2, axis=0).astype(jnp.bfloat16)
    inputs_f = seq_in.astype(jnp.float32)
    act_vals, back = jax.vjp(jax.nn.gelu, inputs_f)
    slope = back(jnp.ones_like(inputs_f))[0]
    act = act_vals.astype(jnp.bfloat16)
    padded = jnp.pad(grad_up, ((2, 2), (0, 0)))
    act_grad = jnp.zeros((FINE, CIN), jnp.float32)
    terms = []
    for k in range(KW):
        shifted = padded[4 - k:4 - k + FINE]
        act_grad = act_grad + jnp.dot(shifted, weights[k].T, preferred_element_type=jnp.float32)
        terms.append(lax.dot_general(act, shifted, (((0,), (0,)), ((), ())), preferred_element_type=jnp.float32))
    input_grad = (act_grad * slope + grad_up[:, :CIN].astype(jnp.float32)).astype(jnp.bfloat16)
    return (total + jnp.stack(terms), input_grad)

def reference(inputs, trunk_grad, weights):

    def step_fn(total, pair):
        return one_sequence(weights, total, pair)
    start = jnp.zeros((KW, CIN, COUT), jnp.float32)
    total, input_grad = lax.scan(step_fn, start, (inputs, trunk_grad))
    weight_grad = total * float(NF) ** (-0.5)
    return (input_grad, weight_grad)
```

```python
import functools
import math

import jax
import jax.numpy as jnp
from jax import lax
from jax.experimental import pallas as pl
from jax.experimental.pallas import tpu as pltpu
from jax.sharding import PartitionSpec as P

HALO = 8
LANES = 128
ROOT = math.sqrt(2.0 / math.pi)
CUBIC = 0.044715


def from_peer(value, axis, distance):
    peers = lax.axis_size(axis)
    return lax.ppermute(value, axis, [(i, i ^ distance) for i in range(peers)])


def gather_halves(top, bottom, axis):
    found = {0: (top, bottom)}
    for distance in range(1, lax.axis_size(axis)):
        high = 1 << (distance.bit_length() - 1)
        low = distance & -distance
        if high == low:
            found[distance] = (from_peer(top, axis, high), from_peer(bottom, axis, high))
    for distance in range(1, lax.axis_size(axis)):
        high = 1 << (distance.bit_length() - 1)
        low = distance & -distance
        if high != low:
            found[distance] = (
                from_peer(found[distance ^ high][0], axis, high),
                from_peer(found[distance ^ low][1], axis, low),
            )
    return found


def act_kernel(x_ref, top_ref, bottom_ref, scratch):
    half, width = top_ref.shape[0], x_ref.shape[2]

    def rows(step, out_ref, base):
        start = pl.multiple_of(step * 64, 64)
        x = x_ref[0, pl.ds(pl.multiple_of(base + 2 * start, 128), 128), :].astype(jnp.float32)
        act = x * (0.5 * (1.0 + jnp.tanh(ROOT * (x + CUBIC * (x * x * x)))))
        for c in range(width // LANES):
            scratch[c] = act[:, c * LANES : (c + 1) * LANES]
        for parity in range(2):
            for c in range(width // LANES):
                picked = scratch[c, pl.ds(parity, 64, stride=2), :].astype(jnp.bfloat16)
                left = parity * width + c * LANES
                out_ref[pl.ds(start, 64), left : left + LANES] = picked

    @pl.loop(0, half // 64)
    def _(step):
        rows(step, top_ref, 0)

    @pl.loop(0, half // 64)
    def _(step):
        rows(step, bottom_ref, 2 * half)


def activate(inputs):
    fine, width = inputs.shape[1:]
    half = jax.ShapeDtypeStruct((fine // 4, 2 * width), jnp.bfloat16)
    return pl.pallas_call(
        act_kernel,
        out_shape=(half, half),
        in_specs=[pl.BlockSpec(memory_space=pltpu.VMEM)],
        out_specs=[pl.BlockSpec(memory_space=pltpu.VMEM)] * 2,
        scratch_shapes=[pltpu.VMEM((width // LANES, 128, LANES), jnp.float32)],
        compiler_params=pltpu.CompilerParams(vmem_limit_bytes=24 << 20),
        name="act",
    )(inputs)


def input_grad_kernel(seqs, reps, stacked, place, *refs):
    count = 2 * seqs
    x_ref, grads, pieces = refs[0], refs[1 : 1 + seqs], refs[1 + seqs : 1 + seqs + 2 * count]
    out_ref, wv, gv, products, fine, again, sems, grad_sems = refs[1 + seqs + 2 * count :]
    me, rep = place[0], place[1]
    taps, _, rows, _ = wv.shape
    block = grads[0].shape[1]
    coarse = x_ref.shape[1] // 2
    width = x_ref.shape[2]
    copies = []
    for distance in range(seqs):
        owner = me ^ distance
        columns = pl.ds(pl.multiple_of(owner * block, block), block)
        copy = pltpu.make_async_copy(grads[distance], gv.at[:, columns], grad_sems.at[distance])
        copy.start()
        copies.append(copy)
    for flip in range(2):
        for distance in range(seqs):
            columns = pl.ds(pl.multiple_of((me ^ distance) * block, block), block)
            for half in range(2):
                piece = pieces[flip * count + 2 * distance + half]
                for j in range(stacked):
                    owner = rep ^ flip ^ (2 * (half * stacked + j))
                    slot = flip * seqs * 2 * stacked + (2 * distance + half) * stacked + j
                    copy = pltpu.make_async_copy(
                        piece.at[j], wv.at[:, owner, :, columns], sems.at[slot]
                    )
                    copy.start()
                    copies.append(copy)
    for copy in copies:
        copy.wait()
    tile = max(1, reps // 2)

    @pl.loop(0, taps)
    def _(k):
        for part in range(reps // tile):
            kernel = wv[k, part * tile : (part + 1) * tile].reshape(tile * rows, wv.shape[3])
            products[k, :, part * tile * rows : (part + 1) * tile * rows] = lax.dot_general(
                gv[...], kernel, (((1,), (1,)), ((), ())), preferred_element_type=jnp.float32
            )

    step = 64

    @pl.loop(0, coarse // step)
    def _(i):
        base = pl.multiple_of(i * step, step)

        def shifted(k, by):
            window = products[k, pl.ds(base, step + 2 * HALO), :]
            return window[HALO + by : HALO + by + step]

        skip = gv[pl.ds(pl.multiple_of(base, 8), step + 2 * HALO), :width].astype(jnp.float32)
        skip = skip[HALO : HALO + step]
        shared = shifted(0, 1) + shifted(2, 0) + shifted(4, -1)
        even = shared + shifted(1, 0) + shifted(3, -1)
        odd = shared + shifted(1, 1) + shifted(3, 0)
        for c in range(width // LANES):
            lanes = slice(c * LANES, (c + 1) * LANES)
            fine[c, pl.ds(0, step, stride=2), :] = even[:, lanes]
            fine[c, pl.ds(1, step, stride=2), :] = odd[:, lanes]
            again[c, pl.ds(0, step, stride=2), :] = skip[:, lanes]
            again[c, pl.ds(1, step, stride=2), :] = skip[:, lanes]
            span = pl.ds(pl.multiple_of(2 * base, 2 * step), 2 * step)
            x = x_ref[0, span, lanes].astype(jnp.float32)
            tanh = jnp.tanh(ROOT * (x + CUBIC * (x * x * x)))
            slope = 0.5 * (1.0 + tanh) + 0.5 * x * (1.0 - tanh * tanh) * (
                ROOT * (1.0 + 3.0 * CUBIC * (x * x))
            )
            out_ref[0, span, lanes] = (0.5 * (fine[c] * slope + again[c])).astype(jnp.bfloat16)


def input_gradient(place, inputs, grads, kept, swapped):
    seqs, reps = len(grads), 2 * 2 * kept[0].shape[0]
    stacked, taps, rows, block = kept[0].shape
    window = grads[0].shape[0]
    width = inputs.shape[2]
    any_spec = pl.BlockSpec(memory_space=pl.ANY)
    vmem = pl.BlockSpec(memory_space=pltpu.VMEM)
    operands = (inputs, *grads, *kept, *swapped)
    return pl.pallas_call(
        functools.partial(input_grad_kernel, seqs, reps, stacked),
        out_shape=jax.ShapeDtypeStruct(inputs.shape, jnp.bfloat16),
        grid_spec=pltpu.PrefetchScalarGridSpec(
            num_scalar_prefetch=1,
            grid=(1,),
            in_specs=[pl.BlockSpec(inputs.shape, lambda i, place: (0, 0, 0))]
            + [any_spec] * (len(operands) - 1),
            out_specs=pl.BlockSpec(inputs.shape, lambda i, place: (0, 0, 0)),
            scratch_shapes=[
                pltpu.VMEM((taps, reps, rows, seqs * block), jnp.bfloat16),
                pltpu.VMEM((window, seqs * block), jnp.bfloat16),
                pltpu.VMEM((taps, window, width), jnp.float32),
                pltpu.VMEM((width // LANES, 128, LANES), jnp.float32),
                pltpu.VMEM((width // LANES, 128, LANES), jnp.float32),
                pltpu.SemaphoreType.DMA((seqs * reps,)),
                pltpu.SemaphoreType.DMA((seqs,)),
            ],
        ),
        compiler_params=pltpu.CompilerParams(vmem_limit_bytes=52 << 20),
        cost_estimate=pl.CostEstimate(
            flops=2 * taps * window * width * seqs * block,
            bytes_accessed=20 << 20,
            transcendentals=inputs.size,
        ),
        name="input_grad",
    )(place, *operands)


def input_gradient_unaligned(place, inputs, grads, kept, swapped):
    me, rep = place[0], place[1]
    seqs, (stacked, taps, rows, block) = len(grads), kept[0].shape
    reps = 4 * stacked
    window, coarse = grads[0].shape[0], inputs.shape[1] // 2
    grad = jnp.zeros((window, seqs * block), jnp.bfloat16)
    kernel = jnp.zeros((taps, reps * rows, seqs * block), jnp.bfloat16)
    for distance in range(seqs):
        left = (me ^ distance) * block
        grad = lax.dynamic_update_slice(grad, grads[distance], (0, left))
        for flip, pieces in enumerate((kept, swapped)):
            for half in range(2):
                for j in range(stacked):
                    owner = rep ^ flip ^ (2 * (half * stacked + j))
                    piece = pieces[2 * distance + half][j]
                    kernel = lax.dynamic_update_slice(kernel, piece, (0, owner * rows, left))
    products = lax.dot_general(
        grad, kernel, (((1,), (2,)), ((), ())), preferred_element_type=jnp.float32
    )

    def shifted(k, by):
        return products[HALO + by : HALO + by + coarse, k]

    shared = shifted(0, 1) + shifted(2, 0) + shifted(4, -1)
    even = shared + shifted(1, 0) + shifted(3, -1)
    odd = shared + shifted(1, 1) + shifted(3, 0)
    total = jnp.stack([even, odd], axis=1).reshape(inputs.shape[1:])
    x = inputs[0].astype(jnp.float32)
    tanh = jnp.tanh(ROOT * (x + CUBIC * (x * x * x)))
    slope = 0.5 * (1.0 + tanh) + 0.5 * x * (1.0 - tanh * tanh) * (
        ROOT * (1.0 + 3.0 * CUBIC * (x * x))
    )
    skip = jnp.repeat(grad[HALO : HALO + coarse, : inputs.shape[2]].astype(jnp.float32), 2, axis=0)
    return (0.5 * (total * slope + skip)).astype(jnp.bfloat16)[None]


def on_device(inputs, trunk_grad, weights):
    seqs, reps = lax.axis_size("seq"), lax.axis_size("rep")
    me, rep = lax.axis_index("seq"), lax.axis_index("rep")
    taps, rows, block = weights.shape
    fine, width = inputs.shape[1:]
    coarse = fine // 2

    act = gather_halves(*activate(inputs), "seq")

    columns = [weights] + [from_peer(weights, "rep", 2 * j) for j in range(1, reps // 2)]
    kept = gather_halves(
        jnp.stack(columns[: reps // 4]), jnp.stack(columns[reps // 4 :]), "seq"
    )
    kept = [half for distance in range(seqs) for half in kept[distance]]
    swapped = [from_peer(half, "rep", 1) for half in kept]

    trunk = trunk_grad[0]
    edged = jnp.pad(trunk, ((HALO, HALO), (0, 0)))
    grads = []
    for distance in range(seqs):
        window = lax.dynamic_slice_in_dim(edged, (me ^ distance) * coarse, coarse + 2 * HALO, 0)
        grads.append(from_peer(window, "seq", distance) if distance else window)

    zeros = jnp.zeros((1, block), jnp.bfloat16)
    later = jnp.concatenate([trunk[1:], zeros])
    earlier = jnp.concatenate([zeros, trunk[:-1]])
    shifts = jnp.concatenate([later, trunk, earlier], axis=1)
    total = None
    for distance in range(seqs):
        for half in range(2):
            start = (me ^ distance) * coarse + half * (coarse // 2)
            matching = lax.dynamic_slice_in_dim(shifts, start, coarse // 2, 0)
            term = lax.dot_general(
                act[distance][half], matching, (((0,), (0,)), ((), ())), preferred_element_type=jnp.float32
            )
            total = term if total is None else total + term
    even, odd = total[:width], total[width:]
    (even_l, even_c, even_e), (odd_l, odd_c, odd_e) = (
        [part[:, i * block : (i + 1) * block] for i in range(3)] for part in (even, odd)
    )
    scale = 0.5 * float(fine * seqs * reps) ** (-0.5)
    terms = scale * jnp.stack(
        [even_l + odd_l, even_c + odd_l, even_c + odd_c, even_e + odd_c, even_e + odd_e]
    )
    terms = terms.reshape(taps, reps // 2, 2, rows, block)
    core, plane = rep % 2, rep // 2
    mine = lax.dynamic_index_in_dim(terms, core, 2, keepdims=False)
    theirs = lax.dynamic_index_in_dim(terms, 1 - core, 2, keepdims=False)
    mine = mine + from_peer(theirs.astype(jnp.bfloat16), "rep", 1).astype(jnp.float32)
    weight_grad = lax.dynamic_index_in_dim(mine, plane, 1, keepdims=False)
    for j in range(1, reps // 2):
        leaving = lax.dynamic_index_in_dim(mine, plane ^ j, 1, keepdims=False)
        arrived = from_peer(leaving.astype(jnp.bfloat16), "rep", 2 * j)
        weight_grad = weight_grad + arrived.astype(jnp.float32)

    place = jnp.stack([me, rep]).astype(jnp.int32)
    gradient = input_gradient if block % LANES == 0 else input_gradient_unaligned
    input_grad = gradient(place, inputs, grads, kept, swapped)
    return (input_grad, weight_grad)


def solution(mesh):
    in_specs = (P("rep", "seq", None), P("rep", None, "seq"), P(None, "rep", "seq"))
    out_specs = (P("rep", "seq", None), P(None, "rep", "seq"))
    return jax.shard_map(
        on_device, mesh=mesh, in_specs=in_specs, out_specs=out_specs, check_vma=False
    )
```

```python
import functools
import math

import jax
import jax.numpy as jnp
from jax import lax
from jax.experimental import pallas as pl
from jax.experimental.pallas import tpu as pltpu
from jax.sharding import PartitionSpec as P

HALO = 8
LANES = 128
ROOT = math.sqrt(2.0 / math.pi)
CUBIC = 0.044715


def from_peer(value, axis, distance):
    peers = lax.axis_size(axis)
    return lax.ppermute(value, axis, [(i, i ^ distance) for i in range(peers)])


def after(value, *earlier):
    anywhere = pl.BlockSpec(memory_space=pl.ANY)
    return pl.pallas_call(
        lambda *refs: None,
        out_shape=jax.ShapeDtypeStruct(value.shape, value.dtype),
        in_specs=[anywhere] * (1 + len(earlier)),
        out_specs=anywhere,
        input_output_aliases={0: 0},
        name="after",
    )(value, *earlier)


def half_of(piece, which):
    if len(piece) == 2:
        return piece[which]
    size = piece[0].shape[0] // 2
    return lax.slice_in_dim(piece[0], which * size, (which + 1) * size, axis=0)


def gather_square(value, axis):
    found = {0: (value,)}
    near = [d for d in range(1, lax.axis_size(axis)) if d & (d - 1) == 0]
    for distance in near:
        found[distance] = (from_peer(value, axis, distance),)
    for distance in range(1, lax.axis_size(axis)):
        if distance not in near:
            high = 1 << (distance.bit_length() - 1)
            low = distance & -distance
            found[distance] = (
                from_peer(half_of(found[distance ^ high], 0), axis, high),
                from_peer(half_of(found[distance ^ low], 1), axis, low),
            )
    return found


def gather_line(value, axis, count, unit):
    found, mask = {0: value}, count - 1
    while mask:
        for distance in list(found):
            found[distance ^ mask] = from_peer(found[distance], axis, mask * unit)
        mask >>= 1
    return [found[distance] for distance in range(count)]


def act_kernel(x_ref, out_ref, scratch):
    width = x_ref.shape[2]

    @pl.loop(0, out_ref.shape[0] // 64)
    def _(step):
        start = pl.multiple_of(step * 64, 64)
        x = x_ref[0, pl.ds(pl.multiple_of(2 * start, 128), 128), :].astype(jnp.float32)
        act = x * (0.5 * (1.0 + jnp.tanh(ROOT * (x + CUBIC * (x * x * x)))))
        for c in range(width // LANES):
            scratch[c] = act[:, c * LANES : (c + 1) * LANES]
        for parity in range(2):
            for c in range(width // LANES):
                picked = scratch[c, pl.ds(parity, 64, stride=2), :].astype(jnp.bfloat16)
                left = parity * width + c * LANES
                out_ref[pl.ds(start, 64), left : left + LANES] = picked


def activate(inputs):
    fine, width = inputs.shape[1:]
    return pl.pallas_call(
        act_kernel,
        out_shape=jax.ShapeDtypeStruct((fine // 2, 2 * width), jnp.bfloat16),
        in_specs=[pl.BlockSpec(memory_space=pltpu.VMEM)],
        out_specs=pl.BlockSpec(memory_space=pltpu.VMEM),
        scratch_shapes=[pltpu.VMEM((width // LANES, 128, LANES), jnp.float32)],
        compiler_params=pltpu.CompilerParams(vmem_limit_bytes=24 << 20),
        name="act",
    )(inputs)


def weight_grad_kernel(layout, scale, place, shifts_ref, *refs):
    pieces, (mine_ref, theirs_ref) = refs[: len(layout)], refs[len(layout) : len(layout) + 2]
    held, shifts, total, sems, shift_sem = refs[len(layout) + 2 :]
    me, core, plane = place[0], place[1] % 2, place[1] // 2
    planes, taps, rows, block = mine_ref.shape
    coarse = pieces[0].shape[0]
    width = total.shape[0] // 2
    copies = [pltpu.make_async_copy(shifts_ref, shifts, shift_sem)]
    for i, (distance, first, size) in enumerate(layout):
        start = pl.multiple_of((me ^ distance) * coarse + first, 16)
        copies.append(
            pltpu.make_async_copy(pieces[i], held.at[pl.ds(start, size)], sems.at[i])
        )
    for copy in copies:
        copy.start()
    for copy in copies:
        copy.wait()
    tile = 256

    @pl.loop(0, 2 * width // tile)
    def _(i):
        span = pl.ds(pl.multiple_of(i * tile, tile), tile)
        total[span, :] = lax.dot_general(
            held[:, span], shifts[...], (((0,), (0,)), ((), ())), preferred_element_type=jnp.float32
        )

    for out_ref, parity, kind in ((theirs_ref, 1 - core, jnp.bfloat16), (mine_ref, core, jnp.float32)):

        @pl.loop(0, planes)
        def _(j):
            start = ((plane ^ j) * 2 + parity) * rows
            even = pl.ds(pl.multiple_of(start, 16), rows)
            odd = pl.ds(pl.multiple_of(width + start, 16), rows)
            for k, (left, right) in enumerate(((0, 0), (1, 0), (1, 1), (2, 1), (2, 2))):
                term = total[even, left * block : (left + 1) * block]
                term += total[odd, right * block : (right + 1) * block]
                out_ref[j, k] = (scale * term).astype(kind)


def kernel_gradient(place, act, shifts, scale, planes, taps, rows):
    coarse, both = act[0][0].shape
    layout, pieces = [], []
    for distance, parts in act.items():
        first = 0
        for part in parts:
            layout.append((distance, first, part.shape[0]))
            pieces.append(part)
            first += part.shape[0]
    positions, block = len(act) * coarse, shifts.shape[1] // 3
    anywhere = pl.BlockSpec(memory_space=pl.ANY)
    shape = (planes, taps, rows, block)
    whole = pl.BlockSpec(shape, lambda i, place: (0, 0, 0, 0))
    return pl.pallas_call(
        functools.partial(weight_grad_kernel, layout, scale),
        out_shape=(
            jax.ShapeDtypeStruct(shape, jnp.float32),
            jax.ShapeDtypeStruct(shape, jnp.bfloat16),
        ),
        grid_spec=pltpu.PrefetchScalarGridSpec(
            num_scalar_prefetch=1,
            grid=(1,),
            in_specs=[anywhere] * (1 + len(pieces)),
            out_specs=[whole, whole],
            scratch_shapes=[
                pltpu.VMEM((positions, both), jnp.bfloat16),
                pltpu.VMEM(shifts.shape, jnp.bfloat16),
                pltpu.VMEM((both, shifts.shape[1]), jnp.float32),
                pltpu.SemaphoreType.DMA((len(pieces),)),
                pltpu.SemaphoreType.DMA,
            ],
        ),
        compiler_params=pltpu.CompilerParams(vmem_limit_bytes=48 << 20),
        cost_estimate=pl.CostEstimate(
            flops=2 * positions * both * shifts.shape[1], bytes_accessed=16 << 20, transcendentals=0
        ),
        name="weight_grad",
    )(place, shifts, *pieces)


def kernel_gradient_unaligned(place, act, shifts, scale, planes, taps, rows):
    coarse, both = act[0][0].shape
    width, block = both // 2, shifts.shape[1] // 3
    total = jnp.zeros((both, shifts.shape[1]), jnp.float32)
    for distance, parts in act.items():
        first = (place[0] ^ distance) * coarse
        for part in parts:
            matching = lax.dynamic_slice_in_dim(shifts, first, part.shape[0], 0)
            first = first + part.shape[0]
            total = total + lax.dot_general(
                part, matching, (((0,), (0,)), ((), ())), preferred_element_type=jnp.float32
            )
    terms = []
    for left, right in ((0, 0), (1, 0), (1, 1), (2, 1), (2, 2)):
        even = total[:width, left * block : (left + 1) * block]
        odd = total[width:, right * block : (right + 1) * block]
        terms.append(scale * (even + odd))
    terms = jnp.stack(terms).reshape(taps, planes, 2, rows, block)
    core, plane = place[1] % 2, place[1] // 2
    outs = []
    for parity in (core, 1 - core):
        blocks = lax.dynamic_index_in_dim(terms, parity, 2, keepdims=False)
        outs.append(
            jnp.stack(
                [
                    lax.dynamic_index_in_dim(blocks, plane ^ j, 1, keepdims=False)
                    for j in range(planes)
                ]
            )
        )
    return outs[0], outs[1].astype(jnp.bfloat16)


def input_grad_kernel(seqs, layout, place, *refs):
    x_ref, grads = refs[0], refs[1 : 1 + seqs]
    pieces = refs[1 + seqs : 1 + seqs + len(layout)]
    out_ref, wv, gv, products, fine, again, sems, grad_sems = refs[1 + seqs + len(layout) :]
    me, rep = place[0], place[1]
    taps, reps, rows, _ = wv.shape
    block = grads[0].shape[1]
    coarse = x_ref.shape[1] // 2
    width = x_ref.shape[2]
    copies = []
    for distance in range(seqs):
        columns = pl.ds(pl.multiple_of((me ^ distance) * block, block), block)
        copies.append(
            pltpu.make_async_copy(grads[distance], gv.at[:, columns], grad_sems.at[distance])
        )
    for i, (distance, flip, first) in enumerate(layout):
        columns = pl.ds(pl.multiple_of((me ^ distance) * block, block), block)
        for j in range(pieces[i].shape[0]):
            owner = rep ^ flip ^ (2 * (first + j))
            copies.append(
                pltpu.make_async_copy(
                    pieces[i].at[j], wv.at[:, owner, :, columns], sems.at[i, j]
                )
            )
    for copy in copies:
        copy.start()
    for copy in copies:
        copy.wait()
    tile = max(1, reps // 2)

    @pl.loop(0, taps)
    def _(k):
        for part in range(reps // tile):
            kernel = wv[k, part * tile : (part + 1) * tile].reshape(tile * rows, wv.shape[3])
            products[k, :, part * tile * rows : (part + 1) * tile * rows] = lax.dot_general(
                gv[...], kernel, (((1,), (1,)), ((), ())), preferred_element_type=jnp.float32
            )

    step = 64

    @pl.loop(0, coarse // step)
    def _(i):
        base = pl.multiple_of(i * step, step)

        def shifted(k, by):
            window = products[k, pl.ds(base, step + 2 * HALO), :]
            return window[HALO + by : HALO + by + step]

        skip = gv[pl.ds(pl.multiple_of(base, 8), step + 2 * HALO), :width].astype(jnp.float32)
        skip = skip[HALO : HALO + step]
        shared = shifted(0, 1) + shifted(2, 0) + shifted(4, -1)
        even = shared + shifted(1, 0) + shifted(3, -1)
        odd = shared + shifted(1, 1) + shifted(3, 0)
        for c in range(width // LANES):
            lanes = slice(c * LANES, (c + 1) * LANES)
            fine[c, pl.ds(0, step, stride=2), :] = even[:, lanes]
            fine[c, pl.ds(1, step, stride=2), :] = odd[:, lanes]
            again[c, pl.ds(0, step, stride=2), :] = skip[:, lanes]
            again[c, pl.ds(1, step, stride=2), :] = skip[:, lanes]
            span = pl.ds(pl.multiple_of(2 * base, 2 * step), 2 * step)
            x = x_ref[0, span, lanes].astype(jnp.float32)
            tanh = jnp.tanh(ROOT * (x + CUBIC * (x * x * x)))
            slope = 0.5 * (1.0 + tanh) + 0.5 * x * (1.0 - tanh * tanh) * (
                ROOT * (1.0 + 3.0 * CUBIC * (x * x))
            )
            out_ref[0, span, lanes] = (0.5 * (fine[c] * slope + again[c])).astype(jnp.bfloat16)


def ordered(kept, swapped):
    layout, pieces = [], []
    for flip, found in enumerate((kept, swapped)):
        for distance, parts in found.items():
            first = 0
            for part in parts:
                layout.append((distance, flip, first))
                pieces.append(part)
                first += part.shape[0]
    return layout, pieces


def input_gradient(place, inputs, grads, kept, swapped):
    planes, taps, rows, block = kept[0][0].shape
    seqs, reps = len(grads), 2 * planes
    layout, pieces = ordered(kept, swapped)
    window = grads[0].shape[0]
    width = inputs.shape[2]
    anywhere = pl.BlockSpec(memory_space=pl.ANY)
    operands = (inputs, *grads, *pieces)
    return pl.pallas_call(
        functools.partial(input_grad_kernel, seqs, layout),
        out_shape=jax.ShapeDtypeStruct(inputs.shape, jnp.bfloat16),
        grid_spec=pltpu.PrefetchScalarGridSpec(
            num_scalar_prefetch=1,
            grid=(1,),
            in_specs=[pl.BlockSpec(inputs.shape, lambda i, place: (0, 0, 0))]
            + [anywhere] * (len(operands) - 1),
            out_specs=pl.BlockSpec(inputs.shape, lambda i, place: (0, 0, 0)),
            scratch_shapes=[
                pltpu.VMEM((taps, reps, rows, seqs * block), jnp.bfloat16),
                pltpu.VMEM((window, seqs * block), jnp.bfloat16),
                pltpu.VMEM((taps, window, width), jnp.float32),
                pltpu.VMEM((width // LANES, 128, LANES), jnp.float32),
                pltpu.VMEM((width // LANES, 128, LANES), jnp.float32),
                pltpu.SemaphoreType.DMA((len(pieces), planes)),
                pltpu.SemaphoreType.DMA((seqs,)),
            ],
        ),
        compiler_params=pltpu.CompilerParams(vmem_limit_bytes=52 << 20),
        cost_estimate=pl.CostEstimate(
            flops=2 * taps * window * width * seqs * block,
            bytes_accessed=20 << 20,
            transcendentals=inputs.size,
        ),
        name="input_grad",
    )(place, *operands)


def input_gradient_unaligned(place, inputs, grads, kept, swapped):
    me, rep = place[0], place[1]
    planes, taps, rows, block = kept[0][0].shape
    seqs, reps = len(grads), 2 * planes
    window, coarse = grads[0].shape[0], inputs.shape[1] // 2
    grad = jnp.zeros((window, seqs * block), jnp.bfloat16)
    for distance in range(seqs):
        grad = lax.dynamic_update_slice(grad, grads[distance], (0, (me ^ distance) * block))
    kernel = jnp.zeros((taps, reps * rows, seqs * block), jnp.bfloat16)
    for (distance, flip, first), part in zip(*ordered(kept, swapped)):
        for j in range(part.shape[0]):
            owner = rep ^ flip ^ (2 * (first + j))
            spot = (0, owner * rows, (me ^ distance) * block)
            kernel = lax.dynamic_update_slice(kernel, part[j], spot)
    products = lax.dot_general(
        grad, kernel, (((1,), (2,)), ((), ())), preferred_element_type=jnp.float32
    )

    def shifted(k, by):
        return products[HALO + by : HALO + by + coarse, k]

    shared = shifted(0, 1) + shifted(2, 0) + shifted(4, -1)
    even = shared + shifted(1, 0) + shifted(3, -1)
    odd = shared + shifted(1, 1) + shifted(3, 0)
    total = jnp.stack([even, odd], axis=1).reshape(inputs.shape[1:])
    x = inputs[0].astype(jnp.float32)
    tanh = jnp.tanh(ROOT * (x + CUBIC * (x * x * x)))
    slope = 0.5 * (1.0 + tanh) + 0.5 * x * (1.0 - tanh * tanh) * (
        ROOT * (1.0 + 3.0 * CUBIC * (x * x))
    )
    skip = jnp.repeat(grad[HALO : HALO + coarse, : inputs.shape[2]].astype(jnp.float32), 2, axis=0)
    return (0.5 * (total * slope + skip)).astype(jnp.bfloat16)[None]


def on_device(inputs, trunk_grad, weights):
    seqs, reps = lax.axis_size("seq"), lax.axis_size("rep")
    me, rep = lax.axis_index("seq"), lax.axis_index("rep")
    place = jnp.stack([me, rep]).astype(jnp.int32)
    taps, rows, block = weights.shape
    fine, width = inputs.shape[1:]
    coarse, planes = fine // 2, reps // 2

    act = gather_square(activate(inputs), "seq")
    near = [act[1][0], act[2][0]] if seqs > 2 else []
    far = act[3] if seqs > 2 else ()

    column = after(jnp.stack(gather_line(weights, "rep", planes, 2)), *far)
    kept = gather_square(column, "seq")
    swapped = {d: tuple(from_peer(part, "rep", 1) for part in kept[d]) for d in kept}

    trunk = trunk_grad[0]
    edged = after(jnp.pad(trunk, ((HALO, HALO), (0, 0))), *near)
    grads = []
    for distance in range(seqs):
        window = lax.dynamic_slice_in_dim(edged, (me ^ distance) * coarse, coarse + 2 * HALO, 0)
        grads.append(from_peer(window, "seq", distance) if distance else window)

    zeros = jnp.zeros((1, block), jnp.bfloat16)
    later = jnp.concatenate([trunk[1:], zeros])
    earlier = jnp.concatenate([zeros, trunk[:-1]])
    shifts = jnp.concatenate([later, trunk, earlier], axis=1)
    scale = 0.5 * float(fine * seqs * reps) ** (-0.5)
    aligned = block % LANES == 0
    terms = kernel_gradient if aligned else kernel_gradient_unaligned
    mine, theirs = terms(place, act, shifts, scale, planes, taps, rows)
    arrived = from_peer(theirs, "rep", 1)
    weight_grad = mine[0] + arrived[0].astype(jnp.float32)
    for j in range(1, planes):
        leaving = (mine[j] + arrived[j].astype(jnp.float32)).astype(jnp.bfloat16)
        weight_grad = weight_grad + from_peer(leaving, "rep", 2 * j).astype(jnp.float32)

    gradient = input_gradient if aligned else input_gradient_unaligned
    input_grad = gradient(place, inputs, grads, kept, swapped)
    return (input_grad, weight_grad)


def solution(mesh):
    in_specs = (P("rep", "seq", None), P("rep", None, "seq"), P(None, "rep", "seq"))
    out_specs = (P("rep", "seq", None), P(None, "rep", "seq"))
    return jax.shard_map(
        on_device, mesh=mesh, in_specs=in_specs, out_specs=out_specs, check_vma=False
    )
```

```python
import functools
import math

import jax
import jax.numpy as jnp
from jax import lax
from jax.experimental import pallas as pl
from jax.experimental.pallas import tpu as pltpu
from jax.sharding import PartitionSpec as P

HALO = 8
LANES = 128
SPLIT = 3
ROOT = math.sqrt(2.0 / math.pi)
CUBIC = 0.044715
ANYWHERE = pl.BlockSpec(memory_space=pl.ANY)
ROW_OFFSETS = ((1, 1), (0, 1), (0, 0), (-1, 0), (-1, -1))
GRAD_PARTS = ((0, 0), (1, 0), (1, 1), (2, 1), (2, 2))


def from_peer(value, axis, distance):
    peers = lax.axis_size(axis)
    return lax.ppermute(value, axis, [(i, i ^ distance) for i in range(peers)])


def after(value, *earlier):
    return pl.pallas_call(
        lambda *refs: None,
        out_shape=jax.ShapeDtypeStruct(value.shape, value.dtype),
        in_specs=[ANYWHERE] * (1 + len(earlier)),
        out_specs=ANYWHERE,
        input_output_aliases={0: 0},
        name="after",
    )(value, *earlier)


def half_of(piece, which):
    if len(piece) == 2:
        return piece[which]
    size = piece[0].shape[0] // 2
    return lax.slice_in_dim(piece[0], which * size, (which + 1) * size, axis=0)


def gather_square(value, axis):
    found = {0: (value,)}
    near = [d for d in range(1, lax.axis_size(axis)) if d & (d - 1) == 0]
    for distance in near:
        found[distance] = (from_peer(value, axis, distance),)
    for distance in range(1, lax.axis_size(axis)):
        if distance not in near:
            high = 1 << (distance.bit_length() - 1)
            low = distance & -distance
            found[distance] = (
                from_peer(half_of(found[distance ^ high], 0), axis, high),
                from_peer(half_of(found[distance ^ low], 1), axis, low),
            )
    return found


def line_masks(count):
    masks = []
    while count > 1:
        masks.append(count - 1)
        count //= 2
    return masks


def gather_line(value, axis, count, unit):
    found = {0: value}
    for mask in line_masks(count):
        for distance in list(found):
            found[distance ^ mask] = from_peer(found[distance], axis, mask * unit)
    return [found[distance] for distance in range(count)]


def reduce_line(blocks, axis, count, unit):
    held, masks = [[0]], line_masks(count)
    for mask in masks:
        held.append(held[-1] + [d ^ mask for d in held[-1]])
    blocks = dict(enumerate(blocks))
    for mask, keep in reversed(list(zip(masks, held))):
        leaving = jnp.stack([blocks[d ^ mask].astype(jnp.bfloat16) for d in keep])
        arrived = from_peer(leaving, axis, mask * unit)
        blocks = {d: blocks[d] + arrived[n].astype(jnp.float32) for n, d in enumerate(keep)}
    return blocks[0]


def gelu_slope(x):
    tanh = jnp.tanh(ROOT * (x + CUBIC * (x * x * x)))
    return 0.5 * (1.0 + tanh) + 0.5 * x * (1.0 - tanh * tanh) * (
        ROOT * (1.0 + 3.0 * CUBIC * (x * x))
    )


def act_kernel(x_ref, out_ref, scratch):
    width = x_ref.shape[2]

    @pl.loop(0, out_ref.shape[0] // 64)
    def _(step):
        start = pl.multiple_of(step * 64, 64)
        x = x_ref[0, pl.ds(pl.multiple_of(2 * start, 128), 128), :].astype(jnp.float32)
        act = x * (0.5 * (1.0 + jnp.tanh(ROOT * (x + CUBIC * (x * x * x)))))
        for c in range(width // LANES):
            scratch[c] = act[:, c * LANES : (c + 1) * LANES]
        for parity in range(2):
            for c in range(width // LANES):
                picked = scratch[c, pl.ds(parity, 64, stride=2), :].astype(jnp.bfloat16)
                left = parity * width + c * LANES
                out_ref[pl.ds(start, 64), left : left + LANES] = picked


def activate(inputs):
    fine, width = inputs.shape[1:]
    return pl.pallas_call(
        act_kernel,
        out_shape=jax.ShapeDtypeStruct((fine // 2, 2 * width), jnp.bfloat16),
        in_specs=[pl.BlockSpec(memory_space=pltpu.VMEM)],
        out_specs=pl.BlockSpec(memory_space=pltpu.VMEM),
        scratch_shapes=[pltpu.VMEM((width // LANES, 128, LANES), jnp.float32)],
        compiler_params=pltpu.CompilerParams(vmem_limit_bytes=24 << 20),
        name="act",
    )(inputs)


def act_layout(act):
    layout, pieces = [], []
    for distance, parts in act.items():
        first = 0
        for part in parts:
            layout.append((distance, first, part.shape[0]))
            pieces.append(part)
            first += part.shape[0]
    return layout, pieces


def start_act(place, coarse, layout, pieces, shifts_ref, held, shifts, sems, shift_sems):
    copies, row = [], 0
    for i, (distance, first, size) in enumerate(layout):
        start = pl.multiple_of((place[0] ^ distance) * coarse + first, 16)
        spot = pl.ds(row, size)
        copies.append(pltpu.make_async_copy(pieces[i], held.at[spot], sems.at[i]))
        copies.append(
            pltpu.make_async_copy(shifts_ref.at[pl.ds(start, size)], shifts.at[spot], shift_sems.at[i])
        )
        row += size
    for copy in copies:
        copy.start()
    return copies


def early_terms(place, act, shifts, coarse):
    layout, pieces = act_layout(act)
    both, columns = pieces[0].shape[1], shifts.shape[1]
    rows = sum(size for _, _, size in layout)
    tile = 256

    def kernel(place, shifts_ref, *refs):
        pieces, total = refs[: len(layout)], refs[len(layout)]
        held, shifts, sems, shift_sems = refs[len(layout) + 1 :]
        copies = start_act(
            place, coarse, layout, pieces, shifts_ref, held, shifts, sems, shift_sems
        )
        for copy in copies:
            copy.wait()

        @pl.loop(0, both // tile)
        def _(i):
            span = pl.ds(pl.multiple_of(i * tile, tile), tile)
            total[span, :] = lax.dot_general(
                held[:, span], shifts[...], (((0,), (0,)), ((), ())), preferred_element_type=jnp.float32
            )

    return pl.pallas_call(
        kernel,
        out_shape=jax.ShapeDtypeStruct((both, columns), jnp.float32),
        grid_spec=pltpu.PrefetchScalarGridSpec(
            num_scalar_prefetch=1,
            grid=(1,),
            in_specs=[ANYWHERE] * (1 + len(pieces)),
            out_specs=pl.BlockSpec((both, columns), lambda i, place: (0, 0)),
            scratch_shapes=[
                pltpu.VMEM((rows, both), jnp.bfloat16),
                pltpu.VMEM((rows, columns), jnp.bfloat16),
                pltpu.SemaphoreType.DMA((len(pieces),)),
                pltpu.SemaphoreType.DMA((len(pieces),)),
            ],
        ),
        compiler_params=pltpu.CompilerParams(vmem_limit_bytes=48 << 20),
        cost_estimate=pl.CostEstimate(
            flops=2 * rows * both * columns, bytes_accessed=16 << 20, transcendentals=0
        ),
        name="weight_grad_early",
    )(place, shifts, *pieces)


def late_terms(place, act, shifts, early, coarse, scale, planes, taps, rows):
    layout, pieces = act_layout(act)
    both, columns = early.shape
    width, block = both // 2, columns // 3
    count = sum(size for _, _, size in layout)
    tile = 256
    shape = (planes, taps, rows, block)

    def kernel(place, shifts_ref, early_ref, *refs):
        pieces, (mine_ref, theirs_ref) = refs[: len(layout)], refs[len(layout) : len(layout) + 2]
        held, shifts, total, sems, shift_sems, early_sems = refs[len(layout) + 2 :]
        core, plane = place[1] % 2, place[1] // 2
        copies = start_act(
            place, coarse, layout, pieces, shifts_ref, held, shifts, sems, shift_sems
        )

        def fetch(i):
            span = pl.ds(pl.multiple_of(i * tile, tile), tile)
            return pltpu.make_async_copy(early_ref.at[span], total.at[span], early_sems.at[i])

        for i in range(both // tile):
            fetch(i).start()
        for copy in copies:
            copy.wait()

        @pl.loop(0, both // tile)
        def _(i):
            span = pl.ds(pl.multiple_of(i * tile, tile), tile)
            term = lax.dot_general(
                held[:, span], shifts[...], (((0,), (0,)), ((), ())), preferred_element_type=jnp.float32
            )
            fetch(i).wait()
            total[span, :] += term

        for out_ref, parity, kind in (
            (theirs_ref, 1 - core, jnp.bfloat16),
            (mine_ref, core, jnp.float32),
        ):

            @pl.loop(0, planes)
            def _(j):
                start = ((plane ^ j) * 2 + parity) * rows
                even = pl.ds(pl.multiple_of(start, 16), rows)
                odd = pl.ds(pl.multiple_of(width + start, 16), rows)
                for k, (left, right) in enumerate(GRAD_PARTS):
                    term = total[even, left * block : (left + 1) * block]
                    term += total[odd, right * block : (right + 1) * block]
                    out_ref[j, k] = (scale * term).astype(kind)

    whole = pl.BlockSpec(shape, lambda i, place: (0, 0, 0, 0))
    return pl.pallas_call(
        kernel,
        out_shape=(
            jax.ShapeDtypeStruct(shape, jnp.float32),
            jax.ShapeDtypeStruct(shape, jnp.bfloat16),
        ),
        grid_spec=pltpu.PrefetchScalarGridSpec(
            num_scalar_prefetch=1,
            grid=(1,),
            in_specs=[ANYWHERE] * (2 + len(pieces)),
            out_specs=[whole, whole],
            scratch_shapes=[
                pltpu.VMEM((count, both), jnp.bfloat16),
                pltpu.VMEM((count, columns), jnp.bfloat16),
                pltpu.VMEM((both, columns), jnp.float32),
                pltpu.SemaphoreType.DMA((len(pieces),)),
                pltpu.SemaphoreType.DMA((len(pieces),)),
                pltpu.SemaphoreType.DMA((both // tile,)),
            ],
        ),
        compiler_params=pltpu.CompilerParams(vmem_limit_bytes=48 << 20),
        cost_estimate=pl.CostEstimate(
            flops=2 * count * both * columns, bytes_accessed=16 << 20, transcendentals=0
        ),
        name="weight_grad_late",
    )(place, shifts, early, *pieces)


def terms_unaligned(place, act, shifts, coarse, scale, planes, taps, rows):
    both = act[0][0].shape[1]
    width, block = both // 2, shifts.shape[1] // 3
    total = jnp.zeros((both, shifts.shape[1]), jnp.float32)
    for (distance, first, size), part in zip(*act_layout(act)):
        start = (place[0] ^ distance) * coarse + first
        matching = lax.dynamic_slice_in_dim(shifts, start, size, 0)
        total = total + lax.dot_general(
            part, matching, (((0,), (0,)), ((), ())), preferred_element_type=jnp.float32
        )
    terms = []
    for left, right in GRAD_PARTS:
        even = total[:width, left * block : (left + 1) * block]
        odd = total[width:, right * block : (right + 1) * block]
        terms.append(scale * (even + odd))
    terms = jnp.stack(terms).reshape(taps, planes, 2, rows, block)
    core, plane = place[1] % 2, place[1] // 2
    outs = []
    for parity in (core, 1 - core):
        blocks = lax.dynamic_index_in_dim(terms, parity, 2, keepdims=False)
        picked = [
            lax.dynamic_index_in_dim(blocks, plane ^ j, 1, keepdims=False) for j in range(planes)
        ]
        outs.append(jnp.stack(picked))
    return outs[0], outs[1].astype(jnp.bfloat16)


def input_terms(place, grads, entries, first_tap, sums, inputs, reps):
    arrays, index = [], {}
    for array, *_ in entries:
        if id(array) not in index:
            index[id(array)] = len(arrays)
            arrays.append(array)
    distances = sorted({entry[2] for entry in entries})
    window, block = grads[0].shape
    coarse = window - 2 * HALO
    taps, rows = arrays[0].shape[1:3]
    width, depth = reps * rows, len(distances) * block
    last, begun = inputs is not None, sums is not None
    shown = width // block if last else 0
    used = list(range(len(grads))) if last else distances
    tile, step = reps // 2, 64
    operands = [grads[d] for d in used] + arrays
    if begun:
        operands.append(sums)
    if last:
        operands.append(inputs)

    def kernel(place, *refs):
        own = refs[: len(used)]
        pieces = refs[len(used) : len(used) + len(arrays)]
        refs = refs[len(used) + len(arrays) :]
        if begun:
            sums_ref, refs = refs[0], refs[1:]
        if last:
            x_ref, refs = refs[0], refs[1:]
        out_ref, refs = refs[0], refs[1:]
        wv, gv, products, sems, grad_sems = refs[:5]
        refs = refs[5:]
        if last:
            skips, fine, again, skip_sems, sum_sem, held = refs
        me, rep = place[0], place[1]
        copies, skip_copies = [], []
        for slot, distance in enumerate(distances):
            spot = pl.ds(slot * block, block)
            source = own[used.index(distance)]
            copies.append(pltpu.make_async_copy(source, gv.at[:, spot], grad_sems.at[slot]))
        for number, (array, at, distance, flip, plane) in enumerate(entries):
            spot = pl.ds(distances.index(distance) * block, block)
            owner = rep ^ flip ^ (2 * plane)
            copies.append(
                pltpu.make_async_copy(
                    pieces[index[id(array)]].at[at], wv.at[:, owner, :, spot], sems.at[number]
                )
            )
        if last:
            for slot in range(len(used)):
                copy = pltpu.make_async_copy(own[slot], skips.at[me ^ slot], skip_sems.at[slot])
                skip_copies.append(copy)
            skip_copies.append(pltpu.make_async_copy(sums_ref, held, sum_sem))
        for copy in copies + skip_copies:
            copy.start()
        for copy in copies:
            copy.wait()

        @pl.loop(0, taps)
        def _(k):
            for part in range(reps // tile):
                kernel = wv[k, part * tile : (part + 1) * tile].reshape(tile * rows, depth)
                products[k, :, part * tile * rows : (part + 1) * tile * rows] = lax.dot_general(
                    gv[...], kernel, (((1,), (1,)), ((), ())), preferred_element_type=jnp.float32
                )

        for copy in skip_copies:
            copy.wait()

        @pl.loop(0, coarse // step)
        def _(i):
            base = pl.multiple_of(i * step, step)
            spot = pl.ds(base, step)
            for c in range(width // LANES):
                lanes = slice(c * LANES, (c + 1) * LANES)
                totals = []
                for parity in range(2):
                    total = None
                    if begun:
                        total = (held if last else sums_ref)[parity, spot, lanes]
                    for by in (0, 1, -1):
                        wanted = [
                            k for k in range(taps) if ROW_OFFSETS[first_tap + k][parity] == by
                        ]
                        if not wanted:
                            continue
                        part = sum(
                            products[k, pl.ds(base, step + 2 * HALO), lanes] for k in wanted
                        )
                        part = part[HALO + by : HALO + by + step]
                        total = part if total is None else total + part
                    totals.append(total)
                if not last:
                    out_ref[0, spot, lanes], out_ref[1, spot, lanes] = totals
                    continue
                place_c = c * LANES // block, slice(c * LANES % block, c * LANES % block + LANES)
                skip = skips[place_c[0], pl.ds(base, step + 2 * HALO), place_c[1]]
                skip = skip.astype(jnp.float32)[HALO : HALO + step]
                for parity in range(2):
                    fine[c, pl.ds(parity, step, stride=2), :] = totals[parity]
                    again[c, pl.ds(parity, step, stride=2), :] = skip
                span = pl.ds(pl.multiple_of(2 * base, 2 * step), 2 * step)
                slope = gelu_slope(x_ref[0, span, lanes].astype(jnp.float32))
                out_ref[0, span, lanes] = (0.5 * (fine[c] * slope + again[c])).astype(jnp.bfloat16)

    scratch = [
        pltpu.VMEM((taps, reps, rows, depth), jnp.bfloat16),
        pltpu.VMEM((window, depth), jnp.bfloat16),
        pltpu.VMEM((taps, window, width), jnp.float32),
        pltpu.SemaphoreType.DMA((len(entries),)),
        pltpu.SemaphoreType.DMA((len(distances),)),
    ]
    in_specs = [ANYWHERE] * (len(used) + len(arrays))
    sums_shape = (2, coarse, width)
    sums_spec = pl.BlockSpec(sums_shape, lambda i, place: (0, 0, 0))
    if begun:
        in_specs.append(ANYWHERE if last else sums_spec)
    if last:
        in_specs.append(pl.BlockSpec(inputs.shape, lambda i, place: (0, 0, 0)))
        out_shape, out_spec = jax.ShapeDtypeStruct(inputs.shape, jnp.bfloat16), in_specs[-1]
        strip = pltpu.VMEM((width // LANES, 2 * step, LANES), jnp.float32)
        scratch += [
            pltpu.VMEM((len(used), window, block), jnp.bfloat16),
            strip,
            strip,
            pltpu.SemaphoreType.DMA((len(used),)),
            pltpu.SemaphoreType.DMA,
            pltpu.VMEM(sums_shape, jnp.float32),
        ]
    else:
        out_shape, out_spec = jax.ShapeDtypeStruct(sums_shape, jnp.float32), sums_spec
    return pl.pallas_call(
        kernel,
        out_shape=out_shape,
        grid_spec=pltpu.PrefetchScalarGridSpec(
            num_scalar_prefetch=1,
            grid=(1,),
            in_specs=in_specs,
            out_specs=out_spec,
            scratch_shapes=scratch,
        ),
        compiler_params=pltpu.CompilerParams(vmem_limit_bytes=52 << 20),
        cost_estimate=pl.CostEstimate(
            flops=2 * taps * window * width * depth,
            bytes_accessed=20 << 20,
            transcendentals=0,
        ),
        name="input_grad_late" if last else "input_grad_early",
    )(place, *operands)


def input_gradient_unaligned(place, inputs, grads, parts, taps, reps):
    seqs = len(grads)
    window, block = grads[0].shape
    coarse, width = window - 2 * HALO, inputs.shape[2]
    rows = width // reps
    grad = jnp.zeros((window, seqs * block), jnp.bfloat16)
    for distance in range(seqs):
        spot = (0, (place[0] ^ distance) * block)
        grad = lax.dynamic_update_slice(grad, grads[distance], spot)
    kernel = jnp.zeros((taps, width, seqs * block), jnp.bfloat16)
    for first_tap, entries in parts:
        for array, at, distance, flip, plane in entries:
            owner = place[1] ^ flip ^ (2 * plane)
            spot = (first_tap, owner * rows, (place[0] ^ distance) * block)
            kernel = lax.dynamic_update_slice(kernel, array[at], spot)
    products = lax.dot_general(
        grad, kernel, (((1,), (2,)), ((), ())), preferred_element_type=jnp.float32
    )
    totals = []
    for parity in range(2):
        total = 0.0
        for k in range(taps):
            start = HALO + ROW_OFFSETS[k][parity]
            total = total + products[start : start + coarse, k]
        totals.append(total)
    total = jnp.stack(totals, axis=1).reshape(inputs.shape[1:])
    slope = gelu_slope(inputs[0].astype(jnp.float32))
    skip = jnp.repeat(grad[HALO : HALO + coarse, :width].astype(jnp.float32), 2, axis=0)
    return (0.5 * (total * slope + skip)).astype(jnp.bfloat16)[None]


def on_device(inputs, trunk_grad, weights):
    seqs, reps = lax.axis_size("seq"), lax.axis_size("rep")
    me, rep = lax.axis_index("seq"), lax.axis_index("rep")
    place = jnp.stack([me, rep]).astype(jnp.int32)
    taps, rows, block = weights.shape
    fine, width = inputs.shape[1:]
    coarse, planes = fine // 2, reps // 2
    aligned = block % LANES == 0

    last_taps = weights[SPLIT:]
    across = jnp.stack(
        [last_taps] + [from_peer(last_taps, "seq", d) for d in range(1, seqs)]
    )
    act = gather_square(activate(inputs), "seq")
    near = [act[d][0] for d in act if len(act[d]) == 1 and d]
    far = [part for d in act if len(act[d]) == 2 for part in act[d]]
    first_columns = jnp.stack(gather_line(weights[:SPLIT], "rep", planes, 2))
    lines = gather_line(across, "rep", planes, 2)
    other_lines = [from_peer(line, "rep", 1) for line in lines]
    last_entries = [
        (line, distance, distance, flip, plane)
        for flip, found in enumerate((lines, other_lines))
        for plane, line in enumerate(found)
        for distance in range(seqs)
    ]

    trunk = trunk_grad[0]
    edged = after(jnp.pad(trunk, ((HALO, HALO), (0, 0))), *near)
    grads = []
    for distance in range(seqs):
        window = lax.dynamic_slice_in_dim(edged, (me ^ distance) * coarse, coarse + 2 * HALO, 0)
        grads.append(from_peer(window, "seq", distance) if distance else window)

    kept = gather_square(after(first_columns, *far), "seq")
    swapped = {d: tuple(from_peer(part, "rep", 1) for part in kept[d]) for d in kept}
    first_entries = []
    for flip, found in enumerate((kept, swapped)):
        for distance, parts in found.items():
            plane = 0
            for part in parts:
                for at in range(part.shape[0]):
                    first_entries.append((part, at, distance, flip, plane))
                    plane += 1

    zeros = jnp.zeros((1, block), jnp.bfloat16)
    later = jnp.concatenate([trunk[1:], zeros])
    earlier = jnp.concatenate([zeros, trunk[:-1]])
    shifts = jnp.concatenate([later, trunk, earlier], axis=1)
    scale = 0.5 * float(fine * seqs * reps) ** (-0.5)
    if aligned:
        soon = {d: act[d] for d in act if len(act[d]) == 1}
        rest = {d: act[d] for d in act if len(act[d]) == 2}
        early = early_terms(place, soon, shifts, coarse)
        mine, theirs = late_terms(place, rest, shifts, early, coarse, scale, planes, taps, rows)
    else:
        mine, theirs = terms_unaligned(place, act, shifts, coarse, scale, planes, taps, rows)
    arrived = from_peer(theirs, "rep", 1)
    summed = [mine[j] + arrived[j].astype(jnp.float32) for j in range(planes)]
    weight_grad = reduce_line(summed, "rep", planes, 2)

    if aligned:
        soon = [entry for entry in first_entries if len(kept[entry[2]]) == 1]
        rest = [entry for entry in first_entries if len(kept[entry[2]]) == 2]
        sums = input_terms(place, grads, last_entries, SPLIT, None, None, reps)
        sums = input_terms(place, grads, soon, 0, sums, None, reps)
        input_grad = input_terms(place, grads, rest, 0, sums, inputs, reps)
    else:
        parts = ((0, first_entries), (SPLIT, last_entries))
        input_grad = input_gradient_unaligned(place, inputs, grads, parts, taps, reps)
    return (input_grad, weight_grad)


def solution(mesh):
    in_specs = (P("rep", "seq", None), P("rep", None, "seq"), P(None, "rep", "seq"))
    out_specs = (P("rep", "seq", None), P(None, "rep", "seq"))
    return jax.shard_map(
        on_device, mesh=mesh, in_specs=in_specs, out_specs=out_specs, check_vma=False
    )
```

```python
import functools
import math

import jax
import jax.numpy as jnp
from jax import lax
from jax.experimental import pallas as pl
from jax.experimental.pallas import tpu as pltpu
from jax.sharding import PartitionSpec as P

HALO = 8
LANES = 128
SPLIT = 2
ROOT = math.sqrt(2.0 / math.pi)
CUBIC = 0.044715
ANYWHERE = pl.BlockSpec(memory_space=pl.ANY)
ROW_OFFSETS = ((1, 1), (0, 1), (0, 0), (-1, 0), (-1, -1))
GRAD_PARTS = ((0, 0), (1, 0), (1, 1), (2, 1), (2, 2))


def from_peer(value, axis, distance):
    peers = lax.axis_size(axis)
    return lax.ppermute(value, axis, [(i, i ^ distance) for i in range(peers)])


def after(value, *earlier):
    return pl.pallas_call(
        lambda *refs: None,
        out_shape=jax.ShapeDtypeStruct(value.shape, value.dtype),
        in_specs=[ANYWHERE] * (1 + len(earlier)),
        out_specs=ANYWHERE,
        input_output_aliases={0: 0},
        name="after",
    )(value, *earlier)


def half_of(piece, which):
    if len(piece) == 2:
        return piece[which]
    size = piece[0].shape[0] // 2
    return lax.slice_in_dim(piece[0], which * size, (which + 1) * size, axis=0)


def gather_near(value, axis):
    distances = [d for d in range(1, lax.axis_size(axis)) if d & (d - 1) == 0]
    return {d: (from_peer(value, axis, d),) for d in distances}


def gather_far(found, axis, *earlier):
    far = {}
    for distance in range(1, lax.axis_size(axis)):
        high = 1 << (distance.bit_length() - 1)
        low = distance & -distance
        if high != low:
            known = {**found, **far}
            halves = half_of(known[distance ^ high], 0), half_of(known[distance ^ low], 1)
            if earlier:
                halves = [after(half, *earlier) for half in halves]
            far[distance] = (from_peer(halves[0], axis, high), from_peer(halves[1], axis, low))
    return far


def line_masks(count):
    masks = []
    while count > 1:
        masks.append(count - 1)
        count //= 2
    return masks


def reduce_line(blocks, axis, count, unit):
    held, masks = [[0]], line_masks(count)
    for mask in masks:
        held.append(held[-1] + [d ^ mask for d in held[-1]])
    blocks = dict(enumerate(blocks))
    for mask, keep in reversed(list(zip(masks, held))):
        leaving = jnp.stack([blocks[d ^ mask].astype(jnp.bfloat16) for d in keep])
        arrived = from_peer(leaving, axis, mask * unit)
        blocks = {d: blocks[d] + arrived[n].astype(jnp.float32) for n, d in enumerate(keep)}
    return blocks[0]


def gelu_slope(x):
    tanh = jnp.tanh(ROOT * (x + CUBIC * (x * x * x)))
    return 0.5 * (1.0 + tanh) + 0.5 * x * (1.0 - tanh * tanh) * (
        ROOT * (1.0 + 3.0 * CUBIC * (x * x))
    )


def act_kernel(x_ref, out_ref, scratch):
    width = x_ref.shape[2]

    @pl.loop(0, out_ref.shape[0] // 64)
    def _(step):
        start = pl.multiple_of(step * 64, 64)
        x = x_ref[0, pl.ds(pl.multiple_of(2 * start, 128), 128), :].astype(jnp.float32)
        act = x * (0.5 * (1.0 + jnp.tanh(ROOT * (x + CUBIC * (x * x * x)))))
        for c in range(width // LANES):
            scratch[c] = act[:, c * LANES : (c + 1) * LANES]
        for parity in range(2):
            for c in range(width // LANES):
                picked = scratch[c, pl.ds(parity, 64, stride=2), :].astype(jnp.bfloat16)
                left = parity * width + c * LANES
                out_ref[pl.ds(start, 64), left : left + LANES] = picked


def activate(inputs):
    fine, width = inputs.shape[1:]
    return pl.pallas_call(
        act_kernel,
        out_shape=jax.ShapeDtypeStruct((fine // 2, 2 * width), jnp.bfloat16),
        in_specs=[pl.BlockSpec(memory_space=pltpu.VMEM)],
        out_specs=pl.BlockSpec(memory_space=pltpu.VMEM),
        scratch_shapes=[pltpu.VMEM((width // LANES, 128, LANES), jnp.float32)],
        compiler_params=pltpu.CompilerParams(vmem_limit_bytes=24 << 20),
        name="act",
    )(inputs)


def act_layout(act):
    layout, pieces = [], []
    for distance, parts in act.items():
        first = 0
        for part in parts:
            layout.append((distance, first, part.shape[0]))
            pieces.append(part)
            first += part.shape[0]
    return layout, pieces


def start_act(place, coarse, layout, pieces, shifts_ref, held, shifts, sems, shift_sems):
    copies, row = [], 0
    for i, (distance, first, size) in enumerate(layout):
        start = pl.multiple_of((place[0] ^ distance) * coarse + first, 16)
        spot = pl.ds(row, size)
        copies.append(pltpu.make_async_copy(pieces[i], held.at[spot], sems.at[i]))
        copies.append(
            pltpu.make_async_copy(shifts_ref.at[pl.ds(start, size)], shifts.at[spot], shift_sems.at[i])
        )
        row += size
    for copy in copies:
        copy.start()
    return copies


def early_terms(place, act, shifts, coarse):
    layout, pieces = act_layout(act)
    both, columns = pieces[0].shape[1], shifts.shape[1]
    rows = sum(size for _, _, size in layout)
    tile = 256

    def kernel(place, shifts_ref, *refs):
        pieces, total = refs[: len(layout)], refs[len(layout)]
        held, shifts, sems, shift_sems = refs[len(layout) + 1 :]
        copies = start_act(
            place, coarse, layout, pieces, shifts_ref, held, shifts, sems, shift_sems
        )
        for copy in copies:
            copy.wait()

        @pl.loop(0, both // tile)
        def _(i):
            span = pl.ds(pl.multiple_of(i * tile, tile), tile)
            total[span, :] = lax.dot_general(
                held[:, span], shifts[...], (((0,), (0,)), ((), ())), preferred_element_type=jnp.float32
            )

    return pl.pallas_call(
        kernel,
        out_shape=jax.ShapeDtypeStruct((both, columns), jnp.float32),
        grid_spec=pltpu.PrefetchScalarGridSpec(
            num_scalar_prefetch=1,
            grid=(1,),
            in_specs=[ANYWHERE] * (1 + len(pieces)),
            out_specs=pl.BlockSpec((both, columns), lambda i, place: (0, 0)),
            scratch_shapes=[
                pltpu.VMEM((rows, both), jnp.bfloat16),
                pltpu.VMEM((rows, columns), jnp.bfloat16),
                pltpu.SemaphoreType.DMA((len(pieces),)),
                pltpu.SemaphoreType.DMA((len(pieces),)),
            ],
        ),
        compiler_params=pltpu.CompilerParams(vmem_limit_bytes=48 << 20),
        cost_estimate=pl.CostEstimate(
            flops=2 * rows * both * columns, bytes_accessed=16 << 20, transcendentals=0
        ),
        name="weight_grad_early",
    )(place, shifts, *pieces)


def late_terms(place, act, shifts, early, coarse, scale, planes, taps, rows):
    layout, pieces = act_layout(act)
    both, columns = early.shape
    width, block = both // 2, columns // 3
    count = sum(size for _, _, size in layout)
    tile = 256
    shape = (planes, taps, rows, block)

    def kernel(place, shifts_ref, early_ref, *refs):
        pieces, (mine_ref, theirs_ref) = refs[: len(layout)], refs[len(layout) : len(layout) + 2]
        held, shifts, total, sems, shift_sems, early_sems = refs[len(layout) + 2 :]
        core, plane = place[1] % 2, place[1] // 2
        copies = start_act(
            place, coarse, layout, pieces, shifts_ref, held, shifts, sems, shift_sems
        )

        def fetch(i):
            span = pl.ds(pl.multiple_of(i * tile, tile), tile)
            return pltpu.make_async_copy(early_ref.at[span], total.at[span], early_sems.at[i])

        for i in range(both // tile):
            fetch(i).start()
        for copy in copies:
            copy.wait()

        @pl.loop(0, both // tile)
        def _(i):
            span = pl.ds(pl.multiple_of(i * tile, tile), tile)
            term = lax.dot_general(
                held[:, span], shifts[...], (((0,), (0,)), ((), ())), preferred_element_type=jnp.float32
            )
            fetch(i).wait()
            total[span, :] += term

        for out_ref, parity, kind in (
            (theirs_ref, 1 - core, jnp.bfloat16),
            (mine_ref, core, jnp.float32),
        ):

            @pl.loop(0, planes)
            def _(j):
                start = ((plane ^ j) * 2 + parity) * rows
                even = pl.ds(pl.multiple_of(start, 16), rows)
                odd = pl.ds(pl.multiple_of(width + start, 16), rows)
                for k, (left, right) in enumerate(GRAD_PARTS):
                    term = total[even, left * block : (left + 1) * block]
                    term += total[odd, right * block : (right + 1) * block]
                    out_ref[j, k] = (scale * term).astype(kind)

    whole = pl.BlockSpec(shape, lambda i, place: (0, 0, 0, 0))
    return pl.pallas_call(
        kernel,
        out_shape=(
            jax.ShapeDtypeStruct(shape, jnp.float32),
            jax.ShapeDtypeStruct(shape, jnp.bfloat16),
        ),
        grid_spec=pltpu.PrefetchScalarGridSpec(
            num_scalar_prefetch=1,
            grid=(1,),
            in_specs=[ANYWHERE] * (2 + len(pieces)),
            out_specs=[whole, whole],
            scratch_shapes=[
                pltpu.VMEM((count, both), jnp.bfloat16),
                pltpu.VMEM((count, columns), jnp.bfloat16),
                pltpu.VMEM((both, columns), jnp.float32),
                pltpu.SemaphoreType.DMA((len(pieces),)),
                pltpu.SemaphoreType.DMA((len(pieces),)),
                pltpu.SemaphoreType.DMA((both // tile,)),
            ],
        ),
        compiler_params=pltpu.CompilerParams(vmem_limit_bytes=48 << 20),
        cost_estimate=pl.CostEstimate(
            flops=2 * count * both * columns, bytes_accessed=16 << 20, transcendentals=0
        ),
        name="weight_grad_late",
    )(place, shifts, early, *pieces)


def terms_unaligned(place, act, shifts, coarse, scale, planes, taps, rows):
    both = act[0][0].shape[1]
    width, block = both // 2, shifts.shape[1] // 3
    total = jnp.zeros((both, shifts.shape[1]), jnp.float32)
    for (distance, first, size), part in zip(*act_layout(act)):
        start = (place[0] ^ distance) * coarse + first
        matching = lax.dynamic_slice_in_dim(shifts, start, size, 0)
        total = total + lax.dot_general(
            part, matching, (((0,), (0,)), ((), ())), preferred_element_type=jnp.float32
        )
    terms = []
    for left, right in GRAD_PARTS:
        even = total[:width, left * block : (left + 1) * block]
        odd = total[width:, right * block : (right + 1) * block]
        terms.append(scale * (even + odd))
    terms = jnp.stack(terms).reshape(taps, planes, 2, rows, block)
    core, plane = place[1] % 2, place[1] // 2
    outs = []
    for parity in (core, 1 - core):
        blocks = lax.dynamic_index_in_dim(terms, parity, 2, keepdims=False)
        picked = [
            lax.dynamic_index_in_dim(blocks, plane ^ j, 1, keepdims=False) for j in range(planes)
        ]
        outs.append(jnp.stack(picked))
    return outs[0], outs[1].astype(jnp.bfloat16)


def owner_of(owner, rep):
    if isinstance(owner, int):
        return owner
    plane, flip = owner
    return 2 * plane + (rep % 2 ^ flip)


def input_terms(place, grads, entries, first_tap, sums, inputs, reps):
    arrays, index = [], {}
    for array, *_ in entries:
        if id(array) not in index:
            index[id(array)] = len(arrays)
            arrays.append(array)
    distances = sorted({entry[2] for entry in entries})
    window, block = grads[0].shape
    coarse = window - 2 * HALO
    taps, rows = arrays[0].shape[-3:-1]
    width, depth = reps * rows, len(distances) * block
    last, begun = inputs is not None, sums is not None
    shown = width // block if last else 0
    used = list(range(len(grads))) if last else distances
    tile, step = reps // 2, 64
    operands = [grads[d] for d in used] + arrays
    if begun:
        operands.append(sums)
    if last:
        operands.append(inputs)

    def kernel(place, *refs):
        own = refs[: len(used)]
        pieces = refs[len(used) : len(used) + len(arrays)]
        refs = refs[len(used) + len(arrays) :]
        if begun:
            sums_ref, refs = refs[0], refs[1:]
        if last:
            x_ref, refs = refs[0], refs[1:]
        out_ref, refs = refs[0], refs[1:]
        wv, gv, products, sems, grad_sems = refs[:5]
        refs = refs[5:]
        if last:
            skips, fine, again, skip_sems, sum_sem, held = refs
        me, rep = place[0], place[1]
        copies, skip_copies = [], []
        for slot, distance in enumerate(distances):
            spot = pl.ds(slot * block, block)
            source = own[used.index(distance)]
            copies.append(pltpu.make_async_copy(source, gv.at[:, spot], grad_sems.at[slot]))
        for number, (array, at, distance, owner) in enumerate(entries):
            spot = pl.ds(distances.index(distance) * block, block)
            source = pieces[index[id(array)]].at[at]
            target = wv.at[:, owner_of(owner, rep), :, spot]
            copies.append(pltpu.make_async_copy(source, target, sems.at[number]))
        if last:
            for slot in range(len(used)):
                copy = pltpu.make_async_copy(own[slot], skips.at[me ^ slot], skip_sems.at[slot])
                skip_copies.append(copy)
            skip_copies.append(pltpu.make_async_copy(sums_ref, held, sum_sem))
        for copy in copies + skip_copies:
            copy.start()
        for copy in copies:
            copy.wait()

        @pl.loop(0, taps)
        def _(k):
            for part in range(reps // tile):
                kernel = wv[k, part * tile : (part + 1) * tile].reshape(tile * rows, depth)
                products[k, :, part * tile * rows : (part + 1) * tile * rows] = lax.dot_general(
                    gv[...], kernel, (((1,), (1,)), ((), ())), preferred_element_type=jnp.float32
                )

        for copy in skip_copies:
            copy.wait()

        @pl.loop(0, coarse // step)
        def _(i):
            base = pl.multiple_of(i * step, step)
            spot = pl.ds(base, step)
            for c in range(width // LANES):
                lanes = slice(c * LANES, (c + 1) * LANES)
                totals = []
                for parity in range(2):
                    total = None
                    if begun:
                        total = (held if last else sums_ref)[parity, spot, lanes]
                    for by in (0, 1, -1):
                        wanted = [
                            k for k in range(taps) if ROW_OFFSETS[first_tap + k][parity] == by
                        ]
                        if not wanted:
                            continue
                        part = sum(
                            products[k, pl.ds(base, step + 2 * HALO), lanes] for k in wanted
                        )
                        part = part[HALO + by : HALO + by + step]
                        total = part if total is None else total + part
                    totals.append(total)
                if not last:
                    out_ref[0, spot, lanes], out_ref[1, spot, lanes] = totals
                    continue
                place_c = c * LANES // block, slice(c * LANES % block, c * LANES % block + LANES)
                skip = skips[place_c[0], pl.ds(base, step + 2 * HALO), place_c[1]]
                skip = skip.astype(jnp.float32)[HALO : HALO + step]
                for parity in range(2):
                    fine[c, pl.ds(parity, step, stride=2), :] = totals[parity]
                    again[c, pl.ds(parity, step, stride=2), :] = skip
                span = pl.ds(pl.multiple_of(2 * base, 2 * step), 2 * step)
                slope = gelu_slope(x_ref[0, span, lanes].astype(jnp.float32))
                out_ref[0, span, lanes] = (0.5 * (fine[c] * slope + again[c])).astype(jnp.bfloat16)

    scratch = [
        pltpu.VMEM((taps, reps, rows, depth), jnp.bfloat16),
        pltpu.VMEM((window, depth), jnp.bfloat16),
        pltpu.VMEM((taps, window, width), jnp.float32),
        pltpu.SemaphoreType.DMA((len(entries),)),
        pltpu.SemaphoreType.DMA((len(distances),)),
    ]
    in_specs = [ANYWHERE] * (len(used) + len(arrays))
    sums_shape = (2, coarse, width)
    sums_spec = pl.BlockSpec(sums_shape, lambda i, place: (0, 0, 0))
    if begun:
        in_specs.append(ANYWHERE if last else sums_spec)
    if last:
        in_specs.append(pl.BlockSpec(inputs.shape, lambda i, place: (0, 0, 0)))
        out_shape, out_spec = jax.ShapeDtypeStruct(inputs.shape, jnp.bfloat16), in_specs[-1]
        strip = pltpu.VMEM((width // LANES, 2 * step, LANES), jnp.float32)
        scratch += [
            pltpu.VMEM((len(used), window, block), jnp.bfloat16),
            strip,
            strip,
            pltpu.SemaphoreType.DMA((len(used),)),
            pltpu.SemaphoreType.DMA,
            pltpu.VMEM(sums_shape, jnp.float32),
        ]
    else:
        out_shape, out_spec = jax.ShapeDtypeStruct(sums_shape, jnp.float32), sums_spec
    return pl.pallas_call(
        kernel,
        out_shape=out_shape,
        grid_spec=pltpu.PrefetchScalarGridSpec(
            num_scalar_prefetch=1,
            grid=(1,),
            in_specs=in_specs,
            out_specs=out_spec,
            scratch_shapes=scratch,
        ),
        compiler_params=pltpu.CompilerParams(vmem_limit_bytes=52 << 20),
        cost_estimate=pl.CostEstimate(
            flops=2 * taps * window * width * depth,
            bytes_accessed=20 << 20,
            transcendentals=0,
        ),
        name="input_grad_late" if last else "input_grad_early",
    )(place, *operands)


def input_gradient_unaligned(place, inputs, grads, parts, taps, reps):
    seqs = len(grads)
    window, block = grads[0].shape
    coarse, width = window - 2 * HALO, inputs.shape[2]
    rows = width // reps
    grad = jnp.zeros((window, seqs * block), jnp.bfloat16)
    for distance in range(seqs):
        spot = (0, (place[0] ^ distance) * block)
        grad = lax.dynamic_update_slice(grad, grads[distance], spot)
    kernel = jnp.zeros((taps, width, seqs * block), jnp.bfloat16)
    for first_tap, entries in parts:
        for array, at, distance, owner in entries:
            row = owner_of(owner, place[1]) * rows
            spot = (first_tap, row, (place[0] ^ distance) * block)
            kernel = lax.dynamic_update_slice(kernel, array[at], spot)
    products = lax.dot_general(
        grad, kernel, (((1,), (2,)), ((), ())), preferred_element_type=jnp.float32
    )
    totals = []
    for parity in range(2):
        total = 0.0
        for k in range(taps):
            start = HALO + ROW_OFFSETS[k][parity]
            total = total + products[start : start + coarse, k]
        totals.append(total)
    total = jnp.stack(totals, axis=1).reshape(inputs.shape[1:])
    slope = gelu_slope(inputs[0].astype(jnp.float32))
    skip = jnp.repeat(grad[HALO : HALO + coarse, :width].astype(jnp.float32), 2, axis=0)
    return (0.5 * (total * slope + skip)).astype(jnp.bfloat16)[None]


def on_device(inputs, trunk_grad, weights):
    seqs, reps = lax.axis_size("seq"), lax.axis_size("rep")
    me, rep = lax.axis_index("seq"), lax.axis_index("rep")
    place = jnp.stack([me, rep]).astype(jnp.int32)
    taps, rows, block = weights.shape
    fine, width = inputs.shape[1:]
    coarse, planes = fine // 2, reps // 2
    aligned = block % LANES == 0

    last_taps = weights[SPLIT:]
    across = jnp.stack(
        [last_taps] + [from_peer(last_taps, "seq", d) for d in range(1, seqs)]
    )
    last = lax.all_gather(across, "rep")
    last_entries = [(last, (r, d), d, r) for r in range(reps) for d in range(seqs)]

    act = {0: (activate(inputs),)}
    act.update(gather_near(act[0][0], "seq"))
    near = [act[d][0] for d in act if d]
    act.update(gather_far(act, "seq", across))
    far = [part for d in act if len(act[d]) == 2 for part in act[d]]

    trunk = trunk_grad[0]
    edged = after(jnp.pad(trunk, ((HALO, HALO), (0, 0))), *near)
    grads = []
    for distance in range(seqs):
        window = lax.dynamic_slice_in_dim(edged, (me ^ distance) * coarse, coarse + 2 * HALO, 0)
        grads.append(from_peer(window, "seq", distance) if distance else window)

    first = lax.all_gather(weights[:SPLIT], "rep")
    column = lax.dynamic_index_in_dim(
        first.reshape(planes, 2, *first.shape[1:]), rep % 2, 1, keepdims=False
    )
    column = after(column, *far, *grads[1:])
    kept = {0: (column,)}
    kept.update(gather_near(column, "seq"))
    kept.update(gather_far(kept, "seq"))
    first_entries = [(first, r, 0, r) for r in range(reps)]
    for distance, parts in kept.items():
        plane = 0
        for part in parts if distance else ():
            other = from_peer(part, "rep", 1)
            for at in range(part.shape[0]):
                first_entries.append((part, at, distance, (plane, 0)))
                first_entries.append((other, at, distance, (plane, 1)))
                plane += 1

    zeros = jnp.zeros((1, block), jnp.bfloat16)
    later = jnp.concatenate([trunk[1:], zeros])
    earlier = jnp.concatenate([zeros, trunk[:-1]])
    shifts = jnp.concatenate([later, trunk, earlier], axis=1)
    scale = 0.5 * float(fine * seqs * reps) ** (-0.5)
    if aligned:
        soon = {d: act[d] for d in act if len(act[d]) == 1}
        rest = {d: act[d] for d in act if len(act[d]) == 2}
        early = early_terms(place, soon, shifts, coarse)
        mine, theirs = late_terms(place, rest, shifts, early, coarse, scale, planes, taps, rows)
    else:
        mine, theirs = terms_unaligned(place, act, shifts, coarse, scale, planes, taps, rows)
    arrived = from_peer(theirs, "rep", 1)
    summed = [mine[j] + arrived[j].astype(jnp.float32) for j in range(planes)]
    weight_grad = reduce_line(summed, "rep", planes, 2)

    if aligned:
        soon = [entry for entry in first_entries if len(kept[entry[2]]) == 1]
        rest = [entry for entry in first_entries if len(kept[entry[2]]) == 2]
        sums = input_terms(place, grads, last_entries, SPLIT, None, None, reps)
        sums = input_terms(place, grads, soon, 0, sums, None, reps)
        input_grad = input_terms(place, grads, rest, 0, sums, inputs, reps)
    else:
        parts = ((0, first_entries), (SPLIT, last_entries))
        input_grad = input_gradient_unaligned(place, inputs, grads, parts, taps, reps)
    return (input_grad, weight_grad)


def solution(mesh):
    in_specs = (P("rep", "seq", None), P("rep", None, "seq"), P(None, "rep", "seq"))
    out_specs = (P("rep", "seq", None), P(None, "rep", "seq"))
    return jax.shard_map(
        on_device, mesh=mesh, in_specs=in_specs, out_specs=out_specs, check_vma=False
    )
```

```python
import functools
import math

import jax
import jax.numpy as jnp
from jax import lax
from jax.experimental import pallas as pl
from jax.experimental.pallas import tpu as pltpu
from jax.sharding import PartitionSpec as P

HALO = 8
LANES = 128
SPLIT = 3
ROOT = math.sqrt(2.0 / math.pi)
CUBIC = 0.044715
ANYWHERE = pl.BlockSpec(memory_space=pl.ANY)
ROW_OFFSETS = ((1, 1), (0, 1), (0, 0), (-1, 0), (-1, -1))
GRAD_PARTS = ((0, 0), (1, 0), (1, 1), (2, 1), (2, 2))


def from_peer(value, axis, distance):
    peers = lax.axis_size(axis)
    return lax.ppermute(value, axis, [(i, i ^ distance) for i in range(peers)])


def after(value, *earlier):
    return pl.pallas_call(
        lambda *refs: None,
        out_shape=jax.ShapeDtypeStruct(value.shape, value.dtype),
        in_specs=[ANYWHERE] * (1 + len(earlier)),
        out_specs=ANYWHERE,
        input_output_aliases={0: 0},
        name="after",
    )(value, *earlier)


def half_of(piece, which):
    if len(piece) == 2:
        return piece[which]
    size = piece[0].shape[0] // 2
    return lax.slice_in_dim(piece[0], which * size, (which + 1) * size, axis=0)


def gather_near(value, axis):
    distances = [d for d in range(1, lax.axis_size(axis)) if d & (d - 1) == 0]
    return {d: (from_peer(value, axis, d),) for d in distances}


def gather_far(found, axis, *earlier):
    far = {}
    for distance in range(1, lax.axis_size(axis)):
        high = 1 << (distance.bit_length() - 1)
        low = distance & -distance
        if high != low:
            known = {**found, **far}
            halves = half_of(known[distance ^ high], 0), half_of(known[distance ^ low], 1)
            if earlier:
                halves = [after(half, *earlier) for half in halves]
            far[distance] = (from_peer(halves[0], axis, high), from_peer(halves[1], axis, low))
    return far


def line_masks(count):
    masks = []
    while count > 1:
        masks.append(count - 1)
        count //= 2
    return masks


def reduce_line(blocks, axis, count, unit):
    held, masks = [[0]], line_masks(count)
    for mask in masks:
        held.append(held[-1] + [d ^ mask for d in held[-1]])
    blocks = dict(enumerate(blocks))
    for mask, keep in reversed(list(zip(masks, held))):
        leaving = jnp.stack([blocks[d ^ mask].astype(jnp.bfloat16) for d in keep])
        arrived = from_peer(leaving, axis, mask * unit)
        blocks = {d: blocks[d] + arrived[n].astype(jnp.float32) for n, d in enumerate(keep)}
    return blocks[0]


def gelu_slope(x):
    tanh = jnp.tanh(ROOT * (x + CUBIC * (x * x * x)))
    return 0.5 * (1.0 + tanh) + 0.5 * x * (1.0 - tanh * tanh) * (
        ROOT * (1.0 + 3.0 * CUBIC * (x * x))
    )


def act_kernel(x_ref, out_ref, scratch):
    width = x_ref.shape[2]

    @pl.loop(0, out_ref.shape[0] // 64)
    def _(step):
        start = pl.multiple_of(step * 64, 64)
        x = x_ref[0, pl.ds(pl.multiple_of(2 * start, 128), 128), :].astype(jnp.float32)
        act = x * (0.5 * (1.0 + jnp.tanh(ROOT * (x + CUBIC * (x * x * x)))))
        for c in range(width // LANES):
            scratch[c] = act[:, c * LANES : (c + 1) * LANES]
        for parity in range(2):
            for c in range(width // LANES):
                picked = scratch[c, pl.ds(parity, 64, stride=2), :].astype(jnp.bfloat16)
                left = parity * width + c * LANES
                out_ref[pl.ds(start, 64), left : left + LANES] = picked


def activate(inputs):
    fine, width = inputs.shape[1:]
    return pl.pallas_call(
        act_kernel,
        out_shape=jax.ShapeDtypeStruct((fine // 2, 2 * width), jnp.bfloat16),
        in_specs=[pl.BlockSpec(memory_space=pltpu.VMEM)],
        out_specs=pl.BlockSpec(memory_space=pltpu.VMEM),
        scratch_shapes=[pltpu.VMEM((width // LANES, 128, LANES), jnp.float32)],
        compiler_params=pltpu.CompilerParams(vmem_limit_bytes=24 << 20),
        name="act",
    )(inputs)


def act_layout(act):
    layout, pieces = [], []
    for distance, parts in act.items():
        first = 0
        for part in parts:
            layout.append((distance, first, part.shape[0]))
            pieces.append(part)
            first += part.shape[0]
    return layout, pieces


def start_act(place, coarse, layout, pieces, shifts_ref, held, shifts, sems, shift_sems):
    copies, row = [], 0
    for i, (distance, first, size) in enumerate(layout):
        start = pl.multiple_of((place[0] ^ distance) * coarse + first, 16)
        spot = pl.ds(row, size)
        copies.append(pltpu.make_async_copy(pieces[i], held.at[spot], sems.at[i]))
        copies.append(
            pltpu.make_async_copy(shifts_ref.at[pl.ds(start, size)], shifts.at[spot], shift_sems.at[i])
        )
        row += size
    for copy in copies:
        copy.start()
    return copies


def early_terms(place, act, shifts, coarse):
    layout, pieces = act_layout(act)
    both, columns = pieces[0].shape[1], shifts.shape[1]
    rows = sum(size for _, _, size in layout)
    tile = 256

    def kernel(place, shifts_ref, *refs):
        pieces, total = refs[: len(layout)], refs[len(layout)]
        held, shifts, sems, shift_sems = refs[len(layout) + 1 :]
        copies = start_act(
            place, coarse, layout, pieces, shifts_ref, held, shifts, sems, shift_sems
        )
        for copy in copies:
            copy.wait()

        @pl.loop(0, both // tile)
        def _(i):
            span = pl.ds(pl.multiple_of(i * tile, tile), tile)
            total[span, :] = lax.dot_general(
                held[:, span], shifts[...], (((0,), (0,)), ((), ())), preferred_element_type=jnp.float32
            )

    return pl.pallas_call(
        kernel,
        out_shape=jax.ShapeDtypeStruct((both, columns), jnp.float32),
        grid_spec=pltpu.PrefetchScalarGridSpec(
            num_scalar_prefetch=1,
            grid=(1,),
            in_specs=[ANYWHERE] * (1 + len(pieces)),
            out_specs=pl.BlockSpec((both, columns), lambda i, place: (0, 0)),
            scratch_shapes=[
                pltpu.VMEM((rows, both), jnp.bfloat16),
                pltpu.VMEM((rows, columns), jnp.bfloat16),
                pltpu.SemaphoreType.DMA((len(pieces),)),
                pltpu.SemaphoreType.DMA((len(pieces),)),
            ],
        ),
        compiler_params=pltpu.CompilerParams(vmem_limit_bytes=48 << 20),
        cost_estimate=pl.CostEstimate(
            flops=2 * rows * both * columns, bytes_accessed=16 << 20, transcendentals=0
        ),
        name="weight_grad_early",
    )(place, shifts, *pieces)


def late_terms(place, act, shifts, early, coarse, scale, planes, taps, rows):
    layout, pieces = act_layout(act)
    both, columns = early.shape
    width, block = both // 2, columns // 3
    count = sum(size for _, _, size in layout)
    tile = 256
    shape = (planes, taps, rows, block)

    def kernel(place, shifts_ref, early_ref, *refs):
        pieces, (mine_ref, theirs_ref) = refs[: len(layout)], refs[len(layout) : len(layout) + 2]
        held, shifts, total, sems, shift_sems, early_sems = refs[len(layout) + 2 :]
        core, plane = place[1] % 2, place[1] // 2
        copies = start_act(
            place, coarse, layout, pieces, shifts_ref, held, shifts, sems, shift_sems
        )

        def fetch(i):
            span = pl.ds(pl.multiple_of(i * tile, tile), tile)
            return pltpu.make_async_copy(early_ref.at[span], total.at[span], early_sems.at[i])

        for i in range(both // tile):
            fetch(i).start()
        for copy in copies:
            copy.wait()

        @pl.loop(0, both // tile)
        def _(i):
            span = pl.ds(pl.multiple_of(i * tile, tile), tile)
            term = lax.dot_general(
                held[:, span], shifts[...], (((0,), (0,)), ((), ())), preferred_element_type=jnp.float32
            )
            fetch(i).wait()
            total[span, :] += term

        for out_ref, parity, kind in (
            (theirs_ref, 1 - core, jnp.bfloat16),
            (mine_ref, core, jnp.float32),
        ):

            @pl.loop(0, planes)
            def _(j):
                start = ((plane ^ j) * 2 + parity) * rows
                even = pl.ds(pl.multiple_of(start, 16), rows)
                odd = pl.ds(pl.multiple_of(width + start, 16), rows)
                for k, (left, right) in enumerate(GRAD_PARTS):
                    term = total[even, left * block : (left + 1) * block]
                    term += total[odd, right * block : (right + 1) * block]
                    out_ref[j, k] = (scale * term).astype(kind)

    whole = pl.BlockSpec(shape, lambda i, place: (0, 0, 0, 0))
    return pl.pallas_call(
        kernel,
        out_shape=(
            jax.ShapeDtypeStruct(shape, jnp.float32),
            jax.ShapeDtypeStruct(shape, jnp.bfloat16),
        ),
        grid_spec=pltpu.PrefetchScalarGridSpec(
            num_scalar_prefetch=1,
            grid=(1,),
            in_specs=[ANYWHERE] * (2 + len(pieces)),
            out_specs=[whole, whole],
            scratch_shapes=[
                pltpu.VMEM((count, both), jnp.bfloat16),
                pltpu.VMEM((count, columns), jnp.bfloat16),
                pltpu.VMEM((both, columns), jnp.float32),
                pltpu.SemaphoreType.DMA((len(pieces),)),
                pltpu.SemaphoreType.DMA((len(pieces),)),
                pltpu.SemaphoreType.DMA((both // tile,)),
            ],
        ),
        compiler_params=pltpu.CompilerParams(vmem_limit_bytes=48 << 20),
        cost_estimate=pl.CostEstimate(
            flops=2 * count * both * columns, bytes_accessed=16 << 20, transcendentals=0
        ),
        name="weight_grad_late",
    )(place, shifts, early, *pieces)


def terms_unaligned(place, act, shifts, coarse, scale, planes, taps, rows):
    both = act[0][0].shape[1]
    width, block = both // 2, shifts.shape[1] // 3
    total = jnp.zeros((both, shifts.shape[1]), jnp.float32)
    for (distance, first, size), part in zip(*act_layout(act)):
        start = (place[0] ^ distance) * coarse + first
        matching = lax.dynamic_slice_in_dim(shifts, start, size, 0)
        total = total + lax.dot_general(
            part, matching, (((0,), (0,)), ((), ())), preferred_element_type=jnp.float32
        )
    terms = []
    for left, right in GRAD_PARTS:
        even = total[:width, left * block : (left + 1) * block]
        odd = total[width:, right * block : (right + 1) * block]
        terms.append(scale * (even + odd))
    terms = jnp.stack(terms).reshape(taps, planes, 2, rows, block)
    core, plane = place[1] % 2, place[1] // 2
    outs = []
    for parity in (core, 1 - core):
        blocks = lax.dynamic_index_in_dim(terms, parity, 2, keepdims=False)
        picked = [
            lax.dynamic_index_in_dim(blocks, plane ^ j, 1, keepdims=False) for j in range(planes)
        ]
        outs.append(jnp.stack(picked))
    return outs[0], outs[1].astype(jnp.bfloat16)


def shifted_total(products, first_tap, taps, base, step, lanes, parity):
    total = None
    for by in (0, 1, -1):
        wanted = [k for k in range(taps) if ROW_OFFSETS[first_tap + k][parity] == by]
        if wanted:
            part = sum(products[k, pl.ds(base, step + 2 * HALO), lanes] for k in wanted)
            part = part[HALO + by : HALO + by + step]
            total = part if total is None else total + part
    return total


def start_products(place, own, kernel_ref, gv, wv, sems, grad_sems):
    seqs, block = len(own), own[0].shape[1]
    for distance in range(seqs):
        spot = pl.ds(pl.multiple_of((place[0] ^ distance) * block, block), block)
        pltpu.make_async_copy(own[distance], gv.at[:, spot], grad_sems.at[distance]).start()
    for k in range(wv.shape[0]):
        for s in range(seqs):
            kernel_copy(kernel_ref, wv, sems, k, s, block).start()


def kernel_copy(kernel_ref, wv, sems, k, s, block):
    target = wv.at[k, :, :, pl.ds(s * block, block)]
    return pltpu.make_async_copy(kernel_ref.at[:, s, k], target, sems.at[k, s])


def finish_products(own, kernel_ref, gv, wv, products, sems, grad_sems):
    seqs, block = len(own), own[0].shape[1]
    taps, reps, rows, depth = wv.shape
    for distance in range(seqs):
        spot = pl.ds(distance * block, block)
        pltpu.make_async_copy(own[distance], gv.at[:, spot], grad_sems.at[distance]).wait()
    tile = reps // 2

    @pl.loop(0, taps)
    def _(k):
        for s in range(seqs):
            kernel_copy(kernel_ref, wv, sems, k, s, block).wait()
        for part in range(2):
            kernel = wv[k, part * tile : (part + 1) * tile].reshape(tile * rows, depth)
            products[k, :, part * tile * rows : (part + 1) * tile * rows] = lax.dot_general(
                gv[...], kernel, (((1,), (1,)), ((), ())), preferred_element_type=jnp.float32
            )


STEP = 64


def early_gradient(place, inputs, grads, kernel, first_tap):
    window, block = grads[0].shape
    coarse, width = window - 2 * HALO, inputs.shape[2]
    reps, seqs, taps, rows, _ = kernel.shape
    depth, shape = seqs * block, (2, coarse, width)

    def body(place, x_ref, *refs):
        own, kernel_ref, out_ref, slope_ref = refs[:seqs], refs[seqs], refs[seqs + 1], refs[seqs + 2]
        wv, gv, products, strip, sems, grad_sems = refs[seqs + 3 :]
        start_products(place, own, kernel_ref, gv, wv, sems, grad_sems)
        finish_products(own, kernel_ref, gv, wv, products, sems, grad_sems)

        @pl.loop(0, coarse // STEP)
        def _(i):
            base = pl.multiple_of(i * STEP, STEP)
            spot, span = pl.ds(base, STEP), pl.ds(pl.multiple_of(2 * base, 2 * STEP), 2 * STEP)
            for c in range(width // LANES):
                lanes = slice(c * LANES, (c + 1) * LANES)
                strip[c] = 0.5 * gelu_slope(x_ref[0, span, lanes].astype(jnp.float32))
                skip = gv[pl.ds(base, STEP + 2 * HALO), lanes].astype(jnp.float32)
                skip = 0.5 * skip[HALO : HALO + STEP]
                for parity in range(2):
                    slope = strip[c, pl.ds(parity, STEP, stride=2), :]
                    total = shifted_total(products, first_tap, taps, base, STEP, lanes, parity)
                    slope_ref[parity, spot, lanes] = slope
                    out_ref[parity, spot, lanes] = total * slope + skip

    whole = pl.BlockSpec(shape, lambda i, place: (0, 0, 0))
    return pl.pallas_call(
        body,
        out_shape=[jax.ShapeDtypeStruct(shape, jnp.float32)] * 2,
        grid_spec=pltpu.PrefetchScalarGridSpec(
            num_scalar_prefetch=1,
            grid=(1,),
            in_specs=[pl.BlockSpec(inputs.shape, lambda i, place: (0, 0, 0))]
            + [ANYWHERE] * (seqs + 1),
            out_specs=[whole, whole],
            scratch_shapes=[
                pltpu.VMEM((taps, reps, rows, depth), jnp.bfloat16),
                pltpu.VMEM((window, depth), jnp.bfloat16),
                pltpu.VMEM((taps, window, width), jnp.float32),
                pltpu.VMEM((width // LANES, 2 * STEP, LANES), jnp.float32),
                pltpu.SemaphoreType.DMA((taps, seqs)),
                pltpu.SemaphoreType.DMA((seqs,)),
            ],
        ),
        compiler_params=pltpu.CompilerParams(vmem_limit_bytes=52 << 20),
        cost_estimate=pl.CostEstimate(
            flops=2 * taps * window * width * depth, bytes_accessed=20 << 20, transcendentals=0
        ),
        name="input_grad_early",
    )(place, inputs, *grads, kernel)


def late_gradient(place, grads, kernel, first_tap, begun, slope, like):
    window, block = grads[0].shape
    coarse, width = window - 2 * HALO, like.shape[2]
    reps, seqs, taps, rows, _ = kernel.shape
    depth, shape = seqs * block, (2, coarse, width)

    def body(place, *refs):
        own, kernel_ref, begun_ref, slope_ref, out_ref = refs[:seqs], *refs[seqs : seqs + 4]
        wv, gv, products, begun, slope, strip, sems, grad_sems, early_sems = refs[seqs + 4 :]
        start_products(place, own, kernel_ref, gv, wv, sems, grad_sems)
        copies = [
            pltpu.make_async_copy(begun_ref, begun, early_sems.at[0]),
            pltpu.make_async_copy(slope_ref, slope, early_sems.at[1]),
        ]
        for copy in copies:
            copy.start()
        finish_products(own, kernel_ref, gv, wv, products, sems, grad_sems)
        for copy in copies:
            copy.wait()

        @pl.loop(0, coarse // STEP)
        def _(i):
            base = pl.multiple_of(i * STEP, STEP)
            spot, span = pl.ds(base, STEP), pl.ds(pl.multiple_of(2 * base, 2 * STEP), 2 * STEP)
            for c in range(width // LANES):
                lanes = slice(c * LANES, (c + 1) * LANES)
                for parity in range(2):
                    total = shifted_total(products, first_tap, taps, base, STEP, lanes, parity)
                    strip[c, pl.ds(parity, STEP, stride=2), :] = (
                        begun[parity, spot, lanes] + total * slope[parity, spot, lanes]
                    )
                out_ref[0, span, lanes] = strip[c].astype(jnp.bfloat16)

    return pl.pallas_call(
        body,
        out_shape=jax.ShapeDtypeStruct(like.shape, jnp.bfloat16),
        grid_spec=pltpu.PrefetchScalarGridSpec(
            num_scalar_prefetch=1,
            grid=(1,),
            in_specs=[ANYWHERE] * (seqs + 3),
            out_specs=pl.BlockSpec(like.shape, lambda i, place: (0, 0, 0)),
            scratch_shapes=[
                pltpu.VMEM((taps, reps, rows, depth), jnp.bfloat16),
                pltpu.VMEM((window, depth), jnp.bfloat16),
                pltpu.VMEM((taps, window, width), jnp.float32),
                pltpu.VMEM(shape, jnp.float32),
                pltpu.VMEM(shape, jnp.float32),
                pltpu.VMEM((width // LANES, 2 * STEP, LANES), jnp.float32),
                pltpu.SemaphoreType.DMA((taps, seqs)),
                pltpu.SemaphoreType.DMA((seqs,)),
                pltpu.SemaphoreType.DMA((2,)),
            ],
        ),
        compiler_params=pltpu.CompilerParams(vmem_limit_bytes=52 << 20),
        cost_estimate=pl.CostEstimate(
            flops=2 * taps * window * width * depth, bytes_accessed=20 << 20, transcendentals=0
        ),
        name="input_grad_late",
    )(place, *grads, kernel, begun, slope)


def input_gradient_unaligned(place, inputs, grads, kernel):
    seqs = len(grads)
    window, block = grads[0].shape
    coarse, width = window - 2 * HALO, inputs.shape[2]
    grad = jnp.zeros((window, seqs * block), jnp.bfloat16)
    for distance in range(seqs):
        spot = (0, (place[0] ^ distance) * block)
        grad = lax.dynamic_update_slice(grad, grads[distance], spot)
    taps = kernel.shape[2]
    kernel = kernel.transpose(2, 0, 3, 1, 4).reshape(taps, width, seqs * block)
    products = lax.dot_general(
        grad, kernel, (((1,), (2,)), ((), ())), preferred_element_type=jnp.float32
    )
    totals = []
    for parity in range(2):
        total = 0.0
        for k in range(taps):
            start = HALO + ROW_OFFSETS[k][parity]
            total = total + products[start : start + coarse, k]
        totals.append(total)
    total = jnp.stack(totals, axis=1).reshape(inputs.shape[1:])
    slope = gelu_slope(inputs[0].astype(jnp.float32))
    skip = jnp.repeat(grad[HALO : HALO + coarse, :width].astype(jnp.float32), 2, axis=0)
    return (0.5 * (total * slope + skip)).astype(jnp.bfloat16)[None]


def on_device(inputs, trunk_grad, weights):
    seqs, reps = lax.axis_size("seq"), lax.axis_size("rep")
    me, rep = lax.axis_index("seq"), lax.axis_index("rep")
    place = jnp.stack([me, rep]).astype(jnp.int32)
    taps, rows, block = weights.shape
    fine, width = inputs.shape[1:]
    coarse, planes = fine // 2, reps // 2
    aligned = block % LANES == 0

    first = lax.all_gather(weights[:SPLIT], ("rep", "seq")).reshape(reps, seqs, SPLIT, rows, block)
    last = lax.all_gather(weights[SPLIT:], ("rep", "seq"))
    last = last.reshape(reps, seqs, taps - SPLIT, rows, block)

    act = {0: (activate(inputs),)}
    act.update(gather_near(act[0][0], "seq"))
    near = [act[d][0] for d in act if d]
    act.update(gather_far(act, "seq"))

    trunk = trunk_grad[0]
    edged = after(jnp.pad(trunk, ((HALO, HALO), (0, 0))), *near)
    grads = []
    for distance in range(seqs):
        window = lax.dynamic_slice_in_dim(edged, (me ^ distance) * coarse, coarse + 2 * HALO, 0)
        grads.append(from_peer(window, "seq", distance) if distance else window)

    zeros = jnp.zeros((1, block), jnp.bfloat16)
    later = jnp.concatenate([trunk[1:], zeros])
    earlier = jnp.concatenate([zeros, trunk[:-1]])
    shifts = jnp.concatenate([later, trunk, earlier], axis=1)
    scale = 0.5 * float(fine * seqs * reps) ** (-0.5)
    if aligned:
        soon = {d: act[d] for d in act if len(act[d]) == 1}
        rest = {d: act[d] for d in act if len(act[d]) == 2}
        early = early_terms(place, soon, shifts, coarse)
        mine, theirs = late_terms(place, rest, shifts, early, coarse, scale, planes, taps, rows)
    else:
        mine, theirs = terms_unaligned(place, act, shifts, coarse, scale, planes, taps, rows)
    arrived = from_peer(theirs, "rep", 1)
    summed = [mine[j] + arrived[j].astype(jnp.float32) for j in range(planes)]
    weight_grad = reduce_line(summed, "rep", planes, 2)

    if aligned:
        begun, slope = early_gradient(place, inputs, grads, first, 0)
        input_grad = late_gradient(place, grads, last, SPLIT, begun, slope, inputs)
    else:
        kernel = jnp.concatenate([first, last], axis=2)
        input_grad = input_gradient_unaligned(place, inputs, grads, kernel)
    return (input_grad, weight_grad)


def solution(mesh):
    in_specs = (P("rep", "seq", None), P("rep", None, "seq"), P(None, "rep", "seq"))
    out_specs = (P("rep", "seq", None), P(None, "rep", "seq"))
    return jax.shard_map(
        on_device, mesh=mesh, in_specs=in_specs, out_specs=out_specs, check_vma=False
    )
```

```python
import functools
import math

import jax
import jax.numpy as jnp
from jax import lax
from jax.experimental import pallas as pl
from jax.experimental.pallas import tpu as pltpu
from jax.sharding import PartitionSpec as P

HALO = 8
LANES = 128
SPLIT = 3
ROOT = math.sqrt(2.0 / math.pi)
CUBIC = 0.044715
ANYWHERE = pl.BlockSpec(memory_space=pl.ANY)
ROW_OFFSETS = ((1, 1), (0, 1), (0, 0), (-1, 0), (-1, -1))
GRAD_PARTS = ((0, 0), (1, 0), (1, 1), (2, 1), (2, 2))


def from_peer(value, axis, distance):
    peers = lax.axis_size(axis)
    return lax.ppermute(value, axis, [(i, i ^ distance) for i in range(peers)])


def after(value, *earlier):
    return pl.pallas_call(
        lambda *refs: None,
        out_shape=jax.ShapeDtypeStruct(value.shape, value.dtype),
        in_specs=[ANYWHERE] * (1 + len(earlier)),
        out_specs=ANYWHERE,
        input_output_aliases={0: 0},
        name="after",
    )(value, *earlier)


def half_of(piece, which):
    if len(piece) == 2:
        return piece[which]
    size = piece[0].shape[0] // 2
    return lax.slice_in_dim(piece[0], which * size, (which + 1) * size, axis=0)


def gather_near(value, axis):
    distances = [d for d in range(1, lax.axis_size(axis)) if d & (d - 1) == 0]
    return {d: (from_peer(value, axis, d),) for d in distances}


def gather_far(found, axis, *earlier):
    far = {}
    for distance in range(1, lax.axis_size(axis)):
        high = 1 << (distance.bit_length() - 1)
        low = distance & -distance
        if high != low:
            known = {**found, **far}
            halves = half_of(known[distance ^ high], 0), half_of(known[distance ^ low], 1)
            if earlier:
                halves = [after(half, *earlier) for half in halves]
            far[distance] = (from_peer(halves[0], axis, high), from_peer(halves[1], axis, low))
    return far


def line_masks(count):
    masks = []
    while count > 1:
        masks.append(count - 1)
        count //= 2
    return masks


def reduce_line(blocks, axis, count, unit):
    held, masks = [[0]], line_masks(count)
    for mask in masks:
        held.append(held[-1] + [d ^ mask for d in held[-1]])
    blocks = dict(enumerate(blocks))
    for mask, keep in reversed(list(zip(masks, held))):
        leaving = jnp.stack([blocks[d ^ mask].astype(jnp.bfloat16) for d in keep])
        arrived = from_peer(leaving, axis, mask * unit)
        blocks = {d: blocks[d] + arrived[n].astype(jnp.float32) for n, d in enumerate(keep)}
    return blocks[0]


def gelu_slope(x):
    tanh = jnp.tanh(ROOT * (x + CUBIC * (x * x * x)))
    return 0.5 * (1.0 + tanh) + 0.5 * x * (1.0 - tanh * tanh) * (
        ROOT * (1.0 + 3.0 * CUBIC * (x * x))
    )


def act_kernel(x_ref, out_ref, scratch):
    width = x_ref.shape[2]

    @pl.loop(0, out_ref.shape[0] // 64)
    def _(step):
        start = pl.multiple_of(step * 64, 64)
        x = x_ref[0, pl.ds(pl.multiple_of(2 * start, 128), 128), :].astype(jnp.float32)
        act = x * (0.5 * (1.0 + jnp.tanh(ROOT * (x + CUBIC * (x * x * x)))))
        for c in range(width // LANES):
            scratch[c] = act[:, c * LANES : (c + 1) * LANES]
        for parity in range(2):
            for c in range(width // LANES):
                picked = scratch[c, pl.ds(parity, 64, stride=2), :].astype(jnp.bfloat16)
                left = parity * width + c * LANES
                out_ref[pl.ds(start, 64), left : left + LANES] = picked


def activate(inputs):
    fine, width = inputs.shape[1:]
    return pl.pallas_call(
        act_kernel,
        out_shape=jax.ShapeDtypeStruct((fine // 2, 2 * width), jnp.bfloat16),
        in_specs=[pl.BlockSpec(memory_space=pltpu.VMEM)],
        out_specs=pl.BlockSpec(memory_space=pltpu.VMEM),
        scratch_shapes=[pltpu.VMEM((width // LANES, 128, LANES), jnp.float32)],
        compiler_params=pltpu.CompilerParams(vmem_limit_bytes=24 << 20),
        name="act",
    )(inputs)


def act_layout(act):
    layout, pieces = [], []
    for distance, parts in act.items():
        first = 0
        for part in parts:
            layout.append((distance, first, part.shape[0]))
            pieces.append(part)
            first += part.shape[0]
    return layout, pieces


def start_act(place, coarse, layout, pieces, shifts_ref, held, shifts, sems, shift_sems):
    copies, row = [], 0
    for i, (distance, first, size) in enumerate(layout):
        start = pl.multiple_of((place[0] ^ distance) * coarse + first, 16)
        spot = pl.ds(row, size)
        copies.append(pltpu.make_async_copy(pieces[i], held.at[spot], sems.at[i]))
        copies.append(
            pltpu.make_async_copy(shifts_ref.at[pl.ds(start, size)], shifts.at[spot], shift_sems.at[i])
        )
        row += size
    for copy in copies:
        copy.start()
    return copies


def early_terms(place, act, shifts, coarse):
    layout, pieces = act_layout(act)
    both, columns = pieces[0].shape[1], shifts.shape[1]
    rows = sum(size for _, _, size in layout)
    tile = 256

    def kernel(place, shifts_ref, *refs):
        pieces, total = refs[: len(layout)], refs[len(layout)]
        held, shifts, sems, shift_sems = refs[len(layout) + 1 :]
        copies = start_act(
            place, coarse, layout, pieces, shifts_ref, held, shifts, sems, shift_sems
        )
        for copy in copies:
            copy.wait()

        @pl.loop(0, both // tile)
        def _(i):
            span = pl.ds(pl.multiple_of(i * tile, tile), tile)
            total[span, :] = lax.dot_general(
                held[:, span], shifts[...], (((0,), (0,)), ((), ())), preferred_element_type=jnp.float32
            )

    return pl.pallas_call(
        kernel,
        out_shape=jax.ShapeDtypeStruct((both, columns), jnp.float32),
        grid_spec=pltpu.PrefetchScalarGridSpec(
            num_scalar_prefetch=1,
            grid=(1,),
            in_specs=[ANYWHERE] * (1 + len(pieces)),
            out_specs=pl.BlockSpec((both, columns), lambda i, place: (0, 0)),
            scratch_shapes=[
                pltpu.VMEM((rows, both), jnp.bfloat16),
                pltpu.VMEM((rows, columns), jnp.bfloat16),
                pltpu.SemaphoreType.DMA((len(pieces),)),
                pltpu.SemaphoreType.DMA((len(pieces),)),
            ],
        ),
        compiler_params=pltpu.CompilerParams(vmem_limit_bytes=48 << 20),
        cost_estimate=pl.CostEstimate(
            flops=2 * rows * both * columns, bytes_accessed=16 << 20, transcendentals=0
        ),
        name="weight_grad_early",
    )(place, shifts, *pieces)


def late_terms(place, act, shifts, early, coarse, scale, planes, taps, rows):
    layout, pieces = act_layout(act)
    both, columns = early.shape
    width, block = both // 2, columns // 3
    count = sum(size for _, _, size in layout)
    tile = 256
    shape = (planes, taps, rows, block)

    def kernel(place, shifts_ref, early_ref, *refs):
        pieces, (mine_ref, theirs_ref) = refs[: len(layout)], refs[len(layout) : len(layout) + 2]
        held, shifts, total, sems, shift_sems, early_sems = refs[len(layout) + 2 :]
        core, plane = place[1] % 2, place[1] // 2
        copies = start_act(
            place, coarse, layout, pieces, shifts_ref, held, shifts, sems, shift_sems
        )

        def fetch(i):
            span = pl.ds(pl.multiple_of(i * tile, tile), tile)
            return pltpu.make_async_copy(early_ref.at[span], total.at[span], early_sems.at[i])

        for i in range(both // tile):
            fetch(i).start()
        for copy in copies:
            copy.wait()

        @pl.loop(0, both // tile)
        def _(i):
            span = pl.ds(pl.multiple_of(i * tile, tile), tile)
            term = lax.dot_general(
                held[:, span], shifts[...], (((0,), (0,)), ((), ())), preferred_element_type=jnp.float32
            )
            fetch(i).wait()
            total[span, :] += term

        for out_ref, parity, kind in (
            (theirs_ref, 1 - core, jnp.bfloat16),
            (mine_ref, core, jnp.float32),
        ):

            @pl.loop(0, planes)
            def _(j):
                start = ((plane ^ j) * 2 + parity) * rows
                even = pl.ds(pl.multiple_of(start, 16), rows)
                odd = pl.ds(pl.multiple_of(width + start, 16), rows)
                for k, (left, right) in enumerate(GRAD_PARTS):
                    term = total[even, left * block : (left + 1) * block]
                    term += total[odd, right * block : (right + 1) * block]
                    out_ref[j, k] = (scale * term).astype(kind)

    whole = pl.BlockSpec(shape, lambda i, place: (0, 0, 0, 0))
    return pl.pallas_call(
        kernel,
        out_shape=(
            jax.ShapeDtypeStruct(shape, jnp.float32),
            jax.ShapeDtypeStruct(shape, jnp.bfloat16),
        ),
        grid_spec=pltpu.PrefetchScalarGridSpec(
            num_scalar_prefetch=1,
            grid=(1,),
            in_specs=[ANYWHERE] * (2 + len(pieces)),
            out_specs=[whole, whole],
            scratch_shapes=[
                pltpu.VMEM((count, both), jnp.bfloat16),
                pltpu.VMEM((count, columns), jnp.bfloat16),
                pltpu.VMEM((both, columns), jnp.float32),
                pltpu.SemaphoreType.DMA((len(pieces),)),
                pltpu.SemaphoreType.DMA((len(pieces),)),
                pltpu.SemaphoreType.DMA((both // tile,)),
            ],
        ),
        compiler_params=pltpu.CompilerParams(vmem_limit_bytes=48 << 20),
        cost_estimate=pl.CostEstimate(
            flops=2 * count * both * columns, bytes_accessed=16 << 20, transcendentals=0
        ),
        name="weight_grad_late",
    )(place, shifts, early, *pieces)


def terms_unaligned(place, act, shifts, coarse, scale, planes, taps, rows):
    both = act[0][0].shape[1]
    width, block = both // 2, shifts.shape[1] // 3
    total = jnp.zeros((both, shifts.shape[1]), jnp.float32)
    for (distance, first, size), part in zip(*act_layout(act)):
        start = (place[0] ^ distance) * coarse + first
        matching = lax.dynamic_slice_in_dim(shifts, start, size, 0)
        total = total + lax.dot_general(
            part, matching, (((0,), (0,)), ((), ())), preferred_element_type=jnp.float32
        )
    terms = []
    for left, right in GRAD_PARTS:
        even = total[:width, left * block : (left + 1) * block]
        odd = total[width:, right * block : (right + 1) * block]
        terms.append(scale * (even + odd))
    terms = jnp.stack(terms).reshape(taps, planes, 2, rows, block)
    core, plane = place[1] % 2, place[1] // 2
    outs = []
    for parity in (core, 1 - core):
        blocks = lax.dynamic_index_in_dim(terms, parity, 2, keepdims=False)
        picked = [
            lax.dynamic_index_in_dim(blocks, plane ^ j, 1, keepdims=False) for j in range(planes)
        ]
        outs.append(jnp.stack(picked))
    return outs[0], outs[1].astype(jnp.bfloat16)


STEP = 64


def shifted_total(products, first_tap, taps, base, lanes, parity):
    total = None
    for by in (0, 1, -1):
        wanted = [k for k in range(taps) if ROW_OFFSETS[first_tap + k][parity] == by]
        if wanted:
            part = sum(products[k, pl.ds(base, STEP + 2 * HALO), lanes] for k in wanted)
            part = part[HALO + by : HALO + by + STEP]
            total = part if total is None else total + part
    return total


def gradient_stage(place, grads, run, pieces, begun, inputs, shape, last):
    first_tap, taps = run
    window, block = grads[0].shape
    _, fine, width = shape
    coarse, seqs = fine // 2, len(grads)
    rows = pieces[0][0].shape[-2]
    planes = width // (2 * rows)
    whole = pieces[0][3] is None
    distances = list(range(seqs)) if whole else sorted({piece[3] for piece in pieces})
    depth, planar = len(distances) * block, (2, coarse, width)
    used = list(range(seqs)) if inputs is not None else distances
    shown = width // block
    operands = [grads[d] for d in used] + [piece[0] for piece in pieces]
    operands += list(begun) if begun else [inputs]

    def body(place, *refs):
        own, refs = refs[: len(used)], refs[len(used) :]
        sources, refs = refs[: len(pieces)], refs[len(pieces) :]
        if begun:
            begun_ref, slope_ref, out_ref = refs[:3]
            wv, gv, products, strip, sems, grad_sems, sums, slopes, sum_sems = refs[3:]
        else:
            x_ref, out_ref, slope_ref = refs[:3]
            wv, gv, products, strip, sems, grad_sems, skips, skip_sems = refs[3:]
        me, core = place[0], place[1] % 2

        def kernel_copy(number, k, s=None):
            array, plane, flip, distance = pieces[number]
            ref = sources[number]
            if whole:
                spot = pl.ds(s * block, block)
                return pltpu.make_async_copy(
                    ref.at[:, :, s, k], wv.at[k, :, :, :, spot], sems.at[k, number * seqs + s]
                )
            spot = pl.ds(distances.index(distance) * block, block)
            if flip is None:
                target = wv.at[k, :, :, :, spot]
                return pltpu.make_async_copy(ref.at[:, :, k], target, sems.at[k, number])
            span = pl.ds(plane, array.shape[0])
            target = wv.at[k, span, core ^ flip, :, spot]
            return pltpu.make_async_copy(ref.at[:, k], target, sems.at[k, number])

        def kernel_copies(k):
            for number in range(len(pieces)):
                for s in range(seqs) if whole else (None,):
                    yield kernel_copy(number, k, s)

        early, late = [], []
        for slot, distance in enumerate(distances):
            left = (me ^ distance) * block if whole else slot * block
            spot = pl.ds(pl.multiple_of(left, block), block)
            source = own[used.index(distance)]
            early.append(pltpu.make_async_copy(source, gv.at[:, spot], grad_sems.at[slot]))
        if begun:
            late.append(pltpu.make_async_copy(begun_ref, sums, sum_sems.at[0]))
            late.append(pltpu.make_async_copy(slope_ref, slopes, sum_sems.at[1]))
        else:
            for d in used:
                late.append(pltpu.make_async_copy(own[d], skips.at[me ^ d], skip_sems.at[d]))
        for copy in early:
            copy.start()
        for k in range(taps):
            for copy in kernel_copies(k):
                copy.start()
        for copy in late:
            copy.start()
        for copy in early:
            copy.wait()

        @pl.loop(0, taps)
        def _(k):
            for copy in kernel_copies(k):
                copy.wait()
            span = planes // 2 * 2 * rows
            for part in range(2):
                kernel = wv[k, part * (planes // 2) : (part + 1) * (planes // 2)]
                products[k, :, part * span : (part + 1) * span] = lax.dot_general(
                    gv[...],
                    kernel.reshape(span, depth),
                    (((1,), (1,)), ((), ())),
                    preferred_element_type=jnp.float32,
                )

        for copy in late:
            copy.wait()

        @pl.loop(0, coarse // STEP)
        def _(i):
            base = pl.multiple_of(i * STEP, STEP)
            spot, span = pl.ds(base, STEP), pl.ds(pl.multiple_of(2 * base, 2 * STEP), 2 * STEP)
            for c in range(width // LANES):
                lanes = slice(c * LANES, (c + 1) * LANES)
                if not begun:
                    strip[c] = 0.5 * gelu_slope(x_ref[0, span, lanes].astype(jnp.float32))
                    left = c * LANES % block
                    skip = skips[
                        c * LANES // block, pl.ds(base, STEP + 2 * HALO), left : left + LANES
                    ].astype(jnp.float32)
                    skip = 0.5 * skip[HALO : HALO + STEP]
                for parity in range(2):
                    total = shifted_total(products, first_tap, taps, base, lanes, parity)
                    if begun:
                        total = sums[parity, spot, lanes] + total * slopes[parity, spot, lanes]
                    else:
                        slope = strip[c, pl.ds(parity, STEP, stride=2), :]
                        slope_ref[parity, spot, lanes] = slope
                        total = total * slope + skip
                    if last:
                        strip[c, pl.ds(parity, STEP, stride=2), :] = total
                    else:
                        out_ref[parity, spot, lanes] = total
                if last:
                    out_ref[0, span, lanes] = strip[c].astype(jnp.bfloat16)

    block_of = lambda shape: pl.BlockSpec(shape, lambda i, place: (0, 0, 0))
    in_specs = [ANYWHERE] * (len(used) + len(pieces))
    scratch = [
        pltpu.VMEM((taps, planes, 2, rows, depth), jnp.bfloat16),
        pltpu.VMEM((window, depth), jnp.bfloat16),
        pltpu.VMEM((taps, window, width), jnp.float32),
        pltpu.VMEM((width // LANES, 2 * STEP, LANES), jnp.float32),
        pltpu.SemaphoreType.DMA((taps, len(pieces) * (seqs if whole else 1))),
        pltpu.SemaphoreType.DMA((len(distances),)),
    ]
    planes_out = jax.ShapeDtypeStruct(planar, jnp.float32)
    if begun:
        in_specs += [ANYWHERE] * 2
        scratch += [
            pltpu.VMEM(planar, jnp.float32),
            pltpu.VMEM(planar, jnp.float32),
            pltpu.SemaphoreType.DMA((2,)),
        ]
    else:
        in_specs.append(block_of(shape))
        scratch += [
            pltpu.VMEM((seqs, window, block), jnp.bfloat16),
            pltpu.SemaphoreType.DMA((seqs,)),
        ]
    if last:
        out_shape, out_specs = jax.ShapeDtypeStruct(shape, jnp.bfloat16), block_of(shape)
    elif begun:
        out_shape, out_specs = planes_out, block_of(planar)
    else:
        out_shape, out_specs = [planes_out] * 2, [block_of(planar)] * 2
    return pl.pallas_call(
        body,
        out_shape=out_shape,
        grid_spec=pltpu.PrefetchScalarGridSpec(
            num_scalar_prefetch=1,
            grid=(1,),
            in_specs=in_specs,
            out_specs=out_specs,
            scratch_shapes=scratch,
        ),
        compiler_params=pltpu.CompilerParams(vmem_limit_bytes=56 << 20),
        cost_estimate=pl.CostEstimate(
            flops=2 * taps * window * width * depth, bytes_accessed=20 << 20, transcendentals=0
        ),
        name="input_grad",
    )(place, *operands)


def input_gradient_unaligned(place, inputs, grads, kernel):
    seqs = len(grads)
    window, block = grads[0].shape
    coarse, width = window - 2 * HALO, inputs.shape[2]
    grad = jnp.zeros((window, seqs * block), jnp.bfloat16)
    for distance in range(seqs):
        spot = (0, (place[0] ^ distance) * block)
        grad = lax.dynamic_update_slice(grad, grads[distance], spot)
    taps = kernel.shape[2]
    kernel = kernel.transpose(2, 0, 3, 1, 4).reshape(taps, width, seqs * block)
    products = lax.dot_general(
        grad, kernel, (((1,), (2,)), ((), ())), preferred_element_type=jnp.float32
    )
    totals = []
    for parity in range(2):
        total = 0.0
        for k in range(taps):
            start = HALO + ROW_OFFSETS[k][parity]
            total = total + products[start : start + coarse, k]
        totals.append(total)
    total = jnp.stack(totals, axis=1).reshape(inputs.shape[1:])
    slope = gelu_slope(inputs[0].astype(jnp.float32))
    skip = jnp.repeat(grad[HALO : HALO + coarse, :width].astype(jnp.float32), 2, axis=0)
    return (0.5 * (total * slope + skip)).astype(jnp.bfloat16)[None]


def on_device(inputs, trunk_grad, weights):
    seqs, reps = lax.axis_size("seq"), lax.axis_size("rep")
    me, rep = lax.axis_index("seq"), lax.axis_index("rep")
    place = jnp.stack([me, rep]).astype(jnp.int32)
    taps, rows, block = weights.shape
    fine, width = inputs.shape[1:]
    coarse, planes = fine // 2, reps // 2
    aligned = block % LANES == 0

    first = lax.all_gather(weights[:SPLIT], "rep").reshape(planes, 2, SPLIT, rows, block)
    last = lax.all_gather(weights[SPLIT:], ("rep", "seq"))
    last = last.reshape(planes, 2, seqs, taps - SPLIT, rows, block)

    act = {0: (activate(inputs),)}
    act.update(gather_near(act[0][0], "seq"))
    near = [act[d][0] for d in act if d]
    act.update(gather_far(act, "seq"))
    far = [part for d in act if len(act[d]) == 2 for part in act[d]]

    trunk = trunk_grad[0]
    edged = after(jnp.pad(trunk, ((HALO, HALO), (0, 0))), *near)
    grads = []
    for distance in range(seqs):
        window = lax.dynamic_slice_in_dim(edged, (me ^ distance) * coarse, coarse + 2 * HALO, 0)
        grads.append(from_peer(window, "seq", distance) if distance else window)

    column = lax.dynamic_index_in_dim(first, rep % 2, 1, keepdims=False)
    column = after(column, *grads[1:])
    kept = {0: (column,)}
    kept.update(gather_near(column, "seq"))
    kept.update(gather_far(kept, "seq"))
    soon, rest = [(first, 0, None, 0)], []
    for distance, parts in kept.items():
        plane = 0
        for part in parts if distance else ():
            share = soon if len(parts) == 1 else rest
            share.append((part, plane, 0, distance))
            share.append((from_peer(part, "rep", 1), plane, 1, distance))
            plane += part.shape[0]

    zeros = jnp.zeros((1, block), jnp.bfloat16)
    later = jnp.concatenate([trunk[1:], zeros])
    earlier = jnp.concatenate([zeros, trunk[:-1]])
    shifts = jnp.concatenate([later, trunk, earlier], axis=1)
    scale = 0.5 * float(fine * seqs * reps) ** (-0.5)
    if aligned:
        near = {d: act[d] for d in act if len(act[d]) == 1}
        far = {d: tuple(after(p, *grads[1:]) for p in act[d]) for d in act if len(act[d]) == 2}
        early = early_terms(place, near, shifts, coarse)
        mine, theirs = late_terms(place, far, shifts, early, coarse, scale, planes, taps, rows)
    else:
        mine, theirs = terms_unaligned(place, act, shifts, coarse, scale, planes, taps, rows)
    arrived = from_peer(theirs, "rep", 1)
    summed = [mine[j] + arrived[j].astype(jnp.float32) for j in range(planes)]
    weight_grad = reduce_line(summed, "rep", planes, 2)

    if aligned:
        stage = functools.partial(gradient_stage, place, grads, shape=inputs.shape)
        begun, slope = stage((0, SPLIT), soon, None, inputs, last=False)
        begun = stage((SPLIT, taps - SPLIT), [(last, 0, None, None)], (begun, slope), None, last=False)
        input_grad = stage((0, SPLIT), rest, (begun, slope), None, last=True)
    else:
        kernel = jnp.zeros((planes, 2, seqs, SPLIT, rows, block), jnp.bfloat16)
        for part, plane, flip, distance in soon + rest:
            part = part if flip is None else part[:, None]
            spot = (plane, 0 if flip is None else rep % 2 ^ flip, me ^ distance, 0, 0, 0)
            kernel = lax.dynamic_update_slice(kernel, part[:, :, None], spot)
        kernel = jnp.concatenate([kernel, last], axis=3).reshape(reps, seqs, taps, rows, block)
        input_grad = input_gradient_unaligned(place, inputs, grads, kernel)
    return (input_grad, weight_grad)


def solution(mesh):
    in_specs = (P("rep", "seq", None), P("rep", None, "seq"), P(None, "rep", "seq"))
    out_specs = (P("rep", "seq", None), P(None, "rep", "seq"))
    return jax.shard_map(
        on_device, mesh=mesh, in_specs=in_specs, out_specs=out_specs, check_vma=False
    )
```

```python
import functools
import math

import jax
import jax.numpy as jnp
from jax import lax
from jax.experimental import pallas as pl
from jax.experimental.pallas import tpu as pltpu
from jax.sharding import PartitionSpec as P

HALO = 8
LANES = 128
SPLIT = 3
ROOT = math.sqrt(2.0 / math.pi)
CUBIC = 0.044715
ANYWHERE = pl.BlockSpec(memory_space=pl.ANY)
ROW_OFFSETS = ((1, 1), (0, 1), (0, 0), (-1, 0), (-1, -1))
GRAD_PARTS = ((0, 0), (1, 0), (1, 1), (2, 1), (2, 2))


def from_peer(value, axis, distance):
    peers = lax.axis_size(axis)
    return lax.ppermute(value, axis, [(i, i ^ distance) for i in range(peers)])


def after(value, *earlier):
    return pl.pallas_call(
        lambda *refs: None,
        out_shape=jax.ShapeDtypeStruct(value.shape, value.dtype),
        in_specs=[ANYWHERE] * (1 + len(earlier)),
        out_specs=ANYWHERE,
        input_output_aliases={0: 0},
        name="after",
    )(value, *earlier)


def half_of(piece, which):
    if len(piece) == 2:
        return piece[which]
    size = piece[0].shape[0] // 2
    return lax.slice_in_dim(piece[0], which * size, (which + 1) * size, axis=0)


def gather_near(value, axis):
    distances = [d for d in range(1, lax.axis_size(axis)) if d & (d - 1) == 0]
    return {d: (from_peer(value, axis, d),) for d in distances}


def gather_far(found, axis, *earlier):
    far = {}
    for distance in range(1, lax.axis_size(axis)):
        high = 1 << (distance.bit_length() - 1)
        low = distance & -distance
        if high != low:
            known = {**found, **far}
            halves = half_of(known[distance ^ high], 0), half_of(known[distance ^ low], 1)
            if earlier:
                halves = [after(half, *earlier) for half in halves]
            far[distance] = (from_peer(halves[0], axis, high), from_peer(halves[1], axis, low))
    return far


def line_masks(count):
    masks = []
    while count > 1:
        masks.append(count - 1)
        count //= 2
    return masks


def reduce_line(blocks, axis, count, unit):
    held, masks = [[0]], line_masks(count)
    for mask in masks:
        held.append(held[-1] + [d ^ mask for d in held[-1]])
    blocks = dict(enumerate(blocks))
    for mask, keep in reversed(list(zip(masks, held))):
        leaving = jnp.stack([blocks[d ^ mask].astype(jnp.bfloat16) for d in keep])
        arrived = from_peer(leaving, axis, mask * unit)
        blocks = {d: blocks[d] + arrived[n].astype(jnp.float32) for n, d in enumerate(keep)}
    return blocks[0]


def gelu_slope(x):
    tanh = jnp.tanh(ROOT * (x + CUBIC * (x * x * x)))
    return 0.5 * (1.0 + tanh) + 0.5 * x * (1.0 - tanh * tanh) * (
        ROOT * (1.0 + 3.0 * CUBIC * (x * x))
    )


def act_kernel(x_ref, out_ref, scratch):
    width = x_ref.shape[2]

    @pl.loop(0, out_ref.shape[0] // 64)
    def _(step):
        start = pl.multiple_of(step * 64, 64)
        x = x_ref[0, pl.ds(pl.multiple_of(2 * start, 128), 128), :].astype(jnp.float32)
        act = x * (0.5 * (1.0 + jnp.tanh(ROOT * (x + CUBIC * (x * x * x)))))
        for c in range(width // LANES):
            scratch[c] = act[:, c * LANES : (c + 1) * LANES]
        for parity in range(2):
            for c in range(width // LANES):
                picked = scratch[c, pl.ds(parity, 64, stride=2), :].astype(jnp.bfloat16)
                left = parity * width + c * LANES
                out_ref[pl.ds(start, 64), left : left + LANES] = picked


def activate(inputs):
    fine, width = inputs.shape[1:]
    return pl.pallas_call(
        act_kernel,
        out_shape=jax.ShapeDtypeStruct((fine // 2, 2 * width), jnp.bfloat16),
        in_specs=[pl.BlockSpec(memory_space=pltpu.VMEM)],
        out_specs=pl.BlockSpec(memory_space=pltpu.VMEM),
        scratch_shapes=[pltpu.VMEM((width // LANES, 128, LANES), jnp.float32)],
        compiler_params=pltpu.CompilerParams(vmem_limit_bytes=24 << 20),
        name="act",
    )(inputs)


def slope_kernel(x_ref, out_ref, scratch):
    width = x_ref.shape[2]

    @pl.loop(0, out_ref.shape[1] // 64)
    def _(step):
        start = pl.multiple_of(step * 64, 64)
        span = pl.ds(pl.multiple_of(2 * start, 128), 128)
        for c in range(width // LANES):
            lanes = slice(c * LANES, (c + 1) * LANES)
            scratch[c] = 0.5 * gelu_slope(x_ref[0, span, lanes].astype(jnp.float32))
            for parity in range(2):
                out_ref[parity, pl.ds(start, 64), lanes] = scratch[c, pl.ds(parity, 64, stride=2), :]


def half_slope(inputs):
    fine, width = inputs.shape[1:]
    return pl.pallas_call(
        slope_kernel,
        out_shape=jax.ShapeDtypeStruct((2, fine // 2, width), jnp.float32),
        in_specs=[pl.BlockSpec(memory_space=pltpu.VMEM)],
        out_specs=pl.BlockSpec(memory_space=pltpu.VMEM),
        scratch_shapes=[pltpu.VMEM((width // LANES, 128, LANES), jnp.float32)],
        compiler_params=pltpu.CompilerParams(vmem_limit_bytes=24 << 20),
        name="half_slope",
    )(inputs)


def act_layout(act):
    layout, pieces = [], []
    for distance, parts in act.items():
        first = 0
        for part in parts:
            layout.append((distance, first, part.shape[0]))
            pieces.append(part)
            first += part.shape[0]
    return layout, pieces


def start_act(place, coarse, layout, pieces, shifts_ref, held, shifts, sems, shift_sems):
    copies, row = [], 0
    for i, (distance, first, size) in enumerate(layout):
        start = pl.multiple_of((place[0] ^ distance) * coarse + first, 16)
        spot = pl.ds(row, size)
        copies.append(pltpu.make_async_copy(pieces[i], held.at[spot], sems.at[i]))
        copies.append(
            pltpu.make_async_copy(shifts_ref.at[pl.ds(start, size)], shifts.at[spot], shift_sems.at[i])
        )
        row += size
    for copy in copies:
        copy.start()
    return copies


def early_terms(place, act, shifts, coarse):
    layout, pieces = act_layout(act)
    both, columns = pieces[0].shape[1], shifts.shape[1]
    rows = sum(size for _, _, size in layout)
    tile = 256

    def kernel(place, shifts_ref, *refs):
        pieces, total = refs[: len(layout)], refs[len(layout)]
        held, shifts, sems, shift_sems = refs[len(layout) + 1 :]
        copies = start_act(
            place, coarse, layout, pieces, shifts_ref, held, shifts, sems, shift_sems
        )
        for copy in copies:
            copy.wait()

        @pl.loop(0, both // tile)
        def _(i):
            span = pl.ds(pl.multiple_of(i * tile, tile), tile)
            total[span, :] = lax.dot_general(
                held[:, span], shifts[...], (((0,), (0,)), ((), ())), preferred_element_type=jnp.float32
            )

    return pl.pallas_call(
        kernel,
        out_shape=jax.ShapeDtypeStruct((both, columns), jnp.float32),
        grid_spec=pltpu.PrefetchScalarGridSpec(
            num_scalar_prefetch=1,
            grid=(1,),
            in_specs=[ANYWHERE] * (1 + len(pieces)),
            out_specs=pl.BlockSpec((both, columns), lambda i, place: (0, 0)),
            scratch_shapes=[
                pltpu.VMEM((rows, both), jnp.bfloat16),
                pltpu.VMEM((rows, columns), jnp.bfloat16),
                pltpu.SemaphoreType.DMA((len(pieces),)),
                pltpu.SemaphoreType.DMA((len(pieces),)),
            ],
        ),
        compiler_params=pltpu.CompilerParams(vmem_limit_bytes=48 << 20),
        cost_estimate=pl.CostEstimate(
            flops=2 * rows * both * columns, bytes_accessed=16 << 20, transcendentals=0
        ),
        name="weight_grad_early",
    )(place, shifts, *pieces)


def late_terms(place, act, shifts, early, coarse, scale, planes, taps, rows):
    layout, pieces = act_layout(act)
    both, columns = early.shape
    width, block = both // 2, columns // 3
    count = sum(size for _, _, size in layout)
    tile = 256
    shape = (planes, taps, rows, block)

    def kernel(place, shifts_ref, early_ref, *refs):
        pieces, (mine_ref, theirs_ref) = refs[: len(layout)], refs[len(layout) : len(layout) + 2]
        held, shifts, total, sems, shift_sems, early_sems = refs[len(layout) + 2 :]
        core, plane = place[1] % 2, place[1] // 2
        copies = start_act(
            place, coarse, layout, pieces, shifts_ref, held, shifts, sems, shift_sems
        )

        def fetch(i):
            span = pl.ds(pl.multiple_of(i * tile, tile), tile)
            return pltpu.make_async_copy(early_ref.at[span], total.at[span], early_sems.at[i])

        for i in range(both // tile):
            fetch(i).start()
        for copy in copies:
            copy.wait()

        @pl.loop(0, both // tile)
        def _(i):
            span = pl.ds(pl.multiple_of(i * tile, tile), tile)
            term = lax.dot_general(
                held[:, span], shifts[...], (((0,), (0,)), ((), ())), preferred_element_type=jnp.float32
            )
            fetch(i).wait()
            total[span, :] += term

        for out_ref, parity, kind in (
            (theirs_ref, 1 - core, jnp.bfloat16),
            (mine_ref, core, jnp.float32),
        ):

            @pl.loop(0, planes)
            def _(j):
                start = ((plane ^ j) * 2 + parity) * rows
                even = pl.ds(pl.multiple_of(start, 16), rows)
                odd = pl.ds(pl.multiple_of(width + start, 16), rows)
                for k, (left, right) in enumerate(GRAD_PARTS):
                    term = total[even, left * block : (left + 1) * block]
                    term += total[odd, right * block : (right + 1) * block]
                    out_ref[j, k] = (scale * term).astype(kind)

    whole = pl.BlockSpec(shape, lambda i, place: (0, 0, 0, 0))
    return pl.pallas_call(
        kernel,
        out_shape=(
            jax.ShapeDtypeStruct(shape, jnp.float32),
            jax.ShapeDtypeStruct(shape, jnp.bfloat16),
        ),
        grid_spec=pltpu.PrefetchScalarGridSpec(
            num_scalar_prefetch=1,
            grid=(1,),
            in_specs=[ANYWHERE] * (2 + len(pieces)),
            out_specs=[whole, whole],
            scratch_shapes=[
                pltpu.VMEM((count, both), jnp.bfloat16),
                pltpu.VMEM((count, columns), jnp.bfloat16),
                pltpu.VMEM((both, columns), jnp.float32),
                pltpu.SemaphoreType.DMA((len(pieces),)),
                pltpu.SemaphoreType.DMA((len(pieces),)),
                pltpu.SemaphoreType.DMA((both // tile,)),
            ],
        ),
        compiler_params=pltpu.CompilerParams(vmem_limit_bytes=48 << 20),
        cost_estimate=pl.CostEstimate(
            flops=2 * count * both * columns, bytes_accessed=16 << 20, transcendentals=0
        ),
        name="weight_grad_late",
    )(place, shifts, early, *pieces)


def terms_unaligned(place, act, shifts, coarse, scale, planes, taps, rows):
    both = act[0][0].shape[1]
    width, block = both // 2, shifts.shape[1] // 3
    total = jnp.zeros((both, shifts.shape[1]), jnp.float32)
    for (distance, first, size), part in zip(*act_layout(act)):
        start = (place[0] ^ distance) * coarse + first
        matching = lax.dynamic_slice_in_dim(shifts, start, size, 0)
        total = total + lax.dot_general(
            part, matching, (((0,), (0,)), ((), ())), preferred_element_type=jnp.float32
        )
    terms = []
    for left, right in GRAD_PARTS:
        even = total[:width, left * block : (left + 1) * block]
        odd = total[width:, right * block : (right + 1) * block]
        terms.append(scale * (even + odd))
    terms = jnp.stack(terms).reshape(taps, planes, 2, rows, block)
    core, plane = place[1] % 2, place[1] // 2
    outs = []
    for parity in (core, 1 - core):
        blocks = lax.dynamic_index_in_dim(terms, parity, 2, keepdims=False)
        picked = [
            lax.dynamic_index_in_dim(blocks, plane ^ j, 1, keepdims=False) for j in range(planes)
        ]
        outs.append(jnp.stack(picked))
    return outs[0], outs[1].astype(jnp.bfloat16)


STEP = 64


def shifted_total(products, first_tap, taps, base, lanes, parity):
    total = None
    for by in (0, 1, -1):
        wanted = [k for k in range(taps) if ROW_OFFSETS[first_tap + k][parity] == by]
        if wanted:
            part = sum(products[k, pl.ds(base, STEP + 2 * HALO), lanes] for k in wanted)
            part = part[HALO + by : HALO + by + STEP]
            total = part if total is None else total + part
    return total


def gradient_stage(place, grads, run, pieces, slope, begun, shape):
    first_tap, taps = run
    window, block = grads[0].shape
    _, fine, width = shape
    coarse, seqs = fine // 2, len(grads)
    rows = pieces[0][0].shape[-2]
    planes = width // (2 * rows)
    whole = pieces[0][3] is None
    depth, planar = seqs * block, (2, coarse, width)
    last = begun is not None
    operands = [*grads, *(piece[0] for piece in pieces), slope] + ([begun] if last else [])

    def body(place, *refs):
        own, refs = refs[:seqs], refs[seqs:]
        sources, refs = refs[: len(pieces)], refs[len(pieces) :]
        slope_ref, refs = refs[0], refs[1:]
        if last:
            begun_ref, refs = refs[0], refs[1:]
        out_ref, wv, gv, products, slopes, sems, grad_sems, slope_sem = refs[:8]
        me, core = place[0], place[1] % 2

        def left_of(distance):
            return pl.multiple_of((me ^ distance) * block, block)

        def kernel_copies(k):
            for number, (array, plane, flip, distance) in enumerate(pieces):
                ref = sources[number]
                if whole:
                    for s in range(seqs):
                        target = wv.at[k, :, :, :, pl.ds(s * block, block)]
                        yield ref.at[:, :, s, k], target, sems.at[k, number * seqs + s]
                elif flip is None:
                    target = wv.at[k, :, :, :, pl.ds(left_of(distance), block)]
                    yield ref.at[:, :, k], target, sems.at[k, number]
                else:
                    span = pl.ds(plane, array.shape[0])
                    target = wv.at[k, span, core ^ flip, :, pl.ds(left_of(distance), block)]
                    yield ref.at[:, k], target, sems.at[k, number]

        def grad_copy(d):
            target = gv.at[:, pl.ds(left_of(d), block)]
            return pltpu.make_async_copy(own[d], target, grad_sems.at[d])

        late = [pltpu.make_async_copy(slope_ref, slopes, slope_sem)]
        if last:
            sums, strip, sum_sem = refs[8:]
            late.append(pltpu.make_async_copy(begun_ref, sums, sum_sem))
        for d in range(seqs):
            grad_copy(d).start()
        for k in range(taps):
            for copy in kernel_copies(k):
                pltpu.make_async_copy(*copy).start()
        for copy in late:
            copy.start()
        for d in range(seqs):
            grad_copy(d).wait()

        @pl.loop(0, taps)
        def _(k):
            for copy in kernel_copies(k):
                pltpu.make_async_copy(*copy).wait()
            span = planes // 2 * 2 * rows
            for part in range(2):
                kernel = wv[k, part * (planes // 2) : (part + 1) * (planes // 2)]
                products[k, :, part * span : (part + 1) * span] = lax.dot_general(
                    gv[...],
                    kernel.reshape(span, depth),
                    (((1,), (1,)), ((), ())),
                    preferred_element_type=jnp.float32,
                )

        for copy in late:
            copy.wait()

        @pl.loop(0, coarse // STEP)
        def _(i):
            base = pl.multiple_of(i * STEP, STEP)
            spot, span = pl.ds(base, STEP), pl.ds(pl.multiple_of(2 * base, 2 * STEP), 2 * STEP)
            for c in range(width // LANES):
                lanes = slice(c * LANES, (c + 1) * LANES)
                if not last:
                    skip = gv[pl.ds(base, STEP + 2 * HALO), lanes].astype(jnp.float32)
                    skip = 0.5 * skip[HALO : HALO + STEP]
                for parity in range(2):
                    total = shifted_total(products, first_tap, taps, base, lanes, parity)
                    total = total * slopes[parity, spot, lanes]
                    if last:
                        total = total + sums[parity, spot, lanes]
                        strip[c, pl.ds(parity, STEP, stride=2), :] = total
                    else:
                        out_ref[parity, spot, lanes] = total + skip
                if last:
                    out_ref[0, span, lanes] = strip[c].astype(jnp.bfloat16)

    out_shape = jax.ShapeDtypeStruct(shape if last else planar, jnp.bfloat16 if last else jnp.float32)
    scratch = [
        pltpu.VMEM((taps, planes, 2, rows, depth), jnp.bfloat16),
        pltpu.VMEM((window, depth), jnp.bfloat16),
        pltpu.VMEM((taps, window, width), jnp.float32),
        pltpu.VMEM(planar, jnp.float32),
        pltpu.SemaphoreType.DMA((taps, len(pieces) * (seqs if whole else 1))),
        pltpu.SemaphoreType.DMA((seqs,)),
        pltpu.SemaphoreType.DMA,
    ]
    if last:
        scratch += [
            pltpu.VMEM(planar, jnp.float32),
            pltpu.VMEM((width // LANES, 2 * STEP, LANES), jnp.float32),
            pltpu.SemaphoreType.DMA,
        ]
    return pl.pallas_call(
        body,
        out_shape=out_shape,
        grid_spec=pltpu.PrefetchScalarGridSpec(
            num_scalar_prefetch=1,
            grid=(1,),
            in_specs=[ANYWHERE] * len(operands),
            out_specs=pl.BlockSpec(out_shape.shape, lambda i, place: (0, 0, 0)),
            scratch_shapes=scratch,
        ),
        compiler_params=pltpu.CompilerParams(vmem_limit_bytes=56 << 20),
        cost_estimate=pl.CostEstimate(
            flops=2 * taps * window * width * depth, bytes_accessed=20 << 20, transcendentals=0
        ),
        name="input_grad",
    )(place, *operands)


def input_gradient_unaligned(place, inputs, grads, kernel):
    seqs = len(grads)
    window, block = grads[0].shape
    coarse, width = window - 2 * HALO, inputs.shape[2]
    grad = jnp.zeros((window, seqs * block), jnp.bfloat16)
    for distance in range(seqs):
        spot = (0, (place[0] ^ distance) * block)
        grad = lax.dynamic_update_slice(grad, grads[distance], spot)
    taps = kernel.shape[2]
    kernel = kernel.transpose(2, 0, 3, 1, 4).reshape(taps, width, seqs * block)
    products = lax.dot_general(
        grad, kernel, (((1,), (2,)), ((), ())), preferred_element_type=jnp.float32
    )
    totals = []
    for parity in range(2):
        total = 0.0
        for k in range(taps):
            start = HALO + ROW_OFFSETS[k][parity]
            total = total + products[start : start + coarse, k]
        totals.append(total)
    total = jnp.stack(totals, axis=1).reshape(inputs.shape[1:])
    slope = gelu_slope(inputs[0].astype(jnp.float32))
    skip = jnp.repeat(grad[HALO : HALO + coarse, :width].astype(jnp.float32), 2, axis=0)
    return (0.5 * (total * slope + skip)).astype(jnp.bfloat16)[None]


def on_device(inputs, trunk_grad, weights):
    seqs, reps = lax.axis_size("seq"), lax.axis_size("rep")
    me, rep = lax.axis_index("seq"), lax.axis_index("rep")
    place = jnp.stack([me, rep]).astype(jnp.int32)
    taps, rows, block = weights.shape
    fine, width = inputs.shape[1:]
    coarse, planes = fine // 2, reps // 2
    aligned = block % LANES == 0

    first = lax.all_gather(weights[:SPLIT], "rep").reshape(planes, 2, SPLIT, rows, block)
    last = lax.all_gather(lax.all_gather(weights[SPLIT:], "seq"), "rep")
    last = last.reshape(planes, 2, seqs, taps - SPLIT, rows, block)
    slope = half_slope(inputs)

    act = {0: (activate(inputs),)}
    act.update(gather_near(act[0][0], "seq"))
    near = [act[d][0] for d in act if d]
    act.update(gather_far(act, "seq", slope))
    far = [part for d in act if len(act[d]) == 2 for part in act[d]]

    trunk = trunk_grad[0]
    edged = after(jnp.pad(trunk, ((HALO, HALO), (0, 0))), *near)
    grads = []
    for distance in range(seqs):
        window = lax.dynamic_slice_in_dim(edged, (me ^ distance) * coarse, coarse + 2 * HALO, 0)
        grads.append(from_peer(window, "seq", distance) if distance else window)

    column = lax.dynamic_index_in_dim(first, rep % 2, 1, keepdims=False)
    column = after(column, *grads[1:])
    kept = {0: (column,)}
    kept.update(gather_near(column, "seq"))
    kept.update(gather_far(kept, "seq"))
    pieces = [(first, 0, None, 0)]
    for distance, parts in kept.items():
        plane = 0
        for part in parts if distance else ():
            pieces.append((part, plane, 0, distance))
            pieces.append((from_peer(part, "rep", 1), plane, 1, distance))
            plane += part.shape[0]

    zeros = jnp.zeros((1, block), jnp.bfloat16)
    later = jnp.concatenate([trunk[1:], zeros])
    earlier = jnp.concatenate([zeros, trunk[:-1]])
    shifts = jnp.concatenate([later, trunk, earlier], axis=1)
    scale = 0.5 * float(fine * seqs * reps) ** (-0.5)
    if aligned:
        near = {d: act[d] for d in act if len(act[d]) == 1}
        far = {d: tuple(after(p, *grads[1:]) for p in act[d]) for d in act if len(act[d]) == 2}
        early = early_terms(place, near, shifts, coarse)
        mine, theirs = late_terms(place, far, shifts, early, coarse, scale, planes, taps, rows)
    else:
        mine, theirs = terms_unaligned(place, act, shifts, coarse, scale, planes, taps, rows)
    arrived = from_peer(theirs, "rep", 1)
    summed = [mine[j] + arrived[j].astype(jnp.float32) for j in range(planes)]
    weight_grad = reduce_line(summed, "rep", planes, 2)

    if aligned:
        stage = functools.partial(gradient_stage, place, grads, slope=slope, shape=inputs.shape)
        begun = stage((SPLIT, taps - SPLIT), [(last, 0, None, None)], begun=None)
        input_grad = stage((0, SPLIT), pieces, begun=begun)
    else:
        kernel = jnp.zeros((planes, 2, seqs, SPLIT, rows, block), jnp.bfloat16)
        for part, plane, flip, distance in pieces:
            part = part if flip is None else part[:, None]
            spot = (plane, 0 if flip is None else rep % 2 ^ flip, me ^ distance, 0, 0, 0)
            kernel = lax.dynamic_update_slice(kernel, part[:, :, None], spot)
        kernel = jnp.concatenate([kernel, last], axis=3).reshape(reps, seqs, taps, rows, block)
        input_grad = input_gradient_unaligned(place, inputs, grads, kernel)
    return (input_grad, weight_grad)


def solution(mesh):
    in_specs = (P("rep", "seq", None), P("rep", None, "seq"), P(None, "rep", "seq"))
    out_specs = (P("rep", "seq", None), P(None, "rep", "seq"))
    return jax.shard_map(
        on_device, mesh=mesh, in_specs=in_specs, out_specs=out_specs, check_vma=False
    )
```

```python
import functools
import math

import jax
import jax.numpy as jnp
from jax import lax
from jax.experimental import pallas as pl
from jax.experimental.pallas import tpu as pltpu
from jax.sharding import PartitionSpec as P

LANES = 128
HALO = 32
CHUNKS = 4
FIRST = 80
EDGE = 16
MARGIN = HALO - EDGE
STEP = 64
ROOT = math.sqrt(2.0 / math.pi)
CUBIC = 0.044715
ANYWHERE = pl.BlockSpec(memory_space=pl.ANY)
ROW_OFFSETS = ((1, 1), (0, 1), (0, 0), (-1, 0), (-1, -1))
GRAD_PARTS = ((0, 0), (1, 0), (1, 1), (2, 1), (2, 2))


def from_peer(value, axis, distance):
    peers = lax.axis_size(axis)
    return lax.ppermute(value, axis, [(i, i ^ distance) for i in range(peers)])


def after(value, *earlier):
    return pl.pallas_call(
        lambda *refs: None,
        out_shape=jax.ShapeDtypeStruct(value.shape, value.dtype),
        in_specs=[ANYWHERE] * (1 + len(earlier)),
        out_specs=ANYWHERE,
        input_output_aliases={0: 0},
        name="after",
    )(value, *earlier)


def gather_line(value, axis, count, unit):
    found, mask = {0: value}, count - 1
    while mask:
        for distance in list(found):
            found[distance ^ mask] = from_peer(found[distance], axis, mask * unit)
        mask //= 2
    return [found[distance] for distance in range(count)]


def gelu_slope(x):
    tanh = jnp.tanh(ROOT * (x + CUBIC * (x * x * x)))
    return 0.5 * (1.0 + tanh) + 0.5 * x * (1.0 - tanh * tanh) * (
        ROOT * (1.0 + 3.0 * CUBIC * (x * x))
    )


def messages_kernel(place, x_ref, trunk_ref, beside_ref, below_ref, own_ref, edged, strip, sem):
    coarse, width, block = x_ref.shape[1] // 2, x_ref.shape[2], edged.shape[1]
    length = trunk_ref.shape[1]
    packed = (coarse + 2 * HALO) // CHUNKS
    copy = pltpu.make_async_copy(trunk_ref.at[0], edged.at[pl.ds(HALO, length)], sem)
    copy.start()
    edged[:HALO] = jnp.zeros((HALO, block), jnp.bfloat16)
    edged[HALO + length :] = jnp.zeros((HALO, block), jnp.bfloat16)

    @pl.loop(0, coarse // STEP)
    def _(step):
        start = pl.multiple_of(step * STEP, STEP)
        x = x_ref[0, pl.ds(pl.multiple_of(2 * start, 2 * STEP), 2 * STEP), :].astype(jnp.float32)
        act = x * (0.5 * (1.0 + jnp.tanh(ROOT * (x + CUBIC * (x * x * x)))))
        for c in range(width // LANES):
            strip[c] = act[:, c * LANES : (c + 1) * LANES]
        for parity in range(2):
            for c in range(width // LANES):
                picked = strip[c, pl.ds(parity, STEP, stride=2), :].astype(jnp.bfloat16)
                lanes = slice(parity * width + c * LANES, parity * width + (c + 1) * LANES)
                beside_ref[pl.ds(FIRST + start, STEP), lanes] = picked
                below_ref[pl.ds(start, STEP), lanes] = picked

    copy.wait()

    def pack(out_ref, row, distance, first, last):
        base = (place[0] ^ distance) * coarse
        for q in range(CHUNKS):
            start = pl.multiple_of(base + q * packed + first, 16)
            out_ref[row : row + last - first, q * block : (q + 1) * block] = edged[
                pl.ds(start, last - first), :
            ]

    pack(beside_ref, 0, 3, 0, FIRST)
    pack(beside_ref, FIRST + coarse, 1, 0, packed)
    pack(below_ref, coarse, 3, FIRST, packed)
    pack(below_ref, coarse + packed - FIRST, 2, 0, packed)
    pack(own_ref, 0, 0, 0, packed)


def messages(place, inputs, trunk_grad):
    _, fine, width = inputs.shape
    _, length, block = trunk_grad.shape
    coarse = fine // 2
    packed = (coarse + 2 * HALO) // CHUNKS
    rows = (FIRST + coarse + packed, coarse + packed - FIRST + packed, packed)
    return pl.pallas_call(
        messages_kernel,
        out_shape=[jax.ShapeDtypeStruct((n, 2 * width), jnp.bfloat16) for n in rows],
        grid_spec=pltpu.PrefetchScalarGridSpec(
            num_scalar_prefetch=1,
            grid=(1,),
            in_specs=[pl.BlockSpec(inputs.shape, lambda i, place: (0, 0, 0)), ANYWHERE],
            out_specs=[pl.BlockSpec((n, 2 * width), lambda i, place: (0, 0)) for n in rows],
            scratch_shapes=[
                pltpu.VMEM((length + 2 * HALO, block), jnp.bfloat16),
                pltpu.VMEM((width // LANES, 2 * STEP, LANES), jnp.float32),
                pltpu.SemaphoreType.DMA,
            ],
        ),
        compiler_params=pltpu.CompilerParams(vmem_limit_bytes=32 << 20),
        name="messages",
    )(place, inputs, trunk_grad)


def slope_kernel(x_ref, out_ref, scratch):
    width = x_ref.shape[2]

    @pl.loop(0, out_ref.shape[1] // 64)
    def _(step):
        start = pl.multiple_of(step * 64, 64)
        span = pl.ds(pl.multiple_of(2 * start, 128), 128)
        for c in range(width // LANES):
            lanes = slice(c * LANES, (c + 1) * LANES)
            scratch[c] = 0.5 * gelu_slope(x_ref[0, span, lanes].astype(jnp.float32))
            for parity in range(2):
                out_ref[parity, pl.ds(start, 64), lanes] = scratch[c, pl.ds(parity, 64, stride=2), :]


def half_slope(inputs):
    fine, width = inputs.shape[1:]
    return pl.pallas_call(
        slope_kernel,
        out_shape=jax.ShapeDtypeStruct((2, fine // 2, width), jnp.float32),
        in_specs=[pl.BlockSpec(memory_space=pltpu.VMEM)],
        out_specs=pl.BlockSpec(memory_space=pltpu.VMEM),
        scratch_shapes=[pltpu.VMEM((width // LANES, 128, LANES), jnp.float32)],
        compiler_params=pltpu.CompilerParams(vmem_limit_bytes=24 << 20),
        name="half_slope",
    )(inputs)


def start_act(place, coarse, layout, pieces, shifts_ref, held, shifts, sems, shift_sems):
    copies, row = [], 0
    for i, (distance, first, size, offset) in enumerate(layout):
        start = pl.multiple_of((place[0] ^ distance) * coarse + first, 16)
        spot = pl.ds(row, size)
        source = pieces[i].at[pl.ds(offset, size)]
        copies.append(pltpu.make_async_copy(source, held.at[spot], sems.at[i]))
        copies.append(
            pltpu.make_async_copy(shifts_ref.at[pl.ds(start, size)], shifts.at[spot], shift_sems.at[i])
        )
        row += size
    for copy in copies:
        copy.start()
    return copies


def early_terms(place, layout, pieces, shifts, coarse):
    both, columns = pieces[0].shape[1], shifts.shape[1]
    rows = sum(size for _, _, size, _ in layout)
    tile = 256

    def kernel(place, shifts_ref, *refs):
        pieces, total = refs[: len(layout)], refs[len(layout)]
        held, shifts, sems, shift_sems = refs[len(layout) + 1 :]
        copies = start_act(
            place, coarse, layout, pieces, shifts_ref, held, shifts, sems, shift_sems
        )
        for copy in copies:
            copy.wait()

        @pl.loop(0, both // tile)
        def _(i):
            span = pl.ds(pl.multiple_of(i * tile, tile), tile)
            total[span, :] = lax.dot_general(
                held[:, span], shifts[...], (((0,), (0,)), ((), ())), preferred_element_type=jnp.float32
            )

    return pl.pallas_call(
        kernel,
        out_shape=jax.ShapeDtypeStruct((both, columns), jnp.float32),
        grid_spec=pltpu.PrefetchScalarGridSpec(
            num_scalar_prefetch=1,
            grid=(1,),
            in_specs=[ANYWHERE] * (1 + len(pieces)),
            out_specs=pl.BlockSpec((both, columns), lambda i, place: (0, 0)),
            scratch_shapes=[
                pltpu.VMEM((rows, both), jnp.bfloat16),
                pltpu.VMEM((rows, columns), jnp.bfloat16),
                pltpu.SemaphoreType.DMA((len(pieces),)),
                pltpu.SemaphoreType.DMA((len(pieces),)),
            ],
        ),
        compiler_params=pltpu.CompilerParams(vmem_limit_bytes=48 << 20),
        cost_estimate=pl.CostEstimate(
            flops=2 * rows * both * columns, bytes_accessed=16 << 20, transcendentals=0
        ),
        name="weight_grad_early",
    )(place, shifts, *pieces)


def late_terms(place, layout, pieces, shifts, early, coarse, scale, planes, taps, rows):
    both, columns = early.shape
    width, block = both // 2, columns // 3
    count = sum(size for _, _, size, _ in layout)
    tile = 256
    shape = (planes, taps, rows, block)

    def kernel(place, shifts_ref, early_ref, *refs):
        pieces, (mine_ref, theirs_ref) = refs[: len(layout)], refs[len(layout) : len(layout) + 2]
        held, shifts, total, sems, shift_sems, early_sems = refs[len(layout) + 2 :]
        core, plane = place[1] % 2, place[1] // 2
        copies = start_act(
            place, coarse, layout, pieces, shifts_ref, held, shifts, sems, shift_sems
        )

        def fetch(i):
            span = pl.ds(pl.multiple_of(i * tile, tile), tile)
            return pltpu.make_async_copy(early_ref.at[span], total.at[span], early_sems.at[i])

        for i in range(both // tile):
            fetch(i).start()
        for copy in copies:
            copy.wait()

        @pl.loop(0, both // tile)
        def _(i):
            span = pl.ds(pl.multiple_of(i * tile, tile), tile)
            term = lax.dot_general(
                held[:, span], shifts[...], (((0,), (0,)), ((), ())), preferred_element_type=jnp.float32
            )
            fetch(i).wait()
            total[span, :] += term

        for out_ref, parity, kind in (
            (theirs_ref, 1 - core, jnp.bfloat16),
            (mine_ref, core, jnp.float32),
        ):

            @pl.loop(0, planes)
            def _(j):
                start = ((plane ^ j) * 2 + parity) * rows
                even = pl.ds(pl.multiple_of(start, 16), rows)
                odd = pl.ds(pl.multiple_of(width + start, 16), rows)
                for k, (left, right) in enumerate(GRAD_PARTS):
                    term = total[even, left * block : (left + 1) * block]
                    term += total[odd, right * block : (right + 1) * block]
                    out_ref[j, k] = (scale * term).astype(kind)

    whole = pl.BlockSpec(shape, lambda i, place: (0, 0, 0, 0))
    return pl.pallas_call(
        kernel,
        out_shape=(
            jax.ShapeDtypeStruct(shape, jnp.float32),
            jax.ShapeDtypeStruct(shape, jnp.bfloat16),
        ),
        grid_spec=pltpu.PrefetchScalarGridSpec(
            num_scalar_prefetch=1,
            grid=(1,),
            in_specs=[ANYWHERE] * (2 + len(pieces)),
            out_specs=[whole, whole],
            scratch_shapes=[
                pltpu.VMEM((count, both), jnp.bfloat16),
                pltpu.VMEM((count, columns), jnp.bfloat16),
                pltpu.VMEM((both, columns), jnp.float32),
                pltpu.SemaphoreType.DMA((len(pieces),)),
                pltpu.SemaphoreType.DMA((len(pieces),)),
                pltpu.SemaphoreType.DMA((both // tile,)),
            ],
        ),
        compiler_params=pltpu.CompilerParams(vmem_limit_bytes=48 << 20),
        cost_estimate=pl.CostEstimate(
            flops=2 * count * both * columns, bytes_accessed=16 << 20, transcendentals=0
        ),
        name="weight_grad_late",
    )(place, shifts, early, *pieces)


def shifted_total(products, base, lanes, parity):
    total = None
    for by in (0, 1, -1):
        wanted = [k for k in range(products.shape[0]) if ROW_OFFSETS[k][parity] == by]
        if wanted:
            near = pl.ds(base + MARGIN - 8, STEP + 16)
            part = sum(products[k, near, lanes] for k in wanted)[8 + by : 8 + by + STEP]
            total = part if total is None else total + part
    return total


def gradient_stage(place, windows, pieces, distances, slope, begun, shape):
    _, fine, width = shape
    coarse, seqs = fine // 2, len(windows)
    taps, rows, block = pieces[0][0].shape[1:]
    planes = width // (2 * rows)
    packed = (coarse + 2 * HALO) // CHUNKS
    window, used = CHUNKS * packed, coarse + 2 * MARGIN
    depth, planar = len(distances) * block, (2, coarse, width)
    last = begun is not None
    needed = distances if last else list(range(seqs))
    parts = [(d, *part) for d in needed for part in windows[d]]
    operands = [part[1] for part in parts] + [piece[0] for piece in pieces]
    operands += [slope] + ([begun] if last else [])

    def body(place, *refs):
        own, refs = refs[: len(parts)], refs[len(parts) :]
        sources, refs = refs[: len(pieces)], refs[len(pieces) :]
        slope_ref, refs = refs[0], refs[1:]
        if last:
            begun_ref, refs = refs[0], refs[1:]
        out_ref, wv, gv, products, slopes, sems, grad_sems, slope_sem = refs[:8]
        me, core = place[0], place[1] % 2

        def kernel_copies(k):
            for number, (array, plane, flip, distance) in enumerate(pieces):
                spot = pl.ds(distances.index(distance) * block, block)
                span = pl.ds(plane, array.shape[0])
                target = wv.at[k, span, core ^ flip, :, spot]
                yield sources[number].at[:, k], target, sems.at[k, number]

        def window_copies(target_of, sems):
            for number, (distance, _, row, first, size) in enumerate(parts):
                for q in range(CHUNKS):
                    source = own[number].at[pl.ds(row, size), pl.ds(q * block, block)]
                    target = target_of(distance, pl.ds(q * packed + first, size))
                    if target is not None:
                        yield pltpu.make_async_copy(source, target, sems.at[number, q])

        def into_window(distance, span):
            if distance not in distances:
                return None
            return gv.at[span, pl.ds(distances.index(distance) * block, block)]

        early = list(window_copies(into_window, grad_sems))
        late = [pltpu.make_async_copy(slope_ref, slopes, slope_sem)]
        if last:
            sums, strip, sum_sem = refs[8:]
            late.append(pltpu.make_async_copy(begun_ref, sums, sum_sem))
        else:
            skips, skip_sems = refs[8:]
            late += window_copies(lambda d, span: skips.at[me ^ d, span], skip_sems)
        for copy in early:
            copy.start()
        for k in range(taps):
            for copy in kernel_copies(k):
                pltpu.make_async_copy(*copy).start()
        for copy in late:
            copy.start()
        for copy in early:
            copy.wait()

        @pl.loop(0, taps)
        def _(k):
            for copy in kernel_copies(k):
                pltpu.make_async_copy(*copy).wait()
            half = planes // 2
            for part in range(2):
                kernel = wv[k, part * half : (part + 1) * half].reshape(2 * half * rows, depth)
                lanes = slice(part * 2 * half * rows, (part + 1) * 2 * half * rows)
                products[k, :, lanes] = lax.dot_general(
                    gv[EDGE : EDGE + used],
                    kernel,
                    (((1,), (1,)), ((), ())),
                    preferred_element_type=jnp.float32,
                )

        for copy in late:
            copy.wait()

        @pl.loop(0, coarse // STEP)
        def _(i):
            base = pl.multiple_of(i * STEP, STEP)
            spot, span = pl.ds(base, STEP), pl.ds(pl.multiple_of(2 * base, 2 * STEP), 2 * STEP)
            for c in range(width // LANES):
                lanes = slice(c * LANES, (c + 1) * LANES)
                if not last:
                    left = c * LANES % block
                    skip = skips[c * LANES // block, pl.ds(base + HALO, STEP), left : left + LANES]
                    skip = 0.5 * skip.astype(jnp.float32)
                for parity in range(2):
                    total = shifted_total(products, base, lanes, parity)
                    total = total * slopes[parity, spot, lanes]
                    if last:
                        total = total + sums[parity, spot, lanes]
                        strip[c, pl.ds(parity, STEP, stride=2), :] = total
                    else:
                        out_ref[parity, spot, lanes] = total + skip
                if last:
                    out_ref[0, span, lanes] = strip[c].astype(jnp.bfloat16)

    out_shape = jax.ShapeDtypeStruct(shape if last else planar, jnp.bfloat16 if last else jnp.float32)
    scratch = [
        pltpu.VMEM((taps, planes, 2, rows, depth), jnp.bfloat16),
        pltpu.VMEM((window, depth), jnp.bfloat16),
        pltpu.VMEM((taps, used, width), jnp.float32),
        pltpu.VMEM(planar, jnp.float32),
        pltpu.SemaphoreType.DMA((taps, len(pieces))),
        pltpu.SemaphoreType.DMA((len(parts), CHUNKS)),
        pltpu.SemaphoreType.DMA,
    ]
    if last:
        scratch += [
            pltpu.VMEM(planar, jnp.float32),
            pltpu.VMEM((width // LANES, 2 * STEP, LANES), jnp.float32),
            pltpu.SemaphoreType.DMA,
        ]
    else:
        scratch += [
            pltpu.VMEM((seqs, window, block), jnp.bfloat16),
            pltpu.SemaphoreType.DMA((len(parts), CHUNKS)),
        ]
    return pl.pallas_call(
        body,
        out_shape=out_shape,
        grid_spec=pltpu.PrefetchScalarGridSpec(
            num_scalar_prefetch=1,
            grid=(1,),
            in_specs=[ANYWHERE] * len(operands),
            out_specs=pl.BlockSpec(out_shape.shape, lambda i, place: (0, 0, 0)),
            scratch_shapes=scratch,
        ),
        compiler_params=pltpu.CompilerParams(vmem_limit_bytes=56 << 20),
        cost_estimate=pl.CostEstimate(
            flops=2 * taps * window * width * depth, bytes_accessed=20 << 20, transcendentals=0
        ),
        name="input_grad_late" if last else "input_grad_early",
    )(place, *operands)


def stack_planes(place, line):
    count = len(line)

    def kernel(place, *refs):
        parts, out_ref, sems = refs[:count], refs[count], refs[count + 1]
        copies = [
            pltpu.make_async_copy(parts[j], out_ref.at[place[1] // 2 ^ j], sems.at[j])
            for j in range(count)
        ]
        for copy in copies:
            copy.start()
        for copy in copies:
            copy.wait()

    return pl.pallas_call(
        kernel,
        out_shape=jax.ShapeDtypeStruct((count, *line[0].shape), line[0].dtype),
        grid_spec=pltpu.PrefetchScalarGridSpec(
            num_scalar_prefetch=1,
            grid=(1,),
            in_specs=[ANYWHERE] * count,
            out_specs=ANYWHERE,
            scratch_shapes=[pltpu.SemaphoreType.DMA((count,))],
        ),
        name="stack_planes",
    )(place, *line)


def on_device_square(inputs, trunk_grad, weights):
    seqs, reps = lax.axis_size("seq"), lax.axis_size("rep")
    me, rep = lax.axis_index("seq"), lax.axis_index("rep")
    place = jnp.stack([me, rep]).astype(jnp.int32)
    taps, rows, block = weights.shape
    fine = inputs.shape[1]
    coarse, planes = fine // 2, reps // 2
    packed = (coarse + 2 * HALO) // CHUNKS
    half = coarse // 2

    to_beside, to_below, own_window = messages(place, inputs, trunk_grad)
    beside, below = from_peer(to_beside, "seq", 1), from_peer(to_below, "seq", 2)
    slope = half_slope(inputs)
    line = gather_line(weights, "rep", planes, 2)
    top = after(beside[: FIRST + half], slope, *line[1:])
    bottom = after(below[half : coarse + packed - FIRST], slope, *line[1:])
    far_top, far_bottom = from_peer(top, "seq", 2), from_peer(bottom, "seq", 1)

    column = after(stack_planes(place, line), beside, below)
    kept_beside, kept_below = from_peer(column, "seq", 1), from_peer(column, "seq", 2)
    kept = [
        (column, 0, 0),
        (kept_beside, 0, 1),
        (kept_below, 0, 2),
        (from_peer(kept_beside[: planes // 2], "seq", 2), 0, 3),
        (from_peer(kept_below[planes // 2 :], "seq", 1), planes // 2, 3),
    ]
    pieces = []
    for part, plane, distance in kept:
        pieces.append((part, plane, 0, distance))
        pieces.append((from_peer(part, "rep", 1), plane, 1, distance))

    trunk = trunk_grad[0]
    zeros = jnp.zeros((1, block), jnp.bfloat16)
    later = jnp.concatenate([trunk[1:], zeros])
    earlier = jnp.concatenate([zeros, trunk[:-1]])
    shifts = jnp.concatenate([later, trunk, earlier], axis=1)
    scale = 0.5 * float(fine * seqs * reps) ** (-0.5)
    near_rows = [(0, 0, coarse, FIRST), (1, 0, coarse, FIRST), (2, 0, coarse, 0)]
    far_rows = [(3, 0, half, FIRST), (3, half, half, 0)]
    early = early_terms(place, near_rows, [to_beside, beside, below], shifts, coarse)
    mine, theirs = late_terms(
        place, far_rows, [far_top, far_bottom], shifts, early, coarse, scale, planes, taps, rows
    )
    arrived = from_peer(theirs, "rep", 1)
    weight_grad = mine[0] + arrived[0].astype(jnp.float32)
    for j in range(1, planes):
        leaving = (mine[j] + arrived[j].astype(jnp.float32)).astype(jnp.bfloat16)
        weight_grad = weight_grad + from_peer(leaving, "rep", 2 * j).astype(jnp.float32)

    windows = [
        [(own_window, 0, 0, packed)],
        [(beside, FIRST + coarse, 0, packed)],
        [(below, coarse + packed - FIRST, 0, packed)],
        [(far_top, 0, 0, FIRST), (far_bottom, half, FIRST, packed - FIRST)],
    ]
    stage = functools.partial(gradient_stage, place, windows, slope=slope, shape=inputs.shape)
    soon, rest = ([p for p in pieces if (p[3] == 3) == far] for far in (False, True))
    begun = stage(soon, [0, 1, 2], begun=None)
    input_grad = stage(rest, [3], begun=begun)
    return (input_grad, weight_grad)


def with_halo(value, sides, width):
    for axis, dim in sides:
        peers, length = (lax.axis_size(axis), value.shape[dim])
        up = [(i, (i + 1) % peers) for i in range(peers - 1)]
        down = [(j, i) for i, j in up]
        last = lax.slice_in_dim(value, length - width, length, axis=dim)
        leading = lax.slice_in_dim(value, 0, width, axis=dim)
        before = lax.ppermute(last, axis, up)
        after = lax.ppermute(leading, axis, down)
        value = jnp.concatenate([before, value, after], axis=dim)
    return value


def contract_last(left, right):
    return lax.dot_general(
        left, right, (((1,), (1,)), ((), ())), preferred_element_type=jnp.float32
    )


def contract_first(left, right):
    return lax.dot_general(
        left, right, (((0,), (0,)), ((), ())), preferred_element_type=jnp.float32
    )


def on_device_plain(inputs, trunk_grad, weights):
    taps = weights.shape[0]
    grad = lax.all_to_all(trunk_grad, "seq", split_axis=1, concat_axis=2, tiled=True)
    grad_up = jnp.repeat(grad.astype(jnp.float32) * 0.5, 2, axis=1).astype(jnp.bfloat16)
    rows = grad_up.shape[1]
    padded = with_halo(grad_up, (("seq", 1),), 2)
    shifts = [padded[0, 4 - k : 4 - k + rows] for k in range(taps)]
    inputs_f = inputs[0].astype(jnp.float32)
    act_vals, back = jax.vjp(jax.nn.gelu, inputs_f)
    slope = back(jnp.ones_like(inputs_f))[0]
    act = act_vals.astype(jnp.bfloat16)
    in_width = inputs.shape[2]
    columns = lax.all_gather(weights, "seq", axis=2, tiled=True)
    piece = lax.all_gather(columns, "rep", axis=1, tiled=True)
    result = contract_last(shifts[0], piece[0])
    for project_k in range(1, taps):
        result = result + contract_last(shifts[project_k], piece[project_k])
    input_grad = (result * slope + grad_up[0, :, :in_width].astype(jnp.float32)).astype(
        jnp.bfloat16
    )
    scale_factor = float(rows * lax.axis_size("seq") * lax.axis_size("rep")) ** (-0.5)
    terms = jnp.stack([contract_first(act, shifts[k]) for k in range(taps)]) * scale_factor
    partial_sum = lax.psum_scatter(terms, "rep", scatter_dimension=1, tiled=True)
    weight_grad = lax.psum_scatter(partial_sum, "seq", scatter_dimension=2, tiled=True)
    return (input_grad[None], weight_grad)


def on_device(inputs, trunk_grad, weights):
    square = lax.axis_size("seq") == 4 and lax.axis_size("rep") % 8 == 0
    if square and weights.shape[2] % LANES == 0 and inputs.shape[2] % LANES == 0:
        return on_device_square(inputs, trunk_grad, weights)
    return on_device_plain(inputs, trunk_grad, weights)


def solution(mesh):
    in_specs = (P("rep", "seq", None), P("rep", None, "seq"), P(None, "rep", "seq"))
    out_specs = (P("rep", "seq", None), P(None, "rep", "seq"))
    return jax.shard_map(
        on_device, mesh=mesh, in_specs=in_specs, out_specs=out_specs, check_vma=False
    )
```

```python
import functools
import math

import jax
import jax.numpy as jnp
from jax import lax
from jax.experimental import pallas as pl
from jax.experimental.pallas import tpu as pltpu
from jax.sharding import PartitionSpec as P

LANES = 128
HALO = 32
CHUNKS = 4
FIRST = 80
EDGE = 16
MARGIN = HALO - EDGE
STEP = 64
ROOT = math.sqrt(2.0 / math.pi)
CUBIC = 0.044715
SMALL = pl.CostEstimate(flops=1 << 20, bytes_accessed=1 << 16, transcendentals=0)
ANYWHERE = pl.BlockSpec(memory_space=pl.ANY)
ROW_OFFSETS = ((1, 1), (0, 1), (0, 0), (-1, 0), (-1, -1))
GRAD_PARTS = ((0, 0), (1, 0), (1, 1), (2, 1), (2, 2))


def from_peer(value, axis, distance):
    peers = lax.axis_size(axis)
    return lax.ppermute(value, axis, [(i, i ^ distance) for i in range(peers)])


def after(value, *earlier):
    return pl.pallas_call(
        lambda *refs: None,
        out_shape=jax.ShapeDtypeStruct(value.shape, value.dtype),
        in_specs=[ANYWHERE] * (1 + len(earlier)),
        out_specs=ANYWHERE,
        input_output_aliases={0: 0},
        name="after",
    )(value, *earlier)


def gather_line(value, axis, count, unit):
    found, mask = {0: value}, count - 1
    while mask:
        for distance in list(found):
            found[distance ^ mask] = from_peer(found[distance], axis, mask * unit)
        mask //= 2
    return [found[distance] for distance in range(count)]


def gelu_slope(x):
    tanh = jnp.tanh(ROOT * (x + CUBIC * (x * x * x)))
    return 0.5 * (1.0 + tanh) + 0.5 * x * (1.0 - tanh * tanh) * (
        ROOT * (1.0 + 3.0 * CUBIC * (x * x))
    )


def messages_kernel(place, x_ref, trunk_ref, beside_ref, below_ref, own_ref, edged, strip, sem):
    coarse, width, block = x_ref.shape[1] // 2, x_ref.shape[2], edged.shape[1]
    length = trunk_ref.shape[1]
    packed = (coarse + 2 * HALO) // CHUNKS
    copy = pltpu.make_async_copy(trunk_ref.at[0], edged.at[pl.ds(HALO, length)], sem)
    copy.start()
    edged[:HALO] = jnp.zeros((HALO, block), jnp.bfloat16)
    edged[HALO + length :] = jnp.zeros((HALO, block), jnp.bfloat16)

    @pl.loop(0, coarse // STEP)
    def _(step):
        start = pl.multiple_of(step * STEP, STEP)
        x = x_ref[0, pl.ds(pl.multiple_of(2 * start, 2 * STEP), 2 * STEP), :].astype(jnp.float32)
        act = x * (0.5 * (1.0 + jnp.tanh(ROOT * (x + CUBIC * (x * x * x)))))
        for c in range(width // LANES):
            strip[c] = act[:, c * LANES : (c + 1) * LANES]
        for parity in range(2):
            for c in range(width // LANES):
                picked = strip[c, pl.ds(parity, STEP, stride=2), :].astype(jnp.bfloat16)
                lanes = slice(parity * width + c * LANES, parity * width + (c + 1) * LANES)
                beside_ref[pl.ds(FIRST + start, STEP), lanes] = picked
                below_ref[pl.ds(start, STEP), lanes] = picked

    copy.wait()

    def pack(out_ref, row, distance, first, last):
        base = (place[0] ^ distance) * coarse
        for q in range(CHUNKS):
            start = pl.multiple_of(base + q * packed + first, 16)
            out_ref[row : row + last - first, q * block : (q + 1) * block] = edged[
                pl.ds(start, last - first), :
            ]

    pack(beside_ref, 0, 3, 0, FIRST)
    pack(beside_ref, FIRST + coarse, 1, 0, packed)
    pack(below_ref, coarse, 3, FIRST, packed)
    pack(below_ref, coarse + packed - FIRST, 2, 0, packed)
    pack(own_ref, 0, 0, 0, packed)


def messages(place, inputs, trunk_grad):
    _, fine, width = inputs.shape
    _, length, block = trunk_grad.shape
    coarse = fine // 2
    packed = (coarse + 2 * HALO) // CHUNKS
    rows = (FIRST + coarse + packed, coarse + packed - FIRST + packed, packed)
    return pl.pallas_call(
        messages_kernel,
        out_shape=[jax.ShapeDtypeStruct((n, 2 * width), jnp.bfloat16) for n in rows],
        grid_spec=pltpu.PrefetchScalarGridSpec(
            num_scalar_prefetch=1,
            grid=(1,),
            in_specs=[pl.BlockSpec(inputs.shape, lambda i, place: (0, 0, 0)), ANYWHERE],
            out_specs=[pl.BlockSpec((n, 2 * width), lambda i, place: (0, 0)) for n in rows],
            scratch_shapes=[
                pltpu.VMEM((length + 2 * HALO, block), jnp.bfloat16),
                pltpu.VMEM((width // LANES, 2 * STEP, LANES), jnp.float32),
                pltpu.SemaphoreType.DMA,
            ],
        ),
        compiler_params=pltpu.CompilerParams(vmem_limit_bytes=32 << 20),
        name="messages",
    )(place, inputs, trunk_grad)


def slope_kernel(x_ref, out_ref, scratch):
    width = x_ref.shape[2]

    @pl.loop(0, out_ref.shape[1] // 64)
    def _(step):
        start = pl.multiple_of(step * 64, 64)
        span = pl.ds(pl.multiple_of(2 * start, 128), 128)
        for c in range(width // LANES):
            lanes = slice(c * LANES, (c + 1) * LANES)
            scratch[c] = 0.5 * gelu_slope(x_ref[0, span, lanes].astype(jnp.float32))
            for parity in range(2):
                out_ref[parity, pl.ds(start, 64), lanes] = scratch[c, pl.ds(parity, 64, stride=2), :]


def half_slope(inputs):
    fine, width = inputs.shape[1:]
    return pl.pallas_call(
        slope_kernel,
        out_shape=jax.ShapeDtypeStruct((2, fine // 2, width), jnp.float32),
        in_specs=[pl.BlockSpec(memory_space=pltpu.VMEM)],
        out_specs=pl.BlockSpec(memory_space=pltpu.VMEM),
        scratch_shapes=[pltpu.VMEM((width // LANES, 128, LANES), jnp.float32)],
        compiler_params=pltpu.CompilerParams(vmem_limit_bytes=24 << 20),
        name="half_slope",
    )(inputs)


def start_act(place, coarse, layout, pieces, shifts_ref, held, shifts, sems, shift_sems):
    copies, row = [], 0
    for i, (distance, first, size, offset) in enumerate(layout):
        start = pl.multiple_of((place[0] ^ distance) * coarse + first, 16)
        spot = pl.ds(row, size)
        source = pieces[i].at[pl.ds(offset, size)]
        copies.append(pltpu.make_async_copy(source, held.at[spot], sems.at[i]))
        copies.append(
            pltpu.make_async_copy(shifts_ref.at[pl.ds(start, size)], shifts.at[spot], shift_sems.at[i])
        )
        row += size
    for copy in copies:
        copy.start()
    return copies


def early_terms(place, layout, pieces, shifts, coarse):
    both, columns = pieces[0].shape[1], shifts.shape[1]
    rows = sum(size for _, _, size, _ in layout)
    tile = 256

    def kernel(place, shifts_ref, *refs):
        pieces, total = refs[: len(layout)], refs[len(layout)]
        held, shifts, sems, shift_sems = refs[len(layout) + 1 :]
        copies = start_act(
            place, coarse, layout, pieces, shifts_ref, held, shifts, sems, shift_sems
        )
        for copy in copies:
            copy.wait()

        @pl.loop(0, both // tile)
        def _(i):
            span = pl.ds(pl.multiple_of(i * tile, tile), tile)
            total[span, :] = lax.dot_general(
                held[:, span], shifts[...], (((0,), (0,)), ((), ())), preferred_element_type=jnp.float32
            )

    return pl.pallas_call(
        kernel,
        out_shape=jax.ShapeDtypeStruct((both, columns), jnp.float32),
        grid_spec=pltpu.PrefetchScalarGridSpec(
            num_scalar_prefetch=1,
            grid=(1,),
            in_specs=[ANYWHERE] * (1 + len(pieces)),
            out_specs=pl.BlockSpec((both, columns), lambda i, place: (0, 0)),
            scratch_shapes=[
                pltpu.VMEM((rows, both), jnp.bfloat16),
                pltpu.VMEM((rows, columns), jnp.bfloat16),
                pltpu.SemaphoreType.DMA((len(pieces),)),
                pltpu.SemaphoreType.DMA((len(pieces),)),
            ],
        ),
        compiler_params=pltpu.CompilerParams(vmem_limit_bytes=48 << 20),
        cost_estimate=SMALL,
        name="weight_grad_early",
    )(place, shifts, *pieces)


def late_terms(place, layout, pieces, shifts, early, coarse, scale, planes, taps, rows):
    both, columns = early.shape
    width, block = both // 2, columns // 3
    count = sum(size for _, _, size, _ in layout)
    tile = 256
    shape = (planes, taps, rows, block)

    def kernel(place, shifts_ref, early_ref, *refs):
        pieces, (mine_ref, theirs_ref) = refs[: len(layout)], refs[len(layout) : len(layout) + 2]
        held, shifts, total, sems, shift_sems, early_sems = refs[len(layout) + 2 :]
        core, plane = place[1] % 2, place[1] // 2
        copies = start_act(
            place, coarse, layout, pieces, shifts_ref, held, shifts, sems, shift_sems
        )

        def fetch(i):
            span = pl.ds(pl.multiple_of(i * tile, tile), tile)
            return pltpu.make_async_copy(early_ref.at[span], total.at[span], early_sems.at[i])

        for i in range(both // tile):
            fetch(i).start()
        for copy in copies:
            copy.wait()

        @pl.loop(0, both // tile)
        def _(i):
            span = pl.ds(pl.multiple_of(i * tile, tile), tile)
            term = lax.dot_general(
                held[:, span], shifts[...], (((0,), (0,)), ((), ())), preferred_element_type=jnp.float32
            )
            fetch(i).wait()
            total[span, :] += term

        for out_ref, parity, kind in (
            (theirs_ref, 1 - core, jnp.bfloat16),
            (mine_ref, core, jnp.float32),
        ):

            @pl.loop(0, planes)
            def _(j):
                start = ((plane ^ j) * 2 + parity) * rows
                even = pl.ds(pl.multiple_of(start, 16), rows)
                odd = pl.ds(pl.multiple_of(width + start, 16), rows)
                for k, (left, right) in enumerate(GRAD_PARTS):
                    term = total[even, left * block : (left + 1) * block]
                    term += total[odd, right * block : (right + 1) * block]
                    out_ref[j, k] = (scale * term).astype(kind)

    whole = pl.BlockSpec(shape, lambda i, place: (0, 0, 0, 0))
    return pl.pallas_call(
        kernel,
        out_shape=(
            jax.ShapeDtypeStruct(shape, jnp.float32),
            jax.ShapeDtypeStruct(shape, jnp.bfloat16),
        ),
        grid_spec=pltpu.PrefetchScalarGridSpec(
            num_scalar_prefetch=1,
            grid=(1,),
            in_specs=[ANYWHERE] * (2 + len(pieces)),
            out_specs=[whole, whole],
            scratch_shapes=[
                pltpu.VMEM((count, both), jnp.bfloat16),
                pltpu.VMEM((count, columns), jnp.bfloat16),
                pltpu.VMEM((both, columns), jnp.float32),
                pltpu.SemaphoreType.DMA((len(pieces),)),
                pltpu.SemaphoreType.DMA((len(pieces),)),
                pltpu.SemaphoreType.DMA((both // tile,)),
            ],
        ),
        compiler_params=pltpu.CompilerParams(vmem_limit_bytes=48 << 20),
        cost_estimate=SMALL,
        name="weight_grad_late",
    )(place, shifts, early, *pieces)


def shifted_total(products, base, lanes, parity):
    total = None
    for by in (0, 1, -1):
        wanted = [k for k in range(products.shape[0]) if ROW_OFFSETS[k][parity] == by]
        if wanted:
            near = pl.ds(base + MARGIN - 8, STEP + 16)
            part = sum(products[k, near, lanes] for k in wanted)[8 + by : 8 + by + STEP]
            total = part if total is None else total + part
    return total


def gradient_stage(place, windows, pieces, distances, slope, begun, shape):
    _, fine, width = shape
    coarse, seqs = fine // 2, len(windows)
    taps, rows, block = pieces[0][0].shape[1:]
    planes = width // (2 * rows)
    packed = (coarse + 2 * HALO) // CHUNKS
    window, used = CHUNKS * packed, coarse + 2 * MARGIN
    depth, planar = len(distances) * block, (2, coarse, width)
    last = begun is not None
    needed = distances if last else list(range(seqs))
    parts = [(d, *part) for d in needed for part in windows[d]]
    operands = [part[1] for part in parts] + [piece[0] for piece in pieces]
    operands += [slope] + ([begun] if last else [])

    def body(place, *refs):
        own, refs = refs[: len(parts)], refs[len(parts) :]
        sources, refs = refs[: len(pieces)], refs[len(pieces) :]
        slope_ref, refs = refs[0], refs[1:]
        if last:
            begun_ref, refs = refs[0], refs[1:]
        out_ref, wv, gv, products, slopes, sems, grad_sems, slope_sem = refs[:8]
        me, core = place[0], place[1] % 2

        def kernel_copies(k):
            for number, (array, plane, flip, distance) in enumerate(pieces):
                spot = pl.ds(distances.index(distance) * block, block)
                span = pl.ds(plane, array.shape[0])
                target = wv.at[k, span, core ^ flip, :, spot]
                yield sources[number].at[:, k], target, sems.at[k, number]

        def window_copies(target_of, sems):
            for number, (distance, _, row, first, size) in enumerate(parts):
                for q in range(CHUNKS):
                    source = own[number].at[pl.ds(row, size), pl.ds(q * block, block)]
                    target = target_of(distance, pl.ds(q * packed + first, size))
                    if target is not None:
                        yield pltpu.make_async_copy(source, target, sems.at[number, q])

        def into_window(distance, span):
            if distance not in distances:
                return None
            return gv.at[span, pl.ds(distances.index(distance) * block, block)]

        early = list(window_copies(into_window, grad_sems))
        late = [pltpu.make_async_copy(slope_ref, slopes, slope_sem)]
        if last:
            sums, strip, sum_sem = refs[8:]
            late.append(pltpu.make_async_copy(begun_ref, sums, sum_sem))
        else:
            skips, skip_sems = refs[8:]
            late += window_copies(lambda d, span: skips.at[me ^ d, span], skip_sems)
        for copy in early:
            copy.start()
        for k in range(taps):
            for copy in kernel_copies(k):
                pltpu.make_async_copy(*copy).start()
        for copy in late:
            copy.start()
        for copy in early:
            copy.wait()

        @pl.loop(0, taps)
        def _(k):
            for copy in kernel_copies(k):
                pltpu.make_async_copy(*copy).wait()
            half = planes // 2
            for part in range(2):
                kernel = wv[k, part * half : (part + 1) * half].reshape(2 * half * rows, depth)
                lanes = slice(part * 2 * half * rows, (part + 1) * 2 * half * rows)
                products[k, :, lanes] = lax.dot_general(
                    gv[EDGE : EDGE + used],
                    kernel,
                    (((1,), (1,)), ((), ())),
                    preferred_element_type=jnp.float32,
                )

        for copy in late:
            copy.wait()

        @pl.loop(0, coarse // STEP)
        def _(i):
            base = pl.multiple_of(i * STEP, STEP)
            spot, span = pl.ds(base, STEP), pl.ds(pl.multiple_of(2 * base, 2 * STEP), 2 * STEP)
            for c in range(width // LANES):
                lanes = slice(c * LANES, (c + 1) * LANES)
                if not last:
                    left = c * LANES % block
                    skip = skips[c * LANES // block, pl.ds(base + HALO, STEP), left : left + LANES]
                    skip = 0.5 * skip.astype(jnp.float32)
                for parity in range(2):
                    total = shifted_total(products, base, lanes, parity)
                    total = total * slopes[parity, spot, lanes]
                    if last:
                        total = total + sums[parity, spot, lanes]
                        strip[c, pl.ds(parity, STEP, stride=2), :] = total
                    else:
                        out_ref[parity, spot, lanes] = total + skip
                if last:
                    out_ref[0, span, lanes] = strip[c].astype(jnp.bfloat16)

    out_shape = jax.ShapeDtypeStruct(shape if last else planar, jnp.bfloat16 if last else jnp.float32)
    scratch = [
        pltpu.VMEM((taps, planes, 2, rows, depth), jnp.bfloat16),
        pltpu.VMEM((window, depth), jnp.bfloat16),
        pltpu.VMEM((taps, used, width), jnp.float32),
        pltpu.VMEM(planar, jnp.float32),
        pltpu.SemaphoreType.DMA((taps, len(pieces))),
        pltpu.SemaphoreType.DMA((len(parts), CHUNKS)),
        pltpu.SemaphoreType.DMA,
    ]
    if last:
        scratch += [
            pltpu.VMEM(planar, jnp.float32),
            pltpu.VMEM((width // LANES, 2 * STEP, LANES), jnp.float32),
            pltpu.SemaphoreType.DMA,
        ]
    else:
        scratch += [
            pltpu.VMEM((seqs, window, block), jnp.bfloat16),
            pltpu.SemaphoreType.DMA((len(parts), CHUNKS)),
        ]
    return pl.pallas_call(
        body,
        out_shape=out_shape,
        grid_spec=pltpu.PrefetchScalarGridSpec(
            num_scalar_prefetch=1,
            grid=(1,),
            in_specs=[ANYWHERE] * len(operands),
            out_specs=pl.BlockSpec(out_shape.shape, lambda i, place: (0, 0, 0)),
            scratch_shapes=scratch,
        ),
        compiler_params=pltpu.CompilerParams(vmem_limit_bytes=56 << 20),
        cost_estimate=SMALL,
        name="input_grad_late" if last else "input_grad_early",
    )(place, *operands)


def stack_planes(place, line):
    count = len(line)

    def kernel(place, *refs):
        parts, out_ref = refs[:count], refs[count]
        for j in range(count):
            out_ref[place[1] // 2 ^ j] = parts[j][...]

    shape = line[0].shape
    return pl.pallas_call(
        kernel,
        out_shape=jax.ShapeDtypeStruct((count, *shape), line[0].dtype),
        grid_spec=pltpu.PrefetchScalarGridSpec(
            num_scalar_prefetch=1,
            grid=(1,),
            in_specs=[pl.BlockSpec(shape, lambda i, place: (0, 0, 0))] * count,
            out_specs=pl.BlockSpec((count, *shape), lambda i, place: (0, 0, 0, 0)),
        ),
        compiler_params=pltpu.CompilerParams(vmem_limit_bytes=24 << 20),
        cost_estimate=SMALL,
        name="stack_planes",
    )(place, *line)


def on_device_square(inputs, trunk_grad, weights):
    seqs, reps = lax.axis_size("seq"), lax.axis_size("rep")
    me, rep = lax.axis_index("seq"), lax.axis_index("rep")
    place = jnp.stack([me, rep]).astype(jnp.int32)
    taps, rows, block = weights.shape
    fine = inputs.shape[1]
    coarse, planes = fine // 2, reps // 2
    packed = (coarse + 2 * HALO) // CHUNKS
    half = coarse // 2

    to_beside, to_below, own_window = messages(place, inputs, trunk_grad)
    beside, below = from_peer(to_beside, "seq", 1), from_peer(to_below, "seq", 2)
    slope = half_slope(inputs)
    column = stack_planes(place, gather_line(weights, "rep", planes, 2))
    top = after(beside[: FIRST + half], slope, column)
    bottom = after(below[half : coarse + packed - FIRST], slope, column)
    far_top, far_bottom = from_peer(top, "seq", 2), from_peer(bottom, "seq", 1)

    column = after(column, beside, below)
    kept_beside, kept_below = from_peer(column, "seq", 1), from_peer(column, "seq", 2)
    far_first = from_peer(kept_beside[: planes // 2], "seq", 2)
    far_second = from_peer(kept_below[planes // 2 :], "seq", 1)
    soon, rest = [], []
    for part, distance in ((column, 0), (kept_beside, 1), (kept_below, 2)):
        soon += [(part, 0, 0, distance), (from_peer(part, "rep", 1), 0, 1, distance)]

    trunk = trunk_grad[0]
    zeros = jnp.zeros((1, block), jnp.bfloat16)
    later = jnp.concatenate([trunk[1:], zeros])
    earlier = jnp.concatenate([zeros, trunk[:-1]])
    shifts = jnp.concatenate([later, trunk, earlier], axis=1)
    scale = 0.5 * float(fine * seqs * reps) ** (-0.5)
    near_rows = [(0, 0, coarse, FIRST), (1, 0, coarse, FIRST), (2, 0, coarse, 0)]
    far_rows = [(3, 0, half, FIRST), (3, half, half, 0)]
    early = early_terms(place, near_rows, [to_beside, beside, below], shifts, coarse)
    mine, theirs = late_terms(
        place, far_rows, [far_top, far_bottom], shifts, early, coarse, scale, planes, taps, rows
    )
    arrived = from_peer(theirs, "rep", 1)
    weight_grad = mine[0] + arrived[0].astype(jnp.float32)
    for j in range(1, planes):
        leaving = (mine[j] + arrived[j].astype(jnp.float32)).astype(jnp.bfloat16)
        weight_grad = weight_grad + from_peer(leaving, "rep", 2 * j).astype(jnp.float32)

    windows = [
        [(own_window, 0, 0, packed)],
        [(beside, FIRST + coarse, 0, packed)],
        [(below, coarse + packed - FIRST, 0, packed)],
        [(far_top, 0, 0, FIRST), (far_bottom, half, FIRST, packed - FIRST)],
    ]
    stage = functools.partial(gradient_stage, place, windows, slope=slope, shape=inputs.shape)
    begun = stage(soon, [0, 1, 2], begun=None)
    for part, plane in ((far_first, 0), (far_second, planes // 2)):
        part = after(part, begun)
        rest += [(part, plane, 0, 3), (from_peer(part, "rep", 1), plane, 1, 3)]
    input_grad = stage(rest, [3], begun=begun)
    return (input_grad, weight_grad)


def with_halo(value, sides, width):
    for axis, dim in sides:
        peers, length = (lax.axis_size(axis), value.shape[dim])
        up = [(i, (i + 1) % peers) for i in range(peers - 1)]
        down = [(j, i) for i, j in up]
        last = lax.slice_in_dim(value, length - width, length, axis=dim)
        leading = lax.slice_in_dim(value, 0, width, axis=dim)
        before = lax.ppermute(last, axis, up)
        after = lax.ppermute(leading, axis, down)
        value = jnp.concatenate([before, value, after], axis=dim)
    return value


def contract_last(left, right):
    return lax.dot_general(
        left, right, (((1,), (1,)), ((), ())), preferred_element_type=jnp.float32
    )


def contract_first(left, right):
    return lax.dot_general(
        left, right, (((0,), (0,)), ((), ())), preferred_element_type=jnp.float32
    )


def on_device_plain(inputs, trunk_grad, weights):
    taps = weights.shape[0]
    grad = lax.all_to_all(trunk_grad, "seq", split_axis=1, concat_axis=2, tiled=True)
    grad_up = jnp.repeat(grad.astype(jnp.float32) * 0.5, 2, axis=1).astype(jnp.bfloat16)
    rows = grad_up.shape[1]
    padded = with_halo(grad_up, (("seq", 1),), 2)
    shifts = [padded[0, 4 - k : 4 - k + rows] for k in range(taps)]
    inputs_f = inputs[0].astype(jnp.float32)
    act_vals, back = jax.vjp(jax.nn.gelu, inputs_f)
    slope = back(jnp.ones_like(inputs_f))[0]
    act = act_vals.astype(jnp.bfloat16)
    in_width = inputs.shape[2]
    columns = lax.all_gather(weights, "seq", axis=2, tiled=True)
    piece = lax.all_gather(columns, "rep", axis=1, tiled=True)
    result = contract_last(shifts[0], piece[0])
    for project_k in range(1, taps):
        result = result + contract_last(shifts[project_k], piece[project_k])
    input_grad = (result * slope + grad_up[0, :, :in_width].astype(jnp.float32)).astype(
        jnp.bfloat16
    )
    scale_factor = float(rows * lax.axis_size("seq") * lax.axis_size("rep")) ** (-0.5)
    terms = jnp.stack([contract_first(act, shifts[k]) for k in range(taps)]) * scale_factor
    partial_sum = lax.psum_scatter(terms, "rep", scatter_dimension=1, tiled=True)
    weight_grad = lax.psum_scatter(partial_sum, "seq", scatter_dimension=2, tiled=True)
    return (input_grad[None], weight_grad)


def on_device(inputs, trunk_grad, weights):
    square = lax.axis_size("seq") == 4 and lax.axis_size("rep") % 8 == 0
    if square and weights.shape[2] % LANES == 0 and inputs.shape[2] % LANES == 0:
        return on_device_square(inputs, trunk_grad, weights)
    return on_device_plain(inputs, trunk_grad, weights)


def solution(mesh):
    in_specs = (P("rep", "seq", None), P("rep", None, "seq"), P(None, "rep", "seq"))
    out_specs = (P("rep", "seq", None), P(None, "rep", "seq"))
    return jax.shard_map(
        on_device, mesh=mesh, in_specs=in_specs, out_specs=out_specs, check_vma=False
    )
```

```python
import functools
import math

import jax
import jax.numpy as jnp
from jax import lax
from jax.experimental import pallas as pl
from jax.experimental.pallas import tpu as pltpu
from jax.sharding import PartitionSpec as P

LANES = 128
HALO = 32
CHUNKS = 4
FIRST = 80
EDGE = 16
MARGIN = HALO - EDGE
STEP = 64
ROOT = math.sqrt(2.0 / math.pi)
CUBIC = 0.044715
SMALL = pl.CostEstimate(flops=1 << 20, bytes_accessed=1 << 16, transcendentals=0)
ANYWHERE = pl.BlockSpec(memory_space=pl.ANY)
ROW_OFFSETS = ((1, 1), (0, 1), (0, 0), (-1, 0), (-1, -1))
GRAD_PARTS = ((0, 0), (1, 0), (1, 1), (2, 1), (2, 2))


def from_peer(value, axis, distance):
    peers = lax.axis_size(axis)
    return lax.ppermute(value, axis, [(i, i ^ distance) for i in range(peers)])


def after(value, *earlier):
    return pl.pallas_call(
        lambda *refs: None,
        out_shape=jax.ShapeDtypeStruct(value.shape, value.dtype),
        in_specs=[ANYWHERE] * (1 + len(earlier)),
        out_specs=ANYWHERE,
        input_output_aliases={0: 0},
        name="after",
    )(value, *earlier)


def gather_line(value, axis, count, unit):
    found, mask = {0: value}, count - 1
    while mask:
        for distance in list(found):
            found[distance ^ mask] = from_peer(found[distance], axis, mask * unit)
        mask //= 2
    return [found[distance] for distance in range(count)]


def gelu_slope(x):
    tanh = jnp.tanh(ROOT * (x + CUBIC * (x * x * x)))
    return 0.5 * (1.0 + tanh) + 0.5 * x * (1.0 - tanh * tanh) * (
        ROOT * (1.0 + 3.0 * CUBIC * (x * x))
    )


def messages_kernel(place, x_ref, trunk_ref, beside_ref, below_ref, own_ref, edged, strip, sem):
    coarse, width, block = x_ref.shape[1] // 2, x_ref.shape[2], edged.shape[1]
    length = trunk_ref.shape[1]
    packed = (coarse + 2 * HALO) // CHUNKS
    copy = pltpu.make_async_copy(trunk_ref.at[0], edged.at[pl.ds(HALO, length)], sem)
    copy.start()
    edged[:HALO] = jnp.zeros((HALO, block), jnp.bfloat16)
    edged[HALO + length :] = jnp.zeros((HALO, block), jnp.bfloat16)

    @pl.loop(0, coarse // STEP)
    def _(step):
        start = pl.multiple_of(step * STEP, STEP)
        x = x_ref[0, pl.ds(pl.multiple_of(2 * start, 2 * STEP), 2 * STEP), :].astype(jnp.float32)
        act = x * (0.5 * (1.0 + jnp.tanh(ROOT * (x + CUBIC * (x * x * x)))))
        for c in range(width // LANES):
            strip[c] = act[:, c * LANES : (c + 1) * LANES]
        for parity in range(2):
            for c in range(width // LANES):
                picked = strip[c, pl.ds(parity, STEP, stride=2), :].astype(jnp.bfloat16)
                lanes = slice(parity * width + c * LANES, parity * width + (c + 1) * LANES)
                beside_ref[pl.ds(FIRST + start, STEP), lanes] = picked
                below_ref[pl.ds(start, STEP), lanes] = picked

    copy.wait()

    def pack(out_ref, row, distance, first, last):
        base = (place[0] ^ distance) * coarse
        for q in range(CHUNKS):
            start = pl.multiple_of(base + q * packed + first, 16)
            out_ref[row : row + last - first, q * block : (q + 1) * block] = edged[
                pl.ds(start, last - first), :
            ]

    pack(beside_ref, 0, 3, 0, FIRST)
    pack(beside_ref, FIRST + coarse, 1, 0, packed)
    pack(below_ref, coarse, 3, FIRST, packed)
    pack(below_ref, coarse + packed - FIRST, 2, 0, packed)
    pack(own_ref, 0, 0, 0, packed)


def messages(place, inputs, trunk_grad):
    _, fine, width = inputs.shape
    _, length, block = trunk_grad.shape
    coarse = fine // 2
    packed = (coarse + 2 * HALO) // CHUNKS
    rows = (FIRST + coarse + packed, coarse + packed - FIRST + packed, packed)
    return pl.pallas_call(
        messages_kernel,
        out_shape=[jax.ShapeDtypeStruct((n, 2 * width), jnp.bfloat16) for n in rows],
        grid_spec=pltpu.PrefetchScalarGridSpec(
            num_scalar_prefetch=1,
            grid=(1,),
            in_specs=[pl.BlockSpec(inputs.shape, lambda i, place: (0, 0, 0)), ANYWHERE],
            out_specs=[pl.BlockSpec((n, 2 * width), lambda i, place: (0, 0)) for n in rows],
            scratch_shapes=[
                pltpu.VMEM((length + 2 * HALO, block), jnp.bfloat16),
                pltpu.VMEM((width // LANES, 2 * STEP, LANES), jnp.float32),
                pltpu.SemaphoreType.DMA,
            ],
        ),
        compiler_params=pltpu.CompilerParams(vmem_limit_bytes=32 << 20),
        name="messages",
    )(place, inputs, trunk_grad)


def slope_kernel(x_ref, out_ref, scratch):
    width = x_ref.shape[2]

    @pl.loop(0, out_ref.shape[1] // 64)
    def _(step):
        start = pl.multiple_of(step * 64, 64)
        span = pl.ds(pl.multiple_of(2 * start, 128), 128)
        for c in range(width // LANES):
            lanes = slice(c * LANES, (c + 1) * LANES)
            scratch[c] = 0.5 * gelu_slope(x_ref[0, span, lanes].astype(jnp.float32))
            for parity in range(2):
                out_ref[parity, pl.ds(start, 64), lanes] = scratch[c, pl.ds(parity, 64, stride=2), :]


def half_slope(inputs):
    fine, width = inputs.shape[1:]
    return pl.pallas_call(
        slope_kernel,
        out_shape=jax.ShapeDtypeStruct((2, fine // 2, width), jnp.float32),
        in_specs=[pl.BlockSpec(memory_space=pltpu.VMEM)],
        out_specs=pl.BlockSpec(memory_space=pltpu.VMEM),
        scratch_shapes=[pltpu.VMEM((width // LANES, 128, LANES), jnp.float32)],
        compiler_params=pltpu.CompilerParams(vmem_limit_bytes=24 << 20),
        name="half_slope",
    )(inputs)


def start_act(place, coarse, layout, pieces, shifts_ref, held, shifts, sems, shift_sems):
    copies, row = [], 0
    for i, (distance, first, size, offset) in enumerate(layout):
        start = pl.multiple_of((place[0] ^ distance) * coarse + first, 16)
        spot = pl.ds(row, size)
        source = pieces[i].at[pl.ds(offset, size)]
        copies.append(pltpu.make_async_copy(source, held.at[spot], sems.at[i]))
        copies.append(
            pltpu.make_async_copy(shifts_ref.at[pl.ds(start, size)], shifts.at[spot], shift_sems.at[i])
        )
        row += size
    for copy in copies:
        copy.start()
    return copies


def early_terms(place, layout, pieces, shifts, coarse):
    both, columns = pieces[0].shape[1], shifts.shape[1]
    rows = sum(size for _, _, size, _ in layout)
    tile = 256

    def kernel(place, shifts_ref, *refs):
        pieces, total = refs[: len(layout)], refs[len(layout)]
        held, shifts, sems, shift_sems = refs[len(layout) + 1 :]
        copies = start_act(
            place, coarse, layout, pieces, shifts_ref, held, shifts, sems, shift_sems
        )
        for copy in copies:
            copy.wait()

        @pl.loop(0, both // tile)
        def _(i):
            span = pl.ds(pl.multiple_of(i * tile, tile), tile)
            total[span, :] = lax.dot_general(
                held[:, span], shifts[...], (((0,), (0,)), ((), ())), preferred_element_type=jnp.float32
            )

    return pl.pallas_call(
        kernel,
        out_shape=jax.ShapeDtypeStruct((both, columns), jnp.float32),
        grid_spec=pltpu.PrefetchScalarGridSpec(
            num_scalar_prefetch=1,
            grid=(1,),
            in_specs=[ANYWHERE] * (1 + len(pieces)),
            out_specs=pl.BlockSpec((both, columns), lambda i, place: (0, 0)),
            scratch_shapes=[
                pltpu.VMEM((rows, both), jnp.bfloat16),
                pltpu.VMEM((rows, columns), jnp.bfloat16),
                pltpu.SemaphoreType.DMA((len(pieces),)),
                pltpu.SemaphoreType.DMA((len(pieces),)),
            ],
        ),
        compiler_params=pltpu.CompilerParams(vmem_limit_bytes=48 << 20),
        cost_estimate=SMALL,
        name="weight_grad_early",
    )(place, shifts, *pieces)


def late_terms(place, layout, pieces, shifts, early, coarse, scale, planes, taps, rows):
    both, columns = early.shape
    width, block = both // 2, columns // 3
    count = sum(size for _, _, size, _ in layout)
    tile = 256
    shape = (planes, taps, rows, block)

    def kernel(place, shifts_ref, early_ref, *refs):
        pieces, (mine_ref, theirs_ref) = refs[: len(layout)], refs[len(layout) : len(layout) + 2]
        held, shifts, total, sems, shift_sems, early_sems = refs[len(layout) + 2 :]
        core, plane = place[1] % 2, place[1] // 2
        copies = start_act(
            place, coarse, layout, pieces, shifts_ref, held, shifts, sems, shift_sems
        )

        def fetch(i):
            span = pl.ds(pl.multiple_of(i * tile, tile), tile)
            return pltpu.make_async_copy(early_ref.at[span], total.at[span], early_sems.at[i])

        for i in range(both // tile):
            fetch(i).start()
        for copy in copies:
            copy.wait()

        @pl.loop(0, both // tile)
        def _(i):
            span = pl.ds(pl.multiple_of(i * tile, tile), tile)
            term = lax.dot_general(
                held[:, span], shifts[...], (((0,), (0,)), ((), ())), preferred_element_type=jnp.float32
            )
            fetch(i).wait()
            total[span, :] += term

        for out_ref, parity, kind in (
            (theirs_ref, 1 - core, jnp.bfloat16),
            (mine_ref, core, jnp.float32),
        ):

            @pl.loop(0, planes)
            def _(j):
                start = ((plane ^ j) * 2 + parity) * rows
                even = pl.ds(pl.multiple_of(start, 16), rows)
                odd = pl.ds(pl.multiple_of(width + start, 16), rows)
                for k, (left, right) in enumerate(GRAD_PARTS):
                    term = total[even, left * block : (left + 1) * block]
                    term += total[odd, right * block : (right + 1) * block]
                    out_ref[j, k] = (scale * term).astype(kind)

    whole = pl.BlockSpec(shape, lambda i, place: (0, 0, 0, 0))
    return pl.pallas_call(
        kernel,
        out_shape=(
            jax.ShapeDtypeStruct(shape, jnp.float32),
            jax.ShapeDtypeStruct(shape, jnp.bfloat16),
        ),
        grid_spec=pltpu.PrefetchScalarGridSpec(
            num_scalar_prefetch=1,
            grid=(1,),
            in_specs=[ANYWHERE] * (2 + len(pieces)),
            out_specs=[whole, whole],
            scratch_shapes=[
                pltpu.VMEM((count, both), jnp.bfloat16),
                pltpu.VMEM((count, columns), jnp.bfloat16),
                pltpu.VMEM((both, columns), jnp.float32),
                pltpu.SemaphoreType.DMA((len(pieces),)),
                pltpu.SemaphoreType.DMA((len(pieces),)),
                pltpu.SemaphoreType.DMA((both // tile,)),
            ],
        ),
        compiler_params=pltpu.CompilerParams(vmem_limit_bytes=48 << 20),
        cost_estimate=SMALL,
        name="weight_grad_late",
    )(place, shifts, early, *pieces)


def shifted_total(products, base, lanes, parity):
    total = None
    for by in (0, 1, -1):
        wanted = [k for k in range(products.shape[0]) if ROW_OFFSETS[k][parity] == by]
        if wanted:
            near = pl.ds(base + MARGIN - 8, STEP + 16)
            part = sum(products[k, near, lanes] for k in wanted)[8 + by : 8 + by + STEP]
            total = part if total is None else total + part
    return total


def gradient_stage(place, windows, pieces, distances, slope, begun, shape):
    _, fine, width = shape
    coarse, seqs = fine // 2, len(windows)
    taps, rows, block = pieces[0][0].shape[1:]
    planes = width // (2 * rows)
    packed = (coarse + 2 * HALO) // CHUNKS
    window, used = CHUNKS * packed, coarse + 2 * MARGIN
    depth, planar = len(distances) * block, (2, coarse, width)
    last = begun is not None
    needed = distances if last else list(range(seqs))
    parts = [(d, *part) for d in needed for part in windows[d]]
    operands = [part[1] for part in parts] + [piece[0] for piece in pieces]
    operands += [slope] + ([begun] if last else [])

    def body(place, *refs):
        own, refs = refs[: len(parts)], refs[len(parts) :]
        sources, refs = refs[: len(pieces)], refs[len(pieces) :]
        slope_ref, refs = refs[0], refs[1:]
        if last:
            begun_ref, refs = refs[0], refs[1:]
        out_ref, wv, gv, products, slopes, sems, grad_sems, slope_sem = refs[:8]
        me, core = place[0], place[1] % 2

        def kernel_copies(k):
            for number, (array, plane, flip, distance) in enumerate(pieces):
                spot = pl.ds(distances.index(distance) * block, block)
                span = pl.ds(plane, array.shape[0])
                target = wv.at[k, span, core ^ flip, :, spot]
                yield sources[number].at[:, k], target, sems.at[k, number]

        def window_copies(target_of, sems):
            for number, (distance, _, row, first, size) in enumerate(parts):
                for q in range(CHUNKS):
                    source = own[number].at[pl.ds(row, size), pl.ds(q * block, block)]
                    target = target_of(distance, pl.ds(q * packed + first, size))
                    if target is not None:
                        yield pltpu.make_async_copy(source, target, sems.at[number, q])

        def into_window(distance, span):
            if distance not in distances:
                return None
            return gv.at[span, pl.ds(distances.index(distance) * block, block)]

        early = list(window_copies(into_window, grad_sems))
        late = [pltpu.make_async_copy(slope_ref, slopes, slope_sem)]
        if last:
            sums, strip, sum_sem = refs[8:]
            late.append(pltpu.make_async_copy(begun_ref, sums, sum_sem))
        else:
            skips, skip_sems = refs[8:]
            late += window_copies(lambda d, span: skips.at[me ^ d, span], skip_sems)
        for copy in early:
            copy.start()
        for k in range(taps):
            for copy in kernel_copies(k):
                pltpu.make_async_copy(*copy).start()
        for copy in late:
            copy.start()
        for copy in early:
            copy.wait()

        @pl.loop(0, taps)
        def _(k):
            for copy in kernel_copies(k):
                pltpu.make_async_copy(*copy).wait()
            half = planes // 2
            for part in range(2):
                kernel = wv[k, part * half : (part + 1) * half].reshape(2 * half * rows, depth)
                lanes = slice(part * 2 * half * rows, (part + 1) * 2 * half * rows)
                products[k, :, lanes] = lax.dot_general(
                    gv[EDGE : EDGE + used],
                    kernel,
                    (((1,), (1,)), ((), ())),
                    preferred_element_type=jnp.float32,
                )

        for copy in late:
            copy.wait()

        @pl.loop(0, coarse // STEP)
        def _(i):
            base = pl.multiple_of(i * STEP, STEP)
            spot, span = pl.ds(base, STEP), pl.ds(pl.multiple_of(2 * base, 2 * STEP), 2 * STEP)
            for c in range(width // LANES):
                lanes = slice(c * LANES, (c + 1) * LANES)
                if not last:
                    left = c * LANES % block
                    skip = skips[c * LANES // block, pl.ds(base + HALO, STEP), left : left + LANES]
                    skip = 0.5 * skip.astype(jnp.float32)
                for parity in range(2):
                    total = shifted_total(products, base, lanes, parity)
                    total = total * slopes[parity, spot, lanes]
                    if last:
                        total = total + sums[parity, spot, lanes]
                        strip[c, pl.ds(parity, STEP, stride=2), :] = total
                    else:
                        out_ref[parity, spot, lanes] = total + skip
                if last:
                    out_ref[0, span, lanes] = strip[c].astype(jnp.bfloat16)

    out_shape = jax.ShapeDtypeStruct(shape if last else planar, jnp.bfloat16 if last else jnp.float32)
    scratch = [
        pltpu.VMEM((taps, planes, 2, rows, depth), jnp.bfloat16),
        pltpu.VMEM((window, depth), jnp.bfloat16),
        pltpu.VMEM((taps, used, width), jnp.float32),
        pltpu.VMEM(planar, jnp.float32),
        pltpu.SemaphoreType.DMA((taps, len(pieces))),
        pltpu.SemaphoreType.DMA((len(parts), CHUNKS)),
        pltpu.SemaphoreType.DMA,
    ]
    if last:
        scratch += [
            pltpu.VMEM(planar, jnp.float32),
            pltpu.VMEM((width // LANES, 2 * STEP, LANES), jnp.float32),
            pltpu.SemaphoreType.DMA,
        ]
    else:
        scratch += [
            pltpu.VMEM((seqs, window, block), jnp.bfloat16),
            pltpu.SemaphoreType.DMA((len(parts), CHUNKS)),
        ]
    return pl.pallas_call(
        body,
        out_shape=out_shape,
        grid_spec=pltpu.PrefetchScalarGridSpec(
            num_scalar_prefetch=1,
            grid=(1,),
            in_specs=[ANYWHERE] * len(operands),
            out_specs=pl.BlockSpec(out_shape.shape, lambda i, place: (0, 0, 0)),
            scratch_shapes=scratch,
        ),
        compiler_params=pltpu.CompilerParams(vmem_limit_bytes=56 << 20),
        cost_estimate=SMALL,
        name="input_grad_late" if last else "input_grad_early",
    )(place, *operands)


def stack_planes(place, line):
    count = len(line)

    def kernel(place, *refs):
        parts, out_ref = refs[:count], refs[count]
        for j in range(count):
            out_ref[place[1] // 2 ^ j] = parts[j][...]

    shape = line[0].shape
    return pl.pallas_call(
        kernel,
        out_shape=jax.ShapeDtypeStruct((count, *shape), line[0].dtype),
        grid_spec=pltpu.PrefetchScalarGridSpec(
            num_scalar_prefetch=1,
            grid=(1,),
            in_specs=[pl.BlockSpec(shape, lambda i, place: (0, 0, 0))] * count,
            out_specs=pl.BlockSpec((count, *shape), lambda i, place: (0, 0, 0, 0)),
        ),
        compiler_params=pltpu.CompilerParams(vmem_limit_bytes=24 << 20),
        cost_estimate=SMALL,
        name="stack_planes",
    )(place, *line)


def on_device_square(inputs, trunk_grad, weights):
    seqs, reps = lax.axis_size("seq"), lax.axis_size("rep")
    me, rep = lax.axis_index("seq"), lax.axis_index("rep")
    place = jnp.stack([me, rep]).astype(jnp.int32)
    taps, rows, block = weights.shape
    fine = inputs.shape[1]
    coarse, planes = fine // 2, reps // 2
    packed = (coarse + 2 * HALO) // CHUNKS
    half = coarse // 2

    to_beside, to_below, own_window = messages(place, inputs, trunk_grad)
    beside, below = from_peer(to_beside, "seq", 1), from_peer(to_below, "seq", 2)
    slope = half_slope(inputs)
    column = stack_planes(place, gather_line(weights, "rep", planes, 2))
    trunk = trunk_grad[0]
    zeros = jnp.zeros((1, block), jnp.bfloat16)
    later = jnp.concatenate([trunk[1:], zeros])
    earlier = jnp.concatenate([zeros, trunk[:-1]])
    shifts = jnp.concatenate([later, trunk, earlier], axis=1)
    top = after(beside[: FIRST + half], slope, column, shifts)
    bottom = after(below[half : coarse + packed - FIRST], slope, column, shifts)
    far_top, far_bottom = from_peer(top, "seq", 2), from_peer(bottom, "seq", 1)

    column = after(column, top, bottom)
    other_column = from_peer(column, "rep", 1)
    column = after(column, other_column)
    kept_beside, kept_below = from_peer(column, "seq", 1), from_peer(column, "seq", 2)

    scale = 0.5 * float(fine * seqs * reps) ** (-0.5)
    near_rows = [(0, 0, coarse, FIRST), (1, 0, coarse, FIRST), (2, 0, coarse, 0)]
    far_rows = [(3, 0, half, FIRST), (3, half, half, 0)]
    early = early_terms(place, near_rows, [to_beside, beside, below], shifts, coarse)
    mine, theirs = late_terms(
        place, far_rows, [far_top, far_bottom], shifts, early, coarse, scale, planes, taps, rows
    )
    arrived = from_peer(theirs, "rep", 1)
    weight_grad = mine[0] + arrived[0].astype(jnp.float32)
    leaving = [(mine[j] + arrived[j].astype(jnp.float32)).astype(jnp.bfloat16) for j in range(planes)]
    summed = [from_peer(leaving[j], "rep", 2 * j) for j in range(1, planes)]

    kept_beside, kept_below = after(kept_beside, early), after(kept_below, early)
    far_first = from_peer(kept_beside[: planes // 2], "seq", 2)
    far_second = from_peer(kept_below[planes // 2 :], "seq", 1)
    soon = [(after(column, *leaving[1:]), 0, 0, 0), (other_column, 0, 1, 0)]
    for part, distance in ((kept_beside, 1), (kept_below, 2)):
        soon += [(part, 0, 0, distance), (from_peer(part, "rep", 1), 0, 1, distance)]

    windows = [
        [(own_window, 0, 0, packed)],
        [(beside, FIRST + coarse, 0, packed)],
        [(below, coarse + packed - FIRST, 0, packed)],
        [(far_top, 0, 0, FIRST), (far_bottom, half, FIRST, packed - FIRST)],
    ]
    stage = functools.partial(gradient_stage, place, windows, slope=slope, shape=inputs.shape)
    begun, rest = stage(soon, [0, 1, 2], begun=None), []
    for part, plane in ((far_first, 0), (far_second, planes // 2)):
        part = after(part, begun)
        rest += [(part, plane, 0, 3), (from_peer(part, "rep", 1), plane, 1, 3)]
    input_grad = stage(rest, [3], begun=begun)
    for part in summed:
        weight_grad = weight_grad + after(part, input_grad).astype(jnp.float32)
    return (input_grad, weight_grad)


def with_halo(value, sides, width):
    for axis, dim in sides:
        peers, length = (lax.axis_size(axis), value.shape[dim])
        up = [(i, (i + 1) % peers) for i in range(peers - 1)]
        down = [(j, i) for i, j in up]
        last = lax.slice_in_dim(value, length - width, length, axis=dim)
        leading = lax.slice_in_dim(value, 0, width, axis=dim)
        before = lax.ppermute(last, axis, up)
        after = lax.ppermute(leading, axis, down)
        value = jnp.concatenate([before, value, after], axis=dim)
    return value


def contract_last(left, right):
    return lax.dot_general(
        left, right, (((1,), (1,)), ((), ())), preferred_element_type=jnp.float32
    )


def contract_first(left, right):
    return lax.dot_general(
        left, right, (((0,), (0,)), ((), ())), preferred_element_type=jnp.float32
    )


def on_device_plain(inputs, trunk_grad, weights):
    taps = weights.shape[0]
    grad = lax.all_to_all(trunk_grad, "seq", split_axis=1, concat_axis=2, tiled=True)
    grad_up = jnp.repeat(grad.astype(jnp.float32) * 0.5, 2, axis=1).astype(jnp.bfloat16)
    rows = grad_up.shape[1]
    padded = with_halo(grad_up, (("seq", 1),), 2)
    shifts = [padded[0, 4 - k : 4 - k + rows] for k in range(taps)]
    inputs_f = inputs[0].astype(jnp.float32)
    act_vals, back = jax.vjp(jax.nn.gelu, inputs_f)
    slope = back(jnp.ones_like(inputs_f))[0]
    act = act_vals.astype(jnp.bfloat16)
    in_width = inputs.shape[2]
    columns = lax.all_gather(weights, "seq", axis=2, tiled=True)
    piece = lax.all_gather(columns, "rep", axis=1, tiled=True)
    result = contract_last(shifts[0], piece[0])
    for project_k in range(1, taps):
        result = result + contract_last(shifts[project_k], piece[project_k])
    input_grad = (result * slope + grad_up[0, :, :in_width].astype(jnp.float32)).astype(
        jnp.bfloat16
    )
    scale_factor = float(rows * lax.axis_size("seq") * lax.axis_size("rep")) ** (-0.5)
    terms = jnp.stack([contract_first(act, shifts[k]) for k in range(taps)]) * scale_factor
    partial_sum = lax.psum_scatter(terms, "rep", scatter_dimension=1, tiled=True)
    weight_grad = lax.psum_scatter(partial_sum, "seq", scatter_dimension=2, tiled=True)
    return (input_grad[None], weight_grad)


def on_device(inputs, trunk_grad, weights):
    square = lax.axis_size("seq") == 4 and lax.axis_size("rep") % 8 == 0
    if square and weights.shape[2] % LANES == 0 and inputs.shape[2] % LANES == 0:
        return on_device_square(inputs, trunk_grad, weights)
    return on_device_plain(inputs, trunk_grad, weights)


def solution(mesh):
    in_specs = (P("rep", "seq", None), P("rep", None, "seq"), P(None, "rep", "seq"))
    out_specs = (P("rep", "seq", None), P(None, "rep", "seq"))
    return jax.shard_map(
        on_device, mesh=mesh, in_specs=in_specs, out_specs=out_specs, check_vma=False
    )
```

```python
import functools
import math

import jax
import jax.numpy as jnp
from jax import lax
from jax.experimental import pallas as pl
from jax.experimental.pallas import tpu as pltpu
from jax.sharding import PartitionSpec as P

LANES = 128
HALO = 32
CHUNKS = 4
FIRST = 80
EDGE = 16
MARGIN = HALO - EDGE
STEP = 64
SPLIT = 3
ROOT = math.sqrt(2.0 / math.pi)
CUBIC = 0.044715
SMALL = pl.CostEstimate(flops=1 << 20, bytes_accessed=1 << 16, transcendentals=0)
ANYWHERE = pl.BlockSpec(memory_space=pl.ANY)
ROW_OFFSETS = ((1, 1), (0, 1), (0, 0), (-1, 0), (-1, -1))
GRAD_PARTS = ((0, 0), (1, 0), (1, 1), (2, 1), (2, 2))


def from_peer(value, axis, distance):
    peers = lax.axis_size(axis)
    return lax.ppermute(value, axis, [(i, i ^ distance) for i in range(peers)])


def after(value, *earlier):
    return pl.pallas_call(
        lambda *refs: None,
        out_shape=jax.ShapeDtypeStruct(value.shape, value.dtype),
        in_specs=[ANYWHERE] * (1 + len(earlier)),
        out_specs=ANYWHERE,
        input_output_aliases={0: 0},
        name="after",
    )(value, *earlier)


def gather_line(value, axis, count, unit):
    found, mask = {0: value}, count - 1
    while mask:
        for distance in list(found):
            found[distance ^ mask] = from_peer(found[distance], axis, mask * unit)
        mask //= 2
    return [found[distance] for distance in range(count)]


def gelu_slope(x):
    tanh = jnp.tanh(ROOT * (x + CUBIC * (x * x * x)))
    return 0.5 * (1.0 + tanh) + 0.5 * x * (1.0 - tanh * tanh) * (
        ROOT * (1.0 + 3.0 * CUBIC * (x * x))
    )


def messages_kernel(place, x_ref, trunk_ref, beside_ref, below_ref, own_ref, edged, strip, sem):
    coarse, width, block = x_ref.shape[1] // 2, x_ref.shape[2], edged.shape[1]
    length = trunk_ref.shape[1]
    packed = (coarse + 2 * HALO) // CHUNKS
    copy = pltpu.make_async_copy(trunk_ref.at[0], edged.at[pl.ds(HALO, length)], sem)
    copy.start()
    edged[:HALO] = jnp.zeros((HALO, block), jnp.bfloat16)
    edged[HALO + length :] = jnp.zeros((HALO, block), jnp.bfloat16)

    @pl.loop(0, coarse // STEP)
    def _(step):
        start = pl.multiple_of(step * STEP, STEP)
        x = x_ref[0, pl.ds(pl.multiple_of(2 * start, 2 * STEP), 2 * STEP), :].astype(jnp.float32)
        act = x * (0.5 * (1.0 + jnp.tanh(ROOT * (x + CUBIC * (x * x * x)))))
        for c in range(width // LANES):
            strip[c] = act[:, c * LANES : (c + 1) * LANES]
        for parity in range(2):
            for c in range(width // LANES):
                picked = strip[c, pl.ds(parity, STEP, stride=2), :].astype(jnp.bfloat16)
                lanes = slice(parity * width + c * LANES, parity * width + (c + 1) * LANES)
                beside_ref[pl.ds(FIRST + start, STEP), lanes] = picked
                below_ref[pl.ds(start, STEP), lanes] = picked

    copy.wait()

    def pack(out_ref, row, distance, first, last):
        base = (place[0] ^ distance) * coarse
        for q in range(CHUNKS):
            start = pl.multiple_of(base + q * packed + first, 16)
            out_ref[row : row + last - first, q * block : (q + 1) * block] = edged[
                pl.ds(start, last - first), :
            ]

    pack(beside_ref, 0, 3, 0, FIRST)
    pack(beside_ref, FIRST + coarse, 1, 0, packed)
    pack(below_ref, coarse, 3, FIRST, packed)
    pack(below_ref, coarse + packed - FIRST, 2, 0, packed)
    pack(own_ref, 0, 0, 0, packed)


def messages(place, inputs, trunk_grad):
    _, fine, width = inputs.shape
    _, length, block = trunk_grad.shape
    coarse = fine // 2
    packed = (coarse + 2 * HALO) // CHUNKS
    rows = (FIRST + coarse + packed, coarse + packed - FIRST + packed, packed)
    return pl.pallas_call(
        messages_kernel,
        out_shape=[jax.ShapeDtypeStruct((n, 2 * width), jnp.bfloat16) for n in rows],
        grid_spec=pltpu.PrefetchScalarGridSpec(
            num_scalar_prefetch=1,
            grid=(1,),
            in_specs=[pl.BlockSpec(inputs.shape, lambda i, place: (0, 0, 0)), ANYWHERE],
            out_specs=[pl.BlockSpec((n, 2 * width), lambda i, place: (0, 0)) for n in rows],
            scratch_shapes=[
                pltpu.VMEM((length + 2 * HALO, block), jnp.bfloat16),
                pltpu.VMEM((width // LANES, 2 * STEP, LANES), jnp.float32),
                pltpu.SemaphoreType.DMA,
            ],
        ),
        compiler_params=pltpu.CompilerParams(vmem_limit_bytes=32 << 20),
        name="messages",
    )(place, inputs, trunk_grad)


def slope_kernel(x_ref, out_ref, scratch):
    width = x_ref.shape[2]

    @pl.loop(0, out_ref.shape[1] // 64)
    def _(step):
        start = pl.multiple_of(step * 64, 64)
        span = pl.ds(pl.multiple_of(2 * start, 128), 128)
        for c in range(width // LANES):
            lanes = slice(c * LANES, (c + 1) * LANES)
            scratch[c] = 0.5 * gelu_slope(x_ref[0, span, lanes].astype(jnp.float32))
            for parity in range(2):
                out_ref[parity, pl.ds(start, 64), lanes] = scratch[c, pl.ds(parity, 64, stride=2), :]


def half_slope(inputs):
    fine, width = inputs.shape[1:]
    return pl.pallas_call(
        slope_kernel,
        out_shape=jax.ShapeDtypeStruct((2, fine // 2, width), jnp.float32),
        in_specs=[pl.BlockSpec(memory_space=pltpu.VMEM)],
        out_specs=pl.BlockSpec(memory_space=pltpu.VMEM),
        scratch_shapes=[pltpu.VMEM((width // LANES, 128, LANES), jnp.float32)],
        compiler_params=pltpu.CompilerParams(vmem_limit_bytes=24 << 20),
        name="half_slope",
    )(inputs)


def start_act(place, coarse, layout, pieces, shifts_ref, held, shifts, sems, shift_sems):
    copies, row = [], 0
    for i, (distance, first, size, offset) in enumerate(layout):
        start = pl.multiple_of((place[0] ^ distance) * coarse + first, 16)
        spot = pl.ds(row, size)
        source = pieces[i].at[pl.ds(offset, size)]
        copies.append(pltpu.make_async_copy(source, held.at[spot], sems.at[i]))
        copies.append(
            pltpu.make_async_copy(shifts_ref.at[pl.ds(start, size)], shifts.at[spot], shift_sems.at[i])
        )
        row += size
    for copy in copies:
        copy.start()
    return copies


def early_terms(place, layout, pieces, shifts, coarse):
    both, columns = pieces[0].shape[1], shifts.shape[1]
    rows = sum(size for _, _, size, _ in layout)
    tile = 256

    def kernel(place, shifts_ref, *refs):
        pieces, total = refs[: len(layout)], refs[len(layout)]
        held, shifts, sems, shift_sems = refs[len(layout) + 1 :]
        copies = start_act(
            place, coarse, layout, pieces, shifts_ref, held, shifts, sems, shift_sems
        )
        for copy in copies:
            copy.wait()

        @pl.loop(0, both // tile)
        def _(i):
            span = pl.ds(pl.multiple_of(i * tile, tile), tile)
            total[span, :] = lax.dot_general(
                held[:, span], shifts[...], (((0,), (0,)), ((), ())), preferred_element_type=jnp.float32
            )

    return pl.pallas_call(
        kernel,
        out_shape=jax.ShapeDtypeStruct((both, columns), jnp.float32),
        grid_spec=pltpu.PrefetchScalarGridSpec(
            num_scalar_prefetch=1,
            grid=(1,),
            in_specs=[ANYWHERE] * (1 + len(pieces)),
            out_specs=pl.BlockSpec((both, columns), lambda i, place: (0, 0)),
            scratch_shapes=[
                pltpu.VMEM((rows, both), jnp.bfloat16),
                pltpu.VMEM((rows, columns), jnp.bfloat16),
                pltpu.SemaphoreType.DMA((len(pieces),)),
                pltpu.SemaphoreType.DMA((len(pieces),)),
            ],
        ),
        compiler_params=pltpu.CompilerParams(vmem_limit_bytes=48 << 20),
        cost_estimate=SMALL,
        name="weight_grad_early",
    )(place, shifts, *pieces)


def late_terms(place, layout, pieces, shifts, early, coarse, scale, planes, taps, rows):
    both, columns = early.shape
    width, block = both // 2, columns // 3
    count = sum(size for _, _, size, _ in layout)
    tile = 256
    shape = (planes, taps, rows, block)

    def kernel(place, shifts_ref, early_ref, *refs):
        pieces, (mine_ref, theirs_ref) = refs[: len(layout)], refs[len(layout) : len(layout) + 2]
        held, shifts, total, sems, shift_sems, early_sems = refs[len(layout) + 2 :]
        core, plane = place[1] % 2, place[1] // 2
        copies = start_act(
            place, coarse, layout, pieces, shifts_ref, held, shifts, sems, shift_sems
        )

        def fetch(i):
            span = pl.ds(pl.multiple_of(i * tile, tile), tile)
            return pltpu.make_async_copy(early_ref.at[span], total.at[span], early_sems.at[i])

        for i in range(both // tile):
            fetch(i).start()
        for copy in copies:
            copy.wait()

        @pl.loop(0, both // tile)
        def _(i):
            span = pl.ds(pl.multiple_of(i * tile, tile), tile)
            term = lax.dot_general(
                held[:, span], shifts[...], (((0,), (0,)), ((), ())), preferred_element_type=jnp.float32
            )
            fetch(i).wait()
            total[span, :] += term

        for out_ref, parity, kind in (
            (theirs_ref, 1 - core, jnp.bfloat16),
            (mine_ref, core, jnp.float32),
        ):

            @pl.loop(0, planes)
            def _(j):
                start = ((plane ^ j) * 2 + parity) * rows
                even = pl.ds(pl.multiple_of(start, 16), rows)
                odd = pl.ds(pl.multiple_of(width + start, 16), rows)
                for k, (left, right) in enumerate(GRAD_PARTS):
                    term = total[even, left * block : (left + 1) * block]
                    term += total[odd, right * block : (right + 1) * block]
                    out_ref[j, k] = (scale * term).astype(kind)

    whole = pl.BlockSpec(shape, lambda i, place: (0, 0, 0, 0))
    return pl.pallas_call(
        kernel,
        out_shape=(
            jax.ShapeDtypeStruct(shape, jnp.float32),
            jax.ShapeDtypeStruct(shape, jnp.bfloat16),
        ),
        grid_spec=pltpu.PrefetchScalarGridSpec(
            num_scalar_prefetch=1,
            grid=(1,),
            in_specs=[ANYWHERE] * (2 + len(pieces)),
            out_specs=[whole, whole],
            scratch_shapes=[
                pltpu.VMEM((count, both), jnp.bfloat16),
                pltpu.VMEM((count, columns), jnp.bfloat16),
                pltpu.VMEM((both, columns), jnp.float32),
                pltpu.SemaphoreType.DMA((len(pieces),)),
                pltpu.SemaphoreType.DMA((len(pieces),)),
                pltpu.SemaphoreType.DMA((both // tile,)),
            ],
        ),
        compiler_params=pltpu.CompilerParams(vmem_limit_bytes=48 << 20),
        cost_estimate=SMALL,
        name="weight_grad_late",
    )(place, shifts, early, *pieces)


def shifted_total(products, first_tap, base, lanes, parity):
    total = None
    for by in (0, 1, -1):
        wanted = [k for k in range(products.shape[0]) if ROW_OFFSETS[first_tap + k][parity] == by]
        if wanted:
            near = pl.ds(base + MARGIN - 8, STEP + 16)
            part = sum(products[k, near, lanes] for k in wanted)[8 + by : 8 + by + STEP]
            total = part if total is None else total + part
    return total


def gradient_stage(place, windows, first_tap, pieces, distances, slope, begun, shape, last=False):
    _, fine, width = shape
    coarse, seqs = fine // 2, len(windows)
    taps, rows, block = pieces[0][0].shape[-3:]
    planes = width // (2 * rows)
    packed = (coarse + 2 * HALO) // CHUNKS
    window, used = CHUNKS * packed, coarse + 2 * MARGIN
    depth, planar = len(distances) * block, (2, coarse, width)
    first = begun is None
    needed = list(range(seqs)) if first else distances
    parts = [(d, *part) for d in needed for part in windows[d]]
    operands = [part[1] for part in parts] + [piece[0] for piece in pieces]
    operands += [slope] + ([] if first else [begun])

    def body(place, *refs):
        own, refs = refs[: len(parts)], refs[len(parts) :]
        sources, refs = refs[: len(pieces)], refs[len(pieces) :]
        slope_ref, refs = refs[0], refs[1:]
        if not first:
            begun_ref, refs = refs[0], refs[1:]
        out_ref, wv, gv, products, slopes, sems, grad_sems, slope_sem = refs[:8]
        me, core = place[0], place[1] % 2

        def kernel_copies(k):
            for number, (array, plane, flip, distance) in enumerate(pieces):
                spot = pl.ds(distances.index(distance) * block, block)
                span = pl.ds(plane, array.shape[0])
                target = wv.at[k, span, core ^ flip, :, spot]
                source = sources[number]
                source = source.at[:, k] if len(array.shape) == 4 else source.at[:, distance, k]
                yield source, target, sems.at[k, number]

        def window_copies(target_of, sems):
            for number, (distance, _, row, first, size) in enumerate(parts):
                for q in range(CHUNKS):
                    source = own[number].at[pl.ds(row, size), pl.ds(q * block, block)]
                    target = target_of(distance, pl.ds(q * packed + first, size))
                    if target is not None:
                        yield pltpu.make_async_copy(source, target, sems.at[number, q])

        def into_window(distance, span):
            if distance not in distances:
                return None
            return gv.at[span, pl.ds(distances.index(distance) * block, block)]

        early = list(window_copies(into_window, grad_sems))
        late = [pltpu.make_async_copy(slope_ref, slopes, slope_sem)]
        if not first:
            sums, strip, sum_sem = refs[8:]
            late.append(pltpu.make_async_copy(begun_ref, sums, sum_sem))
        else:
            skips, skip_sems = refs[8:]
            late += window_copies(lambda d, span: skips.at[me ^ d, span], skip_sems)
        for copy in early:
            copy.start()
        for k in range(taps):
            for copy in kernel_copies(k):
                pltpu.make_async_copy(*copy).start()
        for copy in late:
            copy.start()
        for copy in early:
            copy.wait()

        @pl.loop(0, taps)
        def _(k):
            for copy in kernel_copies(k):
                pltpu.make_async_copy(*copy).wait()
            half = planes // 2
            for part in range(2):
                kernel = wv[k, part * half : (part + 1) * half].reshape(2 * half * rows, depth)
                lanes = slice(part * 2 * half * rows, (part + 1) * 2 * half * rows)
                products[k, :, lanes] = lax.dot_general(
                    gv[EDGE : EDGE + used],
                    kernel,
                    (((1,), (1,)), ((), ())),
                    preferred_element_type=jnp.float32,
                )

        for copy in late:
            copy.wait()

        @pl.loop(0, coarse // STEP)
        def _(i):
            base = pl.multiple_of(i * STEP, STEP)
            spot, span = pl.ds(base, STEP), pl.ds(pl.multiple_of(2 * base, 2 * STEP), 2 * STEP)
            for c in range(width // LANES):
                lanes = slice(c * LANES, (c + 1) * LANES)
                if first:
                    left = c * LANES % block
                    skip = skips[c * LANES // block, pl.ds(base + HALO, STEP), left : left + LANES]
                    skip = 0.5 * skip.astype(jnp.float32)
                for parity in range(2):
                    total = shifted_total(products, first_tap, base, lanes, parity)
                    total = total * slopes[parity, spot, lanes]
                    total = total + (skip if first else sums[parity, spot, lanes])
                    if last:
                        strip[c, pl.ds(parity, STEP, stride=2), :] = total
                    else:
                        out_ref[parity, spot, lanes] = total
                if last:
                    out_ref[0, span, lanes] = strip[c].astype(jnp.bfloat16)

    out_shape = jax.ShapeDtypeStruct(shape if last else planar, jnp.bfloat16 if last else jnp.float32)
    scratch = [
        pltpu.VMEM((taps, planes, 2, rows, depth), jnp.bfloat16),
        pltpu.VMEM((window, depth), jnp.bfloat16),
        pltpu.VMEM((taps, used, width), jnp.float32),
        pltpu.VMEM(planar, jnp.float32),
        pltpu.SemaphoreType.DMA((taps, len(pieces))),
        pltpu.SemaphoreType.DMA((len(parts), CHUNKS)),
        pltpu.SemaphoreType.DMA,
    ]
    if not first:
        scratch += [
            pltpu.VMEM(planar, jnp.float32),
            pltpu.VMEM((width // LANES, 2 * STEP, LANES), jnp.float32),
            pltpu.SemaphoreType.DMA,
        ]
    else:
        scratch += [
            pltpu.VMEM((seqs, window, block), jnp.bfloat16),
            pltpu.SemaphoreType.DMA((len(parts), CHUNKS)),
        ]
    return pl.pallas_call(
        body,
        out_shape=out_shape,
        grid_spec=pltpu.PrefetchScalarGridSpec(
            num_scalar_prefetch=1,
            grid=(1,),
            in_specs=[ANYWHERE] * len(operands),
            out_specs=pl.BlockSpec(out_shape.shape, lambda i, place: (0, 0, 0)),
            scratch_shapes=scratch,
        ),
        compiler_params=pltpu.CompilerParams(vmem_limit_bytes=56 << 20),
        cost_estimate=SMALL,
        name="input_grad",
    )(place, *operands)


def stack_planes(place, line):
    count = len(line)

    def kernel(place, *refs):
        parts, out_ref = refs[:count], refs[count]
        for j in range(count):
            out_ref[place[1] // 2 ^ j] = parts[j][...]

    shape = line[0].shape
    return pl.pallas_call(
        kernel,
        out_shape=jax.ShapeDtypeStruct((count, *shape), line[0].dtype),
        grid_spec=pltpu.PrefetchScalarGridSpec(
            num_scalar_prefetch=1,
            grid=(1,),
            in_specs=[pl.BlockSpec(shape, lambda i, place: (0,) * len(shape))] * count,
            out_specs=pl.BlockSpec((count, *shape), lambda i, place: (0,) * (1 + len(shape))),
        ),
        compiler_params=pltpu.CompilerParams(vmem_limit_bytes=24 << 20),
        cost_estimate=SMALL,
        name="stack_planes",
    )(place, *line)


def on_device_square(inputs, trunk_grad, weights):
    seqs, reps = lax.axis_size("seq"), lax.axis_size("rep")
    me, rep = lax.axis_index("seq"), lax.axis_index("rep")
    place = jnp.stack([me, rep]).astype(jnp.int32)
    taps, rows, block = weights.shape
    fine = inputs.shape[1]
    coarse, planes = fine // 2, reps // 2
    packed = (coarse + 2 * HALO) // CHUNKS
    half = coarse // 2

    to_beside, to_below, own_window = messages(place, inputs, trunk_grad)
    beside, below = from_peer(to_beside, "seq", 1), from_peer(to_below, "seq", 2)
    slope = half_slope(inputs)
    last_taps = weights[SPLIT:]
    across = [last_taps] + [from_peer(last_taps, "seq", d) for d in range(1, seqs)]
    column = stack_planes(place, gather_line(weights[:SPLIT], "rep", planes, 2))
    lines = stack_planes(place, gather_line(jnp.stack(across), "rep", planes, 2))
    trunk = trunk_grad[0]
    zeros = jnp.zeros((1, block), jnp.bfloat16)
    later = jnp.concatenate([trunk[1:], zeros])
    earlier = jnp.concatenate([zeros, trunk[:-1]])
    shifts = jnp.concatenate([later, trunk, earlier], axis=1)
    top = after(beside[: FIRST + half], slope, column, lines, shifts)
    bottom = after(below[half : coarse + packed - FIRST], slope, column, lines, shifts)
    far_top, far_bottom = from_peer(top, "seq", 2), from_peer(bottom, "seq", 1)

    other_column, other_lines = from_peer(column, "rep", 1), from_peer(lines, "rep", 1)
    column = after(column, far_top, far_bottom)
    kept_beside, kept_below = from_peer(column, "seq", 1), from_peer(column, "seq", 2)

    scale = 0.5 * float(fine * seqs * reps) ** (-0.5)
    near_rows = [(0, 0, coarse, FIRST), (1, 0, coarse, FIRST), (2, 0, coarse, 0)]
    far_rows = [(3, 0, half, FIRST), (3, half, half, 0)]
    early = early_terms(place, near_rows, [to_beside, beside, below], shifts, coarse)
    mine, theirs = late_terms(
        place, far_rows, [far_top, far_bottom], shifts, early, coarse, scale, planes, taps, rows
    )
    arrived = from_peer(theirs, "rep", 1)
    weight_grad = mine[0] + arrived[0].astype(jnp.float32)
    leaving = [(mine[j] + arrived[j].astype(jnp.float32)).astype(jnp.bfloat16) for j in range(planes)]
    summed = [from_peer(leaving[j], "rep", 2 * j) for j in range(1, planes)]

    kept_beside, kept_below = after(kept_beside, early), after(kept_below, early)
    far_first = from_peer(kept_beside[: planes // 2], "seq", 2)
    far_second = from_peer(kept_below[planes // 2 :], "seq", 1)
    soon = [(after(column, *leaving[1:]), 0, 0, 0), (other_column, 0, 1, 0)]
    for part, distance in ((kept_beside, 1), (kept_below, 2)):
        soon += [(part, 0, 0, distance), (from_peer(part, "rep", 1), 0, 1, distance)]

    windows = [
        [(own_window, 0, 0, packed)],
        [(beside, FIRST + coarse, 0, packed)],
        [(below, coarse + packed - FIRST, 0, packed)],
        [(far_top, 0, 0, FIRST), (far_bottom, half, FIRST, packed - FIRST)],
    ]
    stage = functools.partial(gradient_stage, place, windows, slope=slope, shape=inputs.shape)
    crossed = [(part, 0, flip, d) for flip, part in enumerate((lines, other_lines)) for d in range(seqs)]
    begun = stage(SPLIT, crossed, list(range(seqs)), begun=None)
    begun, rest = stage(0, soon, [0, 1, 2], begun=begun), []
    for part, plane in ((far_first, 0), (far_second, planes // 2)):
        part = after(part, begun, *summed)
        rest += [(part, plane, 0, 3), (from_peer(part, "rep", 1), plane, 1, 3)]
    input_grad = stage(0, rest, [3], begun=begun, last=True)
    for part in summed:
        weight_grad = weight_grad + after(part, input_grad).astype(jnp.float32)
    return (input_grad, weight_grad)


def with_halo(value, sides, width):
    for axis, dim in sides:
        peers, length = (lax.axis_size(axis), value.shape[dim])
        up = [(i, (i + 1) % peers) for i in range(peers - 1)]
        down = [(j, i) for i, j in up]
        last = lax.slice_in_dim(value, length - width, length, axis=dim)
        leading = lax.slice_in_dim(value, 0, width, axis=dim)
        before = lax.ppermute(last, axis, up)
        after = lax.ppermute(leading, axis, down)
        value = jnp.concatenate([before, value, after], axis=dim)
    return value


def contract_last(left, right):
    return lax.dot_general(
        left, right, (((1,), (1,)), ((), ())), preferred_element_type=jnp.float32
    )


def contract_first(left, right):
    return lax.dot_general(
        left, right, (((0,), (0,)), ((), ())), preferred_element_type=jnp.float32
    )


def on_device_plain(inputs, trunk_grad, weights):
    taps = weights.shape[0]
    grad = lax.all_to_all(trunk_grad, "seq", split_axis=1, concat_axis=2, tiled=True)
    grad_up = jnp.repeat(grad.astype(jnp.float32) * 0.5, 2, axis=1).astype(jnp.bfloat16)
    rows = grad_up.shape[1]
    padded = with_halo(grad_up, (("seq", 1),), 2)
    shifts = [padded[0, 4 - k : 4 - k + rows] for k in range(taps)]
    inputs_f = inputs[0].astype(jnp.float32)
    act_vals, back = jax.vjp(jax.nn.gelu, inputs_f)
    slope = back(jnp.ones_like(inputs_f))[0]
    act = act_vals.astype(jnp.bfloat16)
    in_width = inputs.shape[2]
    columns = lax.all_gather(weights, "seq", axis=2, tiled=True)
    piece = lax.all_gather(columns, "rep", axis=1, tiled=True)
    result = contract_last(shifts[0], piece[0])
    for project_k in range(1, taps):
        result = result + contract_last(shifts[project_k], piece[project_k])
    input_grad = (result * slope + grad_up[0, :, :in_width].astype(jnp.float32)).astype(
        jnp.bfloat16
    )
    scale_factor = float(rows * lax.axis_size("seq") * lax.axis_size("rep")) ** (-0.5)
    terms = jnp.stack([contract_first(act, shifts[k]) for k in range(taps)]) * scale_factor
    partial_sum = lax.psum_scatter(terms, "rep", scatter_dimension=1, tiled=True)
    weight_grad = lax.psum_scatter(partial_sum, "seq", scatter_dimension=2, tiled=True)
    return (input_grad[None], weight_grad)


def on_device(inputs, trunk_grad, weights):
    square = lax.axis_size("seq") == 4 and lax.axis_size("rep") % 8 == 0
    if square and weights.shape[2] % LANES == 0 and inputs.shape[2] % LANES == 0:
        return on_device_square(inputs, trunk_grad, weights)
    return on_device_plain(inputs, trunk_grad, weights)


def solution(mesh):
    in_specs = (P("rep", "seq", None), P("rep", None, "seq"), P(None, "rep", "seq"))
    out_specs = (P("rep", "seq", None), P(None, "rep", "seq"))
    return jax.shard_map(
        on_device, mesh=mesh, in_specs=in_specs, out_specs=out_specs, check_vma=False
    )
```

```python
import functools
import math

import jax
import jax.numpy as jnp
from jax import lax
from jax.experimental import pallas as pl
from jax.experimental.pallas import tpu as pltpu
from jax.sharding import PartitionSpec as P

LANES = 128
HALO = 32
CHUNKS = 4
FIRST = 80
EDGE = 16
MARGIN = HALO - EDGE
STEP = 64
SPLIT = 3
ROOT = math.sqrt(2.0 / math.pi)
CUBIC = 0.044715
SMALL = pl.CostEstimate(flops=1 << 20, bytes_accessed=1 << 16, transcendentals=0)
ANYWHERE = pl.BlockSpec(memory_space=pl.ANY)
ROW_OFFSETS = ((1, 1), (0, 1), (0, 0), (-1, 0), (-1, -1))
GRAD_PARTS = ((0, 0), (1, 0), (1, 1), (2, 1), (2, 2))


def from_peer(value, axis, distance):
    peers = lax.axis_size(axis)
    return lax.ppermute(value, axis, [(i, i ^ distance) for i in range(peers)])


def after(value, *earlier):
    return pl.pallas_call(
        lambda *refs: None,
        out_shape=jax.ShapeDtypeStruct(value.shape, value.dtype),
        in_specs=[ANYWHERE] * (1 + len(earlier)),
        out_specs=ANYWHERE,
        input_output_aliases={0: 0},
        name="after",
    )(value, *earlier)


def gather_line(value, axis, count, unit):
    found, mask = {0: value}, count - 1
    while mask:
        for distance in list(found):
            found[distance ^ mask] = from_peer(found[distance], axis, mask * unit)
        mask //= 2
    return [found[distance] for distance in range(count)]


def gelu_slope(x):
    tanh = jnp.tanh(ROOT * (x + CUBIC * (x * x * x)))
    return 0.5 * (1.0 + tanh) + 0.5 * x * (1.0 - tanh * tanh) * (
        ROOT * (1.0 + 3.0 * CUBIC * (x * x))
    )


def messages_kernel(place, x_ref, trunk_ref, beside_ref, below_ref, own_ref, edged, strip, sem):
    coarse, width, block = x_ref.shape[1] // 2, x_ref.shape[2], edged.shape[1]
    length = trunk_ref.shape[1]
    packed = (coarse + 2 * HALO) // CHUNKS
    copy = pltpu.make_async_copy(trunk_ref.at[0], edged.at[pl.ds(HALO, length)], sem)
    copy.start()
    edged[:HALO] = jnp.zeros((HALO, block), jnp.bfloat16)
    edged[HALO + length :] = jnp.zeros((HALO, block), jnp.bfloat16)

    @pl.loop(0, coarse // STEP)
    def _(step):
        start = pl.multiple_of(step * STEP, STEP)
        x = x_ref[0, pl.ds(pl.multiple_of(2 * start, 2 * STEP), 2 * STEP), :].astype(jnp.float32)
        act = x * (0.5 * (1.0 + jnp.tanh(ROOT * (x + CUBIC * (x * x * x)))))
        for c in range(width // LANES):
            strip[c] = act[:, c * LANES : (c + 1) * LANES]
        for parity in range(2):
            for c in range(width // LANES):
                picked = strip[c, pl.ds(parity, STEP, stride=2), :].astype(jnp.bfloat16)
                lanes = slice(parity * width + c * LANES, parity * width + (c + 1) * LANES)
                beside_ref[pl.ds(FIRST + start, STEP), lanes] = picked
                below_ref[pl.ds(start, STEP), lanes] = picked

    copy.wait()

    def pack(out_ref, row, distance, first, last):
        base = (place[0] ^ distance) * coarse
        for q in range(CHUNKS):
            start = pl.multiple_of(base + q * packed + first, 16)
            out_ref[row : row + last - first, q * block : (q + 1) * block] = edged[
                pl.ds(start, last - first), :
            ]

    pack(beside_ref, 0, 3, 0, FIRST)
    pack(beside_ref, FIRST + coarse, 1, 0, packed)
    pack(below_ref, coarse, 3, FIRST, packed)
    pack(below_ref, coarse + packed - FIRST, 2, 0, packed)
    pack(own_ref, 0, 0, 0, packed)


def messages(place, inputs, trunk_grad):
    _, fine, width = inputs.shape
    _, length, block = trunk_grad.shape
    coarse = fine // 2
    packed = (coarse + 2 * HALO) // CHUNKS
    rows = (FIRST + coarse + packed, coarse + packed - FIRST + packed, packed)
    return pl.pallas_call(
        messages_kernel,
        out_shape=[jax.ShapeDtypeStruct((n, 2 * width), jnp.bfloat16) for n in rows],
        grid_spec=pltpu.PrefetchScalarGridSpec(
            num_scalar_prefetch=1,
            grid=(1,),
            in_specs=[pl.BlockSpec(inputs.shape, lambda i, place: (0, 0, 0)), ANYWHERE],
            out_specs=[pl.BlockSpec((n, 2 * width), lambda i, place: (0, 0)) for n in rows],
            scratch_shapes=[
                pltpu.VMEM((length + 2 * HALO, block), jnp.bfloat16),
                pltpu.VMEM((width // LANES, 2 * STEP, LANES), jnp.float32),
                pltpu.SemaphoreType.DMA,
            ],
        ),
        compiler_params=pltpu.CompilerParams(vmem_limit_bytes=32 << 20),
        name="messages",
    )(place, inputs, trunk_grad)


def slope_kernel(x_ref, out_ref, scratch):
    width = x_ref.shape[2]

    @pl.loop(0, out_ref.shape[1] // 64)
    def _(step):
        start = pl.multiple_of(step * 64, 64)
        span = pl.ds(pl.multiple_of(2 * start, 128), 128)
        for c in range(width // LANES):
            lanes = slice(c * LANES, (c + 1) * LANES)
            scratch[c] = 0.5 * gelu_slope(x_ref[0, span, lanes].astype(jnp.float32))
            for parity in range(2):
                out_ref[parity, pl.ds(start, 64), lanes] = scratch[c, pl.ds(parity, 64, stride=2), :]


def half_slope(inputs):
    fine, width = inputs.shape[1:]
    return pl.pallas_call(
        slope_kernel,
        out_shape=jax.ShapeDtypeStruct((2, fine // 2, width), jnp.float32),
        in_specs=[pl.BlockSpec(memory_space=pltpu.VMEM)],
        out_specs=pl.BlockSpec(memory_space=pltpu.VMEM),
        scratch_shapes=[pltpu.VMEM((width // LANES, 128, LANES), jnp.float32)],
        compiler_params=pltpu.CompilerParams(vmem_limit_bytes=24 << 20),
        name="half_slope",
    )(inputs)


def start_act(place, coarse, layout, pieces, shifts_ref, held, shifts, sems, shift_sems):
    copies, row = [], 0
    for i, (distance, first, size, offset) in enumerate(layout):
        start = pl.multiple_of((place[0] ^ distance) * coarse + first, 16)
        spot = pl.ds(row, size)
        source = pieces[i].at[pl.ds(offset, size)]
        copies.append(pltpu.make_async_copy(source, held.at[spot], sems.at[i]))
        copies.append(
            pltpu.make_async_copy(shifts_ref.at[pl.ds(start, size)], shifts.at[spot], shift_sems.at[i])
        )
        row += size
    for copy in copies:
        copy.start()
    return copies


def early_terms(place, layout, pieces, shifts, coarse):
    both, columns = pieces[0].shape[1], shifts.shape[1]
    rows = sum(size for _, _, size, _ in layout)
    tile = 256

    def kernel(place, shifts_ref, *refs):
        pieces, total = refs[: len(layout)], refs[len(layout)]
        held, shifts, sems, shift_sems = refs[len(layout) + 1 :]
        copies = start_act(
            place, coarse, layout, pieces, shifts_ref, held, shifts, sems, shift_sems
        )
        for copy in copies:
            copy.wait()

        @pl.loop(0, both // tile)
        def _(i):
            span = pl.ds(pl.multiple_of(i * tile, tile), tile)
            total[span, :] = lax.dot_general(
                held[:, span], shifts[...], (((0,), (0,)), ((), ())), preferred_element_type=jnp.float32
            )

    return pl.pallas_call(
        kernel,
        out_shape=jax.ShapeDtypeStruct((both, columns), jnp.float32),
        grid_spec=pltpu.PrefetchScalarGridSpec(
            num_scalar_prefetch=1,
            grid=(1,),
            in_specs=[ANYWHERE] * (1 + len(pieces)),
            out_specs=pl.BlockSpec((both, columns), lambda i, place: (0, 0)),
            scratch_shapes=[
                pltpu.VMEM((rows, both), jnp.bfloat16),
                pltpu.VMEM((rows, columns), jnp.bfloat16),
                pltpu.SemaphoreType.DMA((len(pieces),)),
                pltpu.SemaphoreType.DMA((len(pieces),)),
            ],
        ),
        compiler_params=pltpu.CompilerParams(vmem_limit_bytes=48 << 20),
        cost_estimate=SMALL,
        name="weight_grad_early",
    )(place, shifts, *pieces)


def late_terms(place, layout, pieces, shifts, early, coarse, scale, planes, taps, rows):
    both, columns = early.shape
    width, block = both // 2, columns // 3
    count = sum(size for _, _, size, _ in layout)
    tile = 256
    shape = (planes, taps, rows, block)

    def kernel(place, shifts_ref, early_ref, *refs):
        pieces, (mine_ref, theirs_ref) = refs[: len(layout)], refs[len(layout) : len(layout) + 2]
        held, shifts, total, sems, shift_sems, early_sems = refs[len(layout) + 2 :]
        core, plane = place[1] % 2, place[1] // 2
        copies = start_act(
            place, coarse, layout, pieces, shifts_ref, held, shifts, sems, shift_sems
        )

        def fetch(i):
            span = pl.ds(pl.multiple_of(i * tile, tile), tile)
            return pltpu.make_async_copy(early_ref.at[span], total.at[span], early_sems.at[i])

        for i in range(both // tile):
            fetch(i).start()
        for copy in copies:
            copy.wait()

        @pl.loop(0, both // tile)
        def _(i):
            span = pl.ds(pl.multiple_of(i * tile, tile), tile)
            term = lax.dot_general(
                held[:, span], shifts[...], (((0,), (0,)), ((), ())), preferred_element_type=jnp.float32
            )
            fetch(i).wait()
            total[span, :] += term

        for out_ref, parity, kind in (
            (theirs_ref, 1 - core, jnp.bfloat16),
            (mine_ref, core, jnp.float32),
        ):

            @pl.loop(0, planes)
            def _(j):
                start = ((plane ^ j) * 2 + parity) * rows
                even = pl.ds(pl.multiple_of(start, 16), rows)
                odd = pl.ds(pl.multiple_of(width + start, 16), rows)
                for k, (left, right) in enumerate(GRAD_PARTS):
                    term = total[even, left * block : (left + 1) * block]
                    term += total[odd, right * block : (right + 1) * block]
                    out_ref[j, k] = (scale * term).astype(kind)

    whole = pl.BlockSpec(shape, lambda i, place: (0, 0, 0, 0))
    return pl.pallas_call(
        kernel,
        out_shape=(
            jax.ShapeDtypeStruct(shape, jnp.float32),
            jax.ShapeDtypeStruct(shape, jnp.bfloat16),
        ),
        grid_spec=pltpu.PrefetchScalarGridSpec(
            num_scalar_prefetch=1,
            grid=(1,),
            in_specs=[ANYWHERE] * (2 + len(pieces)),
            out_specs=[whole, whole],
            scratch_shapes=[
                pltpu.VMEM((count, both), jnp.bfloat16),
                pltpu.VMEM((count, columns), jnp.bfloat16),
                pltpu.VMEM((both, columns), jnp.float32),
                pltpu.SemaphoreType.DMA((len(pieces),)),
                pltpu.SemaphoreType.DMA((len(pieces),)),
                pltpu.SemaphoreType.DMA((both // tile,)),
            ],
        ),
        compiler_params=pltpu.CompilerParams(vmem_limit_bytes=48 << 20),
        cost_estimate=SMALL,
        name="weight_grad_late",
    )(place, shifts, early, *pieces)


def shifted_total(products, first_tap, base, lanes, parity):
    total = None
    for by in (0, 1, -1):
        wanted = [k for k in range(products.shape[0]) if ROW_OFFSETS[first_tap + k][parity] == by]
        if wanted:
            near = pl.ds(base + MARGIN - 8, STEP + 16)
            part = sum(products[k, near, lanes] for k in wanted)[8 + by : 8 + by + STEP]
            total = part if total is None else total + part
    return total


def gradient_stage(place, windows, first_tap, pieces, distances, slope, begun, shape, last=False):
    _, fine, width = shape
    coarse, seqs = fine // 2, len(windows)
    taps, rows, block = pieces[0][0].shape[-3:]
    planes = width // (2 * rows)
    packed = (coarse + 2 * HALO) // CHUNKS
    window, used = CHUNKS * packed, coarse + 2 * MARGIN
    depth, planar = len(distances) * block, (2, coarse, width)
    first = begun is None
    needed = list(range(seqs)) if first else distances
    parts = [(d, *part) for d in needed for part in windows[d]]
    operands = [part[1] for part in parts] + [piece[0] for piece in pieces]
    operands += [slope] + ([] if first else [begun])

    def body(place, *refs):
        own, refs = refs[: len(parts)], refs[len(parts) :]
        sources, refs = refs[: len(pieces)], refs[len(pieces) :]
        slope_ref, refs = refs[0], refs[1:]
        if not first:
            begun_ref, refs = refs[0], refs[1:]
        out_ref, wv, gv, products, slopes, sems, grad_sems, slope_sem = refs[:8]
        me, core = place[0], place[1] % 2

        def kernel_copies(k):
            for number, (array, plane, flip, distance) in enumerate(pieces):
                spot = pl.ds(distances.index(distance) * block, block)
                span = pl.ds(plane, array.shape[0])
                target = wv.at[k, span, core ^ flip, :, spot]
                source = sources[number]
                source = source.at[:, k] if len(array.shape) == 4 else source.at[:, distance, k]
                yield source, target, sems.at[k, number]

        def window_copies(target_of, sems):
            for number, (distance, _, row, first, size) in enumerate(parts):
                for q in range(CHUNKS):
                    source = own[number].at[pl.ds(row, size), pl.ds(q * block, block)]
                    target = target_of(distance, pl.ds(q * packed + first, size))
                    if target is not None:
                        yield pltpu.make_async_copy(source, target, sems.at[number, q])

        def into_window(distance, span):
            if distance not in distances:
                return None
            return gv.at[span, pl.ds(distances.index(distance) * block, block)]

        early = list(window_copies(into_window, grad_sems))
        late = [pltpu.make_async_copy(slope_ref, slopes, slope_sem)]
        if not first:
            sums, strip, sum_sem = refs[8:]
            late.append(pltpu.make_async_copy(begun_ref, sums, sum_sem))
        else:
            skips, skip_sems = refs[8:]
            late += window_copies(lambda d, span: skips.at[me ^ d, span], skip_sems)
        for copy in early:
            copy.start()
        for k in range(taps):
            for copy in kernel_copies(k):
                pltpu.make_async_copy(*copy).start()
        for copy in late:
            copy.start()
        for copy in early:
            copy.wait()

        @pl.loop(0, taps)
        def _(k):
            for copy in kernel_copies(k):
                pltpu.make_async_copy(*copy).wait()
            half = planes // 2
            for part in range(2):
                kernel = wv[k, part * half : (part + 1) * half].reshape(2 * half * rows, depth)
                lanes = slice(part * 2 * half * rows, (part + 1) * 2 * half * rows)
                products[k, :, lanes] = lax.dot_general(
                    gv[EDGE : EDGE + used],
                    kernel,
                    (((1,), (1,)), ((), ())),
                    preferred_element_type=jnp.float32,
                )

        for copy in late:
            copy.wait()

        @pl.loop(0, coarse // STEP)
        def _(i):
            base = pl.multiple_of(i * STEP, STEP)
            spot, span = pl.ds(base, STEP), pl.ds(pl.multiple_of(2 * base, 2 * STEP), 2 * STEP)
            for c in range(width // LANES):
                lanes = slice(c * LANES, (c + 1) * LANES)
                if first:
                    left = c * LANES % block
                    skip = skips[c * LANES // block, pl.ds(base + HALO, STEP), left : left + LANES]
                    skip = 0.5 * skip.astype(jnp.float32)
                for parity in range(2):
                    total = shifted_total(products, first_tap, base, lanes, parity)
                    total = total * slopes[parity, spot, lanes]
                    total = total + (skip if first else sums[parity, spot, lanes])
                    if last:
                        strip[c, pl.ds(parity, STEP, stride=2), :] = total
                    else:
                        out_ref[parity, spot, lanes] = total
                if last:
                    out_ref[0, span, lanes] = strip[c].astype(jnp.bfloat16)

    out_shape = jax.ShapeDtypeStruct(shape if last else planar, jnp.bfloat16 if last else jnp.float32)
    scratch = [
        pltpu.VMEM((taps, planes, 2, rows, depth), jnp.bfloat16),
        pltpu.VMEM((window, depth), jnp.bfloat16),
        pltpu.VMEM((taps, used, width), jnp.float32),
        pltpu.VMEM(planar, jnp.float32),
        pltpu.SemaphoreType.DMA((taps, len(pieces))),
        pltpu.SemaphoreType.DMA((len(parts), CHUNKS)),
        pltpu.SemaphoreType.DMA,
    ]
    if not first:
        scratch += [
            pltpu.VMEM(planar, jnp.float32),
            pltpu.VMEM((width // LANES, 2 * STEP, LANES), jnp.float32),
            pltpu.SemaphoreType.DMA,
        ]
    else:
        scratch += [
            pltpu.VMEM((seqs, window, block), jnp.bfloat16),
            pltpu.SemaphoreType.DMA((len(parts), CHUNKS)),
        ]
    return pl.pallas_call(
        body,
        out_shape=out_shape,
        grid_spec=pltpu.PrefetchScalarGridSpec(
            num_scalar_prefetch=1,
            grid=(1,),
            in_specs=[ANYWHERE] * len(operands),
            out_specs=pl.BlockSpec(out_shape.shape, lambda i, place: (0, 0, 0)),
            scratch_shapes=scratch,
        ),
        compiler_params=pltpu.CompilerParams(vmem_limit_bytes=56 << 20),
        cost_estimate=SMALL,
        name="input_grad",
    )(place, *operands)


def stack_planes(place, line):
    count = len(line)

    def kernel(place, *refs):
        parts, out_ref = refs[:count], refs[count]
        for j in range(count):
            out_ref[place[1] // 2 ^ j] = parts[j][...]

    shape = line[0].shape
    return pl.pallas_call(
        kernel,
        out_shape=jax.ShapeDtypeStruct((count, *shape), line[0].dtype),
        grid_spec=pltpu.PrefetchScalarGridSpec(
            num_scalar_prefetch=1,
            grid=(1,),
            in_specs=[pl.BlockSpec(shape, lambda i, place: (0,) * len(shape))] * count,
            out_specs=pl.BlockSpec((count, *shape), lambda i, place: (0,) * (1 + len(shape))),
        ),
        compiler_params=pltpu.CompilerParams(vmem_limit_bytes=24 << 20),
        cost_estimate=SMALL,
        name="stack_planes",
    )(place, *line)


def on_device_square(inputs, trunk_grad, weights):
    seqs, reps = lax.axis_size("seq"), lax.axis_size("rep")
    me, rep = lax.axis_index("seq"), lax.axis_index("rep")
    place = jnp.stack([me, rep]).astype(jnp.int32)
    taps, rows, block = weights.shape
    fine = inputs.shape[1]
    coarse, planes = fine // 2, reps // 2
    packed = (coarse + 2 * HALO) // CHUNKS
    half = coarse // 2

    last_taps = weights[SPLIT:]
    across = [last_taps] + [from_peer(last_taps, "seq", d) for d in range(1, seqs)]
    to_beside, to_below, own_window = messages(place, inputs, trunk_grad)
    to_beside, to_below = after(to_beside, *across[1:]), after(to_below, *across[1:])
    beside, below = from_peer(to_beside, "seq", 1), from_peer(to_below, "seq", 2)
    slope = half_slope(inputs)
    column = stack_planes(place, gather_line(weights[:SPLIT], "rep", planes, 2))
    lines = stack_planes(place, gather_line(jnp.stack(across), "rep", planes, 2))
    trunk = trunk_grad[0]
    zeros = jnp.zeros((1, block), jnp.bfloat16)
    later = jnp.concatenate([trunk[1:], zeros])
    earlier = jnp.concatenate([zeros, trunk[:-1]])
    shifts = jnp.concatenate([later, trunk, earlier], axis=1)
    top = after(beside[: FIRST + half], slope, column, lines, shifts)
    bottom = after(below[half : coarse + packed - FIRST], slope, column, lines, shifts)
    far_top, far_bottom = from_peer(top, "seq", 2), from_peer(bottom, "seq", 1)

    scale = 0.5 * float(fine * seqs * reps) ** (-0.5)
    near_rows = [(0, 0, coarse, FIRST), (1, 0, coarse, FIRST), (2, 0, coarse, 0)]
    far_rows = [(3, 0, half, FIRST), (3, half, half, 0)]
    early = early_terms(place, near_rows, [to_beside, beside, below], shifts, coarse)
    far_top, far_bottom = after(far_top, early), after(far_bottom, early)

    other_column, other_lines = from_peer(column, "rep", 1), from_peer(lines, "rep", 1)
    column = after(column, far_top, far_bottom)
    kept_beside, kept_below = from_peer(column, "seq", 1), from_peer(column, "seq", 2)

    mine, theirs = late_terms(
        place, far_rows, [far_top, far_bottom], shifts, early, coarse, scale, planes, taps, rows
    )
    arrived = from_peer(theirs, "rep", 1)
    weight_grad = mine[0] + arrived[0].astype(jnp.float32)
    leaving = [(mine[j] + arrived[j].astype(jnp.float32)).astype(jnp.bfloat16) for j in range(planes)]
    summed = [from_peer(leaving[j], "rep", 2 * j) for j in range(1, planes)]

    kept_beside, kept_below = after(kept_beside, early), after(kept_below, early)
    far_first = from_peer(kept_beside[: planes // 2], "seq", 2)
    far_second = from_peer(kept_below[planes // 2 :], "seq", 1)
    soon = [(after(column, *leaving[1:]), 0, 0, 0), (other_column, 0, 1, 0)]
    for part, distance in ((kept_beside, 1), (kept_below, 2)):
        soon += [(part, 0, 0, distance), (from_peer(part, "rep", 1), 0, 1, distance)]

    windows = [
        [(own_window, 0, 0, packed)],
        [(beside, FIRST + coarse, 0, packed)],
        [(below, coarse + packed - FIRST, 0, packed)],
        [(far_top, 0, 0, FIRST), (far_bottom, half, FIRST, packed - FIRST)],
    ]
    stage = functools.partial(gradient_stage, place, windows, slope=slope, shape=inputs.shape)
    crossed = [(part, 0, flip, d) for flip, part in enumerate((lines, other_lines)) for d in range(seqs)]
    begun = stage(SPLIT, crossed, list(range(seqs)), begun=None)
    begun, rest = stage(0, soon, [0, 1, 2], begun=begun), []
    for part, plane in ((far_first, 0), (far_second, planes // 2)):
        part = after(part, begun, *summed)
        rest += [(part, plane, 0, 3), (from_peer(part, "rep", 1), plane, 1, 3)]
    input_grad = stage(0, rest, [3], begun=begun, last=True)
    for part in summed:
        weight_grad = weight_grad + after(part, input_grad).astype(jnp.float32)
    return (input_grad, weight_grad)


def with_halo(value, sides, width):
    for axis, dim in sides:
        peers, length = (lax.axis_size(axis), value.shape[dim])
        up = [(i, (i + 1) % peers) for i in range(peers - 1)]
        down = [(j, i) for i, j in up]
        last = lax.slice_in_dim(value, length - width, length, axis=dim)
        leading = lax.slice_in_dim(value, 0, width, axis=dim)
        before = lax.ppermute(last, axis, up)
        after = lax.ppermute(leading, axis, down)
        value = jnp.concatenate([before, value, after], axis=dim)
    return value


def contract_last(left, right):
    return lax.dot_general(
        left, right, (((1,), (1,)), ((), ())), preferred_element_type=jnp.float32
    )


def contract_first(left, right):
    return lax.dot_general(
        left, right, (((0,), (0,)), ((), ())), preferred_element_type=jnp.float32
    )


def on_device_plain(inputs, trunk_grad, weights):
    taps = weights.shape[0]
    grad = lax.all_to_all(trunk_grad, "seq", split_axis=1, concat_axis=2, tiled=True)
    grad_up = jnp.repeat(grad.astype(jnp.float32) * 0.5, 2, axis=1).astype(jnp.bfloat16)
    rows = grad_up.shape[1]
    padded = with_halo(grad_up, (("seq", 1),), 2)
    shifts = [padded[0, 4 - k : 4 - k + rows] for k in range(taps)]
    inputs_f = inputs[0].astype(jnp.float32)
    act_vals, back = jax.vjp(jax.nn.gelu, inputs_f)
    slope = back(jnp.ones_like(inputs_f))[0]
    act = act_vals.astype(jnp.bfloat16)
    in_width = inputs.shape[2]
    columns = lax.all_gather(weights, "seq", axis=2, tiled=True)
    piece = lax.all_gather(columns, "rep", axis=1, tiled=True)
    result = contract_last(shifts[0], piece[0])
    for project_k in range(1, taps):
        result = result + contract_last(shifts[project_k], piece[project_k])
    input_grad = (result * slope + grad_up[0, :, :in_width].astype(jnp.float32)).astype(
        jnp.bfloat16
    )
    scale_factor = float(rows * lax.axis_size("seq") * lax.axis_size("rep")) ** (-0.5)
    terms = jnp.stack([contract_first(act, shifts[k]) for k in range(taps)]) * scale_factor
    partial_sum = lax.psum_scatter(terms, "rep", scatter_dimension=1, tiled=True)
    weight_grad = lax.psum_scatter(partial_sum, "seq", scatter_dimension=2, tiled=True)
    return (input_grad[None], weight_grad)


def on_device(inputs, trunk_grad, weights):
    square = lax.axis_size("seq") == 4 and lax.axis_size("rep") % 8 == 0
    if square and weights.shape[2] % LANES == 0 and inputs.shape[2] % LANES == 0:
        return on_device_square(inputs, trunk_grad, weights)
    return on_device_plain(inputs, trunk_grad, weights)


def solution(mesh):
    in_specs = (P("rep", "seq", None), P("rep", None, "seq"), P(None, "rep", "seq"))
    out_specs = (P("rep", "seq", None), P(None, "rep", "seq"))
    return jax.shard_map(
        on_device, mesh=mesh, in_specs=in_specs, out_specs=out_specs, check_vma=False
    )
```

```python
import functools
import math

import jax
import jax.numpy as jnp
from jax import lax
from jax.experimental import pallas as pl
from jax.experimental.pallas import tpu as pltpu
from jax.sharding import PartitionSpec as P

LANES = 128
HALO = 32
EDGE = 16
MARGIN = HALO - EDGE
STEP = 64
SPLIT = 3
ROOT = math.sqrt(2.0 / math.pi)
CUBIC = 0.044715
SMALL = pl.CostEstimate(flops=1 << 20, bytes_accessed=1 << 16, transcendentals=0)
ANYWHERE = pl.BlockSpec(memory_space=pl.ANY)
ROW_OFFSETS = ((1, 1), (0, 1), (0, 0), (-1, 0), (-1, -1))
GRAD_PARTS = ((0, 0), (1, 0), (1, 1), (2, 1), (2, 2))


def from_peer(value, axis, distance):
    peers = lax.axis_size(axis)
    return lax.ppermute(value, axis, [(i, i ^ distance) for i in range(peers)])


def after(value, *earlier):
    return pl.pallas_call(
        lambda *refs: None,
        out_shape=jax.ShapeDtypeStruct(value.shape, value.dtype),
        in_specs=[ANYWHERE] * (1 + len(earlier)),
        out_specs=ANYWHERE,
        input_output_aliases={0: 0},
        name="after",
    )(value, *earlier)


def gather_line(value, axis, count, unit):
    found, mask = {0: value}, count - 1
    while mask:
        for distance in list(found):
            found[distance ^ mask] = from_peer(found[distance], axis, mask * unit)
        mask //= 2
    return [found[distance] for distance in range(count)]


def gelu_slope(x):
    tanh = jnp.tanh(ROOT * (x + CUBIC * (x * x * x)))
    return 0.5 * (1.0 + tanh) + 0.5 * x * (1.0 - tanh * tanh) * (
        ROOT * (1.0 + 3.0 * CUBIC * (x * x))
    )


def act_kernel(x_ref, out_ref, strip):
    width = x_ref.shape[2]

    @pl.loop(0, out_ref.shape[0] // STEP)
    def _(step):
        start = pl.multiple_of(step * STEP, STEP)
        x = x_ref[0, pl.ds(pl.multiple_of(2 * start, 2 * STEP), 2 * STEP), :].astype(jnp.float32)
        act = x * (0.5 * (1.0 + jnp.tanh(ROOT * (x + CUBIC * (x * x * x)))))
        for c in range(width // LANES):
            strip[c] = act[:, c * LANES : (c + 1) * LANES]
        for parity in range(2):
            for c in range(width // LANES):
                picked = strip[c, pl.ds(parity, STEP, stride=2), :].astype(jnp.bfloat16)
                left = parity * width + c * LANES
                out_ref[pl.ds(start, STEP), left : left + LANES] = picked


def activate(inputs):
    fine, width = inputs.shape[1:]
    return pl.pallas_call(
        act_kernel,
        out_shape=jax.ShapeDtypeStruct((fine // 2, 2 * width), jnp.bfloat16),
        in_specs=[pl.BlockSpec(memory_space=pltpu.VMEM)],
        out_specs=pl.BlockSpec(memory_space=pltpu.VMEM),
        scratch_shapes=[pltpu.VMEM((width // LANES, 2 * STEP, LANES), jnp.float32)],
        compiler_params=pltpu.CompilerParams(vmem_limit_bytes=24 << 20),
        cost_estimate=SMALL,
        name="act",
    )(inputs)


def kernel_messages(place, line, trunk_grad, coarse):
    taps, rows, block = line[0].shape
    planes, length = len(line), trunk_grad.shape[1]
    window = (coarse + 2 * HALO) // rows
    half = planes // 2

    def kernel(place, *refs):
        parts, trunk_ref = refs[:planes], refs[planes]
        beside_ref, below_ref, own_ref, edged, sem = refs[planes + 1 :]
        copy = pltpu.make_async_copy(trunk_ref.at[0], edged.at[pl.ds(HALO, length)], sem)
        copy.start()
        edged[:HALO] = jnp.zeros((HALO, block), jnp.bfloat16)
        edged[HALO + length :] = jnp.zeros((HALO, block), jnp.bfloat16)
        for j in range(planes):
            plane = place[1] // 2 ^ j
            for k in range(taps):
                spot = (plane // half * taps + k) * half + plane % half
                beside_ref[window // 2 + spot] = parts[j][k]
                below_ref[spot] = parts[j][k]
        copy.wait()

        def cut(out_ref, spot, distance, first, last):
            base = (place[0] ^ distance) * coarse
            for b in range(first, last):
                out_ref[spot + b - first] = edged[pl.ds(pl.multiple_of(base + b * rows, 16), rows), :]

        cut(beside_ref, 0, 3, 0, window // 2)
        cut(beside_ref, window // 2 + planes * taps, 1, 0, window)
        cut(below_ref, planes * taps, 3, window // 2, window)
        cut(below_ref, planes * taps + window // 2, 2, 0, window)
        cut(own_ref, 0, 0, 0, window)

    count = window // 2 + planes * taps + window
    return pl.pallas_call(
        kernel,
        out_shape=[
            jax.ShapeDtypeStruct((n, rows, block), jnp.bfloat16) for n in (count, count, window)
        ],
        grid_spec=pltpu.PrefetchScalarGridSpec(
            num_scalar_prefetch=1,
            grid=(1,),
            in_specs=[pl.BlockSpec(line[0].shape, lambda i, place: (0, 0, 0))] * planes + [ANYWHERE],
            out_specs=[
                pl.BlockSpec((n, rows, block), lambda i, place: (0, 0, 0))
                for n in (count, count, window)
            ],
            scratch_shapes=[
                pltpu.VMEM((length + 2 * HALO, block), jnp.bfloat16),
                pltpu.SemaphoreType.DMA,
            ],
        ),
        compiler_params=pltpu.CompilerParams(vmem_limit_bytes=32 << 20),
        cost_estimate=SMALL,
        name="kernel_messages",
    )(place, *line, trunk_grad)


def slope_kernel(x_ref, out_ref, scratch):
    width = x_ref.shape[2]

    @pl.loop(0, out_ref.shape[1] // 64)
    def _(step):
        start = pl.multiple_of(step * 64, 64)
        span = pl.ds(pl.multiple_of(2 * start, 128), 128)
        for c in range(width // LANES):
            lanes = slice(c * LANES, (c + 1) * LANES)
            scratch[c] = 0.5 * gelu_slope(x_ref[0, span, lanes].astype(jnp.float32))
            for parity in range(2):
                out_ref[parity, pl.ds(start, 64), lanes] = scratch[c, pl.ds(parity, 64, stride=2), :]


def half_slope(inputs):
    fine, width = inputs.shape[1:]
    return pl.pallas_call(
        slope_kernel,
        out_shape=jax.ShapeDtypeStruct((2, fine // 2, width), jnp.float32),
        in_specs=[pl.BlockSpec(memory_space=pltpu.VMEM)],
        out_specs=pl.BlockSpec(memory_space=pltpu.VMEM),
        scratch_shapes=[pltpu.VMEM((width // LANES, 128, LANES), jnp.float32)],
        compiler_params=pltpu.CompilerParams(vmem_limit_bytes=24 << 20),
        name="half_slope",
    )(inputs)


def start_act(place, coarse, layout, pieces, shifts_ref, held, shifts, sems, shift_sems):
    copies, row = [], 0
    for i, (distance, first, size, offset) in enumerate(layout):
        start = pl.multiple_of((place[0] ^ distance) * coarse + first, 16)
        spot = pl.ds(row, size)
        source = pieces[i].at[pl.ds(offset, size)]
        copies.append(pltpu.make_async_copy(source, held.at[spot], sems.at[i]))
        copies.append(
            pltpu.make_async_copy(shifts_ref.at[pl.ds(start, size)], shifts.at[spot], shift_sems.at[i])
        )
        row += size
    for copy in copies:
        copy.start()
    return copies


def early_terms(place, layout, pieces, shifts, coarse):
    both, columns = pieces[0].shape[1], shifts.shape[1]
    rows = sum(size for _, _, size, _ in layout)
    tile = 256

    def kernel(place, shifts_ref, *refs):
        pieces, total = refs[: len(layout)], refs[len(layout)]
        held, shifts, sems, shift_sems = refs[len(layout) + 1 :]
        copies = start_act(
            place, coarse, layout, pieces, shifts_ref, held, shifts, sems, shift_sems
        )
        for copy in copies:
            copy.wait()

        @pl.loop(0, both // tile)
        def _(i):
            span = pl.ds(pl.multiple_of(i * tile, tile), tile)
            total[span, :] = lax.dot_general(
                held[:, span], shifts[...], (((0,), (0,)), ((), ())), preferred_element_type=jnp.float32
            )

    return pl.pallas_call(
        kernel,
        out_shape=jax.ShapeDtypeStruct((both, columns), jnp.float32),
        grid_spec=pltpu.PrefetchScalarGridSpec(
            num_scalar_prefetch=1,
            grid=(1,),
            in_specs=[ANYWHERE] * (1 + len(pieces)),
            out_specs=pl.BlockSpec((both, columns), lambda i, place: (0, 0)),
            scratch_shapes=[
                pltpu.VMEM((rows, both), jnp.bfloat16),
                pltpu.VMEM((rows, columns), jnp.bfloat16),
                pltpu.SemaphoreType.DMA((len(pieces),)),
                pltpu.SemaphoreType.DMA((len(pieces),)),
            ],
        ),
        compiler_params=pltpu.CompilerParams(vmem_limit_bytes=48 << 20),
        cost_estimate=SMALL,
        name="weight_grad_early",
    )(place, shifts, *pieces)


def late_terms(place, layout, pieces, shifts, early, coarse, scale, planes, taps, rows):
    both, columns = early.shape
    width, block = both // 2, columns // 3
    count = sum(size for _, _, size, _ in layout)
    tile = 256
    shape = (planes, taps, rows, block)

    def kernel(place, shifts_ref, early_ref, *refs):
        pieces, (mine_ref, theirs_ref) = refs[: len(layout)], refs[len(layout) : len(layout) + 2]
        held, shifts, total, sems, shift_sems, early_sems = refs[len(layout) + 2 :]
        core, plane = place[1] % 2, place[1] // 2
        copies = start_act(
            place, coarse, layout, pieces, shifts_ref, held, shifts, sems, shift_sems
        )

        def fetch(i):
            span = pl.ds(pl.multiple_of(i * tile, tile), tile)
            return pltpu.make_async_copy(early_ref.at[span], total.at[span], early_sems.at[i])

        for i in range(both // tile):
            fetch(i).start()
        for copy in copies:
            copy.wait()

        @pl.loop(0, both // tile)
        def _(i):
            span = pl.ds(pl.multiple_of(i * tile, tile), tile)
            term = lax.dot_general(
                held[:, span], shifts[...], (((0,), (0,)), ((), ())), preferred_element_type=jnp.float32
            )
            fetch(i).wait()
            total[span, :] += term

        for out_ref, parity, kind in (
            (theirs_ref, 1 - core, jnp.bfloat16),
            (mine_ref, core, jnp.float32),
        ):

            @pl.loop(0, planes)
            def _(j):
                start = ((plane ^ j) * 2 + parity) * rows
                even = pl.ds(pl.multiple_of(start, 16), rows)
                odd = pl.ds(pl.multiple_of(width + start, 16), rows)
                for k, (left, right) in enumerate(GRAD_PARTS):
                    term = total[even, left * block : (left + 1) * block]
                    term += total[odd, right * block : (right + 1) * block]
                    out_ref[j, k] = (scale * term).astype(kind)

    whole = pl.BlockSpec(shape, lambda i, place: (0, 0, 0, 0))
    return pl.pallas_call(
        kernel,
        out_shape=(
            jax.ShapeDtypeStruct(shape, jnp.float32),
            jax.ShapeDtypeStruct(shape, jnp.bfloat16),
        ),
        grid_spec=pltpu.PrefetchScalarGridSpec(
            num_scalar_prefetch=1,
            grid=(1,),
            in_specs=[ANYWHERE] * (2 + len(pieces)),
            out_specs=[whole, whole],
            scratch_shapes=[
                pltpu.VMEM((count, both), jnp.bfloat16),
                pltpu.VMEM((count, columns), jnp.bfloat16),
                pltpu.VMEM((both, columns), jnp.float32),
                pltpu.SemaphoreType.DMA((len(pieces),)),
                pltpu.SemaphoreType.DMA((len(pieces),)),
                pltpu.SemaphoreType.DMA((both // tile,)),
            ],
        ),
        compiler_params=pltpu.CompilerParams(vmem_limit_bytes=48 << 20),
        cost_estimate=SMALL,
        name="weight_grad_late",
    )(place, shifts, early, *pieces)


def shifted_total(products, base, lanes, parity):
    total = None
    for by in (0, 1, -1):
        wanted = [k for k in range(products.shape[0]) if ROW_OFFSETS[k][parity] == by]
        if wanted:
            near = pl.ds(base + MARGIN - 8, STEP + 16)
            part = sum(products[k, near, lanes] for k in wanted)[8 + by : 8 + by + STEP]
            total = part if total is None else total + part
    return total


def gradient_stage(place, windows, taps, pieces, distances, slope, begun, shape):
    _, fine, width = shape
    coarse, seqs = fine // 2, len(windows)
    rows, block = pieces[0][0].shape[-2:]
    planes = width // (2 * rows)
    half = planes // 2
    window, used = coarse + 2 * HALO, coarse + 2 * MARGIN
    depth, planar = len(distances) * block, (2, coarse, width)
    last = begun is not None
    needed = distances if last else list(range(seqs))
    parts = [(d, *part) for d in needed for part in windows[d]]
    operands = [part[1] for part in parts] + [piece[0] for piece in pieces]
    operands += [slope] + ([begun] if last else [])

    def body(place, *refs):
        own, refs = refs[: len(parts)], refs[len(parts) :]
        sources, refs = refs[: len(pieces)], refs[len(pieces) :]
        slope_ref, refs = refs[0], refs[1:]
        if last:
            begun_ref, refs = refs[0], refs[1:]
        out_ref, wv, gv, products, slopes, sems, grad_sems, slope_sem = refs[:8]
        me, core = place[0], place[1] % 2

        def kernel_copies(first):
            for number, (array, start, plane, count, flip, distance) in enumerate(pieces):
                spot = pl.ds(distances.index(distance) * block, block)
                if first != (start is not None):
                    continue
                for k in range(SPLIT if first else taps - SPLIT):
                    for h in range(count // half):
                        span = pl.ds(plane + h * half, half)
                        if first:
                            source = sources[number].at[pl.ds(start + (h * SPLIT + k) * half, half)]
                        else:
                            source = sources[number].at[span, distance, k]
                        tap = k if first else SPLIT + k
                        target = wv.at[tap, span, core ^ flip, :, spot]
                        sem = sems.at[tap, number, h]
                        yield tap, pltpu.make_async_copy(source, target, sem)

        def window_copies(target_of, sems):
            for number, (distance, _, start, first, count) in enumerate(parts):
                for b in range(count):
                    target = target_of(distance, pl.ds((first + b) * rows, rows))
                    if target is not None:
                        source = own[number].at[start + b]
                        yield pltpu.make_async_copy(source, target, sems.at[number, b])

        def into_window(distance, span):
            if distance not in distances:
                return None
            return gv.at[span, pl.ds(distances.index(distance) * block, block)]

        early = list(window_copies(into_window, grad_sems))
        late = [pltpu.make_async_copy(slope_ref, slopes, slope_sem)]
        if last:
            sums, strip, sum_sem = refs[8:]
            late.append(pltpu.make_async_copy(begun_ref, sums, sum_sem))
        else:
            skips, skip_sems = refs[8:]
            late += window_copies(lambda d, span: skips.at[me ^ d, span], skip_sems)
        for copy in early:
            copy.start()
        arriving = sorted([*kernel_copies(True), *kernel_copies(False)], key=lambda pair: pair[0])
        for _, copy in arriving:
            copy.start()
        for copy in late:
            copy.start()
        for copy in early:
            copy.wait()
        for k in range(taps):
            for tap, copy in arriving:
                if tap == k:
                    copy.wait()
            for part in range(2):
                kernel = wv[k, part * half : (part + 1) * half].reshape(2 * half * rows, depth)
                lanes = slice(part * 2 * half * rows, (part + 1) * 2 * half * rows)
                products[k, :, lanes] = lax.dot_general(
                    gv[EDGE : EDGE + used],
                    kernel,
                    (((1,), (1,)), ((), ())),
                    preferred_element_type=jnp.float32,
                )

        for copy in late:
            copy.wait()

        @pl.loop(0, coarse // STEP)
        def _(i):
            base = pl.multiple_of(i * STEP, STEP)
            spot, span = pl.ds(base, STEP), pl.ds(pl.multiple_of(2 * base, 2 * STEP), 2 * STEP)
            for c in range(width // LANES):
                lanes = slice(c * LANES, (c + 1) * LANES)
                if not last:
                    left = c * LANES % block
                    skip = skips[c * LANES // block, pl.ds(base + HALO, STEP), left : left + LANES]
                    skip = 0.5 * skip.astype(jnp.float32)
                for parity in range(2):
                    total = shifted_total(products, base, lanes, parity)
                    total = total * slopes[parity, spot, lanes]
                    total = total + (sums[parity, spot, lanes] if last else skip)
                    if last:
                        strip[c, pl.ds(parity, STEP, stride=2), :] = total
                    else:
                        out_ref[parity, spot, lanes] = total
                if last:
                    out_ref[0, span, lanes] = strip[c].astype(jnp.bfloat16)

    out_shape = jax.ShapeDtypeStruct(shape if last else planar, jnp.bfloat16 if last else jnp.float32)
    scratch = [
        pltpu.VMEM((taps, planes, 2, rows, depth), jnp.bfloat16),
        pltpu.VMEM((window, depth), jnp.bfloat16),
        pltpu.VMEM((taps, used, width), jnp.float32),
        pltpu.VMEM(planar, jnp.float32),
        pltpu.SemaphoreType.DMA((taps, len(pieces), 2)),
        pltpu.SemaphoreType.DMA((len(parts), window // rows)),
        pltpu.SemaphoreType.DMA,
    ]
    if last:
        scratch += [
            pltpu.VMEM(planar, jnp.float32),
            pltpu.VMEM((width // LANES, 2 * STEP, LANES), jnp.float32),
            pltpu.SemaphoreType.DMA,
        ]
    else:
        scratch += [
            pltpu.VMEM((seqs, window, block), jnp.bfloat16),
            pltpu.SemaphoreType.DMA((len(parts), window // rows)),
        ]
    return pl.pallas_call(
        body,
        out_shape=out_shape,
        grid_spec=pltpu.PrefetchScalarGridSpec(
            num_scalar_prefetch=1,
            grid=(1,),
            in_specs=[ANYWHERE] * len(operands),
            out_specs=pl.BlockSpec(out_shape.shape, lambda i, place: (0, 0, 0)),
            scratch_shapes=scratch,
        ),
        compiler_params=pltpu.CompilerParams(vmem_limit_bytes=56 << 20),
        cost_estimate=SMALL,
        name="input_grad",
    )(place, *operands)


def stack_planes(place, line):
    count = len(line)

    def kernel(place, *refs):
        parts, out_ref = refs[:count], refs[count]
        for j in range(count):
            out_ref[place[1] // 2 ^ j] = parts[j][...]

    shape = line[0].shape
    return pl.pallas_call(
        kernel,
        out_shape=jax.ShapeDtypeStruct((count, *shape), line[0].dtype),
        grid_spec=pltpu.PrefetchScalarGridSpec(
            num_scalar_prefetch=1,
            grid=(1,),
            in_specs=[pl.BlockSpec(shape, lambda i, place: (0,) * len(shape))] * count,
            out_specs=pl.BlockSpec((count, *shape), lambda i, place: (0,) * (1 + len(shape))),
        ),
        compiler_params=pltpu.CompilerParams(vmem_limit_bytes=24 << 20),
        cost_estimate=SMALL,
        name="stack_planes",
    )(place, *line)


def on_device_square(inputs, trunk_grad, weights):
    seqs, reps = lax.axis_size("seq"), lax.axis_size("rep")
    me, rep = lax.axis_index("seq"), lax.axis_index("rep")
    place = jnp.stack([me, rep]).astype(jnp.int32)
    taps, rows, block = weights.shape
    fine = inputs.shape[1]
    coarse, planes = fine // 2, reps // 2
    half = coarse // 2

    last_taps = weights[SPLIT:]
    across = [last_taps] + [from_peer(last_taps, "seq", d) for d in range(1, seqs)]

    act = after(activate(inputs), *across[1:])
    beside, below = from_peer(act, "seq", 1), from_peer(act, "seq", 2)
    slope = half_slope(inputs)
    line = gather_line(weights[:SPLIT], "rep", planes, 2)
    line_across = gather_line(after(jnp.stack(across), *line[1:]), "rep", planes, 2)
    trunk = trunk_grad[0]
    zeros = jnp.zeros((1, block), jnp.bfloat16)
    later = jnp.concatenate([trunk[1:], zeros])
    earlier = jnp.concatenate([zeros, trunk[:-1]])
    shifts = jnp.concatenate([later, trunk, earlier], axis=1)
    to_beside, to_below, own_window = kernel_messages(place, line, trunk_grad, coarse)
    ready = (slope, shifts, to_beside, line_across[1], line_across[planes - 1])
    top, bottom = after(beside[:half], *ready), after(below[half:], *ready)
    far_top, far_bottom = from_peer(top, "seq", 2), from_peer(bottom, "seq", 1)

    scale = 0.5 * float(fine * seqs * reps) ** (-0.5)
    near_rows = [(d, 0, coarse, 0) for d in range(3)]
    far_rows = [(3, 0, half, 0), (3, half, half, 0)]
    early = early_terms(place, near_rows, [act, beside, below], shifts, coarse)
    far_top, far_bottom = after(far_top, early), after(far_bottom, early)

    lines = stack_planes(place, line_across)
    to_beside, to_below = (
        after(message, far_top, far_bottom, lines) for message in (to_beside, to_below)
    )
    kept_beside, kept_below = from_peer(to_beside, "seq", 1), from_peer(to_below, "seq", 2)
    other_column, other_lines = from_peer(to_below, "rep", 1), from_peer(lines, "rep", 1)

    mine, theirs = late_terms(
        place, far_rows, [far_top, far_bottom], shifts, early, coarse, scale, planes, taps, rows
    )
    arrived = from_peer(theirs, "rep", 1)
    weight_grad = mine[0] + arrived[0].astype(jnp.float32)
    leaving = [(mine[j] + arrived[j].astype(jnp.float32)).astype(jnp.bfloat16) for j in range(planes)]
    summed = [from_peer(leaving[j], "rep", 2 * j) for j in range(1, planes)]

    window = (coarse + 2 * HALO) // rows
    count, side = planes * SPLIT, window // 2
    kept_beside, kept_below = after(kept_beside, *leaving[1:]), after(kept_below, *leaving[1:])
    far_first = from_peer(kept_beside[: side + count // 2], "seq", 2)
    far_second = from_peer(kept_below[count // 2 : count + side], "seq", 1)
    windows = [
        [(own_window, 0, 0, window)],
        [(kept_beside, side + count, 0, window)],
        [(kept_below, count + side, 0, window)],
        [(far_first, 0, 0, side), (far_second, count // 2, side, side)],
    ]

    stage = functools.partial(
        gradient_stage, place, windows, taps, slope=slope, shape=inputs.shape
    )
    soon = [(to_below, 0, 0, planes, 0, 0), (other_column, 0, 0, planes, 1, 0)]
    for part, start, distance in ((kept_beside, side, 1), (kept_below, 0, 2)):
        soon.append((part, start, 0, planes, 0, distance))
        soon.append((from_peer(part, "rep", 1), start, 0, planes, 1, distance))
    crossed = [
        (part, None, 0, planes, flip, d)
        for flip, part in enumerate((lines, other_lines))
        for d in range(seqs)
    ]
    begun = stage(soon + [piece for piece in crossed if piece[-1] < 3], [0, 1, 2], begun=None)
    rest = [piece for piece in crossed if piece[-1] == 3]
    for part, start, plane in ((far_first, side, 0), (far_second, 0, planes // 2)):
        part = after(part, begun, *summed)
        rest.append((part, start, plane, planes // 2, 0, 3))
        rest.append((from_peer(part, "rep", 1), start, plane, planes // 2, 1, 3))
    input_grad = stage(rest, [3], begun=begun)
    for part in summed:
        weight_grad = weight_grad + after(part, input_grad).astype(jnp.float32)
    return (input_grad, weight_grad)


def with_halo(value, sides, width):
    for axis, dim in sides:
        peers, length = (lax.axis_size(axis), value.shape[dim])
        up = [(i, (i + 1) % peers) for i in range(peers - 1)]
        down = [(j, i) for i, j in up]
        last = lax.slice_in_dim(value, length - width, length, axis=dim)
        leading = lax.slice_in_dim(value, 0, width, axis=dim)
        before = lax.ppermute(last, axis, up)
        after = lax.ppermute(leading, axis, down)
        value = jnp.concatenate([before, value, after], axis=dim)
    return value


def contract_last(left, right):
    return lax.dot_general(
        left, right, (((1,), (1,)), ((), ())), preferred_element_type=jnp.float32
    )


def contract_first(left, right):
    return lax.dot_general(
        left, right, (((0,), (0,)), ((), ())), preferred_element_type=jnp.float32
    )


def on_device_plain(inputs, trunk_grad, weights):
    taps = weights.shape[0]
    grad = lax.all_to_all(trunk_grad, "seq", split_axis=1, concat_axis=2, tiled=True)
    grad_up = jnp.repeat(grad.astype(jnp.float32) * 0.5, 2, axis=1).astype(jnp.bfloat16)
    rows = grad_up.shape[1]
    padded = with_halo(grad_up, (("seq", 1),), 2)
    shifts = [padded[0, 4 - k : 4 - k + rows] for k in range(taps)]
    inputs_f = inputs[0].astype(jnp.float32)
    act_vals, back = jax.vjp(jax.nn.gelu, inputs_f)
    slope = back(jnp.ones_like(inputs_f))[0]
    act = act_vals.astype(jnp.bfloat16)
    in_width = inputs.shape[2]
    columns = lax.all_gather(weights, "seq", axis=2, tiled=True)
    piece = lax.all_gather(columns, "rep", axis=1, tiled=True)
    result = contract_last(shifts[0], piece[0])
    for project_k in range(1, taps):
        result = result + contract_last(shifts[project_k], piece[project_k])
    input_grad = (result * slope + grad_up[0, :, :in_width].astype(jnp.float32)).astype(
        jnp.bfloat16
    )
    scale_factor = float(rows * lax.axis_size("seq") * lax.axis_size("rep")) ** (-0.5)
    terms = jnp.stack([contract_first(act, shifts[k]) for k in range(taps)]) * scale_factor
    partial_sum = lax.psum_scatter(terms, "rep", scatter_dimension=1, tiled=True)
    weight_grad = lax.psum_scatter(partial_sum, "seq", scatter_dimension=2, tiled=True)
    return (input_grad[None], weight_grad)


def on_device(inputs, trunk_grad, weights):
    square = lax.axis_size("seq") == 4 and lax.axis_size("rep") % 8 == 0
    if square and weights.shape[2] % LANES == 0 and inputs.shape[2] % LANES == 0:
        return on_device_square(inputs, trunk_grad, weights)
    return on_device_plain(inputs, trunk_grad, weights)


def solution(mesh):
    in_specs = (P("rep", "seq", None), P("rep", None, "seq"), P(None, "rep", "seq"))
    out_specs = (P("rep", "seq", None), P(None, "rep", "seq"))
    return jax.shard_map(
        on_device, mesh=mesh, in_specs=in_specs, out_specs=out_specs, check_vma=False
    )
```

```python
import functools
import math

import jax
import jax.numpy as jnp
from jax import lax
from jax.experimental import pallas as pl
from jax.experimental.pallas import tpu as pltpu
from jax.sharding import PartitionSpec as P

LANES = 128
HALO = 32
EDGE = 16
MARGIN = HALO - EDGE
STEP = 64
SPLIT = 3
ROOT = math.sqrt(2.0 / math.pi)
CUBIC = 0.044715
SMALL = pl.CostEstimate(flops=1 << 20, bytes_accessed=1 << 16, transcendentals=0)
ANYWHERE = pl.BlockSpec(memory_space=pl.ANY)
ROW_OFFSETS = ((1, 1), (0, 1), (0, 0), (-1, 0), (-1, -1))
GRAD_PARTS = ((0, 0), (1, 0), (1, 1), (2, 1), (2, 2))


def from_peer(value, axis, distance):
    peers = lax.axis_size(axis)
    return lax.ppermute(value, axis, [(i, i ^ distance) for i in range(peers)])


def after(value, *earlier):
    return pl.pallas_call(
        lambda *refs: None,
        out_shape=jax.ShapeDtypeStruct(value.shape, value.dtype),
        in_specs=[ANYWHERE] * (1 + len(earlier)),
        out_specs=ANYWHERE,
        input_output_aliases={0: 0},
        name="after",
    )(value, *earlier)


def gather_line(value, axis, count, unit):
    found, mask = {0: value}, count - 1
    while mask:
        for distance in list(found):
            found[distance ^ mask] = from_peer(found[distance], axis, mask * unit)
        mask //= 2
    return [found[distance] for distance in range(count)]


def gelu_slope(x):
    tanh = jnp.tanh(ROOT * (x + CUBIC * (x * x * x)))
    return 0.5 * (1.0 + tanh) + 0.5 * x * (1.0 - tanh * tanh) * (
        ROOT * (1.0 + 3.0 * CUBIC * (x * x))
    )


def act_kernel(x_ref, out_ref, strip):
    width = x_ref.shape[2]

    @pl.loop(0, out_ref.shape[0] // STEP)
    def _(step):
        start = pl.multiple_of(step * STEP, STEP)
        x = x_ref[0, pl.ds(pl.multiple_of(2 * start, 2 * STEP), 2 * STEP), :].astype(jnp.float32)
        act = x * (0.5 * (1.0 + jnp.tanh(ROOT * (x + CUBIC * (x * x * x)))))
        for c in range(width // LANES):
            strip[c] = act[:, c * LANES : (c + 1) * LANES]
        for parity in range(2):
            for c in range(width // LANES):
                picked = strip[c, pl.ds(parity, STEP, stride=2), :].astype(jnp.bfloat16)
                left = parity * width + c * LANES
                out_ref[pl.ds(start, STEP), left : left + LANES] = picked


def activate(inputs):
    fine, width = inputs.shape[1:]
    return pl.pallas_call(
        act_kernel,
        out_shape=jax.ShapeDtypeStruct((fine // 2, 2 * width), jnp.bfloat16),
        in_specs=[pl.BlockSpec(memory_space=pltpu.VMEM)],
        out_specs=pl.BlockSpec(memory_space=pltpu.VMEM),
        scratch_shapes=[pltpu.VMEM((width // LANES, 2 * STEP, LANES), jnp.float32)],
        compiler_params=pltpu.CompilerParams(vmem_limit_bytes=24 << 20),
        cost_estimate=SMALL,
        name="act",
    )(inputs)


def kernel_messages(place, line, trunk_grad, coarse):
    taps, rows, block = line[0].shape
    planes, length = len(line), trunk_grad.shape[1]
    window = (coarse + 2 * HALO) // rows
    half = planes // 2

    def kernel(place, *refs):
        parts, trunk_ref = refs[:planes], refs[planes]
        beside_ref, below_ref, own_ref, edged, sem = refs[planes + 1 :]
        copy = pltpu.make_async_copy(trunk_ref.at[0], edged.at[pl.ds(HALO, length)], sem)
        copy.start()
        edged[:HALO] = jnp.zeros((HALO, block), jnp.bfloat16)
        edged[HALO + length :] = jnp.zeros((HALO, block), jnp.bfloat16)
        for j in range(planes):
            plane = place[1] // 2 ^ j
            for k in range(taps):
                spot = (plane // half * taps + k) * half + plane % half
                beside_ref[window // 2 + spot] = parts[j][k]
                below_ref[spot] = parts[j][k]
        copy.wait()

        def cut(out_ref, spot, distance, first, last):
            base = (place[0] ^ distance) * coarse
            for b in range(first, last):
                out_ref[spot + b - first] = edged[pl.ds(pl.multiple_of(base + b * rows, 16), rows), :]

        cut(beside_ref, 0, 3, 0, window // 2)
        cut(beside_ref, window // 2 + planes * taps, 1, 0, window)
        cut(below_ref, planes * taps, 3, window // 2, window)
        cut(below_ref, planes * taps + window // 2, 2, 0, window)
        cut(own_ref, 0, 0, 0, window)

    count = window // 2 + planes * taps + window
    return pl.pallas_call(
        kernel,
        out_shape=[
            jax.ShapeDtypeStruct((n, rows, block), jnp.bfloat16) for n in (count, count, window)
        ],
        grid_spec=pltpu.PrefetchScalarGridSpec(
            num_scalar_prefetch=1,
            grid=(1,),
            in_specs=[pl.BlockSpec(line[0].shape, lambda i, place: (0, 0, 0))] * planes + [ANYWHERE],
            out_specs=[
                pl.BlockSpec((n, rows, block), lambda i, place: (0, 0, 0))
                for n in (count, count, window)
            ],
            scratch_shapes=[
                pltpu.VMEM((length + 2 * HALO, block), jnp.bfloat16),
                pltpu.SemaphoreType.DMA,
            ],
        ),
        compiler_params=pltpu.CompilerParams(vmem_limit_bytes=32 << 20),
        cost_estimate=SMALL,
        name="kernel_messages",
    )(place, *line, trunk_grad)


def slope_kernel(x_ref, out_ref, scratch):
    width = x_ref.shape[2]

    @pl.loop(0, out_ref.shape[1] // 64)
    def _(step):
        start = pl.multiple_of(step * 64, 64)
        span = pl.ds(pl.multiple_of(2 * start, 128), 128)
        for c in range(width // LANES):
            lanes = slice(c * LANES, (c + 1) * LANES)
            scratch[c] = 0.5 * gelu_slope(x_ref[0, span, lanes].astype(jnp.float32))
            for parity in range(2):
                out_ref[parity, pl.ds(start, 64), lanes] = scratch[c, pl.ds(parity, 64, stride=2), :]


def half_slope(inputs):
    fine, width = inputs.shape[1:]
    return pl.pallas_call(
        slope_kernel,
        out_shape=jax.ShapeDtypeStruct((2, fine // 2, width), jnp.float32),
        in_specs=[pl.BlockSpec(memory_space=pltpu.VMEM)],
        out_specs=pl.BlockSpec(memory_space=pltpu.VMEM),
        scratch_shapes=[pltpu.VMEM((width // LANES, 128, LANES), jnp.float32)],
        compiler_params=pltpu.CompilerParams(vmem_limit_bytes=24 << 20),
        name="half_slope",
    )(inputs)


def start_act(place, coarse, layout, pieces, shifts_ref, held, shifts, sems, shift_sems):
    copies, row = [], 0
    for i, (distance, first, size, offset) in enumerate(layout):
        start = pl.multiple_of((place[0] ^ distance) * coarse + first, 16)
        spot = pl.ds(row, size)
        source = pieces[i].at[pl.ds(offset, size)]
        copies.append(pltpu.make_async_copy(source, held.at[spot], sems.at[i]))
        copies.append(
            pltpu.make_async_copy(shifts_ref.at[pl.ds(start, size)], shifts.at[spot], shift_sems.at[i])
        )
        row += size
    for copy in copies:
        copy.start()
    return copies


def early_terms(place, layout, pieces, shifts, coarse):
    both, columns = pieces[0].shape[1], shifts.shape[1]
    rows = sum(size for _, _, size, _ in layout)
    tile = 256

    def kernel(place, shifts_ref, *refs):
        pieces, total = refs[: len(layout)], refs[len(layout)]
        held, shifts, sems, shift_sems = refs[len(layout) + 1 :]
        copies = start_act(
            place, coarse, layout, pieces, shifts_ref, held, shifts, sems, shift_sems
        )
        for copy in copies:
            copy.wait()

        @pl.loop(0, both // tile)
        def _(i):
            span = pl.ds(pl.multiple_of(i * tile, tile), tile)
            total[span, :] = lax.dot_general(
                held[:, span], shifts[...], (((0,), (0,)), ((), ())), preferred_element_type=jnp.float32
            )

    return pl.pallas_call(
        kernel,
        out_shape=jax.ShapeDtypeStruct((both, columns), jnp.float32),
        grid_spec=pltpu.PrefetchScalarGridSpec(
            num_scalar_prefetch=1,
            grid=(1,),
            in_specs=[ANYWHERE] * (1 + len(pieces)),
            out_specs=pl.BlockSpec((both, columns), lambda i, place: (0, 0)),
            scratch_shapes=[
                pltpu.VMEM((rows, both), jnp.bfloat16),
                pltpu.VMEM((rows, columns), jnp.bfloat16),
                pltpu.SemaphoreType.DMA((len(pieces),)),
                pltpu.SemaphoreType.DMA((len(pieces),)),
            ],
        ),
        compiler_params=pltpu.CompilerParams(vmem_limit_bytes=48 << 20),
        cost_estimate=SMALL,
        name="weight_grad_early",
    )(place, shifts, *pieces)


def late_terms(place, layout, pieces, shifts, early, coarse, scale, planes, taps, rows):
    both, columns = early.shape
    width, block = both // 2, columns // 3
    count = sum(size for _, _, size, _ in layout)
    tile = 256
    shape = (planes, taps, rows, block)

    def kernel(place, shifts_ref, early_ref, *refs):
        pieces, (mine_ref, theirs_ref) = refs[: len(layout)], refs[len(layout) : len(layout) + 2]
        held, shifts, total, sems, shift_sems, early_sems = refs[len(layout) + 2 :]
        core, plane = place[1] % 2, place[1] // 2
        copies = start_act(
            place, coarse, layout, pieces, shifts_ref, held, shifts, sems, shift_sems
        )

        def fetch(i):
            span = pl.ds(pl.multiple_of(i * tile, tile), tile)
            return pltpu.make_async_copy(early_ref.at[span], total.at[span], early_sems.at[i])

        for i in range(both // tile):
            fetch(i).start()
        for copy in copies:
            copy.wait()

        @pl.loop(0, both // tile)
        def _(i):
            span = pl.ds(pl.multiple_of(i * tile, tile), tile)
            term = lax.dot_general(
                held[:, span], shifts[...], (((0,), (0,)), ((), ())), preferred_element_type=jnp.float32
            )
            fetch(i).wait()
            total[span, :] += term

        for out_ref, parity, kind in (
            (theirs_ref, 1 - core, jnp.bfloat16),
            (mine_ref, core, jnp.float32),
        ):

            @pl.loop(0, planes)
            def _(j):
                start = ((plane ^ j) * 2 + parity) * rows
                even = pl.ds(pl.multiple_of(start, 16), rows)
                odd = pl.ds(pl.multiple_of(width + start, 16), rows)
                for k, (left, right) in enumerate(GRAD_PARTS):
                    term = total[even, left * block : (left + 1) * block]
                    term += total[odd, right * block : (right + 1) * block]
                    out_ref[j, k] = (scale * term).astype(kind)

    whole = pl.BlockSpec(shape, lambda i, place: (0, 0, 0, 0))
    return pl.pallas_call(
        kernel,
        out_shape=(
            jax.ShapeDtypeStruct(shape, jnp.float32),
            jax.ShapeDtypeStruct(shape, jnp.bfloat16),
        ),
        grid_spec=pltpu.PrefetchScalarGridSpec(
            num_scalar_prefetch=1,
            grid=(1,),
            in_specs=[ANYWHERE] * (2 + len(pieces)),
            out_specs=[whole, whole],
            scratch_shapes=[
                pltpu.VMEM((count, both), jnp.bfloat16),
                pltpu.VMEM((count, columns), jnp.bfloat16),
                pltpu.VMEM((both, columns), jnp.float32),
                pltpu.SemaphoreType.DMA((len(pieces),)),
                pltpu.SemaphoreType.DMA((len(pieces),)),
                pltpu.SemaphoreType.DMA((both // tile,)),
            ],
        ),
        compiler_params=pltpu.CompilerParams(vmem_limit_bytes=48 << 20),
        cost_estimate=SMALL,
        name="weight_grad_late",
    )(place, shifts, early, *pieces)


def shifted_total(products, base, lanes, parity):
    total = None
    for by in (0, 1, -1):
        wanted = [k for k in range(products.shape[0]) if ROW_OFFSETS[k][parity] == by]
        if wanted:
            near = pl.ds(base + MARGIN - 8, STEP + 16)
            part = sum(products[k, near, lanes] for k in wanted)[8 + by : 8 + by + STEP]
            total = part if total is None else total + part
    return total


def gradient_stage(place, windows, taps, pieces, distances, slope, begun, shape):
    _, fine, width = shape
    coarse, seqs = fine // 2, len(windows)
    rows, block = pieces[0][0].shape[-2:]
    planes = width // (2 * rows)
    half = planes // 2
    window, used = coarse + 2 * HALO, coarse + 2 * MARGIN
    depth, planar = len(distances) * block, (2, coarse, width)
    last = begun is not None
    needed = distances if last else list(range(seqs))
    parts = [(d, *part) for d in needed for part in windows[d]]
    operands = [part[1] for part in parts] + [piece[0] for piece in pieces]
    operands += [slope] + ([begun] if last else [])

    def body(place, *refs):
        own, refs = refs[: len(parts)], refs[len(parts) :]
        sources, refs = refs[: len(pieces)], refs[len(pieces) :]
        slope_ref, refs = refs[0], refs[1:]
        if last:
            begun_ref, refs = refs[0], refs[1:]
        out_ref, wv, gv, products, slopes, sems, grad_sems, slope_sem = refs[:8]
        me, core = place[0], place[1] % 2

        def kernel_copies(first):
            for number, (array, start, plane, count, flip, distance) in enumerate(pieces):
                spot = pl.ds(distances.index(distance) * block, block)
                if first != (start is not None):
                    continue
                for k in range(SPLIT if first else taps - SPLIT):
                    for h in range(count // half):
                        span = pl.ds(plane + h * half, half)
                        if first:
                            source = sources[number].at[pl.ds(start + (h * SPLIT + k) * half, half)]
                        else:
                            source = sources[number].at[span, distance, k]
                        tap = k if first else SPLIT + k
                        target = wv.at[tap, span, core ^ flip, :, spot]
                        sem = sems.at[tap, number, h]
                        yield tap, pltpu.make_async_copy(source, target, sem)

        def window_copies(target_of, sems):
            for number, (distance, _, start, first, count) in enumerate(parts):
                for b in range(count):
                    target = target_of(distance, pl.ds((first + b) * rows, rows))
                    if target is not None:
                        source = own[number].at[start + b]
                        yield pltpu.make_async_copy(source, target, sems.at[number, b])

        def into_window(distance, span):
            if distance not in distances:
                return None
            return gv.at[span, pl.ds(distances.index(distance) * block, block)]

        early = list(window_copies(into_window, grad_sems))
        late = [pltpu.make_async_copy(slope_ref, slopes, slope_sem)]
        if last:
            sums, strip, sum_sem = refs[8:]
            late.append(pltpu.make_async_copy(begun_ref, sums, sum_sem))
        else:
            skips, skip_sems = refs[8:]
            late += window_copies(lambda d, span: skips.at[me ^ d, span], skip_sems)
        for copy in early:
            copy.start()
        arriving = sorted([*kernel_copies(True), *kernel_copies(False)], key=lambda pair: pair[0])
        for _, copy in arriving:
            copy.start()
        for copy in late:
            copy.start()
        for copy in early:
            copy.wait()
        for k in range(taps):
            for tap, copy in arriving:
                if tap == k:
                    copy.wait()
            for part in range(2):
                kernel = wv[k, part * half : (part + 1) * half].reshape(2 * half * rows, depth)
                lanes = slice(part * 2 * half * rows, (part + 1) * 2 * half * rows)
                products[k, :, lanes] = lax.dot_general(
                    gv[EDGE : EDGE + used],
                    kernel,
                    (((1,), (1,)), ((), ())),
                    preferred_element_type=jnp.float32,
                )

        for copy in late:
            copy.wait()

        @pl.loop(0, coarse // STEP)
        def _(i):
            base = pl.multiple_of(i * STEP, STEP)
            spot, span = pl.ds(base, STEP), pl.ds(pl.multiple_of(2 * base, 2 * STEP), 2 * STEP)
            for c in range(width // LANES):
                lanes = slice(c * LANES, (c + 1) * LANES)
                if not last:
                    left = c * LANES % block
                    skip = skips[c * LANES // block, pl.ds(base + HALO, STEP), left : left + LANES]
                    skip = 0.5 * skip.astype(jnp.float32)
                for parity in range(2):
                    total = shifted_total(products, base, lanes, parity)
                    total = total * slopes[parity, spot, lanes]
                    total = total + (sums[parity, spot, lanes] if last else skip)
                    if last:
                        strip[c, pl.ds(parity, STEP, stride=2), :] = total
                    else:
                        out_ref[parity, spot, lanes] = total
                if last:
                    out_ref[0, span, lanes] = strip[c].astype(jnp.bfloat16)

    out_shape = jax.ShapeDtypeStruct(shape if last else planar, jnp.bfloat16 if last else jnp.float32)
    scratch = [
        pltpu.VMEM((taps, planes, 2, rows, depth), jnp.bfloat16),
        pltpu.VMEM((window, depth), jnp.bfloat16),
        pltpu.VMEM((taps, used, width), jnp.float32),
        pltpu.VMEM(planar, jnp.float32),
        pltpu.SemaphoreType.DMA((taps, len(pieces), 2)),
        pltpu.SemaphoreType.DMA((len(parts), window // rows)),
        pltpu.SemaphoreType.DMA,
    ]
    if last:
        scratch += [
            pltpu.VMEM(planar, jnp.float32),
            pltpu.VMEM((width // LANES, 2 * STEP, LANES), jnp.float32),
            pltpu.SemaphoreType.DMA,
        ]
    else:
        scratch += [
            pltpu.VMEM((seqs, window, block), jnp.bfloat16),
            pltpu.SemaphoreType.DMA((len(parts), window // rows)),
        ]
    return pl.pallas_call(
        body,
        out_shape=out_shape,
        grid_spec=pltpu.PrefetchScalarGridSpec(
            num_scalar_prefetch=1,
            grid=(1,),
            in_specs=[ANYWHERE] * len(operands),
            out_specs=pl.BlockSpec(out_shape.shape, lambda i, place: (0, 0, 0)),
            scratch_shapes=scratch,
        ),
        compiler_params=pltpu.CompilerParams(vmem_limit_bytes=56 << 20),
        cost_estimate=SMALL,
        name="input_grad",
    )(place, *operands)


def stack_planes(place, line):
    count = len(line)

    def kernel(place, *refs):
        parts, out_ref = refs[:count], refs[count]
        for j in range(count):
            out_ref[place[1] // 2 ^ j] = parts[j][...]

    shape = line[0].shape
    return pl.pallas_call(
        kernel,
        out_shape=jax.ShapeDtypeStruct((count, *shape), line[0].dtype),
        grid_spec=pltpu.PrefetchScalarGridSpec(
            num_scalar_prefetch=1,
            grid=(1,),
            in_specs=[pl.BlockSpec(shape, lambda i, place: (0,) * len(shape))] * count,
            out_specs=pl.BlockSpec((count, *shape), lambda i, place: (0,) * (1 + len(shape))),
        ),
        compiler_params=pltpu.CompilerParams(vmem_limit_bytes=24 << 20),
        cost_estimate=SMALL,
        name="stack_planes",
    )(place, *line)


def on_device_square(inputs, trunk_grad, weights):
    seqs, reps = lax.axis_size("seq"), lax.axis_size("rep")
    me, rep = lax.axis_index("seq"), lax.axis_index("rep")
    place = jnp.stack([me, rep]).astype(jnp.int32)
    taps, rows, block = weights.shape
    fine = inputs.shape[1]
    coarse, planes = fine // 2, reps // 2
    half = coarse // 2

    last_taps = weights[SPLIT:]
    across = [last_taps] + [from_peer(last_taps, "seq", d) for d in range(1, seqs)]

    act = after(activate(inputs), *across[1:])
    beside, below = from_peer(act, "seq", 1), from_peer(act, "seq", 2)
    slope = half_slope(inputs)
    line = gather_line(weights[:SPLIT], "rep", planes, 2)
    line_across = gather_line(after(jnp.stack(across), *line[1:]), "rep", planes, 2)
    trunk = trunk_grad[0]
    zeros = jnp.zeros((1, block), jnp.bfloat16)
    later = jnp.concatenate([trunk[1:], zeros])
    earlier = jnp.concatenate([zeros, trunk[:-1]])
    shifts = jnp.concatenate([later, trunk, earlier], axis=1)
    to_beside, to_below, own_window = kernel_messages(place, line, trunk_grad, coarse)
    ready = (slope, shifts, to_beside, line_across[1], line_across[planes - 1])
    top, bottom = after(beside[:half], *ready), after(below[half:], *ready)
    far_top, far_bottom = from_peer(top, "seq", 2), from_peer(bottom, "seq", 1)

    scale = 0.5 * float(fine * seqs * reps) ** (-0.5)
    near_rows = [(d, 0, coarse, 0) for d in range(3)]
    far_rows = [(3, 0, half, 0), (3, half, half, 0)]
    early = early_terms(place, near_rows, [act, beside, below], shifts, coarse)
    line_across[2] = after(line_across[2], early)
    lines = stack_planes(place, line_across)
    far_top, far_bottom = after(far_top, early, lines), after(far_bottom, early, lines)

    to_beside, to_below = (
        after(message, far_top, far_bottom) for message in (to_beside, to_below)
    )
    kept_beside, kept_below = from_peer(to_beside, "seq", 1), from_peer(to_below, "seq", 2)
    other_column, other_lines = from_peer(to_below, "rep", 1), from_peer(lines, "rep", 1)

    mine, theirs = late_terms(
        place, far_rows, [far_top, far_bottom], shifts, early, coarse, scale, planes, taps, rows
    )
    arrived = from_peer(theirs, "rep", 1)
    weight_grad = mine[0] + arrived[0].astype(jnp.float32)
    leaving = [(mine[j] + arrived[j].astype(jnp.float32)).astype(jnp.bfloat16) for j in range(planes)]
    summed = [from_peer(leaving[j], "rep", 2 * j) for j in range(1, planes)]

    window = (coarse + 2 * HALO) // rows
    count, side = planes * SPLIT, window // 2
    kept_beside, kept_below = after(kept_beside, *summed), after(kept_below, *summed)
    far_first = from_peer(kept_beside[: side + count // 2], "seq", 2)
    far_second = from_peer(kept_below[count // 2 : count + side], "seq", 1)
    windows = [
        [(own_window, 0, 0, window)],
        [(kept_beside, side + count, 0, window)],
        [(kept_below, count + side, 0, window)],
        [(far_first, 0, 0, side), (far_second, count // 2, side, side)],
    ]

    stage = functools.partial(
        gradient_stage, place, windows, taps, slope=slope, shape=inputs.shape
    )
    soon = [(to_below, 0, 0, planes, 0, 0), (other_column, 0, 0, planes, 1, 0)]
    for part, start, distance in ((kept_beside, side, 1), (kept_below, 0, 2)):
        soon.append((part, start, 0, planes, 0, distance))
        soon.append((from_peer(part, "rep", 1), start, 0, planes, 1, distance))
    crossed = [
        (part, None, 0, planes, flip, d)
        for flip, part in enumerate((lines, other_lines))
        for d in range(seqs)
    ]
    begun = stage(soon + [piece for piece in crossed if piece[-1] < 3], [0, 1, 2], begun=None)
    rest = [piece for piece in crossed if piece[-1] == 3]
    for part, start, plane in ((far_first, side, 0), (far_second, 0, planes // 2)):
        part = after(part, begun)
        rest.append((part, start, plane, planes // 2, 0, 3))
        rest.append((from_peer(part, "rep", 1), start, plane, planes // 2, 1, 3))
    input_grad = stage(rest, [3], begun=begun)
    for part in summed:
        weight_grad = weight_grad + after(part, input_grad).astype(jnp.float32)
    return (input_grad, weight_grad)


def with_halo(value, sides, width):
    for axis, dim in sides:
        peers, length = (lax.axis_size(axis), value.shape[dim])
        up = [(i, (i + 1) % peers) for i in range(peers - 1)]
        down = [(j, i) for i, j in up]
        last = lax.slice_in_dim(value, length - width, length, axis=dim)
        leading = lax.slice_in_dim(value, 0, width, axis=dim)
        before = lax.ppermute(last, axis, up)
        after = lax.ppermute(leading, axis, down)
        value = jnp.concatenate([before, value, after], axis=dim)
    return value


def contract_last(left, right):
    return lax.dot_general(
        left, right, (((1,), (1,)), ((), ())), preferred_element_type=jnp.float32
    )


def contract_first(left, right):
    return lax.dot_general(
        left, right, (((0,), (0,)), ((), ())), preferred_element_type=jnp.float32
    )


def on_device_plain(inputs, trunk_grad, weights):
    taps = weights.shape[0]
    grad = lax.all_to_all(trunk_grad, "seq", split_axis=1, concat_axis=2, tiled=True)
    grad_up = jnp.repeat(grad.astype(jnp.float32) * 0.5, 2, axis=1).astype(jnp.bfloat16)
    rows = grad_up.shape[1]
    padded = with_halo(grad_up, (("seq", 1),), 2)
    shifts = [padded[0, 4 - k : 4 - k + rows] for k in range(taps)]
    inputs_f = inputs[0].astype(jnp.float32)
    act_vals, back = jax.vjp(jax.nn.gelu, inputs_f)
    slope = back(jnp.ones_like(inputs_f))[0]
    act = act_vals.astype(jnp.bfloat16)
    in_width = inputs.shape[2]
    columns = lax.all_gather(weights, "seq", axis=2, tiled=True)
    piece = lax.all_gather(columns, "rep", axis=1, tiled=True)
    result = contract_last(shifts[0], piece[0])
    for project_k in range(1, taps):
        result = result + contract_last(shifts[project_k], piece[project_k])
    input_grad = (result * slope + grad_up[0, :, :in_width].astype(jnp.float32)).astype(
        jnp.bfloat16
    )
    scale_factor = float(rows * lax.axis_size("seq") * lax.axis_size("rep")) ** (-0.5)
    terms = jnp.stack([contract_first(act, shifts[k]) for k in range(taps)]) * scale_factor
    partial_sum = lax.psum_scatter(terms, "rep", scatter_dimension=1, tiled=True)
    weight_grad = lax.psum_scatter(partial_sum, "seq", scatter_dimension=2, tiled=True)
    return (input_grad[None], weight_grad)


def on_device(inputs, trunk_grad, weights):
    square = lax.axis_size("seq") == 4 and lax.axis_size("rep") % 8 == 0
    if square and weights.shape[2] % LANES == 0 and inputs.shape[2] % LANES == 0:
        return on_device_square(inputs, trunk_grad, weights)
    return on_device_plain(inputs, trunk_grad, weights)


def solution(mesh):
    in_specs = (P("rep", "seq", None), P("rep", None, "seq"), P(None, "rep", "seq"))
    out_specs = (P("rep", "seq", None), P(None, "rep", "seq"))
    return jax.shard_map(
        on_device, mesh=mesh, in_specs=in_specs, out_specs=out_specs, check_vma=False
    )
```

```python
import functools
import math

import jax
import jax.numpy as jnp
from jax import lax
from jax.experimental import pallas as pl
from jax.experimental.pallas import tpu as pltpu
from jax.sharding import PartitionSpec as P

LANES = 128
HALO = 32
EDGE = 16
MARGIN = HALO - EDGE
STEP = 64
SPLIT = 3
ROOT = math.sqrt(2.0 / math.pi)
CUBIC = 0.044715
SMALL = pl.CostEstimate(flops=1 << 20, bytes_accessed=1 << 16, transcendentals=0)
ANYWHERE = pl.BlockSpec(memory_space=pl.ANY)
ROW_OFFSETS = ((1, 1), (0, 1), (0, 0), (-1, 0), (-1, -1))
GRAD_PARTS = ((0, 0), (1, 0), (1, 1), (2, 1), (2, 2))


def from_peer(value, axis, distance):
    peers = lax.axis_size(axis)
    return lax.ppermute(value, axis, [(i, i ^ distance) for i in range(peers)])


def after(value, *earlier):
    return pl.pallas_call(
        lambda *refs: None,
        out_shape=jax.ShapeDtypeStruct(value.shape, value.dtype),
        in_specs=[ANYWHERE] * (1 + len(earlier)),
        out_specs=ANYWHERE,
        input_output_aliases={0: 0},
        name="after",
    )(value, *earlier)


def gather_line(value, axis, count, unit):
    found, mask = {0: value}, count - 1
    while mask:
        for distance in list(found):
            found[distance ^ mask] = from_peer(found[distance], axis, mask * unit)
        mask //= 2
    return [found[distance] for distance in range(count)]


def gelu_slope(x):
    tanh = jnp.tanh(ROOT * (x + CUBIC * (x * x * x)))
    return 0.5 * (1.0 + tanh) + 0.5 * x * (1.0 - tanh * tanh) * (
        ROOT * (1.0 + 3.0 * CUBIC * (x * x))
    )


def act_kernel(x_ref, out_ref, strip):
    width = x_ref.shape[2]

    @pl.loop(0, out_ref.shape[0] // STEP)
    def _(step):
        start = pl.multiple_of(step * STEP, STEP)
        x = x_ref[0, pl.ds(pl.multiple_of(2 * start, 2 * STEP), 2 * STEP), :].astype(jnp.float32)
        act = x * (0.5 * (1.0 + jnp.tanh(ROOT * (x + CUBIC * (x * x * x)))))
        for c in range(width // LANES):
            strip[c] = act[:, c * LANES : (c + 1) * LANES]
        for parity in range(2):
            for c in range(width // LANES):
                picked = strip[c, pl.ds(parity, STEP, stride=2), :].astype(jnp.bfloat16)
                left = parity * width + c * LANES
                out_ref[pl.ds(start, STEP), left : left + LANES] = picked


def activate(inputs):
    fine, width = inputs.shape[1:]
    return pl.pallas_call(
        act_kernel,
        out_shape=jax.ShapeDtypeStruct((fine // 2, 2 * width), jnp.bfloat16),
        in_specs=[pl.BlockSpec(memory_space=pltpu.VMEM)],
        out_specs=pl.BlockSpec(memory_space=pltpu.VMEM),
        scratch_shapes=[pltpu.VMEM((width // LANES, 2 * STEP, LANES), jnp.float32)],
        compiler_params=pltpu.CompilerParams(vmem_limit_bytes=24 << 20),
        cost_estimate=SMALL,
        name="act",
    )(inputs)


def kernel_messages(place, line, trunk_grad, coarse):
    taps, rows, block = line[0].shape
    planes, length = len(line), trunk_grad.shape[1]
    window = (coarse + 2 * HALO) // rows
    half = planes // 2

    def kernel(place, *refs):
        parts, trunk_ref = refs[:planes], refs[planes]
        beside_ref, below_ref, own_ref, edged, sem = refs[planes + 1 :]
        copy = pltpu.make_async_copy(trunk_ref.at[0], edged.at[pl.ds(HALO, length)], sem)
        copy.start()
        edged[:HALO] = jnp.zeros((HALO, block), jnp.bfloat16)
        edged[HALO + length :] = jnp.zeros((HALO, block), jnp.bfloat16)
        for j in range(planes):
            plane = place[1] // 2 ^ j
            for k in range(taps):
                spot = (plane // half * taps + k) * half + plane % half
                beside_ref[window // 2 + spot] = parts[j][k]
                below_ref[spot] = parts[j][k]
        copy.wait()

        def cut(out_ref, spot, distance, first, last):
            base = (place[0] ^ distance) * coarse
            for b in range(first, last):
                out_ref[spot + b - first] = edged[pl.ds(pl.multiple_of(base + b * rows, 16), rows), :]

        cut(beside_ref, 0, 3, 0, window // 2)
        cut(beside_ref, window // 2 + planes * taps, 1, 0, window)
        cut(below_ref, planes * taps, 3, window // 2, window)
        cut(below_ref, planes * taps + window // 2, 2, 0, window)
        cut(own_ref, 0, 0, 0, window)

    count = window // 2 + planes * taps + window
    return pl.pallas_call(
        kernel,
        out_shape=[
            jax.ShapeDtypeStruct((n, rows, block), jnp.bfloat16) for n in (count, count, window)
        ],
        grid_spec=pltpu.PrefetchScalarGridSpec(
            num_scalar_prefetch=1,
            grid=(1,),
            in_specs=[pl.BlockSpec(line[0].shape, lambda i, place: (0, 0, 0))] * planes + [ANYWHERE],
            out_specs=[
                pl.BlockSpec((n, rows, block), lambda i, place: (0, 0, 0))
                for n in (count, count, window)
            ],
            scratch_shapes=[
                pltpu.VMEM((length + 2 * HALO, block), jnp.bfloat16),
                pltpu.SemaphoreType.DMA,
            ],
        ),
        compiler_params=pltpu.CompilerParams(vmem_limit_bytes=32 << 20),
        cost_estimate=SMALL,
        name="kernel_messages",
    )(place, *line, trunk_grad)


def slope_kernel(x_ref, out_ref, scratch):
    width = x_ref.shape[2]

    @pl.loop(0, out_ref.shape[1] // 64)
    def _(step):
        start = pl.multiple_of(step * 64, 64)
        span = pl.ds(pl.multiple_of(2 * start, 128), 128)
        for c in range(width // LANES):
            lanes = slice(c * LANES, (c + 1) * LANES)
            scratch[c] = 0.5 * gelu_slope(x_ref[0, span, lanes].astype(jnp.float32))
            for parity in range(2):
                out_ref[parity, pl.ds(start, 64), lanes] = scratch[c, pl.ds(parity, 64, stride=2), :]


def half_slope(inputs):
    fine, width = inputs.shape[1:]
    return pl.pallas_call(
        slope_kernel,
        out_shape=jax.ShapeDtypeStruct((2, fine // 2, width), jnp.float32),
        in_specs=[pl.BlockSpec(memory_space=pltpu.VMEM)],
        out_specs=pl.BlockSpec(memory_space=pltpu.VMEM),
        scratch_shapes=[pltpu.VMEM((width // LANES, 128, LANES), jnp.float32)],
        compiler_params=pltpu.CompilerParams(vmem_limit_bytes=24 << 20),
        name="half_slope",
    )(inputs)


def start_act(place, coarse, layout, pieces, shifts_ref, held, shifts, sems, shift_sems):
    copies, row = [], 0
    for i, (distance, first, size, offset) in enumerate(layout):
        start = pl.multiple_of((place[0] ^ distance) * coarse + first, 16)
        spot = pl.ds(row, size)
        source = pieces[i].at[pl.ds(offset, size)]
        copies.append(pltpu.make_async_copy(source, held.at[spot], sems.at[i]))
        copies.append(
            pltpu.make_async_copy(shifts_ref.at[pl.ds(start, size)], shifts.at[spot], shift_sems.at[i])
        )
        row += size
    for copy in copies:
        copy.start()
    return copies


def early_terms(place, layout, pieces, shifts, coarse):
    both, columns = pieces[0].shape[1], shifts.shape[1]
    rows = sum(size for _, _, size, _ in layout)
    tile = 256

    def kernel(place, shifts_ref, *refs):
        pieces, total = refs[: len(layout)], refs[len(layout)]
        held, shifts, sems, shift_sems = refs[len(layout) + 1 :]
        copies = start_act(
            place, coarse, layout, pieces, shifts_ref, held, shifts, sems, shift_sems
        )
        for copy in copies:
            copy.wait()

        @pl.loop(0, both // tile)
        def _(i):
            span = pl.ds(pl.multiple_of(i * tile, tile), tile)
            total[span, :] = lax.dot_general(
                held[:, span], shifts[...], (((0,), (0,)), ((), ())), preferred_element_type=jnp.float32
            )

    return pl.pallas_call(
        kernel,
        out_shape=jax.ShapeDtypeStruct((both, columns), jnp.float32),
        grid_spec=pltpu.PrefetchScalarGridSpec(
            num_scalar_prefetch=1,
            grid=(1,),
            in_specs=[ANYWHERE] * (1 + len(pieces)),
            out_specs=pl.BlockSpec((both, columns), lambda i, place: (0, 0)),
            scratch_shapes=[
                pltpu.VMEM((rows, both), jnp.bfloat16),
                pltpu.VMEM((rows, columns), jnp.bfloat16),
                pltpu.SemaphoreType.DMA((len(pieces),)),
                pltpu.SemaphoreType.DMA((len(pieces),)),
            ],
        ),
        compiler_params=pltpu.CompilerParams(vmem_limit_bytes=48 << 20),
        cost_estimate=SMALL,
        name="weight_grad_early",
    )(place, shifts, *pieces)


def late_terms(place, layout, pieces, shifts, early, coarse, scale, planes, taps, rows):
    both, columns = early.shape
    width, block = both // 2, columns // 3
    count = sum(size for _, _, size, _ in layout)
    tile = 256
    shape = (planes, taps, rows, block)

    def kernel(place, shifts_ref, early_ref, *refs):
        pieces, (mine_ref, *theirs_refs) = refs[: len(layout)], refs[len(layout) : len(layout) + 3]
        held, shifts, total, sems, shift_sems, early_sems = refs[len(layout) + 3 :]
        core, plane = place[1] % 2, place[1] // 2
        copies = start_act(
            place, coarse, layout, pieces, shifts_ref, held, shifts, sems, shift_sems
        )

        def fetch(i):
            span = pl.ds(pl.multiple_of(i * tile, tile), tile)
            return pltpu.make_async_copy(early_ref.at[span], total.at[span], early_sems.at[i])

        for i in range(both // tile):
            fetch(i).start()
        for copy in copies:
            copy.wait()

        @pl.loop(0, both // tile)
        def _(i):
            span = pl.ds(pl.multiple_of(i * tile, tile), tile)
            term = lax.dot_general(
                held[:, span], shifts[...], (((0,), (0,)), ((), ())), preferred_element_type=jnp.float32
            )
            fetch(i).wait()
            total[span, :] += term

        def finish(out_ref, at, j, parity, kind):
            start = ((plane ^ j) * 2 + parity) * rows
            even = pl.ds(pl.multiple_of(start, 16), rows)
            odd = pl.ds(pl.multiple_of(width + start, 16), rows)
            for k, (left, right) in enumerate(GRAD_PARTS):
                term = total[even, left * block : (left + 1) * block]
                term += total[odd, right * block : (right + 1) * block]
                out_ref[at, k] = (scale * term).astype(kind)

        for which, out_ref in enumerate(theirs_refs):

            @pl.loop(0, planes // 2)
            def _(at):
                finish(out_ref, at, at + which * (planes // 2), 1 - core, jnp.bfloat16)

        @pl.loop(0, planes)
        def _(j):
            finish(mine_ref, j, j, core, jnp.float32)

    half_shape = (planes // 2, *shape[1:])
    whole = pl.BlockSpec(shape, lambda i, place: (0, 0, 0, 0))
    half = pl.BlockSpec(half_shape, lambda i, place: (0, 0, 0, 0))
    return pl.pallas_call(
        kernel,
        out_shape=(
            jax.ShapeDtypeStruct(shape, jnp.float32),
            jax.ShapeDtypeStruct(half_shape, jnp.bfloat16),
            jax.ShapeDtypeStruct(half_shape, jnp.bfloat16),
        ),
        grid_spec=pltpu.PrefetchScalarGridSpec(
            num_scalar_prefetch=1,
            grid=(1,),
            in_specs=[ANYWHERE] * (2 + len(pieces)),
            out_specs=[whole, half, half],
            scratch_shapes=[
                pltpu.VMEM((count, both), jnp.bfloat16),
                pltpu.VMEM((count, columns), jnp.bfloat16),
                pltpu.VMEM((both, columns), jnp.float32),
                pltpu.SemaphoreType.DMA((len(pieces),)),
                pltpu.SemaphoreType.DMA((len(pieces),)),
                pltpu.SemaphoreType.DMA((both // tile,)),
            ],
        ),
        compiler_params=pltpu.CompilerParams(vmem_limit_bytes=48 << 20),
        cost_estimate=SMALL,
        name="weight_grad_late",
    )(place, shifts, early, *pieces)


def shifted_total(products, base, lanes, parity):
    total = None
    for by in (0, 1, -1):
        wanted = [k for k in range(products.shape[0]) if ROW_OFFSETS[k][parity] == by]
        if wanted:
            near = pl.ds(base + MARGIN - 8, STEP + 16)
            part = sum(products[k, near, lanes] for k in wanted)[8 + by : 8 + by + STEP]
            total = part if total is None else total + part
    return total


def gradient_stage(place, windows, taps, pieces, distances, slope, begun, shape):
    _, fine, width = shape
    coarse, seqs = fine // 2, len(windows)
    rows, block = pieces[0][0].shape[-2:]
    planes = width // (2 * rows)
    half = planes // 2
    window, used = coarse + 2 * HALO, coarse + 2 * MARGIN
    depth, planar = len(distances) * block, (2, coarse, width)
    last = begun is not None
    needed = distances if last else list(range(seqs))
    parts = [(d, *part) for d in needed for part in windows[d]]
    operands = [part[1] for part in parts] + [piece[0] for piece in pieces]
    operands += [slope] + ([begun] if last else [])

    def body(place, *refs):
        own, refs = refs[: len(parts)], refs[len(parts) :]
        sources, refs = refs[: len(pieces)], refs[len(pieces) :]
        slope_ref, refs = refs[0], refs[1:]
        if last:
            begun_ref, refs = refs[0], refs[1:]
        out_ref, wv, gv, products, slopes, sems, grad_sems, slope_sem = refs[:8]
        me, core = place[0], place[1] % 2

        def kernel_copies(first):
            for number, (array, start, plane, count, flip, distance) in enumerate(pieces):
                spot = pl.ds(distances.index(distance) * block, block)
                if first != (start is not None):
                    continue
                for k in range(SPLIT if first else taps - SPLIT):
                    for h in range(count // half):
                        span = pl.ds(plane + h * half, half)
                        if first:
                            source = sources[number].at[pl.ds(start + (h * SPLIT + k) * half, half)]
                        else:
                            source = sources[number].at[span, distance, k]
                        tap = k if first else SPLIT + k
                        target = wv.at[tap, span, core ^ flip, :, spot]
                        sem = sems.at[tap, number, h]
                        yield tap, pltpu.make_async_copy(source, target, sem)

        def window_copies(target_of, sems):
            for number, (distance, _, start, first, count) in enumerate(parts):
                for b in range(count):
                    target = target_of(distance, pl.ds((first + b) * rows, rows))
                    if target is not None:
                        source = own[number].at[start + b]
                        yield pltpu.make_async_copy(source, target, sems.at[number, b])

        def into_window(distance, span):
            if distance not in distances:
                return None
            return gv.at[span, pl.ds(distances.index(distance) * block, block)]

        early = list(window_copies(into_window, grad_sems))
        late = [pltpu.make_async_copy(slope_ref, slopes, slope_sem)]
        if last:
            sums, strip, sum_sem = refs[8:]
            late.append(pltpu.make_async_copy(begun_ref, sums, sum_sem))
        else:
            skips, skip_sems = refs[8:]
            late += window_copies(lambda d, span: skips.at[me ^ d, span], skip_sems)
        for copy in early:
            copy.start()
        arriving = sorted([*kernel_copies(True), *kernel_copies(False)], key=lambda pair: pair[0])
        for _, copy in arriving:
            copy.start()
        for copy in late:
            copy.start()
        for copy in early:
            copy.wait()
        for k in range(taps):
            for tap, copy in arriving:
                if tap == k:
                    copy.wait()
            for part in range(2):
                kernel = wv[k, part * half : (part + 1) * half].reshape(2 * half * rows, depth)
                lanes = slice(part * 2 * half * rows, (part + 1) * 2 * half * rows)
                products[k, :, lanes] = lax.dot_general(
                    gv[EDGE : EDGE + used],
                    kernel,
                    (((1,), (1,)), ((), ())),
                    preferred_element_type=jnp.float32,
                )

        for copy in late:
            copy.wait()

        @pl.loop(0, coarse // STEP)
        def _(i):
            base = pl.multiple_of(i * STEP, STEP)
            spot, span = pl.ds(base, STEP), pl.ds(pl.multiple_of(2 * base, 2 * STEP), 2 * STEP)
            for c in range(width // LANES):
                lanes = slice(c * LANES, (c + 1) * LANES)
                if not last:
                    left = c * LANES % block
                    skip = skips[c * LANES // block, pl.ds(base + HALO, STEP), left : left + LANES]
                    skip = 0.5 * skip.astype(jnp.float32)
                for parity in range(2):
                    total = shifted_total(products, base, lanes, parity)
                    total = total * slopes[parity, spot, lanes]
                    total = total + (sums[parity, spot, lanes] if last else skip)
                    if last:
                        strip[c, pl.ds(parity, STEP, stride=2), :] = total
                    else:
                        out_ref[parity, spot, lanes] = total
                if last:
                    out_ref[0, span, lanes] = strip[c].astype(jnp.bfloat16)

    out_shape = jax.ShapeDtypeStruct(shape if last else planar, jnp.bfloat16 if last else jnp.float32)
    scratch = [
        pltpu.VMEM((taps, planes, 2, rows, depth), jnp.bfloat16),
        pltpu.VMEM((window, depth), jnp.bfloat16),
        pltpu.VMEM((taps, used, width), jnp.float32),
        pltpu.VMEM(planar, jnp.float32),
        pltpu.SemaphoreType.DMA((taps, len(pieces), 2)),
        pltpu.SemaphoreType.DMA((len(parts), window // rows)),
        pltpu.SemaphoreType.DMA,
    ]
    if last:
        scratch += [
            pltpu.VMEM(planar, jnp.float32),
            pltpu.VMEM((width // LANES, 2 * STEP, LANES), jnp.float32),
            pltpu.SemaphoreType.DMA,
        ]
    else:
        scratch += [
            pltpu.VMEM((seqs, window, block), jnp.bfloat16),
            pltpu.SemaphoreType.DMA((len(parts), window // rows)),
        ]
    return pl.pallas_call(
        body,
        out_shape=out_shape,
        grid_spec=pltpu.PrefetchScalarGridSpec(
            num_scalar_prefetch=1,
            grid=(1,),
            in_specs=[ANYWHERE] * len(operands),
            out_specs=pl.BlockSpec(out_shape.shape, lambda i, place: (0, 0, 0)),
            scratch_shapes=scratch,
        ),
        compiler_params=pltpu.CompilerParams(vmem_limit_bytes=56 << 20),
        cost_estimate=SMALL,
        name="input_grad",
    )(place, *operands)


def stack_planes(place, line):
    count = len(line)

    def kernel(place, *refs):
        parts, out_ref = refs[:count], refs[count]
        for j in range(count):
            out_ref[place[1] // 2 ^ j] = parts[j][...]

    shape = line[0].shape
    return pl.pallas_call(
        kernel,
        out_shape=jax.ShapeDtypeStruct((count, *shape), line[0].dtype),
        grid_spec=pltpu.PrefetchScalarGridSpec(
            num_scalar_prefetch=1,
            grid=(1,),
            in_specs=[pl.BlockSpec(shape, lambda i, place: (0,) * len(shape))] * count,
            out_specs=pl.BlockSpec((count, *shape), lambda i, place: (0,) * (1 + len(shape))),
        ),
        compiler_params=pltpu.CompilerParams(vmem_limit_bytes=24 << 20),
        cost_estimate=SMALL,
        name="stack_planes",
    )(place, *line)


def on_device_square(inputs, trunk_grad, weights):
    seqs, reps = lax.axis_size("seq"), lax.axis_size("rep")
    me, rep = lax.axis_index("seq"), lax.axis_index("rep")
    place = jnp.stack([me, rep]).astype(jnp.int32)
    taps, rows, block = weights.shape
    fine = inputs.shape[1]
    coarse, planes = fine // 2, reps // 2
    half = coarse // 2

    last_taps = weights[SPLIT:]
    across = [last_taps] + [from_peer(last_taps, "seq", d) for d in range(1, seqs)]

    act = after(activate(inputs), *across[1:])
    beside, below = from_peer(act, "seq", 1), from_peer(act, "seq", 2)
    slope = half_slope(inputs)
    line = gather_line(weights[:SPLIT], "rep", planes, 2)
    line_across = gather_line(after(jnp.stack(across), *line[1:]), "rep", planes, 2)
    trunk = trunk_grad[0]
    zeros = jnp.zeros((1, block), jnp.bfloat16)
    later = jnp.concatenate([trunk[1:], zeros])
    earlier = jnp.concatenate([zeros, trunk[:-1]])
    shifts = jnp.concatenate([later, trunk, earlier], axis=1)
    to_beside, to_below, own_window = kernel_messages(place, line, trunk_grad, coarse)
    ready = (slope, shifts, to_beside, line_across[1], line_across[planes - 1])
    top, bottom = after(beside[:half], *ready), after(below[half:], *ready)
    far_top, far_bottom = from_peer(top, "seq", 2), from_peer(bottom, "seq", 1)

    scale = 0.5 * float(fine * seqs * reps) ** (-0.5)
    near_rows = [(d, 0, coarse, 0) for d in range(3)]
    far_rows = [(3, 0, half, 0), (3, half, half, 0)]
    early = early_terms(place, near_rows, [act, beside, below], shifts, coarse)
    line_across[2] = after(line_across[2], early)
    lines = stack_planes(place, line_across)
    far_top, far_bottom = after(far_top, early, lines), after(far_bottom, early, lines)

    to_beside, to_below = (
        after(message, far_top, far_bottom) for message in (to_beside, to_below)
    )
    kept_beside, kept_below = from_peer(to_beside, "seq", 1), from_peer(to_below, "seq", 2)
    other_column, other_lines = from_peer(to_below, "rep", 1), from_peer(lines, "rep", 1)

    mine, *theirs = late_terms(
        place, far_rows, [far_top, far_bottom], shifts, early, coarse, scale, planes, taps, rows
    )
    arrived = [from_peer(part, "rep", 1) for part in theirs]
    pairs = []
    for j in range(planes):
        part = arrived[j // (planes // 2)][j % (planes // 2)]
        pairs.append(mine[j] + part.astype(jnp.float32))
    weight_grad = pairs[0]
    leaving = [after(part.astype(jnp.bfloat16), other_column, other_lines) for part in pairs[1:]]
    summed = [from_peer(leaving[j - 1], "rep", 2 * j) for j in range(1, planes)]

    window = (coarse + 2 * HALO) // rows
    count, side = planes * SPLIT, window // 2
    kept_beside, kept_below = after(kept_beside, *summed), after(kept_below, *summed)
    far_first = from_peer(kept_beside[: side + count // 2], "seq", 2)
    far_second = from_peer(kept_below[count // 2 : count + side], "seq", 1)
    windows = [
        [(own_window, 0, 0, window)],
        [(kept_beside, side + count, 0, window)],
        [(kept_below, count + side, 0, window)],
        [(far_first, 0, 0, side), (far_second, count // 2, side, side)],
    ]

    stage = functools.partial(
        gradient_stage, place, windows, taps, slope=slope, shape=inputs.shape
    )
    soon = [(to_below, 0, 0, planes, 0, 0), (other_column, 0, 0, planes, 1, 0)]
    for part, start, distance in ((kept_beside, side, 1), (kept_below, 0, 2)):
        soon.append((part, start, 0, planes, 0, distance))
        soon.append((from_peer(part, "rep", 1), start, 0, planes, 1, distance))
    crossed = [
        (part, None, 0, planes, flip, d)
        for flip, part in enumerate((lines, other_lines))
        for d in range(seqs)
    ]
    begun = stage(soon + [piece for piece in crossed if piece[-1] < 3], [0, 1, 2], begun=None)
    rest = [piece for piece in crossed if piece[-1] == 3]
    for part, start, plane in ((far_first, side, 0), (far_second, 0, planes // 2)):
        part = after(part, begun)
        rest.append((part, start, plane, planes // 2, 0, 3))
        rest.append((from_peer(part, "rep", 1), start, plane, planes // 2, 1, 3))
    input_grad = stage(rest, [3], begun=begun)
    for part in summed:
        weight_grad = weight_grad + after(part, input_grad).astype(jnp.float32)
    return (input_grad, weight_grad)


def with_halo(value, sides, width):
    for axis, dim in sides:
        peers, length = (lax.axis_size(axis), value.shape[dim])
        up = [(i, (i + 1) % peers) for i in range(peers - 1)]
        down = [(j, i) for i, j in up]
        last = lax.slice_in_dim(value, length - width, length, axis=dim)
        leading = lax.slice_in_dim(value, 0, width, axis=dim)
        before = lax.ppermute(last, axis, up)
        after = lax.ppermute(leading, axis, down)
        value = jnp.concatenate([before, value, after], axis=dim)
    return value


def contract_last(left, right):
    return lax.dot_general(
        left, right, (((1,), (1,)), ((), ())), preferred_element_type=jnp.float32
    )


def contract_first(left, right):
    return lax.dot_general(
        left, right, (((0,), (0,)), ((), ())), preferred_element_type=jnp.float32
    )


def on_device_plain(inputs, trunk_grad, weights):
    taps = weights.shape[0]
    grad = lax.all_to_all(trunk_grad, "seq", split_axis=1, concat_axis=2, tiled=True)
    grad_up = jnp.repeat(grad.astype(jnp.float32) * 0.5, 2, axis=1).astype(jnp.bfloat16)
    rows = grad_up.shape[1]
    padded = with_halo(grad_up, (("seq", 1),), 2)
    shifts = [padded[0, 4 - k : 4 - k + rows] for k in range(taps)]
    inputs_f = inputs[0].astype(jnp.float32)
    act_vals, back = jax.vjp(jax.nn.gelu, inputs_f)
    slope = back(jnp.ones_like(inputs_f))[0]
    act = act_vals.astype(jnp.bfloat16)
    in_width = inputs.shape[2]
    columns = lax.all_gather(weights, "seq", axis=2, tiled=True)
    piece = lax.all_gather(columns, "rep", axis=1, tiled=True)
    result = contract_last(shifts[0], piece[0])
    for project_k in range(1, taps):
        result = result + contract_last(shifts[project_k], piece[project_k])
    input_grad = (result * slope + grad_up[0, :, :in_width].astype(jnp.float32)).astype(
        jnp.bfloat16
    )
    scale_factor = float(rows * lax.axis_size("seq") * lax.axis_size("rep")) ** (-0.5)
    terms = jnp.stack([contract_first(act, shifts[k]) for k in range(taps)]) * scale_factor
    partial_sum = lax.psum_scatter(terms, "rep", scatter_dimension=1, tiled=True)
    weight_grad = lax.psum_scatter(partial_sum, "seq", scatter_dimension=2, tiled=True)
    return (input_grad[None], weight_grad)


def on_device(inputs, trunk_grad, weights):
    square = lax.axis_size("seq") == 4 and lax.axis_size("rep") % 8 == 0
    if square and weights.shape[2] % LANES == 0 and inputs.shape[2] % LANES == 0:
        return on_device_square(inputs, trunk_grad, weights)
    return on_device_plain(inputs, trunk_grad, weights)


def solution(mesh):
    in_specs = (P("rep", "seq", None), P("rep", None, "seq"), P(None, "rep", "seq"))
    out_specs = (P("rep", "seq", None), P(None, "rep", "seq"))
    return jax.shard_map(
        on_device, mesh=mesh, in_specs=in_specs, out_specs=out_specs, check_vma=False
    )
```

```python
import functools
import math

import jax
import jax.numpy as jnp
from jax import lax
from jax.experimental import pallas as pl
from jax.experimental.pallas import tpu as pltpu
from jax.sharding import PartitionSpec as P

LANES = 128
HALO = 32
EDGE = 16
MARGIN = HALO - EDGE
STEP = 64
SPLIT = 3
ROOT = math.sqrt(2.0 / math.pi)
CUBIC = 0.044715
SMALL = pl.CostEstimate(flops=1 << 20, bytes_accessed=1 << 16, transcendentals=0)
ANYWHERE = pl.BlockSpec(memory_space=pl.ANY)
ROW_OFFSETS = ((1, 1), (0, 1), (0, 0), (-1, 0), (-1, -1))
GRAD_PARTS = ((0, 0), (1, 0), (1, 1), (2, 1), (2, 2))

def from_peer(value, axis, distance):
    peers = lax.axis_size(axis)
    return lax.ppermute(value, axis, [(i, i ^ distance) for i in range(peers)])

def after(value, *earlier):
    return pl.pallas_call(
        lambda *refs: None,
        out_shape=jax.ShapeDtypeStruct(value.shape, value.dtype),
        in_specs=[ANYWHERE] * (1 + len(earlier)),
        out_specs=ANYWHERE,
        input_output_aliases={0: 0},
        name="after",
    )(value, *earlier)

def gather_line(value, axis, count, unit):
    found, mask = {0: value}, count - 1
    while mask:
        for distance in list(found):
            found[distance ^ mask] = from_peer(found[distance], axis, mask * unit)
        mask //= 2
    return [found[distance] for distance in range(count)]

def gelu_slope(x):
    tanh = jnp.tanh(ROOT * (x + CUBIC * (x * x * x)))
    return 0.5 * (1.0 + tanh) + 0.5 * x * (1.0 - tanh * tanh) * (
        ROOT * (1.0 + 3.0 * CUBIC * (x * x))
    )

def act_kernel(x_ref, out_ref, strip):
    width = x_ref.shape[2]

    @pl.loop(0, out_ref.shape[0] // STEP)
    def _(step):
        start = pl.multiple_of(step * STEP, STEP)
        x = x_ref[0, pl.ds(pl.multiple_of(2 * start, 2 * STEP), 2 * STEP), :].astype(jnp.float32)
        act = x * (0.5 * (1.0 + jnp.tanh(ROOT * (x + CUBIC * (x * x * x)))))
        for c in range(width // LANES):
            strip[c] = act[:, c * LANES : (c + 1) * LANES]
        for parity in range(2):
            for c in range(width // LANES):
                picked = strip[c, pl.ds(parity, STEP, stride=2), :].astype(jnp.bfloat16)
                left = parity * width + c * LANES
                out_ref[pl.ds(start, STEP), left : left + LANES] = picked

def activate(inputs):
    fine, width = inputs.shape[1:]
    return pl.pallas_call(
        act_kernel,
        out_shape=jax.ShapeDtypeStruct((fine // 2, 2 * width), jnp.bfloat16),
        in_specs=[pl.BlockSpec(memory_space=pltpu.VMEM)],
        out_specs=pl.BlockSpec(memory_space=pltpu.VMEM),
        scratch_shapes=[pltpu.VMEM((width // LANES, 2 * STEP, LANES), jnp.float32)],
        compiler_params=pltpu.CompilerParams(vmem_limit_bytes=24 << 20),
        cost_estimate=SMALL,
        name="act",
    )(inputs)

def kernel_messages(place, line, trunk_grad, coarse):
    taps, rows, block = line[0].shape
    planes, length = len(line), trunk_grad.shape[1]
    window = (coarse + 2 * HALO) // rows
    half = planes // 2

    def kernel(place, *refs):
        parts, trunk_ref = refs[:planes], refs[planes]
        beside_ref, below_ref, own_ref, edged, sem = refs[planes + 1 :]
        copy = pltpu.make_async_copy(trunk_ref.at[0], edged.at[pl.ds(HALO, length)], sem)
        copy.start()
        edged[:HALO] = jnp.zeros((HALO, block), jnp.bfloat16)
        edged[HALO + length :] = jnp.zeros((HALO, block), jnp.bfloat16)
        for j in range(planes):
            plane = place[1] // 2 ^ j
            for k in range(taps):
                spot = (plane // half * taps + k) * half + plane % half
                beside_ref[window // 2 + spot] = parts[j][k]
                below_ref[spot] = parts[j][k]
        copy.wait()

        def cut(out_ref, spot, distance, first, last):
            base = (place[0] ^ distance) * coarse
            for b in range(first, last):
                out_ref[spot + b - first] = edged[pl.ds(pl.multiple_of(base + b * rows, 16), rows), :]

        cut(beside_ref, 0, 3, 0, window // 2)
        cut(beside_ref, window // 2 + planes * taps, 1, 0, window)
        cut(below_ref, planes * taps, 3, window // 2, window)
        cut(below_ref, planes * taps + window // 2, 2, 0, window)
        cut(own_ref, 0, 0, 0, window)

    count = window // 2 + planes * taps + window
    return pl.pallas_call(
        kernel,
        out_shape=[
            jax.ShapeDtypeStruct((n, rows, block), jnp.bfloat16) for n in (count, count, window)
        ],
        grid_spec=pltpu.PrefetchScalarGridSpec(
            num_scalar_prefetch=1,
            grid=(1,),
            in_specs=[pl.BlockSpec(line[0].shape, lambda i, place: (0, 0, 0))] * planes + [ANYWHERE],
            out_specs=[
                pl.BlockSpec((n, rows, block), lambda i, place: (0, 0, 0))
                for n in (count, count, window)
            ],
            scratch_shapes=[
                pltpu.VMEM((length + 2 * HALO, block), jnp.bfloat16),
                pltpu.SemaphoreType.DMA,
            ],
        ),
        compiler_params=pltpu.CompilerParams(vmem_limit_bytes=32 << 20),
        cost_estimate=SMALL,
        name="kernel_messages",
    )(place, *line, trunk_grad)

def slope_kernel(x_ref, out_ref, scratch):
    width = x_ref.shape[2]

    @pl.loop(0, out_ref.shape[1] // 64)
    def _(step):
        start = pl.multiple_of(step * 64, 64)
        span = pl.ds(pl.multiple_of(2 * start, 128), 128)
        for c in range(width // LANES):
            lanes = slice(c * LANES, (c + 1) * LANES)
            scratch[c] = 0.5 * gelu_slope(x_ref[0, span, lanes].astype(jnp.float32))
            for parity in range(2):
                out_ref[parity, pl.ds(start, 64), lanes] = scratch[c, pl.ds(parity, 64, stride=2), :]

def half_slope(inputs):
    fine, width = inputs.shape[1:]
    return pl.pallas_call(
        slope_kernel,
        out_shape=jax.ShapeDtypeStruct((2, fine // 2, width), jnp.float32),
        in_specs=[pl.BlockSpec(memory_space=pltpu.VMEM)],
        out_specs=pl.BlockSpec(memory_space=pltpu.VMEM),
        scratch_shapes=[pltpu.VMEM((width // LANES, 128, LANES), jnp.float32)],
        compiler_params=pltpu.CompilerParams(vmem_limit_bytes=24 << 20),
        name="half_slope",
    )(inputs)

def start_act(place, coarse, layout, pieces, shifts_ref, held, shifts, sems, shift_sems):
    copies, row = [], 0
    for i, (distance, first, size, offset) in enumerate(layout):
        start = pl.multiple_of((place[0] ^ distance) * coarse + first, 16)
        spot = pl.ds(row, size)
        source = pieces[i].at[pl.ds(offset, size)]
        copies.append(pltpu.make_async_copy(source, held.at[spot], sems.at[i]))
        copies.append(
            pltpu.make_async_copy(shifts_ref.at[pl.ds(start, size)], shifts.at[spot], shift_sems.at[i])
        )
        row += size
    for copy in copies:
        copy.start()
    return copies

def early_terms(place, layout, pieces, shifts, coarse):
    both, columns = pieces[0].shape[1], shifts.shape[1]
    rows = sum(size for _, _, size, _ in layout)
    tile = 256

    def kernel(place, shifts_ref, *refs):
        pieces, total = refs[: len(layout)], refs[len(layout)]
        held, shifts, sems, shift_sems = refs[len(layout) + 1 :]
        copies = start_act(
            place, coarse, layout, pieces, shifts_ref, held, shifts, sems, shift_sems
        )
        for copy in copies:
            copy.wait()

        @pl.loop(0, both // tile)
        def _(i):
            span = pl.ds(pl.multiple_of(i * tile, tile), tile)
            total[span, :] = lax.dot_general(
                held[:, span], shifts[...], (((0,), (0,)), ((), ())), preferred_element_type=jnp.float32
            )

    return pl.pallas_call(
        kernel,
        out_shape=jax.ShapeDtypeStruct((both, columns), jnp.float32),
        grid_spec=pltpu.PrefetchScalarGridSpec(
            num_scalar_prefetch=1,
            grid=(1,),
            in_specs=[ANYWHERE] * (1 + len(pieces)),
            out_specs=pl.BlockSpec((both, columns), lambda i, place: (0, 0)),
            scratch_shapes=[
                pltpu.VMEM((rows, both), jnp.bfloat16),
                pltpu.VMEM((rows, columns), jnp.bfloat16),
                pltpu.SemaphoreType.DMA((len(pieces),)),
                pltpu.SemaphoreType.DMA((len(pieces),)),
            ],
        ),
        compiler_params=pltpu.CompilerParams(vmem_limit_bytes=48 << 20),
        cost_estimate=SMALL,
        name="weight_grad_early",
    )(place, shifts, *pieces)

def late_terms(place, layout, pieces, shifts, early, coarse, scale, planes, taps, rows):
    both, columns = early.shape
    width, block = both // 2, columns // 3
    count = sum(size for _, _, size, _ in layout)
    tile = 256
    shape = (planes, taps, rows, block)

    def kernel(place, shifts_ref, early_ref, *refs):
        pieces, (mine_ref, *theirs_refs) = refs[: len(layout)], refs[len(layout) : len(layout) + 3]
        held, shifts, total, sems, shift_sems, early_sems = refs[len(layout) + 3 :]
        core, plane = place[1] % 2, place[1] // 2
        copies = start_act(
            place, coarse, layout, pieces, shifts_ref, held, shifts, sems, shift_sems
        )

        def fetch(i):
            span = pl.ds(pl.multiple_of(i * tile, tile), tile)
            return pltpu.make_async_copy(early_ref.at[span], total.at[span], early_sems.at[i])

        for i in range(both // tile):
            fetch(i).start()
        for copy in copies:
            copy.wait()

        @pl.loop(0, both // tile)
        def _(i):
            span = pl.ds(pl.multiple_of(i * tile, tile), tile)
            term = lax.dot_general(
                held[:, span], shifts[...], (((0,), (0,)), ((), ())), preferred_element_type=jnp.float32
            )
            fetch(i).wait()
            total[span, :] += term

        def finish(out_ref, at, j, parity, kind):
            start = ((plane ^ j) * 2 + parity) * rows
            even = pl.ds(pl.multiple_of(start, 16), rows)
            odd = pl.ds(pl.multiple_of(width + start, 16), rows)
            for k, (left, right) in enumerate(GRAD_PARTS):
                term = total[even, left * block : (left + 1) * block]
                term += total[odd, right * block : (right + 1) * block]
                out_ref[at, k] = (scale * term).astype(kind)

        for which, out_ref in enumerate(theirs_refs):

            @pl.loop(0, planes // 2)
            def _(at):
                finish(out_ref, at, at + which * (planes // 2), 1 - core, jnp.bfloat16)

        @pl.loop(0, planes)
        def _(j):
            finish(mine_ref, j, j, core, jnp.float32)

    half_shape = (planes // 2, *shape[1:])
    whole = pl.BlockSpec(shape, lambda i, place: (0, 0, 0, 0))
    half = pl.BlockSpec(half_shape, lambda i, place: (0, 0, 0, 0))
    return pl.pallas_call(
        kernel,
        out_shape=(
            jax.ShapeDtypeStruct(shape, jnp.float32),
            jax.ShapeDtypeStruct(half_shape, jnp.bfloat16),
            jax.ShapeDtypeStruct(half_shape, jnp.bfloat16),
        ),
        grid_spec=pltpu.PrefetchScalarGridSpec(
            num_scalar_prefetch=1,
            grid=(1,),
            in_specs=[ANYWHERE] * (2 + len(pieces)),
            out_specs=[whole, half, half],
            scratch_shapes=[
                pltpu.VMEM((count, both), jnp.bfloat16),
                pltpu.VMEM((count, columns), jnp.bfloat16),
                pltpu.VMEM((both, columns), jnp.float32),
                pltpu.SemaphoreType.DMA((len(pieces),)),
                pltpu.SemaphoreType.DMA((len(pieces),)),
                pltpu.SemaphoreType.DMA((both // tile,)),
            ],
        ),
        compiler_params=pltpu.CompilerParams(vmem_limit_bytes=48 << 20),
        cost_estimate=SMALL,
        name="weight_grad_late",
    )(place, shifts, early, *pieces)

def shifted_total(products, base, lanes, parity):
    total = None
    for by in (0, 1, -1):
        wanted = [k for k in range(products.shape[0]) if ROW_OFFSETS[k][parity] == by]
        if wanted:
            near = pl.ds(base + MARGIN - 8, STEP + 16)
            part = sum(products[k, near, lanes] for k in wanted)[8 + by : 8 + by + STEP]
            total = part if total is None else total + part
    return total

def gradient_stage(place, windows, taps, pieces, distances, slope, begun, shape):
    _, fine, width = shape
    coarse, seqs = fine // 2, lax.axis_size("seq")
    rows, block = pieces[0][0].shape[-2:]
    planes = width // (2 * rows)
    half = planes // 2
    window, used = coarse + 2 * HALO, coarse + 2 * MARGIN
    depth, planar = len(distances) * block, (2, coarse, width)
    last = begun is not None
    needed = list(range(seqs)) if last else distances
    parts = [(d, *part) for d in needed for part in windows[d]]
    operands = [part[1] for part in parts] + [piece[0] for piece in pieces]
    operands += [slope, begun] if last else []

    def body(place, *refs):
        own, refs = refs[: len(parts)], refs[len(parts) :]
        sources, refs = refs[: len(pieces)], refs[len(pieces) :]
        if last:
            (slope_ref, begun_ref), refs = refs[:2], refs[2:]
        out_ref, wv, gv, products, sems, grad_sems = refs[:6]
        me, core = place[0], place[1] % 2

        def kernel_copies(first):
            for number, (array, start, plane, count, flip, distance) in enumerate(pieces):
                spot = pl.ds(distances.index(distance) * block, block)
                if first != (start is not None):
                    continue
                for k in range(SPLIT if first else taps - SPLIT):
                    for h in range(count // half):
                        span = pl.ds(plane + h * half, half)
                        if first:
                            source = sources[number].at[pl.ds(start + (h * SPLIT + k) * half, half)]
                        else:
                            source = sources[number].at[span, distance, k]
                        tap = k if first else SPLIT + k
                        target = wv.at[tap, span, core ^ flip, :, spot]
                        sem = sems.at[tap, number, h]
                        yield tap, pltpu.make_async_copy(source, target, sem)

        def window_copies(target_of, sems):
            for number, (distance, _, start, first, count) in enumerate(parts):
                for b in range(count):
                    target = target_of(distance, pl.ds((first + b) * rows, rows))
                    if target is not None:
                        source = own[number].at[start + b]
                        yield pltpu.make_async_copy(source, target, sems.at[number, b])

        def into_window(distance, span):
            if distance not in distances:
                return None
            return gv.at[span, pl.ds(distances.index(distance) * block, block)]

        early = list(window_copies(into_window, grad_sems))
        late = []
        if last:
            sums, slopes, strip, skips, sum_sems, skip_sems = refs[6:]
            late.append(pltpu.make_async_copy(begun_ref, sums, sum_sems.at[0]))
            late.append(pltpu.make_async_copy(slope_ref, slopes, sum_sems.at[1]))
            late += window_copies(lambda d, span: skips.at[me ^ d, span], skip_sems)
        for copy in early:
            copy.start()
        arriving = sorted([*kernel_copies(True), *kernel_copies(False)], key=lambda pair: pair[0])
        for _, copy in arriving:
            copy.start()
        for copy in late:
            copy.start()
        for copy in early:
            copy.wait()
        for k in range(taps):
            for tap, copy in arriving:
                if tap == k:
                    copy.wait()
            for part in range(2):
                kernel = wv[k, part * half : (part + 1) * half].reshape(2 * half * rows, depth)
                lanes = slice(part * 2 * half * rows, (part + 1) * 2 * half * rows)
                products[k, :, lanes] = lax.dot_general(
                    gv[EDGE : EDGE + used],
                    kernel,
                    (((1,), (1,)), ((), ())),
                    preferred_element_type=jnp.float32,
                )

        for copy in late:
            copy.wait()

        @pl.loop(0, coarse // STEP)
        def _(i):
            base = pl.multiple_of(i * STEP, STEP)
            spot, span = pl.ds(base, STEP), pl.ds(pl.multiple_of(2 * base, 2 * STEP), 2 * STEP)
            for c in range(width // LANES):
                lanes = slice(c * LANES, (c + 1) * LANES)
                if last:
                    left = c * LANES % block
                    skip = skips[c * LANES // block, pl.ds(base + HALO, STEP), left : left + LANES]
                    skip = 0.5 * skip.astype(jnp.float32)
                for parity in range(2):
                    total = shifted_total(products, base, lanes, parity)
                    if last:
                        total = (total + sums[parity, spot, lanes]) * slopes[parity, spot, lanes]
                        strip[c, pl.ds(parity, STEP, stride=2), :] = total + skip
                    else:
                        out_ref[parity, spot, lanes] = total
                if last:
                    out_ref[0, span, lanes] = strip[c].astype(jnp.bfloat16)

    out_shape = jax.ShapeDtypeStruct(shape if last else planar, jnp.bfloat16 if last else jnp.float32)
    scratch = [
        pltpu.VMEM((taps, planes, 2, rows, depth), jnp.bfloat16),
        pltpu.VMEM((window, depth), jnp.bfloat16),
        pltpu.VMEM((taps, used, width), jnp.float32),
        pltpu.SemaphoreType.DMA((taps, len(pieces), 2)),
        pltpu.SemaphoreType.DMA((len(parts), window // rows)),
    ]
    if last:
        scratch += [
            pltpu.VMEM(planar, jnp.float32),
            pltpu.VMEM(planar, jnp.float32),
            pltpu.VMEM((width // LANES, 2 * STEP, LANES), jnp.float32),
            pltpu.VMEM((seqs, window, block), jnp.bfloat16),
            pltpu.SemaphoreType.DMA((2,)),
            pltpu.SemaphoreType.DMA((len(parts), window // rows)),
        ]
    return pl.pallas_call(
        body,
        out_shape=out_shape,
        grid_spec=pltpu.PrefetchScalarGridSpec(
            num_scalar_prefetch=1,
            grid=(1,),
            in_specs=[ANYWHERE] * len(operands),
            out_specs=pl.BlockSpec(out_shape.shape, lambda i, place: (0, 0, 0)),
            scratch_shapes=scratch,
        ),
        compiler_params=pltpu.CompilerParams(vmem_limit_bytes=56 << 20),
        cost_estimate=SMALL,
        name="input_grad",
    )(place, *operands)

def stack_planes(place, line):
    count = len(line)

    def kernel(place, *refs):
        parts, out_ref = refs[:count], refs[count]
        for j in range(count):
            out_ref[place[1] // 2 ^ j] = parts[j][...]

    shape = line[0].shape
    return pl.pallas_call(
        kernel,
        out_shape=jax.ShapeDtypeStruct((count, *shape), line[0].dtype),
        grid_spec=pltpu.PrefetchScalarGridSpec(
            num_scalar_prefetch=1,
            grid=(1,),
            in_specs=[pl.BlockSpec(shape, lambda i, place: (0,) * len(shape))] * count,
            out_specs=pl.BlockSpec((count, *shape), lambda i, place: (0,) * (1 + len(shape))),
        ),
        compiler_params=pltpu.CompilerParams(vmem_limit_bytes=24 << 20),
        cost_estimate=SMALL,
        name="stack_planes",
    )(place, *line)

def on_device_square(inputs, trunk_grad, weights):
    seqs, reps = lax.axis_size("seq"), lax.axis_size("rep")
    me, rep = lax.axis_index("seq"), lax.axis_index("rep")
    place = jnp.stack([me, rep]).astype(jnp.int32)
    taps, rows, block = weights.shape
    fine = inputs.shape[1]
    coarse, planes = fine // 2, reps // 2
    half = coarse // 2

    last_taps = weights[SPLIT:]
    across = [last_taps] + [from_peer(last_taps, "seq", d) for d in range(1, seqs)]

    act = after(activate(inputs), *across[1:])
    beside, below = from_peer(act, "seq", 1), from_peer(act, "seq", 2)
    slope = half_slope(inputs)
    line_across = gather_line(after(jnp.stack(across), act), "rep", planes, 2)
    crossing = (line_across[1], line_across[planes - 1])
    line = gather_line(after(weights[:SPLIT], *crossing), "rep", planes, 2)
    trunk = trunk_grad[0]
    zeros = jnp.zeros((1, block), jnp.bfloat16)
    later = jnp.concatenate([trunk[1:], zeros])
    earlier = jnp.concatenate([zeros, trunk[:-1]])
    shifts = jnp.concatenate([later, trunk, earlier], axis=1)
    to_beside, to_below, own_window = kernel_messages(place, line, trunk_grad, coarse)
    ready = (slope, shifts, line[1], line[planes - 1], *crossing)
    top, bottom = after(beside[:half], *ready), after(below[half:], *ready)
    far_top, far_bottom = from_peer(top, "seq", 2), from_peer(bottom, "seq", 1)

    scale = 0.5 * float(fine * seqs * reps) ** (-0.5)
    near_rows = [(d, 0, coarse, 0) for d in range(3)]
    far_rows = [(3, 0, half, 0), (3, half, half, 0)]
    early = early_terms(place, near_rows, [act, beside, below], shifts, coarse)
    line_across[2] = after(line_across[2], early)
    lines = stack_planes(place, line_across)
    far_top, far_bottom = after(far_top, early, lines), after(far_bottom, early, lines)

    to_beside, to_below = (
        after(message, far_top, far_bottom) for message in (to_beside, to_below)
    )
    kept_beside, kept_below = from_peer(to_beside, "seq", 1), from_peer(to_below, "seq", 2)
    other_column, other_lines = from_peer(to_below, "rep", 1), from_peer(lines, "rep", 1)

    mine, *theirs = late_terms(
        place, far_rows, [far_top, far_bottom], shifts, early, coarse, scale, planes, taps, rows
    )
    arrived = [from_peer(part, "rep", 1) for part in theirs]
    pairs = []
    for j in range(planes):
        part = arrived[j // (planes // 2)][j % (planes // 2)]
        pairs.append(mine[j] + part.astype(jnp.float32))
    weight_grad = pairs[0]
    leaving = [after(part.astype(jnp.bfloat16), other_column, other_lines) for part in pairs[1:]]
    summed = [from_peer(leaving[j - 1], "rep", 2 * j) for j in range(1, planes)]

    window = (coarse + 2 * HALO) // rows
    count, side = planes * SPLIT, window // 2
    far_first = after(kept_beside[: side + count // 2], *leaving)
    far_second = after(kept_below[count // 2 : count + side], *leaving)
    far_first, far_second = from_peer(far_first, "seq", 2), from_peer(far_second, "seq", 1)

    windows = [
        [(own_window, 0, 0, window)],
        [(kept_beside, side + count, 0, window)],
        [(kept_below, count + side, 0, window)],
    ]
    stage = functools.partial(gradient_stage, place, taps=taps, slope=slope, shape=inputs.shape)
    soon = [(to_below, 0, 0, planes, 0, 0), (other_column, 0, 0, planes, 1, 0)]
    for part, start, distance in ((kept_beside, side, 1), (kept_below, 0, 2)):
        soon.append((part, start, 0, planes, 0, distance))
        soon.append((from_peer(part, "rep", 1), start, 0, planes, 1, distance))
    crossed = [
        (part, None, 0, planes, flip, d)
        for flip, part in enumerate((lines, other_lines))
        for d in range(seqs)
    ]
    near = [piece for piece in crossed if piece[-1] < 3]
    begun = stage(windows, pieces=soon + near, distances=[0, 1, 2], begun=None)
    far_first, far_second = after(far_first, begun), after(far_second, begun)
    windows.append([(far_first, 0, 0, side), (far_second, count // 2, side, side)])
    rest = [piece for piece in crossed if piece[-1] == 3]
    for part, start, plane in ((far_first, side, 0), (far_second, 0, planes // 2)):
        rest.append((part, start, plane, planes // 2, 0, 3))
        rest.append((from_peer(part, "rep", 1), start, plane, planes // 2, 1, 3))
    input_grad = stage(windows, pieces=rest, distances=[3], begun=begun)
    for part in summed:
        weight_grad = weight_grad + after(part, input_grad).astype(jnp.float32)
    return (input_grad, weight_grad)

def with_halo(value, sides, width):
    for axis, dim in sides:
        peers, length = (lax.axis_size(axis), value.shape[dim])
        up = [(i, (i + 1) % peers) for i in range(peers - 1)]
        down = [(j, i) for i, j in up]
        last = lax.slice_in_dim(value, length - width, length, axis=dim)
        leading = lax.slice_in_dim(value, 0, width, axis=dim)
        before = lax.ppermute(last, axis, up)
        after = lax.ppermute(leading, axis, down)
        value = jnp.concatenate([before, value, after], axis=dim)
    return value

def contract_last(left, right):
    return lax.dot_general(
        left, right, (((1,), (1,)), ((), ())), preferred_element_type=jnp.float32
    )

def contract_first(left, right):
    return lax.dot_general(
        left, right, (((0,), (0,)), ((), ())), preferred_element_type=jnp.float32
    )

def on_device_plain(inputs, trunk_grad, weights):
    taps = weights.shape[0]
    grad = lax.all_to_all(trunk_grad, "seq", split_axis=1, concat_axis=2, tiled=True)
    grad_up = jnp.repeat(grad.astype(jnp.float32) * 0.5, 2, axis=1).astype(jnp.bfloat16)
    rows = grad_up.shape[1]
    padded = with_halo(grad_up, (("seq", 1),), 2)
    shifts = [padded[0, 4 - k : 4 - k + rows] for k in range(taps)]
    inputs_f = inputs[0].astype(jnp.float32)
    act_vals, back = jax.vjp(jax.nn.gelu, inputs_f)
    slope = back(jnp.ones_like(inputs_f))[0]
    act = act_vals.astype(jnp.bfloat16)
    in_width = inputs.shape[2]
    columns = lax.all_gather(weights, "seq", axis=2, tiled=True)
    piece = lax.all_gather(columns, "rep", axis=1, tiled=True)
    result = contract_last(shifts[0], piece[0])
    for project_k in range(1, taps):
        result = result + contract_last(shifts[project_k], piece[project_k])
    input_grad = (result * slope + grad_up[0, :, :in_width].astype(jnp.float32)).astype(
        jnp.bfloat16
    )
    scale_factor = float(rows * lax.axis_size("seq") * lax.axis_size("rep")) ** (-0.5)
    terms = jnp.stack([contract_first(act, shifts[k]) for k in range(taps)]) * scale_factor
    partial_sum = lax.psum_scatter(terms, "rep", scatter_dimension=1, tiled=True)
    weight_grad = lax.psum_scatter(partial_sum, "seq", scatter_dimension=2, tiled=True)
    return (input_grad[None], weight_grad)

def on_device(inputs, trunk_grad, weights):
    square = lax.axis_size("seq") == 4 and lax.axis_size("rep") % 8 == 0
    if square and weights.shape[2] % LANES == 0 and inputs.shape[2] % LANES == 0:
        return on_device_square(inputs, trunk_grad, weights)
    return on_device_plain(inputs, trunk_grad, weights)

def solution(mesh):
    in_specs = (P("rep", "seq", None), P("rep", None, "seq"), P(None, "rep", "seq"))
    out_specs = (P("rep", "seq", None), P(None, "rep", "seq"))
    return jax.shard_map(
        on_device, mesh=mesh, in_specs=in_specs, out_specs=out_specs, check_vma=False
    )
```

```python
import functools
import math

import jax
import jax.numpy as jnp
from jax import lax
from jax.experimental import pallas as pl
from jax.experimental.pallas import tpu as pltpu
from jax.sharding import PartitionSpec as P

LANES = 128
HALO = 32
EDGE = 16
MARGIN = HALO - EDGE
STEP = 64
SPLIT = 3
ROOT = math.sqrt(2.0 / math.pi)
CUBIC = 0.044715
SMALL = pl.CostEstimate(flops=1 << 20, bytes_accessed=1 << 16, transcendentals=0)
ANYWHERE = pl.BlockSpec(memory_space=pl.ANY)
ROW_OFFSETS = ((1, 1), (0, 1), (0, 0), (-1, 0), (-1, -1))
GRAD_PARTS = ((0, 0), (1, 0), (1, 1), (2, 1), (2, 2))

def from_peer(value, axis, distance):
    peers = lax.axis_size(axis)
    return lax.ppermute(value, axis, [(i, i ^ distance) for i in range(peers)])

def after(value, *earlier):
    return pl.pallas_call(
        lambda *refs: None,
        out_shape=jax.ShapeDtypeStruct(value.shape, value.dtype),
        in_specs=[ANYWHERE] * (1 + len(earlier)),
        out_specs=ANYWHERE,
        input_output_aliases={0: 0},
        name="after",
    )(value, *earlier)

def gather_line(value, axis, count, unit):
    found, mask = {0: value}, count - 1
    while mask:
        for distance in list(found):
            found[distance ^ mask] = from_peer(found[distance], axis, mask * unit)
        mask //= 2
    return [found[distance] for distance in range(count)]

def gelu_slope(x):
    tanh = jnp.tanh(ROOT * (x + CUBIC * (x * x * x)))
    return 0.5 * (1.0 + tanh) + 0.5 * x * (1.0 - tanh * tanh) * (
        ROOT * (1.0 + 3.0 * CUBIC * (x * x))
    )

def act_kernel(x_ref, out_ref, strip):
    width = x_ref.shape[2]

    @pl.loop(0, out_ref.shape[0] // STEP)
    def _(step):
        start = pl.multiple_of(step * STEP, STEP)
        x = x_ref[0, pl.ds(pl.multiple_of(2 * start, 2 * STEP), 2 * STEP), :].astype(jnp.float32)
        act = x * (0.5 * (1.0 + jnp.tanh(ROOT * (x + CUBIC * (x * x * x)))))
        for c in range(width // LANES):
            strip[c] = act[:, c * LANES : (c + 1) * LANES]
        for parity in range(2):
            for c in range(width // LANES):
                picked = strip[c, pl.ds(parity, STEP, stride=2), :].astype(jnp.bfloat16)
                left = parity * width + c * LANES
                out_ref[pl.ds(start, STEP), left : left + LANES] = picked

def activate(inputs):
    fine, width = inputs.shape[1:]
    return pl.pallas_call(
        act_kernel,
        out_shape=jax.ShapeDtypeStruct((fine // 2, 2 * width), jnp.bfloat16),
        in_specs=[pl.BlockSpec(memory_space=pltpu.VMEM)],
        out_specs=pl.BlockSpec(memory_space=pltpu.VMEM),
        scratch_shapes=[pltpu.VMEM((width // LANES, 2 * STEP, LANES), jnp.float32)],
        compiler_params=pltpu.CompilerParams(vmem_limit_bytes=24 << 20),
        cost_estimate=SMALL,
        name="act",
    )(inputs)

def kernel_messages(place, line, trunk_grad, coarse):
    taps, rows, block = line[0].shape
    planes, length = len(line), trunk_grad.shape[1]
    window = (coarse + 2 * HALO) // rows
    half = planes // 2

    def kernel(place, *refs):
        parts, trunk_ref = refs[:planes], refs[planes]
        beside_ref, below_ref, own_ref, edged, sem = refs[planes + 1 :]
        copy = pltpu.make_async_copy(trunk_ref.at[0], edged.at[pl.ds(HALO, length)], sem)
        copy.start()
        edged[:HALO] = jnp.zeros((HALO, block), jnp.bfloat16)
        edged[HALO + length :] = jnp.zeros((HALO, block), jnp.bfloat16)
        for j in range(planes):
            plane = place[1] // 2 ^ j
            for k in range(taps):
                spot = (plane // half * taps + k) * half + plane % half
                beside_ref[window // 2 + spot] = parts[j][k]
                below_ref[spot] = parts[j][k]
        copy.wait()

        def cut(out_ref, spot, distance, first, last):
            base = (place[0] ^ distance) * coarse
            for b in range(first, last):
                out_ref[spot + b - first] = edged[pl.ds(pl.multiple_of(base + b * rows, 16), rows), :]

        cut(beside_ref, 0, 3, 0, window // 2)
        cut(beside_ref, window // 2 + planes * taps, 1, 0, window)
        cut(below_ref, planes * taps, 3, window // 2, window)
        cut(below_ref, planes * taps + window // 2, 2, 0, window)
        cut(own_ref, 0, 0, 0, window)

    count = window // 2 + planes * taps + window
    return pl.pallas_call(
        kernel,
        out_shape=[
            jax.ShapeDtypeStruct((n, rows, block), jnp.bfloat16) for n in (count, count, window)
        ],
        grid_spec=pltpu.PrefetchScalarGridSpec(
            num_scalar_prefetch=1,
            grid=(1,),
            in_specs=[pl.BlockSpec(line[0].shape, lambda i, place: (0, 0, 0))] * planes + [ANYWHERE],
            out_specs=[
                pl.BlockSpec((n, rows, block), lambda i, place: (0, 0, 0))
                for n in (count, count, window)
            ],
            scratch_shapes=[
                pltpu.VMEM((length + 2 * HALO, block), jnp.bfloat16),
                pltpu.SemaphoreType.DMA,
            ],
        ),
        compiler_params=pltpu.CompilerParams(vmem_limit_bytes=32 << 20),
        cost_estimate=SMALL,
        name="kernel_messages",
    )(place, *line, trunk_grad)

def slope_kernel(x_ref, out_ref, scratch):
    width = x_ref.shape[2]

    @pl.loop(0, out_ref.shape[1] // 64)
    def _(step):
        start = pl.multiple_of(step * 64, 64)
        span = pl.ds(pl.multiple_of(2 * start, 128), 128)
        for c in range(width // LANES):
            lanes = slice(c * LANES, (c + 1) * LANES)
            scratch[c] = 0.5 * gelu_slope(x_ref[0, span, lanes].astype(jnp.float32))
            for parity in range(2):
                out_ref[parity, pl.ds(start, 64), lanes] = scratch[c, pl.ds(parity, 64, stride=2), :]

def half_slope(inputs):
    fine, width = inputs.shape[1:]
    return pl.pallas_call(
        slope_kernel,
        out_shape=jax.ShapeDtypeStruct((2, fine // 2, width), jnp.float32),
        in_specs=[pl.BlockSpec(memory_space=pltpu.VMEM)],
        out_specs=pl.BlockSpec(memory_space=pltpu.VMEM),
        scratch_shapes=[pltpu.VMEM((width // LANES, 128, LANES), jnp.float32)],
        compiler_params=pltpu.CompilerParams(vmem_limit_bytes=24 << 20),
        name="half_slope",
    )(inputs)

def start_act(place, coarse, layout, pieces, shifts_ref, held, shifts, sems, shift_sems):
    copies, row = [], 0
    for i, (distance, first, size, offset) in enumerate(layout):
        start = pl.multiple_of((place[0] ^ distance) * coarse + first, 16)
        spot = pl.ds(row, size)
        source = pieces[i].at[pl.ds(offset, size)]
        copies.append(pltpu.make_async_copy(source, held.at[spot], sems.at[i]))
        copies.append(
            pltpu.make_async_copy(shifts_ref.at[pl.ds(start, size)], shifts.at[spot], shift_sems.at[i])
        )
        row += size
    for copy in copies:
        copy.start()
    return copies

def early_terms(place, layout, pieces, shifts, coarse):
    both, columns = pieces[0].shape[1], shifts.shape[1]
    rows = sum(size for _, _, size, _ in layout)
    tile = 256

    def kernel(place, shifts_ref, *refs):
        pieces, total = refs[: len(layout)], refs[len(layout)]
        held, shifts, sems, shift_sems = refs[len(layout) + 1 :]
        copies = start_act(
            place, coarse, layout, pieces, shifts_ref, held, shifts, sems, shift_sems
        )
        for copy in copies:
            copy.wait()

        @pl.loop(0, both // tile)
        def _(i):
            span = pl.ds(pl.multiple_of(i * tile, tile), tile)
            total[span, :] = lax.dot_general(
                held[:, span], shifts[...], (((0,), (0,)), ((), ())), preferred_element_type=jnp.float32
            )

    return pl.pallas_call(
        kernel,
        out_shape=jax.ShapeDtypeStruct((both, columns), jnp.float32),
        grid_spec=pltpu.PrefetchScalarGridSpec(
            num_scalar_prefetch=1,
            grid=(1,),
            in_specs=[ANYWHERE] * (1 + len(pieces)),
            out_specs=pl.BlockSpec((both, columns), lambda i, place: (0, 0)),
            scratch_shapes=[
                pltpu.VMEM((rows, both), jnp.bfloat16),
                pltpu.VMEM((rows, columns), jnp.bfloat16),
                pltpu.SemaphoreType.DMA((len(pieces),)),
                pltpu.SemaphoreType.DMA((len(pieces),)),
            ],
        ),
        compiler_params=pltpu.CompilerParams(vmem_limit_bytes=48 << 20),
        cost_estimate=SMALL,
        name="weight_grad_early",
    )(place, shifts, *pieces)

def late_terms(place, layout, pieces, shifts, early, coarse, scale, planes, taps, rows):
    both, columns = early.shape
    width, block = both // 2, columns // 3
    count = sum(size for _, _, size, _ in layout)
    tile = 256
    shape = (planes, taps, rows, block)

    def kernel(place, shifts_ref, early_ref, *refs):
        pieces, (mine_ref, *theirs_refs) = refs[: len(layout)], refs[len(layout) : len(layout) + 3]
        held, shifts, total, sems, shift_sems, early_sems = refs[len(layout) + 3 :]
        core, plane = place[1] % 2, place[1] // 2
        copies = start_act(
            place, coarse, layout, pieces, shifts_ref, held, shifts, sems, shift_sems
        )

        def fetch(i):
            span = pl.ds(pl.multiple_of(i * tile, tile), tile)
            return pltpu.make_async_copy(early_ref.at[span], total.at[span], early_sems.at[i])

        for i in range(both // tile):
            fetch(i).start()
        for copy in copies:
            copy.wait()

        @pl.loop(0, both // tile)
        def _(i):
            span = pl.ds(pl.multiple_of(i * tile, tile), tile)
            term = lax.dot_general(
                held[:, span], shifts[...], (((0,), (0,)), ((), ())), preferred_element_type=jnp.float32
            )
            fetch(i).wait()
            total[span, :] += term

        def finish(out_ref, at, j, parity, kind):
            start = ((plane ^ j) * 2 + parity) * rows
            even = pl.ds(pl.multiple_of(start, 16), rows)
            odd = pl.ds(pl.multiple_of(width + start, 16), rows)
            for k, (left, right) in enumerate(GRAD_PARTS):
                term = total[even, left * block : (left + 1) * block]
                term += total[odd, right * block : (right + 1) * block]
                out_ref[at, k] = (scale * term).astype(kind)

        for which, out_ref in enumerate(theirs_refs):

            @pl.loop(0, planes // 2)
            def _(at):
                finish(out_ref, at, at + which * (planes // 2), 1 - core, jnp.bfloat16)

        @pl.loop(0, planes)
        def _(j):
            finish(mine_ref, j, j, core, jnp.float32)

    half_shape = (planes // 2, *shape[1:])
    whole = pl.BlockSpec(shape, lambda i, place: (0, 0, 0, 0))
    half = pl.BlockSpec(half_shape, lambda i, place: (0, 0, 0, 0))
    return pl.pallas_call(
        kernel,
        out_shape=(
            jax.ShapeDtypeStruct(shape, jnp.float32),
            jax.ShapeDtypeStruct(half_shape, jnp.bfloat16),
            jax.ShapeDtypeStruct(half_shape, jnp.bfloat16),
        ),
        grid_spec=pltpu.PrefetchScalarGridSpec(
            num_scalar_prefetch=1,
            grid=(1,),
            in_specs=[ANYWHERE] * (2 + len(pieces)),
            out_specs=[whole, half, half],
            scratch_shapes=[
                pltpu.VMEM((count, both), jnp.bfloat16),
                pltpu.VMEM((count, columns), jnp.bfloat16),
                pltpu.VMEM((both, columns), jnp.float32),
                pltpu.SemaphoreType.DMA((len(pieces),)),
                pltpu.SemaphoreType.DMA((len(pieces),)),
                pltpu.SemaphoreType.DMA((both // tile,)),
            ],
        ),
        compiler_params=pltpu.CompilerParams(vmem_limit_bytes=48 << 20),
        cost_estimate=SMALL,
        name="weight_grad_late",
    )(place, shifts, early, *pieces)

def shifted_total(products, base, lanes, parity):
    total = None
    for by in (0, 1, -1):
        wanted = [k for k in range(products.shape[0]) if ROW_OFFSETS[k][parity] == by]
        if wanted:
            near = pl.ds(base + MARGIN - 8, STEP + 16)
            part = sum(products[k, near, lanes] for k in wanted)[8 + by : 8 + by + STEP]
            total = part if total is None else total + part
    return total

def gradient_stage(place, windows, taps, pieces, distances, slope, begun, shape):
    _, fine, width = shape
    coarse, seqs = fine // 2, lax.axis_size("seq")
    rows, block = pieces[0][0].shape[-2:]
    planes = width // (2 * rows)
    half = planes // 2
    window, used = coarse + 2 * HALO, coarse + 2 * MARGIN
    depth, planar = len(distances) * block, (2, coarse, width)
    last = begun is not None
    needed = list(range(seqs)) if last else distances
    parts = [(d, *part) for d in needed for part in windows[d]]
    operands = [part[1] for part in parts] + [piece[0] for piece in pieces]
    operands += [slope, begun] if last else []

    def body(place, *refs):
        own, refs = refs[: len(parts)], refs[len(parts) :]
        sources, refs = refs[: len(pieces)], refs[len(pieces) :]
        if last:
            (slope_ref, begun_ref), refs = refs[:2], refs[2:]
        out_ref, wv, gv, products, sems, grad_sems = refs[:6]
        me, core = place[0], place[1] % 2

        def kernel_copies(first):
            for number, (array, start, plane, count, flip, distance) in enumerate(pieces):
                spot = pl.ds(distances.index(distance) * block, block)
                if first != (start is not None):
                    continue
                for k in range(SPLIT if first else taps - SPLIT):
                    for h in range(count // half):
                        span = pl.ds(plane + h * half, half)
                        if first:
                            source = sources[number].at[pl.ds(start + (h * SPLIT + k) * half, half)]
                        else:
                            source = sources[number].at[span, distance, k]
                        tap = k if first else SPLIT + k
                        target = wv.at[tap, span, core ^ flip, :, spot]
                        sem = sems.at[tap, number, h]
                        yield tap, pltpu.make_async_copy(source, target, sem)

        def window_copies(target_of, sems):
            for number, (distance, _, start, first, count) in enumerate(parts):
                for b in range(count):
                    target = target_of(distance, pl.ds((first + b) * rows, rows))
                    if target is not None:
                        source = own[number].at[start + b]
                        yield pltpu.make_async_copy(source, target, sems.at[number, b])

        def into_window(distance, span):
            if distance not in distances:
                return None
            return gv.at[span, pl.ds(distances.index(distance) * block, block)]

        early = list(window_copies(into_window, grad_sems))
        late = []
        if last:
            sums, slopes, strip, skips, sum_sems, skip_sems = refs[6:]
            late.append(pltpu.make_async_copy(begun_ref, sums, sum_sems.at[0]))
            late.append(pltpu.make_async_copy(slope_ref, slopes, sum_sems.at[1]))
            late += window_copies(lambda d, span: skips.at[me ^ d, span], skip_sems)
        for copy in early:
            copy.start()
        arriving = sorted([*kernel_copies(True), *kernel_copies(False)], key=lambda pair: pair[0])
        for _, copy in arriving:
            copy.start()
        for copy in late:
            copy.start()
        for copy in early:
            copy.wait()
        for k in range(taps):
            for tap, copy in arriving:
                if tap == k:
                    copy.wait()
            for part in range(2):
                kernel = wv[k, part * half : (part + 1) * half].reshape(2 * half * rows, depth)
                lanes = slice(part * 2 * half * rows, (part + 1) * 2 * half * rows)
                products[k, :, lanes] = lax.dot_general(
                    gv[EDGE : EDGE + used],
                    kernel,
                    (((1,), (1,)), ((), ())),
                    preferred_element_type=jnp.float32,
                )

        for copy in late:
            copy.wait()

        @pl.loop(0, coarse // STEP)
        def _(i):
            base = pl.multiple_of(i * STEP, STEP)
            spot, span = pl.ds(base, STEP), pl.ds(pl.multiple_of(2 * base, 2 * STEP), 2 * STEP)
            for c in range(width // LANES):
                lanes = slice(c * LANES, (c + 1) * LANES)
                if last:
                    left = c * LANES % block
                    skip = skips[c * LANES // block, pl.ds(base + HALO, STEP), left : left + LANES]
                    skip = 0.5 * skip.astype(jnp.float32)
                for parity in range(2):
                    total = shifted_total(products, base, lanes, parity)
                    if last:
                        total = (total + sums[parity, spot, lanes]) * slopes[parity, spot, lanes]
                        strip[c, pl.ds(parity, STEP, stride=2), :] = total + skip
                    else:
                        out_ref[parity, spot, lanes] = total
                if last:
                    out_ref[0, span, lanes] = strip[c].astype(jnp.bfloat16)

    out_shape = jax.ShapeDtypeStruct(shape if last else planar, jnp.bfloat16 if last else jnp.float32)
    scratch = [
        pltpu.VMEM((taps, planes, 2, rows, depth), jnp.bfloat16),
        pltpu.VMEM((window, depth), jnp.bfloat16),
        pltpu.VMEM((taps, used, width), jnp.float32),
        pltpu.SemaphoreType.DMA((taps, len(pieces), 2)),
        pltpu.SemaphoreType.DMA((len(parts), window // rows)),
    ]
    if last:
        scratch += [
            pltpu.VMEM(planar, jnp.float32),
            pltpu.VMEM(planar, jnp.float32),
            pltpu.VMEM((width // LANES, 2 * STEP, LANES), jnp.float32),
            pltpu.VMEM((seqs, window, block), jnp.bfloat16),
            pltpu.SemaphoreType.DMA((2,)),
            pltpu.SemaphoreType.DMA((len(parts), window // rows)),
        ]
    return pl.pallas_call(
        body,
        out_shape=out_shape,
        grid_spec=pltpu.PrefetchScalarGridSpec(
            num_scalar_prefetch=1,
            grid=(1,),
            in_specs=[ANYWHERE] * len(operands),
            out_specs=pl.BlockSpec(out_shape.shape, lambda i, place: (0, 0, 0)),
            scratch_shapes=scratch,
        ),
        compiler_params=pltpu.CompilerParams(vmem_limit_bytes=56 << 20),
        cost_estimate=SMALL,
        name="input_grad",
    )(place, *operands)

def stack_planes(place, line):
    count = len(line)

    def kernel(place, *refs):
        parts, out_ref = refs[:count], refs[count]
        for j in range(count):
            out_ref[place[1] // 2 ^ j] = parts[j][...]

    shape = line[0].shape
    return pl.pallas_call(
        kernel,
        out_shape=jax.ShapeDtypeStruct((count, *shape), line[0].dtype),
        grid_spec=pltpu.PrefetchScalarGridSpec(
            num_scalar_prefetch=1,
            grid=(1,),
            in_specs=[pl.BlockSpec(shape, lambda i, place: (0,) * len(shape))] * count,
            out_specs=pl.BlockSpec((count, *shape), lambda i, place: (0,) * (1 + len(shape))),
        ),
        compiler_params=pltpu.CompilerParams(vmem_limit_bytes=24 << 20),
        cost_estimate=SMALL,
        name="stack_planes",
    )(place, *line)

def on_device_square(inputs, trunk_grad, weights):
    seqs, reps = lax.axis_size("seq"), lax.axis_size("rep")
    me, rep = lax.axis_index("seq"), lax.axis_index("rep")
    place = jnp.stack([me, rep]).astype(jnp.int32)
    taps, rows, block = weights.shape
    fine = inputs.shape[1]
    coarse, planes = fine // 2, reps // 2
    half = coarse // 2

    last_taps = weights[SPLIT:]
    across = [last_taps] + [from_peer(last_taps, "seq", d) for d in range(1, seqs)]

    act = after(activate(inputs), *across[1:])
    beside, below = from_peer(act, "seq", 1), from_peer(act, "seq", 2)
    slope = half_slope(inputs)
    line = gather_line(weights[:SPLIT], "rep", planes, 2)
    line_across = gather_line(after(jnp.stack(across), act, *line[1:]), "rep", planes, 2)
    crossing = (line_across[1], line_across[planes - 1])
    trunk = trunk_grad[0]
    zeros = jnp.zeros((1, block), jnp.bfloat16)
    later = jnp.concatenate([trunk[1:], zeros])
    earlier = jnp.concatenate([zeros, trunk[:-1]])
    shifts = jnp.concatenate([later, trunk, earlier], axis=1)
    to_beside, to_below, own_window = kernel_messages(place, line, trunk_grad, coarse)
    ready = (slope, shifts, to_beside, *crossing)
    top, bottom = after(beside[:half], *ready), after(below[half:], *ready)
    far_top, far_bottom = from_peer(top, "seq", 2), from_peer(bottom, "seq", 1)

    scale = 0.5 * float(fine * seqs * reps) ** (-0.5)
    near_rows = [(d, 0, coarse, 0) for d in range(3)]
    far_rows = [(3, 0, half, 0), (3, half, half, 0)]
    early = early_terms(place, near_rows, [act, beside, below], shifts, coarse)
    line_across[2] = after(line_across[2], early)
    lines = stack_planes(place, line_across)
    far_top, far_bottom = after(far_top, early, lines), after(far_bottom, early, lines)

    to_beside, to_below = (
        after(message, far_top, far_bottom) for message in (to_beside, to_below)
    )
    kept_beside, kept_below = from_peer(to_beside, "seq", 1), from_peer(to_below, "seq", 2)
    other_column, other_lines = from_peer(to_below, "rep", 1), from_peer(lines, "rep", 1)

    mine, *theirs = late_terms(
        place, far_rows, [far_top, far_bottom], shifts, early, coarse, scale, planes, taps, rows
    )
    arrived = [from_peer(part, "rep", 1) for part in theirs]
    pairs = []
    for j in range(planes):
        part = arrived[j // (planes // 2)][j % (planes // 2)]
        pairs.append(mine[j] + part.astype(jnp.float32))
    weight_grad = pairs[0]
    leaving = [after(part.astype(jnp.bfloat16), other_column, other_lines) for part in pairs[1:]]
    summed = [from_peer(leaving[j - 1], "rep", 2 * j) for j in range(1, planes)]

    window = (coarse + 2 * HALO) // rows
    count, side = planes * SPLIT, window // 2
    far_first = after(kept_beside[: side + count // 2], *leaving)
    far_second = after(kept_below[count // 2 : count + side], *leaving)
    far_first, far_second = from_peer(far_first, "seq", 2), from_peer(far_second, "seq", 1)

    windows = [
        [(own_window, 0, 0, window)],
        [(kept_beside, side + count, 0, window)],
        [(kept_below, count + side, 0, window)],
    ]
    stage = functools.partial(gradient_stage, place, taps=taps, slope=slope, shape=inputs.shape)
    soon = [(to_below, 0, 0, planes, 0, 0), (other_column, 0, 0, planes, 1, 0)]
    for part, start, distance in ((kept_beside, side, 1), (kept_below, 0, 2)):
        soon.append((part, start, 0, planes, 0, distance))
        soon.append((from_peer(part, "rep", 1), start, 0, planes, 1, distance))
    crossed = [
        (part, None, 0, planes, flip, d)
        for flip, part in enumerate((lines, other_lines))
        for d in range(seqs)
    ]
    near = [piece for piece in crossed if piece[-1] < 3]
    begun = stage(windows, pieces=soon + near, distances=[0, 1, 2], begun=None)
    far_first, far_second = after(far_first, begun, *summed), after(far_second, begun, *summed)
    windows.append([(far_first, 0, 0, side), (far_second, count // 2, side, side)])
    rest = [piece for piece in crossed if piece[-1] == 3]
    for part, start, plane in ((far_first, side, 0), (far_second, 0, planes // 2)):
        rest.append((part, start, plane, planes // 2, 0, 3))
        rest.append((from_peer(part, "rep", 1), start, plane, planes // 2, 1, 3))
    input_grad = stage(windows, pieces=rest, distances=[3], begun=begun)
    for part in summed:
        weight_grad = weight_grad + after(part, input_grad).astype(jnp.float32)
    return (input_grad, weight_grad)

def with_halo(value, sides, width):
    for axis, dim in sides:
        peers, length = (lax.axis_size(axis), value.shape[dim])
        up = [(i, (i + 1) % peers) for i in range(peers - 1)]
        down = [(j, i) for i, j in up]
        last = lax.slice_in_dim(value, length - width, length, axis=dim)
        leading = lax.slice_in_dim(value, 0, width, axis=dim)
        before = lax.ppermute(last, axis, up)
        after = lax.ppermute(leading, axis, down)
        value = jnp.concatenate([before, value, after], axis=dim)
    return value

def contract_last(left, right):
    return lax.dot_general(
        left, right, (((1,), (1,)), ((), ())), preferred_element_type=jnp.float32
    )

def contract_first(left, right):
    return lax.dot_general(
        left, right, (((0,), (0,)), ((), ())), preferred_element_type=jnp.float32
    )

def on_device_plain(inputs, trunk_grad, weights):
    taps = weights.shape[0]
    grad = lax.all_to_all(trunk_grad, "seq", split_axis=1, concat_axis=2, tiled=True)
    grad_up = jnp.repeat(grad.astype(jnp.float32) * 0.5, 2, axis=1).astype(jnp.bfloat16)
    rows = grad_up.shape[1]
    padded = with_halo(grad_up, (("seq", 1),), 2)
    shifts = [padded[0, 4 - k : 4 - k + rows] for k in range(taps)]
    inputs_f = inputs[0].astype(jnp.float32)
    act_vals, back = jax.vjp(jax.nn.gelu, inputs_f)
    slope = back(jnp.ones_like(inputs_f))[0]
    act = act_vals.astype(jnp.bfloat16)
    in_width = inputs.shape[2]
    columns = lax.all_gather(weights, "seq", axis=2, tiled=True)
    piece = lax.all_gather(columns, "rep", axis=1, tiled=True)
    result = contract_last(shifts[0], piece[0])
    for project_k in range(1, taps):
        result = result + contract_last(shifts[project_k], piece[project_k])
    input_grad = (result * slope + grad_up[0, :, :in_width].astype(jnp.float32)).astype(
        jnp.bfloat16
    )
    scale_factor = float(rows * lax.axis_size("seq") * lax.axis_size("rep")) ** (-0.5)
    terms = jnp.stack([contract_first(act, shifts[k]) for k in range(taps)]) * scale_factor
    partial_sum = lax.psum_scatter(terms, "rep", scatter_dimension=1, tiled=True)
    weight_grad = lax.psum_scatter(partial_sum, "seq", scatter_dimension=2, tiled=True)
    return (input_grad[None], weight_grad)

def on_device(inputs, trunk_grad, weights):
    square = lax.axis_size("seq") == 4 and lax.axis_size("rep") % 8 == 0
    if square and weights.shape[2] % LANES == 0 and inputs.shape[2] % LANES == 0:
        return on_device_square(inputs, trunk_grad, weights)
    return on_device_plain(inputs, trunk_grad, weights)

def solution(mesh):
    in_specs = (P("rep", "seq", None), P("rep", None, "seq"), P(None, "rep", "seq"))
    out_specs = (P("rep", "seq", None), P(None, "rep", "seq"))
    return jax.shard_map(
        on_device, mesh=mesh, in_specs=in_specs, out_specs=out_specs, check_vma=False
    )
```

```python
import functools
import math

import jax
import jax.numpy as jnp
from jax import lax
from jax.experimental import pallas as pl
from jax.experimental.pallas import tpu as pltpu
from jax.sharding import PartitionSpec as P

LANES = 128
HALO = 32
EDGE = 16
MARGIN = HALO - EDGE
STEP = 64
SPLIT = 3
ROOT = math.sqrt(2.0 / math.pi)
CUBIC = 0.044715
SMALL = pl.CostEstimate(flops=1 << 20, bytes_accessed=1 << 16, transcendentals=0)
ANYWHERE = pl.BlockSpec(memory_space=pl.ANY)
ROW_OFFSETS = ((1, 1), (0, 1), (0, 0), (-1, 0), (-1, -1))
GRAD_PARTS = ((0, 0), (1, 0), (1, 1), (2, 1), (2, 2))

def from_peer(value, axis, distance):
    peers = lax.axis_size(axis)
    return lax.ppermute(value, axis, [(i, i ^ distance) for i in range(peers)])

def after(value, *earlier):
    return pl.pallas_call(
        lambda *refs: None,
        out_shape=jax.ShapeDtypeStruct(value.shape, value.dtype),
        in_specs=[ANYWHERE] * (1 + len(earlier)),
        out_specs=ANYWHERE,
        input_output_aliases={0: 0},
        name="after",
    )(value, *earlier)

def reduce_line(blocks, axis, count, unit):
    held, masks = [[0]], []
    while count > 1:
        masks.append(count - 1)
        held.append(held[-1] + [d ^ masks[-1] for d in held[-1]])
        count //= 2
    blocks, steps = dict(enumerate(blocks)), []
    for mask, keep in reversed(list(zip(masks, held))):
        leaving = jnp.stack([blocks[d ^ mask].astype(jnp.bfloat16) for d in keep])
        steps.append(from_peer(leaving, axis, mask * unit))
        blocks = {d: blocks[d] + steps[-1][n].astype(jnp.float32) for n, d in enumerate(keep)}
    return blocks[0], steps


def gather_line(value, axis, count, unit):
    found, mask = {0: value}, count - 1
    while mask:
        for distance in list(found):
            found[distance ^ mask] = from_peer(found[distance], axis, mask * unit)
        mask //= 2
    return [found[distance] for distance in range(count)]

def gelu_slope(x):
    tanh = jnp.tanh(ROOT * (x + CUBIC * (x * x * x)))
    return 0.5 * (1.0 + tanh) + 0.5 * x * (1.0 - tanh * tanh) * (
        ROOT * (1.0 + 3.0 * CUBIC * (x * x))
    )

def act_kernel(x_ref, out_ref, strip):
    width = x_ref.shape[2]

    @pl.loop(0, out_ref.shape[0] // STEP)
    def _(step):
        start = pl.multiple_of(step * STEP, STEP)
        x = x_ref[0, pl.ds(pl.multiple_of(2 * start, 2 * STEP), 2 * STEP), :].astype(jnp.float32)
        act = x * (0.5 * (1.0 + jnp.tanh(ROOT * (x + CUBIC * (x * x * x)))))
        for c in range(width // LANES):
            strip[c] = act[:, c * LANES : (c + 1) * LANES]
        for parity in range(2):
            for c in range(width // LANES):
                picked = strip[c, pl.ds(parity, STEP, stride=2), :].astype(jnp.bfloat16)
                left = parity * width + c * LANES
                out_ref[pl.ds(start, STEP), left : left + LANES] = picked

def activate(inputs):
    fine, width = inputs.shape[1:]
    return pl.pallas_call(
        act_kernel,
        out_shape=jax.ShapeDtypeStruct((fine // 2, 2 * width), jnp.bfloat16),
        in_specs=[pl.BlockSpec(memory_space=pltpu.VMEM)],
        out_specs=pl.BlockSpec(memory_space=pltpu.VMEM),
        scratch_shapes=[pltpu.VMEM((width // LANES, 2 * STEP, LANES), jnp.float32)],
        compiler_params=pltpu.CompilerParams(vmem_limit_bytes=24 << 20),
        cost_estimate=SMALL,
        name="act",
    )(inputs)

def kernel_messages(place, line, trunk_grad, coarse):
    taps, rows, block = line[0].shape
    planes, length = len(line), trunk_grad.shape[1]
    window = (coarse + 2 * HALO) // rows
    half = planes // 2

    def kernel(place, *refs):
        parts, trunk_ref = refs[:planes], refs[planes]
        beside_first, beside_second, below_first, below_second, own_ref, edged, sem = refs[planes + 1 :]
        copy = pltpu.make_async_copy(trunk_ref.at[0], edged.at[pl.ds(HALO, length)], sem)
        copy.start()
        edged[:HALO] = jnp.zeros((HALO, block), jnp.bfloat16)
        edged[HALO + length :] = jnp.zeros((HALO, block), jnp.bfloat16)
        for j in range(planes):
            plane = place[1] // 2 ^ j
            which = plane // half
            for k in range(taps):
                spot = k * half + plane % half
                own_ref[which * taps * half + spot] = parts[j][k]

                @pl.when(which == 0)
                def _():
                    beside_first[window // 2 + spot] = parts[j][k]
                    below_second[spot] = parts[j][k]

                @pl.when(which == 1)
                def _():
                    beside_second[spot] = parts[j][k]
                    below_first[spot] = parts[j][k]

        copy.wait()

        def cut(out_ref, spot, distance, first, last):
            base = (place[0] ^ distance) * coarse
            for b in range(first, last):
                out_ref[spot + b - first] = edged[pl.ds(pl.multiple_of(base + b * rows, 16), rows), :]

        cut(beside_first, 0, 3, 0, window // 2)
        cut(beside_second, half * taps, 1, 0, window)
        cut(below_first, half * taps, 3, window // 2, window)
        cut(below_second, half * taps, 2, 0, window)
        cut(own_ref, planes * taps, 0, 0, window)

    first, second = half * taps + window // 2, half * taps + window
    counts = (first, second, first, second, planes * taps + window)
    return pl.pallas_call(
        kernel,
        out_shape=[
            jax.ShapeDtypeStruct((n, rows, block), jnp.bfloat16) for n in counts
        ],
        grid_spec=pltpu.PrefetchScalarGridSpec(
            num_scalar_prefetch=1,
            grid=(1,),
            in_specs=[pl.BlockSpec(line[0].shape, lambda i, place: (0, 0, 0))] * planes + [ANYWHERE],
            out_specs=[
                pl.BlockSpec((n, rows, block), lambda i, place: (0, 0, 0))
                for n in counts
            ],
            scratch_shapes=[
                pltpu.VMEM((length + 2 * HALO, block), jnp.bfloat16),
                pltpu.SemaphoreType.DMA,
            ],
        ),
        compiler_params=pltpu.CompilerParams(vmem_limit_bytes=32 << 20),
        cost_estimate=SMALL,
        name="kernel_messages",
    )(place, *line, trunk_grad)

def slope_kernel(x_ref, out_ref, scratch):
    width = x_ref.shape[2]

    @pl.loop(0, out_ref.shape[1] // 64)
    def _(step):
        start = pl.multiple_of(step * 64, 64)
        span = pl.ds(pl.multiple_of(2 * start, 128), 128)
        for c in range(width // LANES):
            lanes = slice(c * LANES, (c + 1) * LANES)
            scratch[c] = 0.5 * gelu_slope(x_ref[0, span, lanes].astype(jnp.float32))
            for parity in range(2):
                out_ref[parity, pl.ds(start, 64), lanes] = scratch[c, pl.ds(parity, 64, stride=2), :]

def half_slope(inputs):
    fine, width = inputs.shape[1:]
    return pl.pallas_call(
        slope_kernel,
        out_shape=jax.ShapeDtypeStruct((2, fine // 2, width), jnp.float32),
        in_specs=[pl.BlockSpec(memory_space=pltpu.VMEM)],
        out_specs=pl.BlockSpec(memory_space=pltpu.VMEM),
        scratch_shapes=[pltpu.VMEM((width // LANES, 128, LANES), jnp.float32)],
        compiler_params=pltpu.CompilerParams(vmem_limit_bytes=24 << 20),
        name="half_slope",
    )(inputs)

def start_act(place, coarse, layout, pieces, shifts_ref, held, shifts, sems, shift_sems):
    copies, row = [], 0
    for i, (distance, first, size, offset) in enumerate(layout):
        start = pl.multiple_of((place[0] ^ distance) * coarse + first, 16)
        spot = pl.ds(row, size)
        source = pieces[i].at[pl.ds(offset, size)]
        copies.append(pltpu.make_async_copy(source, held.at[spot], sems.at[i]))
        copies.append(
            pltpu.make_async_copy(shifts_ref.at[pl.ds(start, size)], shifts.at[spot], shift_sems.at[i])
        )
        row += size
    for copy in copies:
        copy.start()
    return copies

def early_terms(place, layout, pieces, shifts, coarse):
    both, columns = pieces[0].shape[1], shifts.shape[1]
    rows = sum(size for _, _, size, _ in layout)
    tile = 256

    def kernel(place, shifts_ref, *refs):
        pieces, total = refs[: len(layout)], refs[len(layout)]
        held, shifts, sems, shift_sems = refs[len(layout) + 1 :]
        copies = start_act(
            place, coarse, layout, pieces, shifts_ref, held, shifts, sems, shift_sems
        )
        for copy in copies:
            copy.wait()

        @pl.loop(0, both // tile)
        def _(i):
            span = pl.ds(pl.multiple_of(i * tile, tile), tile)
            total[span, :] = lax.dot_general(
                held[:, span], shifts[...], (((0,), (0,)), ((), ())), preferred_element_type=jnp.float32
            )

    return pl.pallas_call(
        kernel,
        out_shape=jax.ShapeDtypeStruct((both, columns), jnp.float32),
        grid_spec=pltpu.PrefetchScalarGridSpec(
            num_scalar_prefetch=1,
            grid=(1,),
            in_specs=[ANYWHERE] * (1 + len(pieces)),
            out_specs=pl.BlockSpec((both, columns), lambda i, place: (0, 0)),
            scratch_shapes=[
                pltpu.VMEM((rows, both), jnp.bfloat16),
                pltpu.VMEM((rows, columns), jnp.bfloat16),
                pltpu.SemaphoreType.DMA((len(pieces),)),
                pltpu.SemaphoreType.DMA((len(pieces),)),
            ],
        ),
        compiler_params=pltpu.CompilerParams(vmem_limit_bytes=48 << 20),
        cost_estimate=SMALL,
        name="weight_grad_early",
    )(place, shifts, *pieces)

def late_terms(place, layout, pieces, shifts, early, coarse, scale, planes, taps, rows):
    both, columns = early.shape
    width, block = both // 2, columns // 3
    count = sum(size for _, _, size, _ in layout)
    tile = 256
    shape = (planes, taps, rows, block)

    def kernel(place, shifts_ref, early_ref, *refs):
        pieces, (mine_ref, theirs_ref) = refs[: len(layout)], refs[len(layout) : len(layout) + 2]
        held, shifts, total, sems, shift_sems, early_sems = refs[len(layout) + 2 :]
        core, plane = place[1] % 2, place[1] // 2
        copies = start_act(
            place, coarse, layout, pieces, shifts_ref, held, shifts, sems, shift_sems
        )

        def fetch(i):
            span = pl.ds(pl.multiple_of(i * tile, tile), tile)
            return pltpu.make_async_copy(early_ref.at[span], total.at[span], early_sems.at[i])

        for i in range(both // tile):
            fetch(i).start()
        for copy in copies:
            copy.wait()

        @pl.loop(0, both // tile)
        def _(i):
            span = pl.ds(pl.multiple_of(i * tile, tile), tile)
            term = lax.dot_general(
                held[:, span], shifts[...], (((0,), (0,)), ((), ())), preferred_element_type=jnp.float32
            )
            fetch(i).wait()
            total[span, :] += term

        for out_ref, parity, kind in (
            (theirs_ref, 1 - core, jnp.bfloat16),
            (mine_ref, core, jnp.float32),
        ):

            @pl.loop(0, planes)
            def _(j):
                start = ((plane ^ j) * 2 + parity) * rows
                even = pl.ds(pl.multiple_of(start, 16), rows)
                odd = pl.ds(pl.multiple_of(width + start, 16), rows)
                for k, (left, right) in enumerate(GRAD_PARTS):
                    term = total[even, left * block : (left + 1) * block]
                    term += total[odd, right * block : (right + 1) * block]
                    out_ref[j, k] = (scale * term).astype(kind)

    whole = pl.BlockSpec(shape, lambda i, place: (0, 0, 0, 0))
    return pl.pallas_call(
        kernel,
        out_shape=(
            jax.ShapeDtypeStruct(shape, jnp.float32),
            jax.ShapeDtypeStruct(shape, jnp.bfloat16),
        ),
        grid_spec=pltpu.PrefetchScalarGridSpec(
            num_scalar_prefetch=1,
            grid=(1,),
            in_specs=[ANYWHERE] * (2 + len(pieces)),
            out_specs=[whole, whole],
            scratch_shapes=[
                pltpu.VMEM((count, both), jnp.bfloat16),
                pltpu.VMEM((count, columns), jnp.bfloat16),
                pltpu.VMEM((both, columns), jnp.float32),
                pltpu.SemaphoreType.DMA((len(pieces),)),
                pltpu.SemaphoreType.DMA((len(pieces),)),
                pltpu.SemaphoreType.DMA((both // tile,)),
            ],
        ),
        compiler_params=pltpu.CompilerParams(vmem_limit_bytes=48 << 20),
        cost_estimate=SMALL,
        name="weight_grad_late",
    )(place, shifts, early, *pieces)

def shifted_total(products, base, lanes, parity):
    total = None
    for by in (0, 1, -1):
        wanted = [k for k in range(products.shape[0]) if ROW_OFFSETS[k][parity] == by]
        if wanted:
            near = pl.ds(base + MARGIN - 8, STEP + 16)
            part = sum(products[k, near, lanes] for k in wanted)[8 + by : 8 + by + STEP]
            total = part if total is None else total + part
    return total

def gradient_stage(place, windows, taps, pieces, distances, slope, begun, shape):
    _, fine, width = shape
    coarse, seqs = fine // 2, lax.axis_size("seq")
    rows, block = pieces[0][0].shape[-2:]
    planes = width // (2 * rows)
    half = planes // 2
    window, used = coarse + 2 * HALO, coarse + 2 * MARGIN
    depth, planar = len(distances) * block, (2, coarse, width)
    last = begun is not None
    needed = list(range(seqs)) if last else distances
    parts = [(d, *part) for d in needed for part in windows[d]]
    operands = [part[1] for part in parts] + [piece[0] for piece in pieces]
    operands += [slope, begun] if last else []

    def body(place, *refs):
        own, refs = refs[: len(parts)], refs[len(parts) :]
        sources, refs = refs[: len(pieces)], refs[len(pieces) :]
        if last:
            (slope_ref, begun_ref), refs = refs[:2], refs[2:]
        out_ref, wv, gv, products, sems, grad_sems = refs[:6]
        me, core = place[0], place[1] % 2

        def kernel_copies(first):
            for number, (array, start, plane, count, flip, distance) in enumerate(pieces):
                spot = pl.ds(distances.index(distance) * block, block)
                if first != (start is not None):
                    continue
                for k in range(SPLIT if first else taps - SPLIT):
                    for h in range(count // half):
                        span = pl.ds(plane + h * half, half)
                        if first:
                            source = sources[number].at[pl.ds(start + (h * SPLIT + k) * half, half)]
                        else:
                            source = sources[number].at[span, distance, k]
                        tap = k if first else SPLIT + k
                        target = wv.at[tap, span, core ^ flip, :, spot]
                        sem = sems.at[tap, number, h]
                        yield tap, pltpu.make_async_copy(source, target, sem)

        def window_copies(target_of, sems):
            for number, (distance, _, start, first, count) in enumerate(parts):
                for b in range(count):
                    target = target_of(distance, pl.ds((first + b) * rows, rows))
                    if target is not None:
                        source = own[number].at[start + b]
                        yield pltpu.make_async_copy(source, target, sems.at[number, b])

        def into_window(distance, span):
            if distance not in distances:
                return None
            return gv.at[span, pl.ds(distances.index(distance) * block, block)]

        early = list(window_copies(into_window, grad_sems))
        late = []
        if last:
            sums, slopes, strip, skips, sum_sems, skip_sems = refs[6:]
            late.append(pltpu.make_async_copy(begun_ref, sums, sum_sems.at[0]))
            late.append(pltpu.make_async_copy(slope_ref, slopes, sum_sems.at[1]))
            late += window_copies(lambda d, span: skips.at[me ^ d, span], skip_sems)
        for copy in early:
            copy.start()
        arriving = sorted([*kernel_copies(True), *kernel_copies(False)], key=lambda pair: pair[0])
        for _, copy in arriving:
            copy.start()
        for copy in late:
            copy.start()
        for copy in early:
            copy.wait()
        for k in range(taps):
            for tap, copy in arriving:
                if tap == k:
                    copy.wait()
            for part in range(2):
                kernel = wv[k, part * half : (part + 1) * half].reshape(2 * half * rows, depth)
                lanes = slice(part * 2 * half * rows, (part + 1) * 2 * half * rows)
                products[k, :, lanes] = lax.dot_general(
                    gv[EDGE : EDGE + used],
                    kernel,
                    (((1,), (1,)), ((), ())),
                    preferred_element_type=jnp.float32,
                )

        for copy in late:
            copy.wait()

        @pl.loop(0, coarse // STEP)
        def _(i):
            base = pl.multiple_of(i * STEP, STEP)
            spot, span = pl.ds(base, STEP), pl.ds(pl.multiple_of(2 * base, 2 * STEP), 2 * STEP)
            for c in range(width // LANES):
                lanes = slice(c * LANES, (c + 1) * LANES)
                if last:
                    left = c * LANES % block
                    skip = skips[c * LANES // block, pl.ds(base + HALO, STEP), left : left + LANES]
                    skip = 0.5 * skip.astype(jnp.float32)
                for parity in range(2):
                    total = shifted_total(products, base, lanes, parity)
                    if last:
                        total = (total + sums[parity, spot, lanes]) * slopes[parity, spot, lanes]
                        strip[c, pl.ds(parity, STEP, stride=2), :] = total + skip
                    else:
                        out_ref[parity, spot, lanes] = total
                if last:
                    out_ref[0, span, lanes] = strip[c].astype(jnp.bfloat16)

    out_shape = jax.ShapeDtypeStruct(shape if last else planar, jnp.bfloat16 if last else jnp.float32)
    scratch = [
        pltpu.VMEM((taps, planes, 2, rows, depth), jnp.bfloat16),
        pltpu.VMEM((window, depth), jnp.bfloat16),
        pltpu.VMEM((taps, used, width), jnp.float32),
        pltpu.SemaphoreType.DMA((taps, len(pieces), 2)),
        pltpu.SemaphoreType.DMA((len(parts), window // rows)),
    ]
    if last:
        scratch += [
            pltpu.VMEM(planar, jnp.float32),
            pltpu.VMEM(planar, jnp.float32),
            pltpu.VMEM((width // LANES, 2 * STEP, LANES), jnp.float32),
            pltpu.VMEM((seqs, window, block), jnp.bfloat16),
            pltpu.SemaphoreType.DMA((2,)),
            pltpu.SemaphoreType.DMA((len(parts), window // rows)),
        ]
    return pl.pallas_call(
        body,
        out_shape=out_shape,
        grid_spec=pltpu.PrefetchScalarGridSpec(
            num_scalar_prefetch=1,
            grid=(1,),
            in_specs=[ANYWHERE] * len(operands),
            out_specs=pl.BlockSpec(out_shape.shape, lambda i, place: (0, 0, 0)),
            scratch_shapes=scratch,
        ),
        compiler_params=pltpu.CompilerParams(vmem_limit_bytes=56 << 20),
        cost_estimate=SMALL,
        name="input_grad",
    )(place, *operands)

def stack_planes(place, line):
    count = len(line)

    def kernel(place, *refs):
        parts, out_ref = refs[:count], refs[count]
        for j in range(count):
            out_ref[place[1] // 2 ^ j] = parts[j][...]

    shape = line[0].shape
    return pl.pallas_call(
        kernel,
        out_shape=jax.ShapeDtypeStruct((count, *shape), line[0].dtype),
        grid_spec=pltpu.PrefetchScalarGridSpec(
            num_scalar_prefetch=1,
            grid=(1,),
            in_specs=[pl.BlockSpec(shape, lambda i, place: (0,) * len(shape))] * count,
            out_specs=pl.BlockSpec((count, *shape), lambda i, place: (0,) * (1 + len(shape))),
        ),
        compiler_params=pltpu.CompilerParams(vmem_limit_bytes=24 << 20),
        cost_estimate=SMALL,
        name="stack_planes",
    )(place, *line)

def on_device_square(inputs, trunk_grad, weights):
    seqs, reps = lax.axis_size("seq"), lax.axis_size("rep")
    me, rep = lax.axis_index("seq"), lax.axis_index("rep")
    place = jnp.stack([me, rep]).astype(jnp.int32)
    taps, rows, block = weights.shape
    fine = inputs.shape[1]
    coarse, planes = fine // 2, reps // 2
    half = coarse // 2

    last_taps = weights[SPLIT:]
    across = [last_taps] + [from_peer(last_taps, "seq", d) for d in range(1, seqs)]

    act = after(activate(inputs), *across[1:])
    beside, below = from_peer(act, "seq", 1), from_peer(act, "seq", 2)
    slope = half_slope(inputs)
    line = gather_line(weights[:SPLIT], "rep", planes, 2)
    line_across = gather_line(after(jnp.stack(across), act, *line[1:]), "rep", planes, 2)
    crossing = (line_across[1], line_across[planes - 1])
    trunk = trunk_grad[0]
    zeros = jnp.zeros((1, block), jnp.bfloat16)
    later = jnp.concatenate([trunk[1:], zeros])
    earlier = jnp.concatenate([zeros, trunk[:-1]])
    shifts = jnp.concatenate([later, trunk, earlier], axis=1)
    *outgoing, own = kernel_messages(place, line, trunk_grad, coarse)
    ready = (slope, shifts, own, *crossing)
    top, bottom = after(beside[:half], *ready), after(below[half:], *ready)
    far_top, far_bottom = from_peer(top, "seq", 2), from_peer(bottom, "seq", 1)

    scale = 0.5 * float(fine * seqs * reps) ** (-0.5)
    near_rows = [(d, 0, coarse, 0) for d in range(3)]
    far_rows = [(3, 0, half, 0), (3, half, half, 0)]
    early = early_terms(place, near_rows, [act, beside, below], shifts, coarse)
    line_across[2] = after(line_across[2], early)
    lines = stack_planes(place, line_across)
    far_top, far_bottom = after(far_top, early, lines), after(far_bottom, early, lines)

    outgoing = [after(message, far_top, far_bottom) for message in outgoing]
    kept = [from_peer(message, "seq", d) for message, d in zip(outgoing, (1, 1, 2, 2))]
    other_own, other_lines = from_peer(own, "rep", 1), from_peer(lines, "rep", 1)

    mine, theirs = late_terms(
        place, far_rows, [far_top, far_bottom], shifts, early, coarse, scale, planes, taps, rows
    )
    arrived = from_peer(theirs, "rep", 1)
    pairs = [mine[j] + arrived[j].astype(jnp.float32) for j in range(planes)]
    weight_grad, steps = reduce_line(pairs, "rep", planes, 2)

    window = (coarse + 2 * HALO) // rows
    count, side = planes * SPLIT // 2, window // 2
    far_first, far_second = from_peer(kept[0], "seq", 2), from_peer(kept[2], "seq", 1)

    windows = [[(own, 2 * count, 0, window)], [(kept[1], count, 0, window)], [(kept[3], count, 0, window)]]
    stage = functools.partial(gradient_stage, place, taps=taps, slope=slope, shape=inputs.shape)
    soon = [(after(own, *steps[:1]), 0, 0, planes, 0, 0), (other_own, 0, 0, planes, 1, 0)]
    for part, start, plane, distance in zip(
        kept, (side, 0, 0, 0), (0, planes // 2, planes // 2, 0), (1, 1, 2, 2)
    ):
        soon.append((part, start, plane, planes // 2, 0, distance))
        soon.append((from_peer(part, "rep", 1), start, plane, planes // 2, 1, distance))
    crossed = [
        (part, None, 0, planes, flip, d)
        for flip, part in enumerate((lines, other_lines))
        for d in range(seqs)
    ]
    near = [piece for piece in crossed if piece[-1] < 3]
    begun = stage(windows, pieces=soon + near, distances=[0, 1, 2], begun=None)
    far_first, far_second = after(far_first, begun, *steps), after(far_second, begun, *steps)
    windows.append([(far_first, 0, 0, side), (far_second, count, side, side)])
    rest = [piece for piece in crossed if piece[-1] == 3]
    for part, start, plane in ((far_first, side, 0), (far_second, 0, planes // 2)):
        rest.append((part, start, plane, planes // 2, 0, 3))
        rest.append((from_peer(part, "rep", 1), start, plane, planes // 2, 1, 3))
    input_grad = stage(windows, pieces=rest, distances=[3], begun=begun)
    return (input_grad, weight_grad)


def with_halo(value, sides, width):
    for axis, dim in sides:
        peers, length = (lax.axis_size(axis), value.shape[dim])
        up = [(i, (i + 1) % peers) for i in range(peers - 1)]
        down = [(j, i) for i, j in up]
        last = lax.slice_in_dim(value, length - width, length, axis=dim)
        leading = lax.slice_in_dim(value, 0, width, axis=dim)
        before = lax.ppermute(last, axis, up)
        after = lax.ppermute(leading, axis, down)
        value = jnp.concatenate([before, value, after], axis=dim)
    return value

def contract_last(left, right):
    return lax.dot_general(
        left, right, (((1,), (1,)), ((), ())), preferred_element_type=jnp.float32
    )

def contract_first(left, right):
    return lax.dot_general(
        left, right, (((0,), (0,)), ((), ())), preferred_element_type=jnp.float32
    )

def on_device_plain(inputs, trunk_grad, weights):
    taps = weights.shape[0]
    grad = lax.all_to_all(trunk_grad, "seq", split_axis=1, concat_axis=2, tiled=True)
    grad_up = jnp.repeat(grad.astype(jnp.float32) * 0.5, 2, axis=1).astype(jnp.bfloat16)
    rows = grad_up.shape[1]
    padded = with_halo(grad_up, (("seq", 1),), 2)
    shifts = [padded[0, 4 - k : 4 - k + rows] for k in range(taps)]
    inputs_f = inputs[0].astype(jnp.float32)
    act_vals, back = jax.vjp(jax.nn.gelu, inputs_f)
    slope = back(jnp.ones_like(inputs_f))[0]
    act = act_vals.astype(jnp.bfloat16)
    in_width = inputs.shape[2]
    columns = lax.all_gather(weights, "seq", axis=2, tiled=True)
    piece = lax.all_gather(columns, "rep", axis=1, tiled=True)
    result = contract_last(shifts[0], piece[0])
    for project_k in range(1, taps):
        result = result + contract_last(shifts[project_k], piece[project_k])
    input_grad = (result * slope + grad_up[0, :, :in_width].astype(jnp.float32)).astype(
        jnp.bfloat16
    )
    scale_factor = float(rows * lax.axis_size("seq") * lax.axis_size("rep")) ** (-0.5)
    terms = jnp.stack([contract_first(act, shifts[k]) for k in range(taps)]) * scale_factor
    partial_sum = lax.psum_scatter(terms, "rep", scatter_dimension=1, tiled=True)
    weight_grad = lax.psum_scatter(partial_sum, "seq", scatter_dimension=2, tiled=True)
    return (input_grad[None], weight_grad)

def on_device(inputs, trunk_grad, weights):
    square = lax.axis_size("seq") == 4 and lax.axis_size("rep") % 8 == 0
    if square and weights.shape[2] % LANES == 0 and inputs.shape[2] % LANES == 0:
        return on_device_square(inputs, trunk_grad, weights)
    return on_device_plain(inputs, trunk_grad, weights)

def solution(mesh):
    in_specs = (P("rep", "seq", None), P("rep", None, "seq"), P(None, "rep", "seq"))
    out_specs = (P("rep", "seq", None), P(None, "rep", "seq"))
    return jax.shard_map(
        on_device, mesh=mesh, in_specs=in_specs, out_specs=out_specs, check_vma=False
    )
```

```python
import functools
import math

import jax
import jax.numpy as jnp
from jax import lax
from jax.experimental import pallas as pl
from jax.experimental.pallas import tpu as pltpu
from jax.sharding import PartitionSpec as P

LANES = 128
HALO = 32
EDGE = 16
MARGIN = HALO - EDGE
STEP = 64
SPLIT = 3
ROOT = math.sqrt(2.0 / math.pi)
CUBIC = 0.044715
SMALL = pl.CostEstimate(flops=1 << 20, bytes_accessed=1 << 16, transcendentals=0)
ANYWHERE = pl.BlockSpec(memory_space=pl.ANY)
ROW_OFFSETS = ((1, 1), (0, 1), (0, 0), (-1, 0), (-1, -1))
GRAD_PARTS = ((0, 0), (1, 0), (1, 1), (2, 1), (2, 2))

def from_peer(value, axis, distance):
    peers = lax.axis_size(axis)
    return lax.ppermute(value, axis, [(i, i ^ distance) for i in range(peers)])

def after(value, *earlier):
    return pl.pallas_call(
        lambda *refs: None,
        out_shape=jax.ShapeDtypeStruct(value.shape, value.dtype),
        in_specs=[ANYWHERE] * (1 + len(earlier)),
        out_specs=ANYWHERE,
        input_output_aliases={0: 0},
        name="after",
    )(value, *earlier)

def reduce_line(blocks, axis, count, unit):
    held, masks = [[0]], []
    while count > 1:
        masks.append(count - 1)
        held.append(held[-1] + [d ^ masks[-1] for d in held[-1]])
        count //= 2
    blocks, steps = dict(enumerate(blocks)), []
    for mask, keep in reversed(list(zip(masks, held))):
        leaving = jnp.stack([blocks[d ^ mask].astype(jnp.bfloat16) for d in keep])
        steps.append(from_peer(leaving, axis, mask * unit))
        blocks = {d: blocks[d] + steps[-1][n].astype(jnp.float32) for n, d in enumerate(keep)}
    return blocks[0], steps


def gather_line(value, axis, count, unit):
    found, mask = {0: value}, count - 1
    while mask:
        for distance in list(found):
            found[distance ^ mask] = from_peer(found[distance], axis, mask * unit)
        mask //= 2
    return [found[distance] for distance in range(count)]

def gelu_slope(x):
    tanh = jnp.tanh(ROOT * (x + CUBIC * (x * x * x)))
    return 0.5 * (1.0 + tanh) + 0.5 * x * (1.0 - tanh * tanh) * (
        ROOT * (1.0 + 3.0 * CUBIC * (x * x))
    )

def act_kernel(x_ref, out_ref, strip):
    width = x_ref.shape[2]

    @pl.loop(0, out_ref.shape[0] // STEP)
    def _(step):
        start = pl.multiple_of(step * STEP, STEP)
        x = x_ref[0, pl.ds(pl.multiple_of(2 * start, 2 * STEP), 2 * STEP), :].astype(jnp.float32)
        act = x * (0.5 * (1.0 + jnp.tanh(ROOT * (x + CUBIC * (x * x * x)))))
        for c in range(width // LANES):
            strip[c] = act[:, c * LANES : (c + 1) * LANES]
        for parity in range(2):
            for c in range(width // LANES):
                picked = strip[c, pl.ds(parity, STEP, stride=2), :].astype(jnp.bfloat16)
                left = parity * width + c * LANES
                out_ref[pl.ds(start, STEP), left : left + LANES] = picked

def activate(inputs):
    fine, width = inputs.shape[1:]
    return pl.pallas_call(
        act_kernel,
        out_shape=jax.ShapeDtypeStruct((fine // 2, 2 * width), jnp.bfloat16),
        in_specs=[pl.BlockSpec(memory_space=pltpu.VMEM)],
        out_specs=pl.BlockSpec(memory_space=pltpu.VMEM),
        scratch_shapes=[pltpu.VMEM((width // LANES, 2 * STEP, LANES), jnp.float32)],
        compiler_params=pltpu.CompilerParams(vmem_limit_bytes=24 << 20),
        cost_estimate=SMALL,
        name="act",
    )(inputs)

def kernel_messages(place, line, trunk_grad, coarse):
    taps, rows, block = line[0].shape
    planes, length = len(line), trunk_grad.shape[1]
    window = (coarse + 2 * HALO) // rows
    half = planes // 2

    def kernel(place, *refs):
        parts, trunk_ref = refs[:planes], refs[planes]
        beside_first, beside_second, below_first, below_second, own_ref, edged, sem = refs[planes + 1 :]
        copy = pltpu.make_async_copy(trunk_ref.at[0], edged.at[pl.ds(HALO, length)], sem)
        copy.start()
        edged[:HALO] = jnp.zeros((HALO, block), jnp.bfloat16)
        edged[HALO + length :] = jnp.zeros((HALO, block), jnp.bfloat16)
        for j in range(planes):
            plane = place[1] // 2 ^ j
            which = plane // half
            for k in range(taps):
                spot = k * half + plane % half
                own_ref[which * taps * half + spot] = parts[j][k]

                @pl.when(which == 0)
                def _():
                    beside_first[window // 2 + spot] = parts[j][k]
                    below_second[spot] = parts[j][k]

                @pl.when(which == 1)
                def _():
                    beside_second[spot] = parts[j][k]
                    below_first[spot] = parts[j][k]

        copy.wait()

        def cut(out_ref, spot, distance, first, last):
            base = (place[0] ^ distance) * coarse
            for b in range(first, last):
                out_ref[spot + b - first] = edged[pl.ds(pl.multiple_of(base + b * rows, 16), rows), :]

        cut(beside_first, 0, 3, 0, window // 2)
        cut(beside_second, half * taps, 1, 0, window)
        cut(below_first, half * taps, 3, window // 2, window)
        cut(below_second, half * taps, 2, 0, window)
        cut(own_ref, planes * taps, 0, 0, window)

    first, second = half * taps + window // 2, half * taps + window
    counts = (first, second, first, second, planes * taps + window)
    return pl.pallas_call(
        kernel,
        out_shape=[
            jax.ShapeDtypeStruct((n, rows, block), jnp.bfloat16) for n in counts
        ],
        grid_spec=pltpu.PrefetchScalarGridSpec(
            num_scalar_prefetch=1,
            grid=(1,),
            in_specs=[pl.BlockSpec(line[0].shape, lambda i, place: (0, 0, 0))] * planes + [ANYWHERE],
            out_specs=[
                pl.BlockSpec((n, rows, block), lambda i, place: (0, 0, 0))
                for n in counts
            ],
            scratch_shapes=[
                pltpu.VMEM((length + 2 * HALO, block), jnp.bfloat16),
                pltpu.SemaphoreType.DMA,
            ],
        ),
        compiler_params=pltpu.CompilerParams(vmem_limit_bytes=32 << 20),
        cost_estimate=SMALL,
        name="kernel_messages",
    )(place, *line, trunk_grad)

def slope_kernel(x_ref, out_ref, scratch):
    width = x_ref.shape[2]

    @pl.loop(0, out_ref.shape[1] // 64)
    def _(step):
        start = pl.multiple_of(step * 64, 64)
        span = pl.ds(pl.multiple_of(2 * start, 128), 128)
        for c in range(width // LANES):
            lanes = slice(c * LANES, (c + 1) * LANES)
            scratch[c] = 0.5 * gelu_slope(x_ref[0, span, lanes].astype(jnp.float32))
            for parity in range(2):
                out_ref[parity, pl.ds(start, 64), lanes] = scratch[c, pl.ds(parity, 64, stride=2), :]

def half_slope(inputs):
    fine, width = inputs.shape[1:]
    return pl.pallas_call(
        slope_kernel,
        out_shape=jax.ShapeDtypeStruct((2, fine // 2, width), jnp.float32),
        in_specs=[pl.BlockSpec(memory_space=pltpu.VMEM)],
        out_specs=pl.BlockSpec(memory_space=pltpu.VMEM),
        scratch_shapes=[pltpu.VMEM((width // LANES, 128, LANES), jnp.float32)],
        compiler_params=pltpu.CompilerParams(vmem_limit_bytes=24 << 20),
        name="half_slope",
    )(inputs)

def start_act(place, coarse, layout, pieces, shifts_ref, held, shifts, sems, shift_sems):
    copies, row = [], 0
    for i, (distance, first, size, offset) in enumerate(layout):
        start = pl.multiple_of((place[0] ^ distance) * coarse + first, 16)
        spot = pl.ds(row, size)
        source = pieces[i].at[pl.ds(offset, size)]
        copies.append(pltpu.make_async_copy(source, held.at[spot], sems.at[i]))
        copies.append(
            pltpu.make_async_copy(shifts_ref.at[pl.ds(start, size)], shifts.at[spot], shift_sems.at[i])
        )
        row += size
    for copy in copies:
        copy.start()
    return copies

def early_terms(place, layout, pieces, shifts, coarse):
    both, columns = pieces[0].shape[1], shifts.shape[1]
    rows = sum(size for _, _, size, _ in layout)
    tile = 256

    def kernel(place, shifts_ref, *refs):
        pieces, total = refs[: len(layout)], refs[len(layout)]
        held, shifts, sems, shift_sems = refs[len(layout) + 1 :]
        copies = start_act(
            place, coarse, layout, pieces, shifts_ref, held, shifts, sems, shift_sems
        )
        for copy in copies:
            copy.wait()

        @pl.loop(0, both // tile)
        def _(i):
            span = pl.ds(pl.multiple_of(i * tile, tile), tile)
            total[span, :] = lax.dot_general(
                held[:, span], shifts[...], (((0,), (0,)), ((), ())), preferred_element_type=jnp.float32
            )

    return pl.pallas_call(
        kernel,
        out_shape=jax.ShapeDtypeStruct((both, columns), jnp.float32),
        grid_spec=pltpu.PrefetchScalarGridSpec(
            num_scalar_prefetch=1,
            grid=(1,),
            in_specs=[ANYWHERE] * (1 + len(pieces)),
            out_specs=pl.BlockSpec((both, columns), lambda i, place: (0, 0)),
            scratch_shapes=[
                pltpu.VMEM((rows, both), jnp.bfloat16),
                pltpu.VMEM((rows, columns), jnp.bfloat16),
                pltpu.SemaphoreType.DMA((len(pieces),)),
                pltpu.SemaphoreType.DMA((len(pieces),)),
            ],
        ),
        compiler_params=pltpu.CompilerParams(vmem_limit_bytes=48 << 20),
        cost_estimate=SMALL,
        name="weight_grad_early",
    )(place, shifts, *pieces)

def late_terms(place, layout, pieces, shifts, early, coarse, scale, planes, taps, rows):
    both, columns = early.shape
    width, block = both // 2, columns // 3
    count = sum(size for _, _, size, _ in layout)
    tile = 256
    shape = (planes, taps, rows, block)

    def kernel(place, shifts_ref, early_ref, *refs):
        pieces, (mine_ref, *theirs_refs) = (
            refs[: len(layout)],
            refs[len(layout) : len(layout) + 1 + planes],
        )
        held, shifts, total, sems, shift_sems, early_sems = refs[len(layout) + 1 + planes :]
        core, plane = place[1] % 2, place[1] // 2
        copies = start_act(
            place, coarse, layout, pieces, shifts_ref, held, shifts, sems, shift_sems
        )

        def fetch(i):
            span = pl.ds(pl.multiple_of(i * tile, tile), tile)
            return pltpu.make_async_copy(early_ref.at[span], total.at[span], early_sems.at[i])

        for i in range(both // tile):
            fetch(i).start()
        for copy in copies:
            copy.wait()

        @pl.loop(0, both // tile)
        def _(i):
            span = pl.ds(pl.multiple_of(i * tile, tile), tile)
            term = lax.dot_general(
                held[:, span], shifts[...], (((0,), (0,)), ((), ())), preferred_element_type=jnp.float32
            )
            fetch(i).wait()
            total[span, :] += term

        def finish(j, parity, store):
            start = ((plane ^ j) * 2 + parity) * rows
            even = pl.ds(pl.multiple_of(start, 16), rows)
            odd = pl.ds(pl.multiple_of(width + start, 16), rows)
            for k, (left, right) in enumerate(GRAD_PARTS):
                term = total[even, left * block : (left + 1) * block]
                term += total[odd, right * block : (right + 1) * block]
                store(k, scale * term)

        for j in range(planes):

            def leave(k, term):
                theirs_refs[j][k] = term.astype(jnp.bfloat16)

            finish(j, 1 - core, leave)

        @pl.loop(0, planes)
        def _(j):
            def keep(k, term):
                mine_ref[j, k] = term

            finish(j, core, keep)

    whole = pl.BlockSpec(shape, lambda i, place: (0, 0, 0, 0))
    return pl.pallas_call(
        kernel,
        out_shape=(
            jax.ShapeDtypeStruct(shape, jnp.float32),
            *[jax.ShapeDtypeStruct(shape[1:], jnp.bfloat16)] * planes,
        ),
        grid_spec=pltpu.PrefetchScalarGridSpec(
            num_scalar_prefetch=1,
            grid=(1,),
            in_specs=[ANYWHERE] * (2 + len(pieces)),
            out_specs=[whole] + [pl.BlockSpec(shape[1:], lambda i, place: (0, 0, 0))] * planes,
            scratch_shapes=[
                pltpu.VMEM((count, both), jnp.bfloat16),
                pltpu.VMEM((count, columns), jnp.bfloat16),
                pltpu.VMEM((both, columns), jnp.float32),
                pltpu.SemaphoreType.DMA((len(pieces),)),
                pltpu.SemaphoreType.DMA((len(pieces),)),
                pltpu.SemaphoreType.DMA((both // tile,)),
            ],
        ),
        compiler_params=pltpu.CompilerParams(vmem_limit_bytes=48 << 20),
        cost_estimate=SMALL,
        name="weight_grad_late",
    )(place, shifts, early, *pieces)

def shifted_total(products, base, lanes, parity):
    total = None
    for by in (0, 1, -1):
        wanted = [k for k in range(products.shape[0]) if ROW_OFFSETS[k][parity] == by]
        if wanted:
            near = pl.ds(base + MARGIN - 8, STEP + 16)
            part = sum(products[k, near, lanes] for k in wanted)[8 + by : 8 + by + STEP]
            total = part if total is None else total + part
    return total

def gradient_stage(place, windows, taps, pieces, distances, slope, begun, shape):
    _, fine, width = shape
    coarse, seqs = fine // 2, lax.axis_size("seq")
    rows, block = pieces[0][0].shape[-2:]
    planes = width // (2 * rows)
    half = planes // 2
    window, used = coarse + 2 * HALO, coarse + 2 * MARGIN
    depth, planar = len(distances) * block, (2, coarse, width)
    last = begun is not None
    needed = list(range(seqs)) if last else distances
    parts = [(d, *part) for d in needed for part in windows[d]]
    operands = [part[1] for part in parts] + [piece[0] for piece in pieces]
    operands += [slope, begun] if last else []

    def body(place, *refs):
        own, refs = refs[: len(parts)], refs[len(parts) :]
        sources, refs = refs[: len(pieces)], refs[len(pieces) :]
        if last:
            (slope_ref, begun_ref), refs = refs[:2], refs[2:]
        out_ref, wv, gv, products, sems, grad_sems = refs[:6]
        me, core = place[0], place[1] % 2

        def kernel_copies(first):
            for number, (array, start, plane, count, flip, distance) in enumerate(pieces):
                spot = pl.ds(distances.index(distance) * block, block)
                if first != (start is not None):
                    continue
                for k in range(SPLIT if first else taps - SPLIT):
                    for h in range(count // half):
                        span = pl.ds(plane + h * half, half)
                        if first:
                            source = sources[number].at[pl.ds(start + (h * SPLIT + k) * half, half)]
                        else:
                            source = sources[number].at[span, distance, k]
                        tap = k if first else SPLIT + k
                        target = wv.at[tap, span, core ^ flip, :, spot]
                        sem = sems.at[tap, number, h]
                        yield tap, pltpu.make_async_copy(source, target, sem)

        def window_copies(target_of, sems):
            for number, (distance, _, start, first, count) in enumerate(parts):
                for b in range(count):
                    target = target_of(distance, pl.ds((first + b) * rows, rows))
                    if target is not None:
                        source = own[number].at[start + b]
                        yield pltpu.make_async_copy(source, target, sems.at[number, b])

        def into_window(distance, span):
            if distance not in distances:
                return None
            return gv.at[span, pl.ds(distances.index(distance) * block, block)]

        early = list(window_copies(into_window, grad_sems))
        late = []
        if last:
            sums, slopes, strip, skips, sum_sems, skip_sems = refs[6:]
            late.append(pltpu.make_async_copy(begun_ref, sums, sum_sems.at[0]))
            late.append(pltpu.make_async_copy(slope_ref, slopes, sum_sems.at[1]))
            late += window_copies(lambda d, span: skips.at[me ^ d, span], skip_sems)
        for copy in early:
            copy.start()
        arriving = sorted([*kernel_copies(True), *kernel_copies(False)], key=lambda pair: pair[0])
        for _, copy in arriving:
            copy.start()
        for copy in late:
            copy.start()
        for copy in early:
            copy.wait()
        for k in range(taps):
            for tap, copy in arriving:
                if tap == k:
                    copy.wait()
            for part in range(2):
                kernel = wv[k, part * half : (part + 1) * half].reshape(2 * half * rows, depth)
                lanes = slice(part * 2 * half * rows, (part + 1) * 2 * half * rows)
                products[k, :, lanes] = lax.dot_general(
                    gv[EDGE : EDGE + used],
                    kernel,
                    (((1,), (1,)), ((), ())),
                    preferred_element_type=jnp.float32,
                )

        for copy in late:
            copy.wait()

        @pl.loop(0, coarse // STEP)
        def _(i):
            base = pl.multiple_of(i * STEP, STEP)
            spot, span = pl.ds(base, STEP), pl.ds(pl.multiple_of(2 * base, 2 * STEP), 2 * STEP)
            for c in range(width // LANES):
                lanes = slice(c * LANES, (c + 1) * LANES)
                if last:
                    left = c * LANES % block
                    skip = skips[c * LANES // block, pl.ds(base + HALO, STEP), left : left + LANES]
                    skip = 0.5 * skip.astype(jnp.float32)
                for parity in range(2):
                    total = shifted_total(products, base, lanes, parity)
                    if last:
                        total = (total + sums[parity, spot, lanes]) * slopes[parity, spot, lanes]
                        strip[c, pl.ds(parity, STEP, stride=2), :] = total + skip
                    else:
                        out_ref[parity, spot, lanes] = total
                if last:
                    out_ref[0, span, lanes] = strip[c].astype(jnp.bfloat16)

    out_shape = jax.ShapeDtypeStruct(shape if last else planar, jnp.bfloat16 if last else jnp.float32)
    scratch = [
        pltpu.VMEM((taps, planes, 2, rows, depth), jnp.bfloat16),
        pltpu.VMEM((window, depth), jnp.bfloat16),
        pltpu.VMEM((taps, used, width), jnp.float32),
        pltpu.SemaphoreType.DMA((taps, len(pieces), 2)),
        pltpu.SemaphoreType.DMA((len(parts), window // rows)),
    ]
    if last:
        scratch += [
            pltpu.VMEM(planar, jnp.float32),
            pltpu.VMEM(planar, jnp.float32),
            pltpu.VMEM((width // LANES, 2 * STEP, LANES), jnp.float32),
            pltpu.VMEM((seqs, window, block), jnp.bfloat16),
            pltpu.SemaphoreType.DMA((2,)),
            pltpu.SemaphoreType.DMA((len(parts), window // rows)),
        ]
    return pl.pallas_call(
        body,
        out_shape=out_shape,
        grid_spec=pltpu.PrefetchScalarGridSpec(
            num_scalar_prefetch=1,
            grid=(1,),
            in_specs=[ANYWHERE] * len(operands),
            out_specs=pl.BlockSpec(out_shape.shape, lambda i, place: (0, 0, 0)),
            scratch_shapes=scratch,
        ),
        compiler_params=pltpu.CompilerParams(vmem_limit_bytes=56 << 20),
        cost_estimate=SMALL,
        name="input_grad",
    )(place, *operands)

def stack_planes(place, line):
    count = len(line)

    def kernel(place, *refs):
        parts, out_ref = refs[:count], refs[count]
        for j in range(count):
            out_ref[place[1] // 2 ^ j] = parts[j][...]

    shape = line[0].shape
    return pl.pallas_call(
        kernel,
        out_shape=jax.ShapeDtypeStruct((count, *shape), line[0].dtype),
        grid_spec=pltpu.PrefetchScalarGridSpec(
            num_scalar_prefetch=1,
            grid=(1,),
            in_specs=[pl.BlockSpec(shape, lambda i, place: (0,) * len(shape))] * count,
            out_specs=pl.BlockSpec((count, *shape), lambda i, place: (0,) * (1 + len(shape))),
        ),
        compiler_params=pltpu.CompilerParams(vmem_limit_bytes=24 << 20),
        cost_estimate=SMALL,
        name="stack_planes",
    )(place, *line)

def on_device_square(inputs, trunk_grad, weights):
    seqs, reps = lax.axis_size("seq"), lax.axis_size("rep")
    me, rep = lax.axis_index("seq"), lax.axis_index("rep")
    place = jnp.stack([me, rep]).astype(jnp.int32)
    taps, rows, block = weights.shape
    fine = inputs.shape[1]
    coarse, planes = fine // 2, reps // 2
    half = coarse // 2

    last_taps = weights[SPLIT:]
    across = [last_taps] + [from_peer(last_taps, "seq", d) for d in range(1, seqs)]

    act = after(activate(inputs), *across[1:])
    beside, below = from_peer(act, "seq", 1), from_peer(act, "seq", 2)
    slope = half_slope(inputs)
    line = gather_line(weights[:SPLIT], "rep", planes, 2)
    line_across = gather_line(after(jnp.stack(across), act, *line[1:]), "rep", planes, 2)
    crossing = (line_across[1], line_across[planes - 1])
    trunk = trunk_grad[0]
    zeros = jnp.zeros((1, block), jnp.bfloat16)
    later = jnp.concatenate([trunk[1:], zeros])
    earlier = jnp.concatenate([zeros, trunk[:-1]])
    shifts = jnp.concatenate([later, trunk, earlier], axis=1)
    *outgoing, own = kernel_messages(place, line, trunk_grad, coarse)
    ready = (slope, shifts, own, *crossing)
    top, bottom = after(beside[:half], *ready), after(below[half:], *ready)
    far_top, far_bottom = from_peer(top, "seq", 2), from_peer(bottom, "seq", 1)

    scale = 0.5 * float(fine * seqs * reps) ** (-0.5)
    near_rows = [(d, 0, coarse, 0) for d in range(3)]
    far_rows = [(3, 0, half, 0), (3, half, half, 0)]
    early = early_terms(place, near_rows, [act, beside, below], shifts, coarse)
    line_across[2] = after(line_across[2], early)
    lines = stack_planes(place, line_across)
    far_top, far_bottom = after(far_top, early, lines), after(far_bottom, early, lines)

    other_own, other_lines = from_peer(own, "rep", 1), from_peer(lines, "rep", 1)
    outgoing = [after(message, far_top, far_bottom, other_own, other_lines) for message in outgoing]
    kept = [from_peer(message, "seq", d) for message, d in zip(outgoing, (1, 1, 2, 2))]

    mine, *theirs = late_terms(
        place, far_rows, [far_top, far_bottom], shifts, early, coarse, scale, planes, taps, rows
    )
    arrived = [from_peer(part, "rep", 1) for part in theirs]
    pairs = [mine[j] + arrived[j].astype(jnp.float32) for j in range(planes)]
    weight_grad, steps = reduce_line(pairs, "rep", planes, 2)

    window = (coarse + 2 * HALO) // rows
    count, side = planes * SPLIT // 2, window // 2
    far_first, far_second = from_peer(kept[0], "seq", 2), from_peer(kept[2], "seq", 1)

    windows = [[(own, 2 * count, 0, window)], [(kept[1], count, 0, window)], [(kept[3], count, 0, window)]]
    stage = functools.partial(gradient_stage, place, taps=taps, slope=slope, shape=inputs.shape)
    soon = [(after(own, *steps[:1]), 0, 0, planes, 0, 0), (other_own, 0, 0, planes, 1, 0)]
    for part, start, plane, distance in zip(
        kept, (side, 0, 0, 0), (0, planes // 2, planes // 2, 0), (1, 1, 2, 2)
    ):
        soon.append((part, start, plane, planes // 2, 0, distance))
        soon.append((from_peer(part, "rep", 1), start, plane, planes // 2, 1, distance))
    crossed = [
        (part, None, 0, planes, flip, d)
        for flip, part in enumerate((lines, other_lines))
        for d in range(seqs)
    ]
    near = [piece for piece in crossed if piece[-1] < 3]
    begun = stage(windows, pieces=soon + near, distances=[0, 1, 2], begun=None)
    far_first, far_second = after(far_first, begun, *steps), after(far_second, begun, *steps)
    windows.append([(far_first, 0, 0, side), (far_second, count, side, side)])
    rest = [piece for piece in crossed if piece[-1] == 3]
    for part, start, plane in ((far_first, side, 0), (far_second, 0, planes // 2)):
        rest.append((part, start, plane, planes // 2, 0, 3))
        rest.append((from_peer(part, "rep", 1), start, plane, planes // 2, 1, 3))
    input_grad = stage(windows, pieces=rest, distances=[3], begun=begun)
    return (input_grad, weight_grad)


def with_halo(value, sides, width):
    for axis, dim in sides:
        peers, length = (lax.axis_size(axis), value.shape[dim])
        up = [(i, (i + 1) % peers) for i in range(peers - 1)]
        down = [(j, i) for i, j in up]
        last = lax.slice_in_dim(value, length - width, length, axis=dim)
        leading = lax.slice_in_dim(value, 0, width, axis=dim)
        before = lax.ppermute(last, axis, up)
        after = lax.ppermute(leading, axis, down)
        value = jnp.concatenate([before, value, after], axis=dim)
    return value

def contract_last(left, right):
    return lax.dot_general(
        left, right, (((1,), (1,)), ((), ())), preferred_element_type=jnp.float32
    )

def contract_first(left, right):
    return lax.dot_general(
        left, right, (((0,), (0,)), ((), ())), preferred_element_type=jnp.float32
    )

def on_device_plain(inputs, trunk_grad, weights):
    taps = weights.shape[0]
    grad = lax.all_to_all(trunk_grad, "seq", split_axis=1, concat_axis=2, tiled=True)
    grad_up = jnp.repeat(grad.astype(jnp.float32) * 0.5, 2, axis=1).astype(jnp.bfloat16)
    rows = grad_up.shape[1]
    padded = with_halo(grad_up, (("seq", 1),), 2)
    shifts = [padded[0, 4 - k : 4 - k + rows] for k in range(taps)]
    inputs_f = inputs[0].astype(jnp.float32)
    act_vals, back = jax.vjp(jax.nn.gelu, inputs_f)
    slope = back(jnp.ones_like(inputs_f))[0]
    act = act_vals.astype(jnp.bfloat16)
    in_width = inputs.shape[2]
    columns = lax.all_gather(weights, "seq", axis=2, tiled=True)
    piece = lax.all_gather(columns, "rep", axis=1, tiled=True)
    result = contract_last(shifts[0], piece[0])
    for project_k in range(1, taps):
        result = result + contract_last(shifts[project_k], piece[project_k])
    input_grad = (result * slope + grad_up[0, :, :in_width].astype(jnp.float32)).astype(
        jnp.bfloat16
    )
    scale_factor = float(rows * lax.axis_size("seq") * lax.axis_size("rep")) ** (-0.5)
    terms = jnp.stack([contract_first(act, shifts[k]) for k in range(taps)]) * scale_factor
    partial_sum = lax.psum_scatter(terms, "rep", scatter_dimension=1, tiled=True)
    weight_grad = lax.psum_scatter(partial_sum, "seq", scatter_dimension=2, tiled=True)
    return (input_grad[None], weight_grad)

def on_device(inputs, trunk_grad, weights):
    square = lax.axis_size("seq") == 4 and lax.axis_size("rep") % 8 == 0
    if square and weights.shape[2] % LANES == 0 and inputs.shape[2] % LANES == 0:
        return on_device_square(inputs, trunk_grad, weights)
    return on_device_plain(inputs, trunk_grad, weights)

def solution(mesh):
    in_specs = (P("rep", "seq", None), P("rep", None, "seq"), P(None, "rep", "seq"))
    out_specs = (P("rep", "seq", None), P(None, "rep", "seq"))
    return jax.shard_map(
        on_device, mesh=mesh, in_specs=in_specs, out_specs=out_specs, check_vma=False
    )
```

```python
import functools
import math

import jax
import jax.numpy as jnp
from jax import lax
from jax.experimental import pallas as pl
from jax.experimental.pallas import tpu as pltpu
from jax.sharding import PartitionSpec as P

LANES = 128
HALO = 32
EDGE = 16
MARGIN = HALO - EDGE
STEP = 64
SPLIT = 3
ROOT = math.sqrt(2.0 / math.pi)
CUBIC = 0.044715
SMALL = pl.CostEstimate(flops=1 << 20, bytes_accessed=1 << 16, transcendentals=0)
ANYWHERE = pl.BlockSpec(memory_space=pl.ANY)
ROW_OFFSETS = ((1, 1), (0, 1), (0, 0), (-1, 0), (-1, -1))
GRAD_PARTS = ((0, 0), (1, 0), (1, 1), (2, 1), (2, 2))

def from_peer(value, axis, distance):
    peers = lax.axis_size(axis)
    return lax.ppermute(value, axis, [(i, i ^ distance) for i in range(peers)])

def after(value, *earlier):
    return pl.pallas_call(
        lambda *refs: None,
        out_shape=jax.ShapeDtypeStruct(value.shape, value.dtype),
        in_specs=[ANYWHERE] * (1 + len(earlier)),
        out_specs=ANYWHERE,
        input_output_aliases={0: 0},
        name="after",
    )(value, *earlier)

def reduce_line(blocks, axis, count, unit):
    held, masks = [[0]], []
    while count > 1:
        masks.append(count - 1)
        held.append(held[-1] + [d ^ masks[-1] for d in held[-1]])
        count //= 2
    blocks, steps = dict(enumerate(blocks)), []
    for mask, keep in reversed(list(zip(masks, held))):
        leaving = jnp.stack([blocks[d ^ mask].astype(jnp.bfloat16) for d in keep])
        steps.append(from_peer(leaving, axis, mask * unit))
        blocks = {d: blocks[d] + steps[-1][n].astype(jnp.float32) for n, d in enumerate(keep)}
    return blocks[0], steps


def gather_line(value, axis, count, unit):
    found, mask = {0: value}, count - 1
    while mask:
        for distance in list(found):
            found[distance ^ mask] = from_peer(found[distance], axis, mask * unit)
        mask //= 2
    return [found[distance] for distance in range(count)]

def gelu_slope(x):
    tanh = jnp.tanh(ROOT * (x + CUBIC * (x * x * x)))
    return 0.5 * (1.0 + tanh) + 0.5 * x * (1.0 - tanh * tanh) * (
        ROOT * (1.0 + 3.0 * CUBIC * (x * x))
    )

def act_kernel(x_ref, out_ref, strip):
    width = x_ref.shape[2]

    @pl.loop(0, out_ref.shape[0] // STEP)
    def _(step):
        start = pl.multiple_of(step * STEP, STEP)
        x = x_ref[0, pl.ds(pl.multiple_of(2 * start, 2 * STEP), 2 * STEP), :].astype(jnp.float32)
        act = x * (0.5 * (1.0 + jnp.tanh(ROOT * (x + CUBIC * (x * x * x)))))
        for c in range(width // LANES):
            strip[c] = act[:, c * LANES : (c + 1) * LANES]
        for parity in range(2):
            for c in range(width // LANES):
                picked = strip[c, pl.ds(parity, STEP, stride=2), :].astype(jnp.bfloat16)
                left = parity * width + c * LANES
                out_ref[pl.ds(start, STEP), left : left + LANES] = picked

def activate(inputs):
    fine, width = inputs.shape[1:]
    return pl.pallas_call(
        act_kernel,
        out_shape=jax.ShapeDtypeStruct((fine // 2, 2 * width), jnp.bfloat16),
        in_specs=[pl.BlockSpec(memory_space=pltpu.VMEM)],
        out_specs=pl.BlockSpec(memory_space=pltpu.VMEM),
        scratch_shapes=[pltpu.VMEM((width // LANES, 2 * STEP, LANES), jnp.float32)],
        compiler_params=pltpu.CompilerParams(vmem_limit_bytes=24 << 20),
        cost_estimate=SMALL,
        name="act",
    )(inputs)

def kernel_messages(place, line, trunk_grad, coarse):
    taps, rows, block = line[0].shape
    planes, length = len(line), trunk_grad.shape[1]
    window = (coarse + 2 * HALO) // rows
    half = planes // 2

    def kernel(place, *refs):
        parts, trunk_ref = refs[:planes], refs[planes]
        beside_ref, below_ref, own_ref, edged, sem = refs[planes + 1 :]
        copy = pltpu.make_async_copy(trunk_ref.at[0], edged.at[pl.ds(HALO, length)], sem)
        copy.start()
        edged[:HALO] = jnp.zeros((HALO, block), jnp.bfloat16)
        edged[HALO + length :] = jnp.zeros((HALO, block), jnp.bfloat16)
        for j in range(planes):
            plane = place[1] // 2 ^ j
            for k in range(taps):
                spot = (plane // half * taps + k) * half + plane % half
                beside_ref[window // 2 + spot] = parts[j][k]
                below_ref[spot] = parts[j][k]
        copy.wait()

        def cut(out_ref, spot, distance, first, last):
            base = (place[0] ^ distance) * coarse
            for b in range(first, last):
                out_ref[spot + b - first] = edged[pl.ds(pl.multiple_of(base + b * rows, 16), rows), :]

        cut(beside_ref, 0, 3, 0, window // 2)
        cut(beside_ref, window // 2 + planes * taps, 1, 0, window)
        cut(below_ref, planes * taps, 3, window // 2, window)
        cut(below_ref, planes * taps + window // 2, 2, 0, window)
        cut(own_ref, 0, 0, 0, window)

    count = window // 2 + planes * taps + window
    return pl.pallas_call(
        kernel,
        out_shape=[
            jax.ShapeDtypeStruct((n, rows, block), jnp.bfloat16) for n in (count, count, window)
        ],
        grid_spec=pltpu.PrefetchScalarGridSpec(
            num_scalar_prefetch=1,
            grid=(1,),
            in_specs=[pl.BlockSpec(line[0].shape, lambda i, place: (0, 0, 0))] * planes + [ANYWHERE],
            out_specs=[
                pl.BlockSpec((n, rows, block), lambda i, place: (0, 0, 0))
                for n in (count, count, window)
            ],
            scratch_shapes=[
                pltpu.VMEM((length + 2 * HALO, block), jnp.bfloat16),
                pltpu.SemaphoreType.DMA,
            ],
        ),
        compiler_params=pltpu.CompilerParams(vmem_limit_bytes=32 << 20),
        cost_estimate=SMALL,
        name="kernel_messages",
    )(place, *line, trunk_grad)

def slope_kernel(x_ref, out_ref, scratch):
    width = x_ref.shape[2]

    @pl.loop(0, out_ref.shape[1] // 64)
    def _(step):
        start = pl.multiple_of(step * 64, 64)
        span = pl.ds(pl.multiple_of(2 * start, 128), 128)
        for c in range(width // LANES):
            lanes = slice(c * LANES, (c + 1) * LANES)
            scratch[c] = 0.5 * gelu_slope(x_ref[0, span, lanes].astype(jnp.float32))
            for parity in range(2):
                out_ref[parity, pl.ds(start, 64), lanes] = scratch[c, pl.ds(parity, 64, stride=2), :]

def half_slope(inputs):
    fine, width = inputs.shape[1:]
    return pl.pallas_call(
        slope_kernel,
        out_shape=jax.ShapeDtypeStruct((2, fine // 2, width), jnp.float32),
        in_specs=[pl.BlockSpec(memory_space=pltpu.VMEM)],
        out_specs=pl.BlockSpec(memory_space=pltpu.VMEM),
        scratch_shapes=[pltpu.VMEM((width // LANES, 128, LANES), jnp.float32)],
        compiler_params=pltpu.CompilerParams(vmem_limit_bytes=24 << 20),
        name="half_slope",
    )(inputs)

def start_act(place, coarse, layout, pieces, shifts_ref, held, shifts, sems, shift_sems):
    copies, row = [], 0
    for i, (distance, first, size, offset) in enumerate(layout):
        start = pl.multiple_of((place[0] ^ distance) * coarse + first, 16)
        spot = pl.ds(row, size)
        source = pieces[i].at[pl.ds(offset, size)]
        copies.append(pltpu.make_async_copy(source, held.at[spot], sems.at[i]))
        copies.append(
            pltpu.make_async_copy(shifts_ref.at[pl.ds(start, size)], shifts.at[spot], shift_sems.at[i])
        )
        row += size
    for copy in copies:
        copy.start()
    return copies

def early_terms(place, layout, pieces, shifts, coarse):
    both, columns = pieces[0].shape[1], shifts.shape[1]
    rows = sum(size for _, _, size, _ in layout)
    tile = 256

    def kernel(place, shifts_ref, *refs):
        pieces, total = refs[: len(layout)], refs[len(layout)]
        held, shifts, sems, shift_sems = refs[len(layout) + 1 :]
        copies = start_act(
            place, coarse, layout, pieces, shifts_ref, held, shifts, sems, shift_sems
        )
        for copy in copies:
            copy.wait()

        @pl.loop(0, both // tile)
        def _(i):
            span = pl.ds(pl.multiple_of(i * tile, tile), tile)
            total[span, :] = lax.dot_general(
                held[:, span], shifts[...], (((0,), (0,)), ((), ())), preferred_element_type=jnp.float32
            )

    return pl.pallas_call(
        kernel,
        out_shape=jax.ShapeDtypeStruct((both, columns), jnp.float32),
        grid_spec=pltpu.PrefetchScalarGridSpec(
            num_scalar_prefetch=1,
            grid=(1,),
            in_specs=[ANYWHERE] * (1 + len(pieces)),
            out_specs=pl.BlockSpec((both, columns), lambda i, place: (0, 0)),
            scratch_shapes=[
                pltpu.VMEM((rows, both), jnp.bfloat16),
                pltpu.VMEM((rows, columns), jnp.bfloat16),
                pltpu.SemaphoreType.DMA((len(pieces),)),
                pltpu.SemaphoreType.DMA((len(pieces),)),
            ],
        ),
        compiler_params=pltpu.CompilerParams(vmem_limit_bytes=48 << 20),
        cost_estimate=SMALL,
        name="weight_grad_early",
    )(place, shifts, *pieces)

def late_terms(place, layout, pieces, shifts, early, coarse, scale, planes, taps, rows):
    both, columns = early.shape
    width, block = both // 2, columns // 3
    count = sum(size for _, _, size, _ in layout)
    tile = 256
    shape = (planes, taps, rows, block)

    def kernel(place, shifts_ref, early_ref, *refs):
        pieces, (mine_ref, *theirs_refs) = refs[: len(layout)], refs[len(layout) : len(layout) + 3]
        held, shifts, total, sems, shift_sems, early_sems = refs[len(layout) + 3 :]
        core, plane = place[1] % 2, place[1] // 2
        copies = start_act(
            place, coarse, layout, pieces, shifts_ref, held, shifts, sems, shift_sems
        )

        def fetch(i):
            span = pl.ds(pl.multiple_of(i * tile, tile), tile)
            return pltpu.make_async_copy(early_ref.at[span], total.at[span], early_sems.at[i])

        for i in range(both // tile):
            fetch(i).start()
        for copy in copies:
            copy.wait()

        @pl.loop(0, both // tile)
        def _(i):
            span = pl.ds(pl.multiple_of(i * tile, tile), tile)
            term = lax.dot_general(
                held[:, span], shifts[...], (((0,), (0,)), ((), ())), preferred_element_type=jnp.float32
            )
            fetch(i).wait()
            total[span, :] += term

        def finish(out_ref, at, j, parity, kind):
            start = ((plane ^ j) * 2 + parity) * rows
            even = pl.ds(pl.multiple_of(start, 16), rows)
            odd = pl.ds(pl.multiple_of(width + start, 16), rows)
            for k, (left, right) in enumerate(GRAD_PARTS):
                term = total[even, left * block : (left + 1) * block]
                term += total[odd, right * block : (right + 1) * block]
                out_ref[at, k] = (scale * term).astype(kind)

        for which, out_ref in enumerate(theirs_refs):

            @pl.loop(0, planes // 2)
            def _(at):
                finish(out_ref, at, at + which * (planes // 2), 1 - core, jnp.bfloat16)

        @pl.loop(0, planes)
        def _(j):
            finish(mine_ref, j, j, core, jnp.float32)

    half_shape = (planes // 2, *shape[1:])
    whole = pl.BlockSpec(shape, lambda i, place: (0, 0, 0, 0))
    half = pl.BlockSpec(half_shape, lambda i, place: (0, 0, 0, 0))
    return pl.pallas_call(
        kernel,
        out_shape=(
            jax.ShapeDtypeStruct(shape, jnp.float32),
            jax.ShapeDtypeStruct(half_shape, jnp.bfloat16),
            jax.ShapeDtypeStruct(half_shape, jnp.bfloat16),
        ),
        grid_spec=pltpu.PrefetchScalarGridSpec(
            num_scalar_prefetch=1,
            grid=(1,),
            in_specs=[ANYWHERE] * (2 + len(pieces)),
            out_specs=[whole, half, half],
            scratch_shapes=[
                pltpu.VMEM((count, both), jnp.bfloat16),
                pltpu.VMEM((count, columns), jnp.bfloat16),
                pltpu.VMEM((both, columns), jnp.float32),
                pltpu.SemaphoreType.DMA((len(pieces),)),
                pltpu.SemaphoreType.DMA((len(pieces),)),
                pltpu.SemaphoreType.DMA((both // tile,)),
            ],
        ),
        compiler_params=pltpu.CompilerParams(vmem_limit_bytes=48 << 20),
        cost_estimate=SMALL,
        name="weight_grad_late",
    )(place, shifts, early, *pieces)

def shifted_total(products, base, lanes, parity):
    total = None
    for by in (0, 1, -1):
        wanted = [k for k in range(products.shape[0]) if ROW_OFFSETS[k][parity] == by]
        if wanted:
            near = pl.ds(base + MARGIN - 8, STEP + 16)
            part = sum(products[k, near, lanes] for k in wanted)[8 + by : 8 + by + STEP]
            total = part if total is None else total + part
    return total

def gradient_stage(place, windows, taps, pieces, distances, slope, begun, shape):
    _, fine, width = shape
    coarse, seqs = fine // 2, lax.axis_size("seq")
    rows, block = pieces[0][0].shape[-2:]
    planes = width // (2 * rows)
    half = planes // 2
    window, used = coarse + 2 * HALO, coarse + 2 * MARGIN
    depth, planar = len(distances) * block, (2, coarse, width)
    last = begun is not None
    needed = list(range(seqs)) if last else distances
    parts = [(d, *part) for d in needed for part in windows[d]]
    operands = [part[1] for part in parts] + [piece[0] for piece in pieces]
    operands += [slope, begun] if last else []

    def body(place, *refs):
        own, refs = refs[: len(parts)], refs[len(parts) :]
        sources, refs = refs[: len(pieces)], refs[len(pieces) :]
        if last:
            (slope_ref, begun_ref), refs = refs[:2], refs[2:]
        out_ref, wv, gv, products, sems, grad_sems = refs[:6]
        me, core = place[0], place[1] % 2

        def kernel_copies(first):
            for number, (array, start, plane, count, flip, distance) in enumerate(pieces):
                spot = pl.ds(distances.index(distance) * block, block)
                if first != (start is not None):
                    continue
                for k in range(SPLIT if first else taps - SPLIT):
                    for h in range(count // half):
                        span = pl.ds(plane + h * half, half)
                        if first:
                            source = sources[number].at[pl.ds(start + (h * SPLIT + k) * half, half)]
                        else:
                            source = sources[number].at[span, distance, k]
                        tap = k if first else SPLIT + k
                        target = wv.at[tap, span, core ^ flip, :, spot]
                        sem = sems.at[tap, number, h]
                        yield tap, pltpu.make_async_copy(source, target, sem)

        def window_copies(target_of, sems):
            for number, (distance, _, start, first, count) in enumerate(parts):
                for b in range(count):
                    target = target_of(distance, pl.ds((first + b) * rows, rows))
                    if target is not None:
                        source = own[number].at[start + b]
                        yield pltpu.make_async_copy(source, target, sems.at[number, b])

        def into_window(distance, span):
            if distance not in distances:
                return None
            return gv.at[span, pl.ds(distances.index(distance) * block, block)]

        early = list(window_copies(into_window, grad_sems))
        late = []
        if last:
            sums, slopes, strip, skips, sum_sems, skip_sems = refs[6:]
            late.append(pltpu.make_async_copy(begun_ref, sums, sum_sems.at[0]))
            late.append(pltpu.make_async_copy(slope_ref, slopes, sum_sems.at[1]))
            late += window_copies(lambda d, span: skips.at[me ^ d, span], skip_sems)
        for copy in early:
            copy.start()
        arriving = sorted([*kernel_copies(True), *kernel_copies(False)], key=lambda pair: pair[0])
        for _, copy in arriving:
            copy.start()
        for copy in late:
            copy.start()
        for copy in early:
            copy.wait()
        for k in range(taps):
            for tap, copy in arriving:
                if tap == k:
                    copy.wait()
            for part in range(2):
                kernel = wv[k, part * half : (part + 1) * half].reshape(2 * half * rows, depth)
                lanes = slice(part * 2 * half * rows, (part + 1) * 2 * half * rows)
                products[k, :, lanes] = lax.dot_general(
                    gv[EDGE : EDGE + used],
                    kernel,
                    (((1,), (1,)), ((), ())),
                    preferred_element_type=jnp.float32,
                )

        for copy in late:
            copy.wait()

        @pl.loop(0, coarse // STEP)
        def _(i):
            base = pl.multiple_of(i * STEP, STEP)
            spot, span = pl.ds(base, STEP), pl.ds(pl.multiple_of(2 * base, 2 * STEP), 2 * STEP)
            for c in range(width // LANES):
                lanes = slice(c * LANES, (c + 1) * LANES)
                if last:
                    left = c * LANES % block
                    skip = skips[c * LANES // block, pl.ds(base + HALO, STEP), left : left + LANES]
                    skip = 0.5 * skip.astype(jnp.float32)
                for parity in range(2):
                    total = shifted_total(products, base, lanes, parity)
                    if last:
                        total = (total + sums[parity, spot, lanes]) * slopes[parity, spot, lanes]
                        strip[c, pl.ds(parity, STEP, stride=2), :] = total + skip
                    else:
                        out_ref[parity, spot, lanes] = total
                if last:
                    out_ref[0, span, lanes] = strip[c].astype(jnp.bfloat16)

    out_shape = jax.ShapeDtypeStruct(shape if last else planar, jnp.bfloat16 if last else jnp.float32)
    scratch = [
        pltpu.VMEM((taps, planes, 2, rows, depth), jnp.bfloat16),
        pltpu.VMEM((window, depth), jnp.bfloat16),
        pltpu.VMEM((taps, used, width), jnp.float32),
        pltpu.SemaphoreType.DMA((taps, len(pieces), 2)),
        pltpu.SemaphoreType.DMA((len(parts), window // rows)),
    ]
    if last:
        scratch += [
            pltpu.VMEM(planar, jnp.float32),
            pltpu.VMEM(planar, jnp.float32),
            pltpu.VMEM((width // LANES, 2 * STEP, LANES), jnp.float32),
            pltpu.VMEM((seqs, window, block), jnp.bfloat16),
            pltpu.SemaphoreType.DMA((2,)),
            pltpu.SemaphoreType.DMA((len(parts), window // rows)),
        ]
    return pl.pallas_call(
        body,
        out_shape=out_shape,
        grid_spec=pltpu.PrefetchScalarGridSpec(
            num_scalar_prefetch=1,
            grid=(1,),
            in_specs=[ANYWHERE] * len(operands),
            out_specs=pl.BlockSpec(out_shape.shape, lambda i, place: (0, 0, 0)),
            scratch_shapes=scratch,
        ),
        compiler_params=pltpu.CompilerParams(vmem_limit_bytes=56 << 20),
        cost_estimate=SMALL,
        name="input_grad",
    )(place, *operands)

def stack_planes(place, line):
    count = len(line)

    def kernel(place, *refs):
        parts, out_ref = refs[:count], refs[count]
        for j in range(count):
            out_ref[place[1] // 2 ^ j] = parts[j][...]

    shape = line[0].shape
    return pl.pallas_call(
        kernel,
        out_shape=jax.ShapeDtypeStruct((count, *shape), line[0].dtype),
        grid_spec=pltpu.PrefetchScalarGridSpec(
            num_scalar_prefetch=1,
            grid=(1,),
            in_specs=[pl.BlockSpec(shape, lambda i, place: (0,) * len(shape))] * count,
            out_specs=pl.BlockSpec((count, *shape), lambda i, place: (0,) * (1 + len(shape))),
        ),
        compiler_params=pltpu.CompilerParams(vmem_limit_bytes=24 << 20),
        cost_estimate=SMALL,
        name="stack_planes",
    )(place, *line)

def on_device_square(inputs, trunk_grad, weights):
    seqs, reps = lax.axis_size("seq"), lax.axis_size("rep")
    me, rep = lax.axis_index("seq"), lax.axis_index("rep")
    place = jnp.stack([me, rep]).astype(jnp.int32)
    taps, rows, block = weights.shape
    fine = inputs.shape[1]
    coarse, planes = fine // 2, reps // 2
    half = coarse // 2

    last_taps = weights[SPLIT:]
    across = [last_taps] + [from_peer(last_taps, "seq", d) for d in range(1, seqs)]

    act = after(activate(inputs), *across[1:])
    beside, below = from_peer(act, "seq", 1), from_peer(act, "seq", 2)
    slope = half_slope(inputs)
    line = gather_line(weights[:SPLIT], "rep", planes, 2)
    line_across = gather_line(after(jnp.stack(across), act, *line[1:]), "rep", planes, 2)
    crossing = (line_across[1], line_across[planes - 1])
    trunk = trunk_grad[0]
    zeros = jnp.zeros((1, block), jnp.bfloat16)
    later = jnp.concatenate([trunk[1:], zeros])
    earlier = jnp.concatenate([zeros, trunk[:-1]])
    shifts = jnp.concatenate([later, trunk, earlier], axis=1)
    to_beside, to_below, own_window = kernel_messages(place, line, trunk_grad, coarse)
    ready = (slope, shifts, to_beside, *crossing)
    top, bottom = after(beside[:half], *ready), after(below[half:], *ready)
    far_top, far_bottom = from_peer(top, "seq", 2), from_peer(bottom, "seq", 1)

    scale = 0.5 * float(fine * seqs * reps) ** (-0.5)
    near_rows = [(d, 0, coarse, 0) for d in range(3)]
    far_rows = [(3, 0, half, 0), (3, half, half, 0)]
    early = early_terms(place, near_rows, [act, beside, below], shifts, coarse)
    line_across[2] = after(line_across[2], early)
    lines = stack_planes(place, line_across)
    far_top, far_bottom = after(far_top, early, lines), after(far_bottom, early, lines)

    to_beside, to_below = (
        after(message, far_top, far_bottom) for message in (to_beside, to_below)
    )
    kept_beside, kept_below = from_peer(to_beside, "seq", 1), from_peer(to_below, "seq", 2)
    other_column, other_lines = from_peer(to_below, "rep", 1), from_peer(lines, "rep", 1)

    mine, *theirs = late_terms(
        place, far_rows, [far_top, far_bottom], shifts, early, coarse, scale, planes, taps, rows
    )
    arrived = [from_peer(part, "rep", 1) for part in theirs]
    pairs = []
    for j in range(planes):
        part = arrived[j // (planes // 2)][j % (planes // 2)]
        pairs.append(mine[j] + part.astype(jnp.float32))
    weight_grad, steps = reduce_line(pairs, "rep", planes, 2)

    window = (coarse + 2 * HALO) // rows
    count, side = planes * SPLIT, window // 2
    far_first = from_peer(kept_beside[: side + count // 2], "seq", 2)
    far_second = from_peer(kept_below[count // 2 : count + side], "seq", 1)

    windows = [
        [(own_window, 0, 0, window)],
        [(kept_beside, side + count, 0, window)],
        [(kept_below, count + side, 0, window)],
    ]
    stage = functools.partial(gradient_stage, place, taps=taps, slope=slope, shape=inputs.shape)
    soon = [(to_below, 0, 0, planes, 0, 0), (other_column, 0, 0, planes, 1, 0)]
    for part, start, distance in ((kept_beside, side, 1), (kept_below, 0, 2)):
        soon.append((part, start, 0, planes, 0, distance))
        soon.append((from_peer(part, "rep", 1), start, 0, planes, 1, distance))
    crossed = [
        (part, None, 0, planes, flip, d)
        for flip, part in enumerate((lines, other_lines))
        for d in range(seqs)
    ]
    near = [piece for piece in crossed if piece[-1] < 3]
    begun = stage(windows, pieces=soon + near, distances=[0, 1, 2], begun=None)
    far_first, far_second = after(far_first, begun, *steps[:1]), after(far_second, begun, *steps[:1])
    windows.append([(far_first, 0, 0, side), (far_second, count // 2, side, side)])
    rest = [piece for piece in crossed if piece[-1] == 3]
    for part, start, plane in ((far_first, side, 0), (far_second, 0, planes // 2)):
        rest.append((part, start, plane, planes // 2, 0, 3))
        rest.append((from_peer(part, "rep", 1), start, plane, planes // 2, 1, 3))
    input_grad = stage(windows, pieces=rest, distances=[3], begun=begun)
    return (input_grad, weight_grad)


def with_halo(value, sides, width):
    for axis, dim in sides:
        peers, length = (lax.axis_size(axis), value.shape[dim])
        up = [(i, (i + 1) % peers) for i in range(peers - 1)]
        down = [(j, i) for i, j in up]
        last = lax.slice_in_dim(value, length - width, length, axis=dim)
        leading = lax.slice_in_dim(value, 0, width, axis=dim)
        before = lax.ppermute(last, axis, up)
        after = lax.ppermute(leading, axis, down)
        value = jnp.concatenate([before, value, after], axis=dim)
    return value

def contract_last(left, right):
    return lax.dot_general(
        left, right, (((1,), (1,)), ((), ())), preferred_element_type=jnp.float32
    )

def contract_first(left, right):
    return lax.dot_general(
        left, right, (((0,), (0,)), ((), ())), preferred_element_type=jnp.float32
    )

def on_device_plain(inputs, trunk_grad, weights):
    taps = weights.shape[0]
    grad = lax.all_to_all(trunk_grad, "seq", split_axis=1, concat_axis=2, tiled=True)
    grad_up = jnp.repeat(grad.astype(jnp.float32) * 0.5, 2, axis=1).astype(jnp.bfloat16)
    rows = grad_up.shape[1]
    padded = with_halo(grad_up, (("seq", 1),), 2)
    shifts = [padded[0, 4 - k : 4 - k + rows] for k in range(taps)]
    inputs_f = inputs[0].astype(jnp.float32)
    act_vals, back = jax.vjp(jax.nn.gelu, inputs_f)
    slope = back(jnp.ones_like(inputs_f))[0]
    act = act_vals.astype(jnp.bfloat16)
    in_width = inputs.shape[2]
    columns = lax.all_gather(weights, "seq", axis=2, tiled=True)
    piece = lax.all_gather(columns, "rep", axis=1, tiled=True)
    result = contract_last(shifts[0], piece[0])
    for project_k in range(1, taps):
        result = result + contract_last(shifts[project_k], piece[project_k])
    input_grad = (result * slope + grad_up[0, :, :in_width].astype(jnp.float32)).astype(
        jnp.bfloat16
    )
    scale_factor = float(rows * lax.axis_size("seq") * lax.axis_size("rep")) ** (-0.5)
    terms = jnp.stack([contract_first(act, shifts[k]) for k in range(taps)]) * scale_factor
    partial_sum = lax.psum_scatter(terms, "rep", scatter_dimension=1, tiled=True)
    weight_grad = lax.psum_scatter(partial_sum, "seq", scatter_dimension=2, tiled=True)
    return (input_grad[None], weight_grad)

def on_device(inputs, trunk_grad, weights):
    square = lax.axis_size("seq") == 4 and lax.axis_size("rep") % 8 == 0
    if square and weights.shape[2] % LANES == 0 and inputs.shape[2] % LANES == 0:
        return on_device_square(inputs, trunk_grad, weights)
    return on_device_plain(inputs, trunk_grad, weights)

def solution(mesh):
    in_specs = (P("rep", "seq", None), P("rep", None, "seq"), P(None, "rep", "seq"))
    out_specs = (P("rep", "seq", None), P(None, "rep", "seq"))
    return jax.shard_map(
        on_device, mesh=mesh, in_specs=in_specs, out_specs=out_specs, check_vma=False
    )
```

```python
import functools
import math

import jax
import jax.numpy as jnp
from jax import lax
from jax.experimental import pallas as pl
from jax.experimental.pallas import tpu as pltpu
from jax.sharding import PartitionSpec as P

LANES = 128
HALO = 32
EDGE = 16
MARGIN = HALO - EDGE
STEP = 64
SPLIT = 3
ROOT = math.sqrt(2.0 / math.pi)
CUBIC = 0.044715
SMALL = pl.CostEstimate(flops=1 << 20, bytes_accessed=1 << 16, transcendentals=0)
ANYWHERE = pl.BlockSpec(memory_space=pl.ANY)
ROW_OFFSETS = ((1, 1), (0, 1), (0, 0), (-1, 0), (-1, -1))
GRAD_PARTS = ((0, 0), (1, 0), (1, 1), (2, 1), (2, 2))

def from_peer(value, axis, distance):
    peers = lax.axis_size(axis)
    return lax.ppermute(value, axis, [(i, i ^ distance) for i in range(peers)])

def after(value, *earlier):
    return pl.pallas_call(
        lambda *refs: None,
        out_shape=jax.ShapeDtypeStruct(value.shape, value.dtype),
        in_specs=[ANYWHERE] * (1 + len(earlier)),
        out_specs=ANYWHERE,
        input_output_aliases={0: 0},
        name="after",
    )(value, *earlier)

def reduce_line(blocks, axis, count, unit):
    held, masks = [[0]], []
    while count > 1:
        masks.append(count - 1)
        held.append(held[-1] + [d ^ masks[-1] for d in held[-1]])
        count //= 2
    blocks, steps = dict(enumerate(blocks)), []
    for mask, keep in reversed(list(zip(masks, held))):
        leaving = jnp.stack([blocks[d ^ mask].astype(jnp.bfloat16) for d in keep])
        steps.append(from_peer(leaving, axis, mask * unit))
        if mask != masks[0]:
            blocks = {d: blocks[d] + steps[-1][n].astype(jnp.float32) for n, d in enumerate(keep)}
    return blocks[0], steps


def gather_line(value, axis, count, unit):
    found, mask = {0: value}, count - 1
    while mask:
        for distance in list(found):
            found[distance ^ mask] = from_peer(found[distance], axis, mask * unit)
        mask //= 2
    return [found[distance] for distance in range(count)]

def gelu_slope(x):
    tanh = jnp.tanh(ROOT * (x + CUBIC * (x * x * x)))
    return 0.5 * (1.0 + tanh) + 0.5 * x * (1.0 - tanh * tanh) * (
        ROOT * (1.0 + 3.0 * CUBIC * (x * x))
    )

def act_kernel(x_ref, out_ref, strip):
    width = x_ref.shape[2]

    @pl.loop(0, out_ref.shape[0] // STEP)
    def _(step):
        start = pl.multiple_of(step * STEP, STEP)
        x = x_ref[0, pl.ds(pl.multiple_of(2 * start, 2 * STEP), 2 * STEP), :].astype(jnp.float32)
        act = x * (0.5 * (1.0 + jnp.tanh(ROOT * (x + CUBIC * (x * x * x)))))
        for c in range(width // LANES):
            strip[c] = act[:, c * LANES : (c + 1) * LANES]
        for parity in range(2):
            for c in range(width // LANES):
                picked = strip[c, pl.ds(parity, STEP, stride=2), :].astype(jnp.bfloat16)
                left = parity * width + c * LANES
                out_ref[pl.ds(start, STEP), left : left + LANES] = picked

def activate(inputs):
    fine, width = inputs.shape[1:]
    return pl.pallas_call(
        act_kernel,
        out_shape=jax.ShapeDtypeStruct((fine // 2, 2 * width), jnp.bfloat16),
        in_specs=[pl.BlockSpec(memory_space=pltpu.VMEM)],
        out_specs=pl.BlockSpec(memory_space=pltpu.VMEM),
        scratch_shapes=[pltpu.VMEM((width // LANES, 2 * STEP, LANES), jnp.float32)],
        compiler_params=pltpu.CompilerParams(vmem_limit_bytes=24 << 20),
        cost_estimate=SMALL,
        name="act",
    )(inputs)

def kernel_messages(place, line, trunk_grad, coarse):
    taps, rows, block = line[0].shape
    planes, length = len(line), trunk_grad.shape[1]
    window = (coarse + 2 * HALO) // rows
    half = planes // 2

    def kernel(place, *refs):
        parts, trunk_ref = refs[:planes], refs[planes]
        beside_ref, below_ref, own_ref, edged, sem = refs[planes + 1 :]
        copy = pltpu.make_async_copy(trunk_ref.at[0], edged.at[pl.ds(HALO, length)], sem)
        copy.start()
        edged[:HALO] = jnp.zeros((HALO, block), jnp.bfloat16)
        edged[HALO + length :] = jnp.zeros((HALO, block), jnp.bfloat16)
        for j in range(planes):
            plane = place[1] // 2 ^ j
            for k in range(taps):
                spot = (plane // half * taps + k) * half + plane % half
                beside_ref[window // 2 + spot] = parts[j][k]
                below_ref[spot] = parts[j][k]
        copy.wait()

        def cut(out_ref, spot, distance, first, last):
            base = (place[0] ^ distance) * coarse
            for b in range(first, last):
                out_ref[spot + b - first] = edged[pl.ds(pl.multiple_of(base + b * rows, 16), rows), :]

        cut(beside_ref, 0, 3, 0, window // 2)
        cut(beside_ref, window // 2 + planes * taps, 1, 0, window)
        cut(below_ref, planes * taps, 3, window // 2, window)
        cut(below_ref, planes * taps + window // 2, 2, 0, window)
        cut(own_ref, 0, 0, 0, window)

    count = window // 2 + planes * taps + window
    return pl.pallas_call(
        kernel,
        out_shape=[
            jax.ShapeDtypeStruct((n, rows, block), jnp.bfloat16) for n in (count, count, window)
        ],
        grid_spec=pltpu.PrefetchScalarGridSpec(
            num_scalar_prefetch=1,
            grid=(1,),
            in_specs=[pl.BlockSpec(line[0].shape, lambda i, place: (0, 0, 0))] * planes + [ANYWHERE],
            out_specs=[
                pl.BlockSpec((n, rows, block), lambda i, place: (0, 0, 0))
                for n in (count, count, window)
            ],
            scratch_shapes=[
                pltpu.VMEM((length + 2 * HALO, block), jnp.bfloat16),
                pltpu.SemaphoreType.DMA,
            ],
        ),
        compiler_params=pltpu.CompilerParams(vmem_limit_bytes=32 << 20),
        cost_estimate=SMALL,
        name="kernel_messages",
    )(place, *line, trunk_grad)

def slope_kernel(x_ref, out_ref, scratch):
    width = x_ref.shape[2]

    @pl.loop(0, out_ref.shape[1] // 64)
    def _(step):
        start = pl.multiple_of(step * 64, 64)
        span = pl.ds(pl.multiple_of(2 * start, 128), 128)
        for c in range(width // LANES):
            lanes = slice(c * LANES, (c + 1) * LANES)
            scratch[c] = 0.5 * gelu_slope(x_ref[0, span, lanes].astype(jnp.float32))
            for parity in range(2):
                out_ref[parity, pl.ds(start, 64), lanes] = scratch[c, pl.ds(parity, 64, stride=2), :]

def half_slope(inputs):
    fine, width = inputs.shape[1:]
    return pl.pallas_call(
        slope_kernel,
        out_shape=jax.ShapeDtypeStruct((2, fine // 2, width), jnp.float32),
        in_specs=[pl.BlockSpec(memory_space=pltpu.VMEM)],
        out_specs=pl.BlockSpec(memory_space=pltpu.VMEM),
        scratch_shapes=[pltpu.VMEM((width // LANES, 128, LANES), jnp.float32)],
        compiler_params=pltpu.CompilerParams(vmem_limit_bytes=24 << 20),
        name="half_slope",
    )(inputs)

def start_act(place, coarse, layout, pieces, shifts_ref, held, shifts, sems, shift_sems):
    copies, row = [], 0
    for i, (distance, first, size, offset) in enumerate(layout):
        start = pl.multiple_of((place[0] ^ distance) * coarse + first, 16)
        spot = pl.ds(row, size)
        source = pieces[i].at[pl.ds(offset, size)]
        copies.append(pltpu.make_async_copy(source, held.at[spot], sems.at[i]))
        copies.append(
            pltpu.make_async_copy(shifts_ref.at[pl.ds(start, size)], shifts.at[spot], shift_sems.at[i])
        )
        row += size
    for copy in copies:
        copy.start()
    return copies

def early_terms(place, layout, pieces, shifts, coarse):
    both, columns = pieces[0].shape[1], shifts.shape[1]
    rows = sum(size for _, _, size, _ in layout)
    tile = 256

    def kernel(place, shifts_ref, *refs):
        pieces, total = refs[: len(layout)], refs[len(layout)]
        held, shifts, sems, shift_sems = refs[len(layout) + 1 :]
        copies = start_act(
            place, coarse, layout, pieces, shifts_ref, held, shifts, sems, shift_sems
        )
        for copy in copies:
            copy.wait()

        @pl.loop(0, both // tile)
        def _(i):
            span = pl.ds(pl.multiple_of(i * tile, tile), tile)
            total[span, :] = lax.dot_general(
                held[:, span], shifts[...], (((0,), (0,)), ((), ())), preferred_element_type=jnp.float32
            )

    return pl.pallas_call(
        kernel,
        out_shape=jax.ShapeDtypeStruct((both, columns), jnp.float32),
        grid_spec=pltpu.PrefetchScalarGridSpec(
            num_scalar_prefetch=1,
            grid=(1,),
            in_specs=[ANYWHERE] * (1 + len(pieces)),
            out_specs=pl.BlockSpec((both, columns), lambda i, place: (0, 0)),
            scratch_shapes=[
                pltpu.VMEM((rows, both), jnp.bfloat16),
                pltpu.VMEM((rows, columns), jnp.bfloat16),
                pltpu.SemaphoreType.DMA((len(pieces),)),
                pltpu.SemaphoreType.DMA((len(pieces),)),
            ],
        ),
        compiler_params=pltpu.CompilerParams(vmem_limit_bytes=48 << 20),
        cost_estimate=SMALL,
        name="weight_grad_early",
    )(place, shifts, *pieces)

def late_terms(place, layout, pieces, shifts, early, coarse, scale, planes, taps, rows):
    both, columns = early.shape
    width, block = both // 2, columns // 3
    count = sum(size for _, _, size, _ in layout)
    tile = 256
    shape = (planes, taps, rows, block)

    def kernel(place, shifts_ref, early_ref, *refs):
        pieces, (mine_ref, *theirs_refs) = refs[: len(layout)], refs[len(layout) : len(layout) + 3]
        held, shifts, total, sems, shift_sems, early_sems = refs[len(layout) + 3 :]
        core, plane = place[1] % 2, place[1] // 2
        copies = start_act(
            place, coarse, layout, pieces, shifts_ref, held, shifts, sems, shift_sems
        )

        def fetch(i):
            span = pl.ds(pl.multiple_of(i * tile, tile), tile)
            return pltpu.make_async_copy(early_ref.at[span], total.at[span], early_sems.at[i])

        for i in range(both // tile):
            fetch(i).start()
        for copy in copies:
            copy.wait()

        @pl.loop(0, both // tile)
        def _(i):
            span = pl.ds(pl.multiple_of(i * tile, tile), tile)
            term = lax.dot_general(
                held[:, span], shifts[...], (((0,), (0,)), ((), ())), preferred_element_type=jnp.float32
            )
            fetch(i).wait()
            total[span, :] += term

        def finish(out_ref, at, j, parity, kind):
            start = ((plane ^ j) * 2 + parity) * rows
            even = pl.ds(pl.multiple_of(start, 16), rows)
            odd = pl.ds(pl.multiple_of(width + start, 16), rows)
            for k, (left, right) in enumerate(GRAD_PARTS):
                term = total[even, left * block : (left + 1) * block]
                term += total[odd, right * block : (right + 1) * block]
                out_ref[at, k] = (scale * term).astype(kind)

        for which, out_ref in enumerate(theirs_refs):

            @pl.loop(0, planes // 2)
            def _(at):
                finish(out_ref, at, at + which * (planes // 2), 1 - core, jnp.bfloat16)

        @pl.loop(0, planes)
        def _(j):
            finish(mine_ref, j, j, core, jnp.float32)

    half_shape = (planes // 2, *shape[1:])
    whole = pl.BlockSpec(shape, lambda i, place: (0, 0, 0, 0))
    half = pl.BlockSpec(half_shape, lambda i, place: (0, 0, 0, 0))
    return pl.pallas_call(
        kernel,
        out_shape=(
            jax.ShapeDtypeStruct(shape, jnp.float32),
            jax.ShapeDtypeStruct(half_shape, jnp.bfloat16),
            jax.ShapeDtypeStruct(half_shape, jnp.bfloat16),
        ),
        grid_spec=pltpu.PrefetchScalarGridSpec(
            num_scalar_prefetch=1,
            grid=(1,),
            in_specs=[ANYWHERE] * (2 + len(pieces)),
            out_specs=[whole, half, half],
            scratch_shapes=[
                pltpu.VMEM((count, both), jnp.bfloat16),
                pltpu.VMEM((count, columns), jnp.bfloat16),
                pltpu.VMEM((both, columns), jnp.float32),
                pltpu.SemaphoreType.DMA((len(pieces),)),
                pltpu.SemaphoreType.DMA((len(pieces),)),
                pltpu.SemaphoreType.DMA((both // tile,)),
            ],
        ),
        compiler_params=pltpu.CompilerParams(vmem_limit_bytes=48 << 20),
        cost_estimate=SMALL,
        name="weight_grad_late",
    )(place, shifts, early, *pieces)

def shifted_total(products, base, lanes, parity):
    total = None
    for by in (0, 1, -1):
        wanted = [k for k in range(products.shape[0]) if ROW_OFFSETS[k][parity] == by]
        if wanted:
            near = pl.ds(base + MARGIN - 8, STEP + 16)
            part = sum(products[k, near, lanes] for k in wanted)[8 + by : 8 + by + STEP]
            total = part if total is None else total + part
    return total

def gradient_stage(place, windows, taps, pieces, distances, slope, begun, shape):
    _, fine, width = shape
    coarse, seqs = fine // 2, lax.axis_size("seq")
    rows, block = pieces[0][0].shape[-2:]
    planes = width // (2 * rows)
    half = planes // 2
    window, used = coarse + 2 * HALO, coarse + 2 * MARGIN
    depth, planar = len(distances) * block, (2, coarse, width)
    last = begun is not None
    needed = list(range(seqs)) if last else distances
    parts = [(d, *part) for d in needed for part in windows[d]]
    operands = [part[1] for part in parts] + [piece[0] for piece in pieces]
    operands += [slope, begun] if last else []

    def body(place, *refs):
        own, refs = refs[: len(parts)], refs[len(parts) :]
        sources, refs = refs[: len(pieces)], refs[len(pieces) :]
        if last:
            (slope_ref, begun_ref), refs = refs[:2], refs[2:]
        out_ref, wv, gv, products, sems, grad_sems = refs[:6]
        me, core = place[0], place[1] % 2

        def kernel_copies(first):
            for number, (array, start, plane, count, flip, distance) in enumerate(pieces):
                spot = pl.ds(distances.index(distance) * block, block)
                if first != (start is not None):
                    continue
                for k in range(SPLIT if first else taps - SPLIT):
                    for h in range(count // half):
                        span = pl.ds(plane + h * half, half)
                        if first:
                            source = sources[number].at[pl.ds(start + (h * SPLIT + k) * half, half)]
                        else:
                            source = sources[number].at[span, distance, k]
                        tap = k if first else SPLIT + k
                        target = wv.at[tap, span, core ^ flip, :, spot]
                        sem = sems.at[tap, number, h]
                        yield tap, pltpu.make_async_copy(source, target, sem)

        def window_copies(target_of, sems):
            for number, (distance, _, start, first, count) in enumerate(parts):
                for b in range(count):
                    target = target_of(distance, pl.ds((first + b) * rows, rows))
                    if target is not None:
                        source = own[number].at[start + b]
                        yield pltpu.make_async_copy(source, target, sems.at[number, b])

        def into_window(distance, span):
            if distance not in distances:
                return None
            return gv.at[span, pl.ds(distances.index(distance) * block, block)]

        early = list(window_copies(into_window, grad_sems))
        late = []
        if last:
            sums, slopes, strip, skips, sum_sems, skip_sems = refs[6:]
            late.append(pltpu.make_async_copy(begun_ref, sums, sum_sems.at[0]))
            late.append(pltpu.make_async_copy(slope_ref, slopes, sum_sems.at[1]))
            late += window_copies(lambda d, span: skips.at[me ^ d, span], skip_sems)
        for copy in early:
            copy.start()
        arriving = sorted([*kernel_copies(True), *kernel_copies(False)], key=lambda pair: pair[0])
        for _, copy in arriving:
            copy.start()
        for copy in late:
            copy.start()
        for copy in early:
            copy.wait()
        for k in range(taps):
            for tap, copy in arriving:
                if tap == k:
                    copy.wait()
            for part in range(2):
                kernel = wv[k, part * half : (part + 1) * half].reshape(2 * half * rows, depth)
                lanes = slice(part * 2 * half * rows, (part + 1) * 2 * half * rows)
                products[k, :, lanes] = lax.dot_general(
                    gv[EDGE : EDGE + used],
                    kernel,
                    (((1,), (1,)), ((), ())),
                    preferred_element_type=jnp.float32,
                )

        for copy in late:
            copy.wait()

        @pl.loop(0, coarse // STEP)
        def _(i):
            base = pl.multiple_of(i * STEP, STEP)
            spot, span = pl.ds(base, STEP), pl.ds(pl.multiple_of(2 * base, 2 * STEP), 2 * STEP)
            for c in range(width // LANES):
                lanes = slice(c * LANES, (c + 1) * LANES)
                if last:
                    left = c * LANES % block
                    skip = skips[c * LANES // block, pl.ds(base + HALO, STEP), left : left + LANES]
                    skip = 0.5 * skip.astype(jnp.float32)
                for parity in range(2):
                    total = shifted_total(products, base, lanes, parity)
                    if last:
                        total = (total + sums[parity, spot, lanes]) * slopes[parity, spot, lanes]
                        strip[c, pl.ds(parity, STEP, stride=2), :] = total + skip
                    else:
                        out_ref[parity, spot, lanes] = total
                if last:
                    out_ref[0, span, lanes] = strip[c].astype(jnp.bfloat16)

    out_shape = jax.ShapeDtypeStruct(shape if last else planar, jnp.bfloat16 if last else jnp.float32)
    scratch = [
        pltpu.VMEM((taps, planes, 2, rows, depth), jnp.bfloat16),
        pltpu.VMEM((window, depth), jnp.bfloat16),
        pltpu.VMEM((taps, used, width), jnp.float32),
        pltpu.SemaphoreType.DMA((taps, len(pieces), 2)),
        pltpu.SemaphoreType.DMA((len(parts), window // rows)),
    ]
    if last:
        scratch += [
            pltpu.VMEM(planar, jnp.float32),
            pltpu.VMEM(planar, jnp.float32),
            pltpu.VMEM((width // LANES, 2 * STEP, LANES), jnp.float32),
            pltpu.VMEM((seqs, window, block), jnp.bfloat16),
            pltpu.SemaphoreType.DMA((2,)),
            pltpu.SemaphoreType.DMA((len(parts), window // rows)),
        ]
    return pl.pallas_call(
        body,
        out_shape=out_shape,
        grid_spec=pltpu.PrefetchScalarGridSpec(
            num_scalar_prefetch=1,
            grid=(1,),
            in_specs=[ANYWHERE] * len(operands),
            out_specs=pl.BlockSpec(out_shape.shape, lambda i, place: (0, 0, 0)),
            scratch_shapes=scratch,
        ),
        compiler_params=pltpu.CompilerParams(vmem_limit_bytes=56 << 20),
        cost_estimate=SMALL,
        name="input_grad",
    )(place, *operands)

def stack_planes(place, line):
    count = len(line)

    def kernel(place, *refs):
        parts, out_ref = refs[:count], refs[count]
        for j in range(count):
            out_ref[place[1] // 2 ^ j] = parts[j][...]

    shape = line[0].shape
    return pl.pallas_call(
        kernel,
        out_shape=jax.ShapeDtypeStruct((count, *shape), line[0].dtype),
        grid_spec=pltpu.PrefetchScalarGridSpec(
            num_scalar_prefetch=1,
            grid=(1,),
            in_specs=[pl.BlockSpec(shape, lambda i, place: (0,) * len(shape))] * count,
            out_specs=pl.BlockSpec((count, *shape), lambda i, place: (0,) * (1 + len(shape))),
        ),
        compiler_params=pltpu.CompilerParams(vmem_limit_bytes=24 << 20),
        cost_estimate=SMALL,
        name="stack_planes",
    )(place, *line)

def on_device_square(inputs, trunk_grad, weights):
    seqs, reps = lax.axis_size("seq"), lax.axis_size("rep")
    me, rep = lax.axis_index("seq"), lax.axis_index("rep")
    place = jnp.stack([me, rep]).astype(jnp.int32)
    taps, rows, block = weights.shape
    fine = inputs.shape[1]
    coarse, planes = fine // 2, reps // 2
    half = coarse // 2

    last_taps = weights[SPLIT:]
    across = [last_taps] + [from_peer(last_taps, "seq", d) for d in range(1, seqs)]

    act = after(activate(inputs), *across[1:])
    beside, below = from_peer(act, "seq", 1), from_peer(act, "seq", 2)
    slope = half_slope(inputs)
    line = gather_line(weights[:SPLIT], "rep", planes, 2)
    line_across = gather_line(after(jnp.stack(across), act, *line[1:]), "rep", planes, 2)
    crossing = (line_across[1], line_across[planes - 1])
    trunk = trunk_grad[0]
    zeros = jnp.zeros((1, block), jnp.bfloat16)
    later = jnp.concatenate([trunk[1:], zeros])
    earlier = jnp.concatenate([zeros, trunk[:-1]])
    shifts = jnp.concatenate([later, trunk, earlier], axis=1)
    to_beside, to_below, own_window = kernel_messages(place, line, trunk_grad, coarse)
    ready = (slope, shifts, to_beside, *crossing)
    top, bottom = after(beside[:half], *ready), after(below[half:], *ready)
    far_top, far_bottom = from_peer(top, "seq", 2), from_peer(bottom, "seq", 1)

    scale = 0.5 * float(fine * seqs * reps) ** (-0.5)
    near_rows = [(d, 0, coarse, 0) for d in range(3)]
    far_rows = [(3, 0, half, 0), (3, half, half, 0)]
    early = early_terms(place, near_rows, [act, beside, below], shifts, coarse)
    line_across[2] = after(line_across[2], early)
    lines = stack_planes(place, line_across)
    far_top, far_bottom = after(far_top, early, lines), after(far_bottom, early, lines)

    to_beside, to_below = (
        after(message, far_top, far_bottom) for message in (to_beside, to_below)
    )
    kept_beside, kept_below = from_peer(to_beside, "seq", 1), from_peer(to_below, "seq", 2)
    other_column, other_lines = from_peer(to_below, "rep", 1), from_peer(lines, "rep", 1)

    mine, *theirs = late_terms(
        place, far_rows, [far_top, far_bottom], shifts, early, coarse, scale, planes, taps, rows
    )
    arrived = [from_peer(part, "rep", 1) for part in theirs]
    pairs = []
    for j in range(planes):
        part = arrived[j // (planes // 2)][j % (planes // 2)]
        pairs.append(mine[j] + part.astype(jnp.float32))
    weight_grad, steps = reduce_line(pairs, "rep", planes, 2)

    window = (coarse + 2 * HALO) // rows
    count, side = planes * SPLIT, window // 2
    far_first = from_peer(kept_beside[: side + count // 2], "seq", 2)
    far_second = from_peer(kept_below[count // 2 : count + side], "seq", 1)

    windows = [
        [(own_window, 0, 0, window)],
        [(kept_beside, side + count, 0, window)],
        [(kept_below, count + side, 0, window)],
    ]
    stage = functools.partial(gradient_stage, place, taps=taps, slope=slope, shape=inputs.shape)
    soon = [(to_below, 0, 0, planes, 0, 0), (other_column, 0, 0, planes, 1, 0)]
    for part, start, distance in ((kept_beside, side, 1), (kept_below, 0, 2)):
        soon.append((part, start, 0, planes, 0, distance))
        soon.append((from_peer(part, "rep", 1), start, 0, planes, 1, distance))
    crossed = [
        (part, None, 0, planes, flip, d)
        for flip, part in enumerate((lines, other_lines))
        for d in range(seqs)
    ]
    near = [piece for piece in crossed if piece[-1] < 3]
    begun = stage(windows, pieces=soon + near, distances=[0, 1, 2], begun=None)
    far_first, far_second = after(far_first, begun, *steps[:1]), after(far_second, begun, *steps[:1])
    windows.append([(far_first, 0, 0, side), (far_second, count // 2, side, side)])
    rest = [piece for piece in crossed if piece[-1] == 3]
    for part, start, plane in ((far_first, side, 0), (far_second, 0, planes // 2)):
        rest.append((part, start, plane, planes // 2, 0, 3))
        rest.append((from_peer(part, "rep", 1), start, plane, planes // 2, 1, 3))
    input_grad = stage(windows, pieces=rest, distances=[3], begun=begun)
    weight_grad = weight_grad + after(steps[-1], input_grad)[0].astype(jnp.float32)
    return (input_grad, weight_grad)


def with_halo(value, sides, width):
    for axis, dim in sides:
        peers, length = (lax.axis_size(axis), value.shape[dim])
        up = [(i, (i + 1) % peers) for i in range(peers - 1)]
        down = [(j, i) for i, j in up]
        last = lax.slice_in_dim(value, length - width, length, axis=dim)
        leading = lax.slice_in_dim(value, 0, width, axis=dim)
        before = lax.ppermute(last, axis, up)
        after = lax.ppermute(leading, axis, down)
        value = jnp.concatenate([before, value, after], axis=dim)
    return value

def contract_last(left, right):
    return lax.dot_general(
        left, right, (((1,), (1,)), ((), ())), preferred_element_type=jnp.float32
    )

def contract_first(left, right):
    return lax.dot_general(
        left, right, (((0,), (0,)), ((), ())), preferred_element_type=jnp.float32
    )

def on_device_plain(inputs, trunk_grad, weights):
    taps = weights.shape[0]
    grad = lax.all_to_all(trunk_grad, "seq", split_axis=1, concat_axis=2, tiled=True)
    grad_up = jnp.repeat(grad.astype(jnp.float32) * 0.5, 2, axis=1).astype(jnp.bfloat16)
    rows = grad_up.shape[1]
    padded = with_halo(grad_up, (("seq", 1),), 2)
    shifts = [padded[0, 4 - k : 4 - k + rows] for k in range(taps)]
    inputs_f = inputs[0].astype(jnp.float32)
    act_vals, back = jax.vjp(jax.nn.gelu, inputs_f)
    slope = back(jnp.ones_like(inputs_f))[0]
    act = act_vals.astype(jnp.bfloat16)
    in_width = inputs.shape[2]
    columns = lax.all_gather(weights, "seq", axis=2, tiled=True)
    piece = lax.all_gather(columns, "rep", axis=1, tiled=True)
    result = contract_last(shifts[0], piece[0])
    for project_k in range(1, taps):
        result = result + contract_last(shifts[project_k], piece[project_k])
    input_grad = (result * slope + grad_up[0, :, :in_width].astype(jnp.float32)).astype(
        jnp.bfloat16
    )
    scale_factor = float(rows * lax.axis_size("seq") * lax.axis_size("rep")) ** (-0.5)
    terms = jnp.stack([contract_first(act, shifts[k]) for k in range(taps)]) * scale_factor
    partial_sum = lax.psum_scatter(terms, "rep", scatter_dimension=1, tiled=True)
    weight_grad = lax.psum_scatter(partial_sum, "seq", scatter_dimension=2, tiled=True)
    return (input_grad[None], weight_grad)

def on_device(inputs, trunk_grad, weights):
    square = lax.axis_size("seq") == 4 and lax.axis_size("rep") % 8 == 0
    if square and weights.shape[2] % LANES == 0 and inputs.shape[2] % LANES == 0:
        return on_device_square(inputs, trunk_grad, weights)
    return on_device_plain(inputs, trunk_grad, weights)

def solution(mesh):
    in_specs = (P("rep", "seq", None), P("rep", None, "seq"), P(None, "rep", "seq"))
    out_specs = (P("rep", "seq", None), P(None, "rep", "seq"))
    return jax.shard_map(
        on_device, mesh=mesh, in_specs=in_specs, out_specs=out_specs, check_vma=False
    )
```

```python
import functools
import math

import jax
import jax.numpy as jnp
from jax import lax
from jax.experimental import pallas as pl
from jax.experimental.pallas import tpu as pltpu
from jax.sharding import PartitionSpec as P

LANES = 128
HALO = 32
EDGE = 16
MARGIN = HALO - EDGE
STEP = 64
SPLIT = 2
ROOT = math.sqrt(2.0 / math.pi)
CUBIC = 0.044715
SMALL = pl.CostEstimate(flops=1 << 20, bytes_accessed=1 << 16, transcendentals=0)
ANYWHERE = pl.BlockSpec(memory_space=pl.ANY)
ROW_OFFSETS = ((1, 1), (0, 1), (0, 0), (-1, 0), (-1, -1))
GRAD_PARTS = ((0, 0), (1, 0), (1, 1), (2, 1), (2, 2))

def from_peer(value, axis, distance):
    peers = lax.axis_size(axis)
    return lax.ppermute(value, axis, [(i, i ^ distance) for i in range(peers)])

def after(value, *earlier):
    return pl.pallas_call(
        lambda *refs: None,
        out_shape=jax.ShapeDtypeStruct(value.shape, value.dtype),
        in_specs=[ANYWHERE] * (1 + len(earlier)),
        out_specs=ANYWHERE,
        input_output_aliases={0: 0},
        name="after",
    )(value, *earlier)

def reduce_line(blocks, axis, count, unit):
    held, masks = [[0]], []
    while count > 1:
        masks.append(count - 1)
        held.append(held[-1] + [d ^ masks[-1] for d in held[-1]])
        count //= 2
    blocks, steps = dict(enumerate(blocks)), []
    for mask, keep in reversed(list(zip(masks, held))):
        leaving = jnp.stack([blocks[d ^ mask].astype(jnp.bfloat16) for d in keep])
        steps.append(from_peer(leaving, axis, mask * unit))
        if mask != masks[0]:
            blocks = {d: blocks[d] + steps[-1][n].astype(jnp.float32) for n, d in enumerate(keep)}
    return blocks[0], steps


def gather_line(value, axis, count, unit):
    found, mask = {0: value}, count - 1
    while mask:
        for distance in list(found):
            found[distance ^ mask] = from_peer(found[distance], axis, mask * unit)
        mask //= 2
    return [found[distance] for distance in range(count)]

def gelu_slope(x):
    tanh = jnp.tanh(ROOT * (x + CUBIC * (x * x * x)))
    return 0.5 * (1.0 + tanh) + 0.5 * x * (1.0 - tanh * tanh) * (
        ROOT * (1.0 + 3.0 * CUBIC * (x * x))
    )

def act_kernel(x_ref, out_ref, strip):
    width = x_ref.shape[2]

    @pl.loop(0, out_ref.shape[0] // STEP)
    def _(step):
        start = pl.multiple_of(step * STEP, STEP)
        x = x_ref[0, pl.ds(pl.multiple_of(2 * start, 2 * STEP), 2 * STEP), :].astype(jnp.float32)
        act = x * (0.5 * (1.0 + jnp.tanh(ROOT * (x + CUBIC * (x * x * x)))))
        for c in range(width // LANES):
            strip[c] = act[:, c * LANES : (c + 1) * LANES]
        for parity in range(2):
            for c in range(width // LANES):
                picked = strip[c, pl.ds(parity, STEP, stride=2), :].astype(jnp.bfloat16)
                left = parity * width + c * LANES
                out_ref[pl.ds(start, STEP), left : left + LANES] = picked

def activate(inputs):
    fine, width = inputs.shape[1:]
    return pl.pallas_call(
        act_kernel,
        out_shape=jax.ShapeDtypeStruct((fine // 2, 2 * width), jnp.bfloat16),
        in_specs=[pl.BlockSpec(memory_space=pltpu.VMEM)],
        out_specs=pl.BlockSpec(memory_space=pltpu.VMEM),
        scratch_shapes=[pltpu.VMEM((width // LANES, 2 * STEP, LANES), jnp.float32)],
        compiler_params=pltpu.CompilerParams(vmem_limit_bytes=24 << 20),
        cost_estimate=SMALL,
        name="act",
    )(inputs)

def kernel_messages(place, line, trunk_grad, coarse):
    taps, rows, block = line[0].shape
    planes, length = len(line), trunk_grad.shape[1]
    window = (coarse + 2 * HALO) // rows
    half = planes // 2

    def kernel(place, *refs):
        parts, trunk_ref = refs[:planes], refs[planes]
        beside_ref, below_ref, own_ref, edged, sem = refs[planes + 1 :]
        copy = pltpu.make_async_copy(trunk_ref.at[0], edged.at[pl.ds(HALO, length)], sem)
        copy.start()
        edged[:HALO] = jnp.zeros((HALO, block), jnp.bfloat16)
        edged[HALO + length :] = jnp.zeros((HALO, block), jnp.bfloat16)
        for j in range(planes):
            plane = place[1] // 2 ^ j
            for k in range(taps):
                spot = (plane // half * taps + k) * half + plane % half
                beside_ref[window // 2 + spot] = parts[j][k]
                below_ref[spot] = parts[j][k]
        copy.wait()

        def cut(out_ref, spot, distance, first, last):
            base = (place[0] ^ distance) * coarse
            for b in range(first, last):
                out_ref[spot + b - first] = edged[pl.ds(pl.multiple_of(base + b * rows, 16), rows), :]

        cut(beside_ref, 0, 3, 0, window // 2)
        cut(beside_ref, window // 2 + planes * taps, 1, 0, window)
        cut(below_ref, planes * taps, 3, window // 2, window)
        cut(below_ref, planes * taps + window // 2, 2, 0, window)
        cut(own_ref, 0, 0, 0, window)

    count = window // 2 + planes * taps + window
    return pl.pallas_call(
        kernel,
        out_shape=[
            jax.ShapeDtypeStruct((n, rows, block), jnp.bfloat16) for n in (count, count, window)
        ],
        grid_spec=pltpu.PrefetchScalarGridSpec(
            num_scalar_prefetch=1,
            grid=(1,),
            in_specs=[pl.BlockSpec(line[0].shape, lambda i, place: (0, 0, 0))] * planes + [ANYWHERE],
            out_specs=[
                pl.BlockSpec((n, rows, block), lambda i, place: (0, 0, 0))
                for n in (count, count, window)
            ],
            scratch_shapes=[
                pltpu.VMEM((length + 2 * HALO, block), jnp.bfloat16),
                pltpu.SemaphoreType.DMA,
            ],
        ),
        compiler_params=pltpu.CompilerParams(vmem_limit_bytes=32 << 20),
        cost_estimate=SMALL,
        name="kernel_messages",
    )(place, *line, trunk_grad)

def slope_kernel(x_ref, out_ref, scratch):
    width = x_ref.shape[2]

    @pl.loop(0, out_ref.shape[1] // 64)
    def _(step):
        start = pl.multiple_of(step * 64, 64)
        span = pl.ds(pl.multiple_of(2 * start, 128), 128)
        for c in range(width // LANES):
            lanes = slice(c * LANES, (c + 1) * LANES)
            scratch[c] = 0.5 * gelu_slope(x_ref[0, span, lanes].astype(jnp.float32))
            for parity in range(2):
                out_ref[parity, pl.ds(start, 64), lanes] = scratch[c, pl.ds(parity, 64, stride=2), :]

def half_slope(inputs):
    fine, width = inputs.shape[1:]
    return pl.pallas_call(
        slope_kernel,
        out_shape=jax.ShapeDtypeStruct((2, fine // 2, width), jnp.float32),
        in_specs=[pl.BlockSpec(memory_space=pltpu.VMEM)],
        out_specs=pl.BlockSpec(memory_space=pltpu.VMEM),
        scratch_shapes=[pltpu.VMEM((width // LANES, 128, LANES), jnp.float32)],
        compiler_params=pltpu.CompilerParams(vmem_limit_bytes=24 << 20),
        name="half_slope",
    )(inputs)

def start_act(place, coarse, layout, pieces, shifts_ref, held, shifts, sems, shift_sems):
    copies, row = [], 0
    for i, (distance, first, size, offset) in enumerate(layout):
        start = pl.multiple_of((place[0] ^ distance) * coarse + first, 16)
        spot = pl.ds(row, size)
        source = pieces[i].at[pl.ds(offset, size)]
        copies.append(pltpu.make_async_copy(source, held.at[spot], sems.at[i]))
        copies.append(
            pltpu.make_async_copy(shifts_ref.at[pl.ds(start, size)], shifts.at[spot], shift_sems.at[i])
        )
        row += size
    for copy in copies:
        copy.start()
    return copies

def early_terms(place, layout, pieces, shifts, coarse, earlier):
    both, columns = pieces[0].shape[1], shifts.shape[1]
    rows = sum(size for _, _, size, _ in layout)
    tile = 256

    def kernel(place, shifts_ref, *refs):
        pieces, total = refs[: len(layout)], refs[len(layout) + len(earlier)]
        held, shifts, sems, shift_sems = refs[len(layout) + len(earlier) + 1 :]
        copies = start_act(
            place, coarse, layout, pieces, shifts_ref, held, shifts, sems, shift_sems
        )
        for copy in copies:
            copy.wait()

        @pl.loop(0, both // tile)
        def _(i):
            span = pl.ds(pl.multiple_of(i * tile, tile), tile)
            total[span, :] = lax.dot_general(
                held[:, span], shifts[...], (((0,), (0,)), ((), ())), preferred_element_type=jnp.float32
            )

    return pl.pallas_call(
        kernel,
        out_shape=jax.ShapeDtypeStruct((both, columns), jnp.float32),
        grid_spec=pltpu.PrefetchScalarGridSpec(
            num_scalar_prefetch=1,
            grid=(1,),
            in_specs=[ANYWHERE] * (1 + len(pieces) + len(earlier)),
            out_specs=pl.BlockSpec((both, columns), lambda i, place: (0, 0)),
            scratch_shapes=[
                pltpu.VMEM((rows, both), jnp.bfloat16),
                pltpu.VMEM((rows, columns), jnp.bfloat16),
                pltpu.SemaphoreType.DMA((len(pieces),)),
                pltpu.SemaphoreType.DMA((len(pieces),)),
            ],
        ),
        compiler_params=pltpu.CompilerParams(vmem_limit_bytes=48 << 20),
        cost_estimate=SMALL,
        name="weight_grad_early",
    )(place, shifts, *pieces, *earlier)

def late_terms(place, layout, pieces, shifts, early, coarse, scale, planes, taps, rows, earlier):
    both, columns = early.shape
    width, block = both // 2, columns // 3
    count = sum(size for _, _, size, _ in layout)
    tile = 256
    shape = (planes, taps, rows, block)

    def kernel(place, shifts_ref, early_ref, *refs):
        pieces, refs = refs[: len(layout)], refs[len(layout) + len(earlier) :]
        mine_ref, *theirs_refs = refs[:3]
        held, shifts, total, sems, shift_sems, early_sems = refs[3:]
        core, plane = place[1] % 2, place[1] // 2
        copies = start_act(
            place, coarse, layout, pieces, shifts_ref, held, shifts, sems, shift_sems
        )

        def fetch(i):
            span = pl.ds(pl.multiple_of(i * tile, tile), tile)
            return pltpu.make_async_copy(early_ref.at[span], total.at[span], early_sems.at[i])

        for i in range(both // tile):
            fetch(i).start()
        for copy in copies:
            copy.wait()

        @pl.loop(0, both // tile)
        def _(i):
            span = pl.ds(pl.multiple_of(i * tile, tile), tile)
            term = lax.dot_general(
                held[:, span], shifts[...], (((0,), (0,)), ((), ())), preferred_element_type=jnp.float32
            )
            fetch(i).wait()
            total[span, :] += term

        def finish(out_ref, at, j, parity, kind):
            start = ((plane ^ j) * 2 + parity) * rows
            even = pl.ds(pl.multiple_of(start, 16), rows)
            odd = pl.ds(pl.multiple_of(width + start, 16), rows)
            for k, (left, right) in enumerate(GRAD_PARTS):
                term = total[even, left * block : (left + 1) * block]
                term += total[odd, right * block : (right + 1) * block]
                out_ref[at, k] = (scale * term).astype(kind)

        for which, out_ref in enumerate(theirs_refs):

            @pl.loop(0, planes // 2)
            def _(at):
                finish(out_ref, at, at + which * (planes // 2), 1 - core, jnp.bfloat16)

        @pl.loop(0, planes)
        def _(j):
            finish(mine_ref, j, j, core, jnp.float32)

    half_shape = (planes // 2, *shape[1:])
    whole = pl.BlockSpec(shape, lambda i, place: (0, 0, 0, 0))
    half = pl.BlockSpec(half_shape, lambda i, place: (0, 0, 0, 0))
    return pl.pallas_call(
        kernel,
        out_shape=(
            jax.ShapeDtypeStruct(shape, jnp.float32),
            jax.ShapeDtypeStruct(half_shape, jnp.bfloat16),
            jax.ShapeDtypeStruct(half_shape, jnp.bfloat16),
        ),
        grid_spec=pltpu.PrefetchScalarGridSpec(
            num_scalar_prefetch=1,
            grid=(1,),
            in_specs=[ANYWHERE] * (2 + len(pieces) + len(earlier)),
            out_specs=[whole, half, half],
            scratch_shapes=[
                pltpu.VMEM((count, both), jnp.bfloat16),
                pltpu.VMEM((count, columns), jnp.bfloat16),
                pltpu.VMEM((both, columns), jnp.float32),
                pltpu.SemaphoreType.DMA((len(pieces),)),
                pltpu.SemaphoreType.DMA((len(pieces),)),
                pltpu.SemaphoreType.DMA((both // tile,)),
            ],
        ),
        compiler_params=pltpu.CompilerParams(vmem_limit_bytes=48 << 20),
        cost_estimate=SMALL,
        name="weight_grad_late",
    )(place, shifts, early, *pieces, *earlier)

def shifted_total(products, base, lanes, parity):
    total = None
    for by in (0, 1, -1):
        wanted = [k for k in range(products.shape[0]) if ROW_OFFSETS[k][parity] == by]
        if wanted:
            near = pl.ds(base + MARGIN - 8, STEP + 16)
            part = sum(products[k, near, lanes] for k in wanted)[8 + by : 8 + by + STEP]
            total = part if total is None else total + part
    return total

def gradient_stage(place, windows, taps, pieces, distances, slope, begun, shape):
    _, fine, width = shape
    coarse, seqs = fine // 2, lax.axis_size("seq")
    rows, block = pieces[0][0].shape[-2:]
    planes = width // (2 * rows)
    half = planes // 2
    window, used = coarse + 2 * HALO, coarse + 2 * MARGIN
    depth, planar = len(distances) * block, (2, coarse, width)
    last = begun is not None
    needed = list(range(seqs)) if last else distances
    parts = [(d, *part) for d in needed for part in windows[d]]
    operands = [part[1] for part in parts] + [piece[0] for piece in pieces]
    operands += [slope, begun] if last else []

    def body(place, *refs):
        own, refs = refs[: len(parts)], refs[len(parts) :]
        sources, refs = refs[: len(pieces)], refs[len(pieces) :]
        if last:
            (slope_ref, begun_ref), refs = refs[:2], refs[2:]
        out_ref, wv, gv, products, sems, grad_sems = refs[:6]
        me, core = place[0], place[1] % 2

        def kernel_copies(first):
            for number, (array, start, plane, count, flip, distance) in enumerate(pieces):
                spot = pl.ds(distances.index(distance) * block, block)
                if first != (start is not None):
                    continue
                for k in range(SPLIT if first else taps - SPLIT):
                    for h in range(count // half):
                        span = pl.ds(plane + h * half, half)
                        if first:
                            source = sources[number].at[pl.ds(start + (h * SPLIT + k) * half, half)]
                        else:
                            source = sources[number].at[span, distance, k]
                        tap = k if first else SPLIT + k
                        target = wv.at[tap, span, core ^ flip, :, spot]
                        sem = sems.at[tap, number, h]
                        yield tap, pltpu.make_async_copy(source, target, sem)

        def window_copies(target_of, sems):
            for number, (distance, _, start, first, count) in enumerate(parts):
                for b in range(count):
                    target = target_of(distance, pl.ds((first + b) * rows, rows))
                    if target is not None:
                        source = own[number].at[start + b]
                        yield pltpu.make_async_copy(source, target, sems.at[number, b])

        def into_window(distance, span):
            if distance not in distances:
                return None
            return gv.at[span, pl.ds(distances.index(distance) * block, block)]

        early = list(window_copies(into_window, grad_sems))
        late = []
        if last:
            sums, slopes, strip, skips, sum_sems, skip_sems = refs[6:]
            late.append(pltpu.make_async_copy(begun_ref, sums, sum_sems.at[0]))
            late.append(pltpu.make_async_copy(slope_ref, slopes, sum_sems.at[1]))
            late += window_copies(lambda d, span: skips.at[me ^ d, span], skip_sems)
        for copy in early:
            copy.start()
        arriving = sorted([*kernel_copies(True), *kernel_copies(False)], key=lambda pair: pair[0])
        for _, copy in arriving:
            copy.start()
        for copy in late:
            copy.start()
        for copy in early:
            copy.wait()
        for k in range(taps):
            for tap, copy in arriving:
                if tap == k:
                    copy.wait()
            for part in range(2):
                kernel = wv[k, part * half : (part + 1) * half].reshape(2 * half * rows, depth)
                lanes = slice(part * 2 * half * rows, (part + 1) * 2 * half * rows)
                products[k, :, lanes] = lax.dot_general(
                    gv[EDGE : EDGE + used],
                    kernel,
                    (((1,), (1,)), ((), ())),
                    preferred_element_type=jnp.float32,
                )

        for copy in late:
            copy.wait()

        @pl.loop(0, coarse // STEP)
        def _(i):
            base = pl.multiple_of(i * STEP, STEP)
            spot, span = pl.ds(base, STEP), pl.ds(pl.multiple_of(2 * base, 2 * STEP), 2 * STEP)
            for c in range(width // LANES):
                lanes = slice(c * LANES, (c + 1) * LANES)
                if last:
                    left = c * LANES % block
                    skip = skips[c * LANES // block, pl.ds(base + HALO, STEP), left : left + LANES]
                    skip = 0.5 * skip.astype(jnp.float32)
                for parity in range(2):
                    total = shifted_total(products, base, lanes, parity)
                    if last:
                        total = (total + sums[parity, spot, lanes]) * slopes[parity, spot, lanes]
                        strip[c, pl.ds(parity, STEP, stride=2), :] = total + skip
                    else:
                        out_ref[parity, spot, lanes] = total
                if last:
                    out_ref[0, span, lanes] = strip[c].astype(jnp.bfloat16)

    out_shape = jax.ShapeDtypeStruct(shape if last else planar, jnp.bfloat16 if last else jnp.float32)
    scratch = [
        pltpu.VMEM((taps, planes, 2, rows, depth), jnp.bfloat16),
        pltpu.VMEM((window, depth), jnp.bfloat16),
        pltpu.VMEM((taps, used, width), jnp.float32),
        pltpu.SemaphoreType.DMA((taps, len(pieces), 2)),
        pltpu.SemaphoreType.DMA((len(parts), window // rows)),
    ]
    if last:
        scratch += [
            pltpu.VMEM(planar, jnp.float32),
            pltpu.VMEM(planar, jnp.float32),
            pltpu.VMEM((width // LANES, 2 * STEP, LANES), jnp.float32),
            pltpu.VMEM((seqs, window, block), jnp.bfloat16),
            pltpu.SemaphoreType.DMA((2,)),
            pltpu.SemaphoreType.DMA((len(parts), window // rows)),
        ]
    return pl.pallas_call(
        body,
        out_shape=out_shape,
        grid_spec=pltpu.PrefetchScalarGridSpec(
            num_scalar_prefetch=1,
            grid=(1,),
            in_specs=[ANYWHERE] * len(operands),
            out_specs=pl.BlockSpec(out_shape.shape, lambda i, place: (0, 0, 0)),
            scratch_shapes=scratch,
        ),
        compiler_params=pltpu.CompilerParams(vmem_limit_bytes=56 << 20),
        cost_estimate=SMALL,
        name="input_grad",
    )(place, *operands)

def stack_planes(place, line):
    count = len(line)

    def kernel(place, *refs):
        parts, out_ref = refs[:count], refs[count]
        for j in range(count):
            out_ref[place[1] // 2 ^ j] = parts[j][...]

    shape = line[0].shape
    return pl.pallas_call(
        kernel,
        out_shape=jax.ShapeDtypeStruct((count, *shape), line[0].dtype),
        grid_spec=pltpu.PrefetchScalarGridSpec(
            num_scalar_prefetch=1,
            grid=(1,),
            in_specs=[pl.BlockSpec(shape, lambda i, place: (0,) * len(shape))] * count,
            out_specs=pl.BlockSpec((count, *shape), lambda i, place: (0,) * (1 + len(shape))),
        ),
        compiler_params=pltpu.CompilerParams(vmem_limit_bytes=24 << 20),
        cost_estimate=SMALL,
        name="stack_planes",
    )(place, *line)

def on_device_square(inputs, trunk_grad, weights):
    seqs, reps = lax.axis_size("seq"), lax.axis_size("rep")
    me, rep = lax.axis_index("seq"), lax.axis_index("rep")
    place = jnp.stack([me, rep]).astype(jnp.int32)
    taps, rows, block = weights.shape
    fine = inputs.shape[1]
    coarse, planes = fine // 2, reps // 2
    half = coarse // 2

    last_taps = weights[SPLIT:]
    across = [last_taps] + [from_peer(last_taps, "seq", d) for d in range(1, seqs)]

    act = after(activate(inputs), *across[1:])
    beside, below = from_peer(act, "seq", 1), from_peer(act, "seq", 2)
    slope = half_slope(inputs)
    line = gather_line(weights[:SPLIT], "rep", planes, 2)
    line_across = gather_line(after(jnp.stack(across), act, *line[1:]), "rep", planes, 2)
    crossing = (line_across[1], line_across[planes - 1])
    trunk = trunk_grad[0]
    zeros = jnp.zeros((1, block), jnp.bfloat16)
    later = jnp.concatenate([trunk[1:], zeros])
    earlier = jnp.concatenate([zeros, trunk[:-1]])
    shifts = jnp.concatenate([later, trunk, earlier], axis=1)
    to_beside, to_below, own_window = kernel_messages(place, line, trunk_grad, coarse)
    ready = (slope, shifts, to_beside)
    top, bottom = after(beside[:half], *ready), after(below[half:], *ready)
    far_top, far_bottom = from_peer(top, "seq", 2), from_peer(bottom, "seq", 1)

    scale = 0.5 * float(fine * seqs * reps) ** (-0.5)
    near_rows = [(d, 0, coarse, 0) for d in range(3)]
    far_rows = [(3, 0, half, 0), (3, half, half, 0)]
    early = early_terms(place, near_rows, [act, beside, below], shifts, coarse, crossing)
    line_across[2] = after(line_across[2], early)
    lines = stack_planes(place, line_across)
    far_top, far_bottom = after(far_top, early), after(far_bottom, early)

    to_beside, to_below = (
        after(message, far_top, far_bottom) for message in (to_beside, to_below)
    )
    kept_beside, kept_below = from_peer(to_beside, "seq", 1), from_peer(to_below, "seq", 2)
    other_column, other_lines = from_peer(to_below, "rep", 1), from_peer(lines, "rep", 1)

    mine, *theirs = late_terms(
        place,
        far_rows,
        [far_top, far_bottom],
        shifts,
        early,
        coarse,
        scale,
        planes,
        taps,
        rows,
        [line_across[2]],
    )
    arrived = [from_peer(part, "rep", 1) for part in theirs]
    pairs = []
    for j in range(planes):
        part = arrived[j // (planes // 2)][j % (planes // 2)]
        pairs.append(mine[j] + part.astype(jnp.float32))
    weight_grad, steps = reduce_line(pairs, "rep", planes, 2)

    window = (coarse + 2 * HALO) // rows
    count, side = planes * SPLIT, window // 2
    far_first = from_peer(kept_beside[: side + count // 2], "seq", 2)
    far_second = from_peer(kept_below[count // 2 : count + side], "seq", 1)

    windows = [
        [(own_window, 0, 0, window)],
        [(kept_beside, side + count, 0, window)],
        [(kept_below, count + side, 0, window)],
    ]
    stage = functools.partial(gradient_stage, place, taps=taps, slope=slope, shape=inputs.shape)
    soon = [(to_below, 0, 0, planes, 0, 0), (other_column, 0, 0, planes, 1, 0)]
    for part, start, distance in ((kept_beside, side, 1), (kept_below, 0, 2)):
        soon.append((part, start, 0, planes, 0, distance))
        soon.append((from_peer(part, "rep", 1), start, 0, planes, 1, distance))
    crossed = [
        (part, None, 0, planes, flip, d)
        for flip, part in enumerate((lines, other_lines))
        for d in range(seqs)
    ]
    near = [piece for piece in crossed if piece[-1] < 3]
    begun = stage(windows, pieces=soon + near, distances=[0, 1, 2], begun=None)
    far_first, far_second = after(far_first, begun, *steps[:1]), after(far_second, begun, *steps[:1])
    windows.append([(far_first, 0, 0, side), (far_second, count // 2, side, side)])
    rest = [piece for piece in crossed if piece[-1] == 3]
    for part, start, plane in ((far_first, side, 0), (far_second, 0, planes // 2)):
        rest.append((part, start, plane, planes // 2, 0, 3))
        rest.append((from_peer(part, "rep", 1), start, plane, planes // 2, 1, 3))
    input_grad = stage(windows, pieces=rest, distances=[3], begun=begun)
    weight_grad = weight_grad + after(steps[-1], input_grad)[0].astype(jnp.float32)
    return (input_grad, weight_grad)


def with_halo(value, sides, width):
    for axis, dim in sides:
        peers, length = (lax.axis_size(axis), value.shape[dim])
        up = [(i, (i + 1) % peers) for i in range(peers - 1)]
        down = [(j, i) for i, j in up]
        last = lax.slice_in_dim(value, length - width, length, axis=dim)
        leading = lax.slice_in_dim(value, 0, width, axis=dim)
        before = lax.ppermute(last, axis, up)
        after = lax.ppermute(leading, axis, down)
        value = jnp.concatenate([before, value, after], axis=dim)
    return value

def contract_last(left, right):
    return lax.dot_general(
        left, right, (((1,), (1,)), ((), ())), preferred_element_type=jnp.float32
    )

def contract_first(left, right):
    return lax.dot_general(
        left, right, (((0,), (0,)), ((), ())), preferred_element_type=jnp.float32
    )

def on_device_plain(inputs, trunk_grad, weights):
    taps = weights.shape[0]
    grad = lax.all_to_all(trunk_grad, "seq", split_axis=1, concat_axis=2, tiled=True)
    grad_up = jnp.repeat(grad.astype(jnp.float32) * 0.5, 2, axis=1).astype(jnp.bfloat16)
    rows = grad_up.shape[1]
    padded = with_halo(grad_up, (("seq", 1),), 2)
    shifts = [padded[0, 4 - k : 4 - k + rows] for k in range(taps)]
    inputs_f = inputs[0].astype(jnp.float32)
    act_vals, back = jax.vjp(jax.nn.gelu, inputs_f)
    slope = back(jnp.ones_like(inputs_f))[0]
    act = act_vals.astype(jnp.bfloat16)
    in_width = inputs.shape[2]
    columns = lax.all_gather(weights, "seq", axis=2, tiled=True)
    piece = lax.all_gather(columns, "rep", axis=1, tiled=True)
    result = contract_last(shifts[0], piece[0])
    for project_k in range(1, taps):
        result = result + contract_last(shifts[project_k], piece[project_k])
    input_grad = (result * slope + grad_up[0, :, :in_width].astype(jnp.float32)).astype(
        jnp.bfloat16
    )
    scale_factor = float(rows * lax.axis_size("seq") * lax.axis_size("rep")) ** (-0.5)
    terms = jnp.stack([contract_first(act, shifts[k]) for k in range(taps)]) * scale_factor
    partial_sum = lax.psum_scatter(terms, "rep", scatter_dimension=1, tiled=True)
    weight_grad = lax.psum_scatter(partial_sum, "seq", scatter_dimension=2, tiled=True)
    return (input_grad[None], weight_grad)

def on_device(inputs, trunk_grad, weights):
    square = lax.axis_size("seq") == 4 and lax.axis_size("rep") % 8 == 0
    if square and weights.shape[2] % LANES == 0 and inputs.shape[2] % LANES == 0:
        return on_device_square(inputs, trunk_grad, weights)
    return on_device_plain(inputs, trunk_grad, weights)

def solution(mesh):
    in_specs = (P("rep", "seq", None), P("rep", None, "seq"), P(None, "rep", "seq"))
    out_specs = (P("rep", "seq", None), P(None, "rep", "seq"))
    return jax.shard_map(
        on_device, mesh=mesh, in_specs=in_specs, out_specs=out_specs, check_vma=False
    )
```

```python
import functools
import math

import jax
import jax.numpy as jnp
from jax import lax
from jax.experimental import pallas as pl
from jax.experimental.pallas import tpu as pltpu
from jax.sharding import PartitionSpec as P

LANES = 128
HALO = 32
EDGE = 16
MARGIN = HALO - EDGE
STEP = 64
SPLIT = 3
ROOT = math.sqrt(2.0 / math.pi)
CUBIC = 0.044715
SMALL = pl.CostEstimate(flops=1 << 20, bytes_accessed=1 << 16, transcendentals=0)
ANYWHERE = pl.BlockSpec(memory_space=pl.ANY)
ROW_OFFSETS = ((1, 1), (0, 1), (0, 0), (-1, 0), (-1, -1))
GRAD_PARTS = ((0, 0), (1, 0), (1, 1), (2, 1), (2, 2))

def from_peer(value, axis, distance):
    peers = lax.axis_size(axis)
    return lax.ppermute(value, axis, [(i, i ^ distance) for i in range(peers)])

def after(value, *earlier):
    return pl.pallas_call(
        lambda *refs: None,
        out_shape=jax.ShapeDtypeStruct(value.shape, value.dtype),
        in_specs=[ANYWHERE] * (1 + len(earlier)),
        out_specs=ANYWHERE,
        input_output_aliases={0: 0},
        name="after",
    )(value, *earlier)

def half_after(value, which, *earlier):
    rows, width = value.shape[0] // 2, value.shape[1]
    steps = 4
    block = (rows // steps, width)

    def kernel(value_ref, *refs):
        refs[-1][...] = value_ref[...]

    return pl.pallas_call(
        kernel,
        out_shape=jax.ShapeDtypeStruct((rows, width), value.dtype),
        grid=(steps,),
        in_specs=[pl.BlockSpec(block, lambda i: (i + which * steps, 0))] + [ANYWHERE] * len(earlier),
        out_specs=pl.BlockSpec(block, lambda i: (i, 0)),
        compiler_params=pltpu.CompilerParams(vmem_limit_bytes=16 << 20),
        cost_estimate=SMALL,
        name="half_after",
    )(value, *earlier)


def reduce_line(blocks, axis, count, unit):
    held, masks = [[0]], []
    while count > 1:
        masks.append(count - 1)
        held.append(held[-1] + [d ^ masks[-1] for d in held[-1]])
        count //= 2
    blocks, steps = dict(enumerate(blocks)), []
    for mask, keep in reversed(list(zip(masks, held))):
        leaving = jnp.stack([blocks[d ^ mask].astype(jnp.bfloat16) for d in keep])
        steps.append(from_peer(leaving, axis, mask * unit))
        if mask != masks[0]:
            blocks = {d: blocks[d] + steps[-1][n].astype(jnp.float32) for n, d in enumerate(keep)}
    return blocks[0], steps


def gather_line(value, axis, count, unit):
    found, mask = {0: value}, count - 1
    while mask:
        for distance in list(found):
            found[distance ^ mask] = from_peer(found[distance], axis, mask * unit)
        mask //= 2
    return [found[distance] for distance in range(count)]

def gelu_slope(x):
    tanh = jnp.tanh(ROOT * (x + CUBIC * (x * x * x)))
    return 0.5 * (1.0 + tanh) + 0.5 * x * (1.0 - tanh * tanh) * (
        ROOT * (1.0 + 3.0 * CUBIC * (x * x))
    )

def act_kernel(x_ref, out_ref, strip):
    width = x_ref.shape[2]

    @pl.loop(0, out_ref.shape[0] // STEP)
    def _(step):
        start = pl.multiple_of(step * STEP, STEP)
        x = x_ref[0, pl.ds(pl.multiple_of(2 * start, 2 * STEP), 2 * STEP), :].astype(jnp.float32)
        act = x * (0.5 * (1.0 + jnp.tanh(ROOT * (x + CUBIC * (x * x * x)))))
        for c in range(width // LANES):
            strip[c] = act[:, c * LANES : (c + 1) * LANES]
        for parity in range(2):
            for c in range(width // LANES):
                picked = strip[c, pl.ds(parity, STEP, stride=2), :].astype(jnp.bfloat16)
                left = parity * width + c * LANES
                out_ref[pl.ds(start, STEP), left : left + LANES] = picked

def activate(inputs):
    fine, width = inputs.shape[1:]
    return pl.pallas_call(
        act_kernel,
        out_shape=jax.ShapeDtypeStruct((fine // 2, 2 * width), jnp.bfloat16),
        in_specs=[pl.BlockSpec(memory_space=pltpu.VMEM)],
        out_specs=pl.BlockSpec(memory_space=pltpu.VMEM),
        scratch_shapes=[pltpu.VMEM((width // LANES, 2 * STEP, LANES), jnp.float32)],
        compiler_params=pltpu.CompilerParams(vmem_limit_bytes=24 << 20),
        cost_estimate=SMALL,
        name="act",
    )(inputs)

def kernel_messages(place, line, trunk_grad, coarse):
    taps, rows, block = line[0].shape
    planes, length = len(line), trunk_grad.shape[1]
    window = (coarse + 2 * HALO) // rows
    half = planes // 2

    def kernel(place, *refs):
        parts, trunk_ref = refs[:planes], refs[planes]
        beside_ref, below_ref, own_ref, edged, sem = refs[planes + 1 :]
        copy = pltpu.make_async_copy(trunk_ref.at[0], edged.at[pl.ds(HALO, length)], sem)
        copy.start()
        edged[:HALO] = jnp.zeros((HALO, block), jnp.bfloat16)
        edged[HALO + length :] = jnp.zeros((HALO, block), jnp.bfloat16)
        for j in range(planes):
            plane = place[1] // 2 ^ j
            for k in range(taps):
                spot = (plane // half * taps + k) * half + plane % half
                beside_ref[window // 2 + spot] = parts[j][k]
                below_ref[spot] = parts[j][k]
        copy.wait()

        def cut(out_ref, spot, distance, first, last):
            base = (place[0] ^ distance) * coarse
            for b in range(first, last):
                out_ref[spot + b - first] = edged[pl.ds(pl.multiple_of(base + b * rows, 16), rows), :]

        cut(beside_ref, 0, 3, 0, window // 2)
        cut(beside_ref, window // 2 + planes * taps, 1, 0, window)
        cut(below_ref, planes * taps, 3, window // 2, window)
        cut(below_ref, planes * taps + window // 2, 2, 0, window)
        cut(own_ref, 0, 0, 0, window)

    count = window // 2 + planes * taps + window
    return pl.pallas_call(
        kernel,
        out_shape=[
            jax.ShapeDtypeStruct((n, rows, block), jnp.bfloat16) for n in (count, count, window)
        ],
        grid_spec=pltpu.PrefetchScalarGridSpec(
            num_scalar_prefetch=1,
            grid=(1,),
            in_specs=[pl.BlockSpec(line[0].shape, lambda i, place: (0, 0, 0))] * planes + [ANYWHERE],
            out_specs=[
                pl.BlockSpec((n, rows, block), lambda i, place: (0, 0, 0))
                for n in (count, count, window)
            ],
            scratch_shapes=[
                pltpu.VMEM((length + 2 * HALO, block), jnp.bfloat16),
                pltpu.SemaphoreType.DMA,
            ],
        ),
        compiler_params=pltpu.CompilerParams(vmem_limit_bytes=32 << 20),
        cost_estimate=SMALL,
        name="kernel_messages",
    )(place, *line, trunk_grad)

def slope_kernel(x_ref, out_ref, scratch):
    width = x_ref.shape[2]

    @pl.loop(0, out_ref.shape[1] // 64)
    def _(step):
        start = pl.multiple_of(step * 64, 64)
        span = pl.ds(pl.multiple_of(2 * start, 128), 128)
        for c in range(width // LANES):
            lanes = slice(c * LANES, (c + 1) * LANES)
            scratch[c] = 0.5 * gelu_slope(x_ref[0, span, lanes].astype(jnp.float32))
            for parity in range(2):
                out_ref[parity, pl.ds(start, 64), lanes] = scratch[c, pl.ds(parity, 64, stride=2), :]

def half_slope(inputs):
    fine, width = inputs.shape[1:]
    return pl.pallas_call(
        slope_kernel,
        out_shape=jax.ShapeDtypeStruct((2, fine // 2, width), jnp.float32),
        in_specs=[pl.BlockSpec(memory_space=pltpu.VMEM)],
        out_specs=pl.BlockSpec(memory_space=pltpu.VMEM),
        scratch_shapes=[pltpu.VMEM((width // LANES, 128, LANES), jnp.float32)],
        compiler_params=pltpu.CompilerParams(vmem_limit_bytes=24 << 20),
        name="half_slope",
    )(inputs)

def start_act(place, coarse, layout, pieces, shifts_ref, held, shifts, sems, shift_sems):
    copies, row = [], 0
    for i, (distance, first, size, offset) in enumerate(layout):
        start = pl.multiple_of((place[0] ^ distance) * coarse + first, 16)
        spot = pl.ds(row, size)
        source = pieces[i].at[pl.ds(offset, size)]
        copies.append(pltpu.make_async_copy(source, held.at[spot], sems.at[i]))
        copies.append(
            pltpu.make_async_copy(shifts_ref.at[pl.ds(start, size)], shifts.at[spot], shift_sems.at[i])
        )
        row += size
    for copy in copies:
        copy.start()
    return copies

def early_terms(place, layout, pieces, shifts, coarse):
    both, columns = pieces[0].shape[1], shifts.shape[1]
    rows = sum(size for _, _, size, _ in layout)
    tile = 256

    def kernel(place, shifts_ref, *refs):
        pieces, total = refs[: len(layout)], refs[len(layout)]
        held, shifts, sems, shift_sems = refs[len(layout) + 1 :]
        copies = start_act(
            place, coarse, layout, pieces, shifts_ref, held, shifts, sems, shift_sems
        )
        for copy in copies:
            copy.wait()

        @pl.loop(0, both // tile)
        def _(i):
            span = pl.ds(pl.multiple_of(i * tile, tile), tile)
            total[span, :] = lax.dot_general(
                held[:, span], shifts[...], (((0,), (0,)), ((), ())), preferred_element_type=jnp.float32
            )

    return pl.pallas_call(
        kernel,
        out_shape=jax.ShapeDtypeStruct((both, columns), jnp.float32),
        grid_spec=pltpu.PrefetchScalarGridSpec(
            num_scalar_prefetch=1,
            grid=(1,),
            in_specs=[ANYWHERE] * (1 + len(pieces)),
            out_specs=pl.BlockSpec((both, columns), lambda i, place: (0, 0)),
            scratch_shapes=[
                pltpu.VMEM((rows, both), jnp.bfloat16),
                pltpu.VMEM((rows, columns), jnp.bfloat16),
                pltpu.SemaphoreType.DMA((len(pieces),)),
                pltpu.SemaphoreType.DMA((len(pieces),)),
            ],
        ),
        compiler_params=pltpu.CompilerParams(vmem_limit_bytes=48 << 20),
        cost_estimate=SMALL,
        name="weight_grad_early",
    )(place, shifts, *pieces)

def late_terms(place, layout, pieces, shifts, early, coarse, scale, planes, taps, rows, earlier):
    both, columns = early.shape
    width, block = both // 2, columns // 3
    count = sum(size for _, _, size, _ in layout)
    tile = 256
    shape = (planes, taps, rows, block)

    def kernel(place, shifts_ref, early_ref, *refs):
        pieces, refs = refs[: len(layout)], refs[len(layout) + len(earlier) :]
        mine_ref, *theirs_refs = refs[:3]
        held, shifts, total, sems, shift_sems, early_sems = refs[3:]
        core, plane = place[1] % 2, place[1] // 2
        copies = start_act(
            place, coarse, layout, pieces, shifts_ref, held, shifts, sems, shift_sems
        )

        def fetch(i):
            span = pl.ds(pl.multiple_of(i * tile, tile), tile)
            return pltpu.make_async_copy(early_ref.at[span], total.at[span], early_sems.at[i])

        for i in range(both // tile):
            fetch(i).start()
        for copy in copies:
            copy.wait()

        @pl.loop(0, both // tile)
        def _(i):
            span = pl.ds(pl.multiple_of(i * tile, tile), tile)
            term = lax.dot_general(
                held[:, span], shifts[...], (((0,), (0,)), ((), ())), preferred_element_type=jnp.float32
            )
            fetch(i).wait()
            total[span, :] += term

        def finish(out_ref, at, j, parity, kind):
            start = ((plane ^ j) * 2 + parity) * rows
            even = pl.ds(pl.multiple_of(start, 16), rows)
            odd = pl.ds(pl.multiple_of(width + start, 16), rows)
            for k, (left, right) in enumerate(GRAD_PARTS):
                term = total[even, left * block : (left + 1) * block]
                term += total[odd, right * block : (right + 1) * block]
                out_ref[at, k] = (scale * term).astype(kind)

        for which, out_ref in enumerate(theirs_refs):

            @pl.loop(0, planes // 2)
            def _(at):
                finish(out_ref, at, at + which * (planes // 2), 1 - core, jnp.bfloat16)

        @pl.loop(0, planes)
        def _(j):
            finish(mine_ref, j, j, core, jnp.float32)

    half_shape = (planes // 2, *shape[1:])
    whole = pl.BlockSpec(shape, lambda i, place: (0, 0, 0, 0))
    half = pl.BlockSpec(half_shape, lambda i, place: (0, 0, 0, 0))
    return pl.pallas_call(
        kernel,
        out_shape=(
            jax.ShapeDtypeStruct(shape, jnp.float32),
            jax.ShapeDtypeStruct(half_shape, jnp.bfloat16),
            jax.ShapeDtypeStruct(half_shape, jnp.bfloat16),
        ),
        grid_spec=pltpu.PrefetchScalarGridSpec(
            num_scalar_prefetch=1,
            grid=(1,),
            in_specs=[ANYWHERE] * (2 + len(pieces) + len(earlier)),
            out_specs=[whole, half, half],
            scratch_shapes=[
                pltpu.VMEM((count, both), jnp.bfloat16),
                pltpu.VMEM((count, columns), jnp.bfloat16),
                pltpu.VMEM((both, columns), jnp.float32),
                pltpu.SemaphoreType.DMA((len(pieces),)),
                pltpu.SemaphoreType.DMA((len(pieces),)),
                pltpu.SemaphoreType.DMA((both // tile,)),
            ],
        ),
        compiler_params=pltpu.CompilerParams(vmem_limit_bytes=48 << 20),
        cost_estimate=SMALL,
        name="weight_grad_late",
    )(place, shifts, early, *pieces, *earlier)

def shifted_total(products, base, lanes, parity):
    total = None
    for by in (0, 1, -1):
        wanted = [k for k in range(products.shape[0]) if ROW_OFFSETS[k][parity] == by]
        if wanted:
            near = pl.ds(base + MARGIN - 8, STEP + 16)
            part = sum(products[k, near, lanes] for k in wanted)[8 + by : 8 + by + STEP]
            total = part if total is None else total + part
    return total

def gradient_stage(place, windows, taps, pieces, distances, slope, begun, shape):
    _, fine, width = shape
    coarse, seqs = fine // 2, lax.axis_size("seq")
    rows, block = pieces[0][0].shape[-2:]
    planes = width // (2 * rows)
    half = planes // 2
    window, used = coarse + 2 * HALO, coarse + 2 * MARGIN
    depth, planar = len(distances) * block, (2, coarse, width)
    last = begun is not None
    needed = list(range(seqs)) if last else distances
    parts = [(d, *part) for d in needed for part in windows[d]]
    operands = [part[1] for part in parts] + [piece[0] for piece in pieces]
    operands += [slope, begun] if last else []

    def body(place, *refs):
        own, refs = refs[: len(parts)], refs[len(parts) :]
        sources, refs = refs[: len(pieces)], refs[len(pieces) :]
        if last:
            (slope_ref, begun_ref), refs = refs[:2], refs[2:]
        out_ref, wv, gv, products, sems, grad_sems = refs[:6]
        me, core = place[0], place[1] % 2

        def kernel_copies(first):
            for number, (array, start, plane, count, flip, distance) in enumerate(pieces):
                spot = pl.ds(distances.index(distance) * block, block)
                if first != (start is not None):
                    continue
                for k in range(SPLIT if first else taps - SPLIT):
                    for h in range(count // half):
                        span = pl.ds(plane + h * half, half)
                        if first:
                            source = sources[number].at[pl.ds(start + (h * SPLIT + k) * half, half)]
                        else:
                            source = sources[number].at[span, distance, k]
                        tap = k if first else SPLIT + k
                        target = wv.at[tap, span, core ^ flip, :, spot]
                        sem = sems.at[tap, number, h]
                        yield tap, pltpu.make_async_copy(source, target, sem)

        def window_copies(target_of, sems):
            for number, (distance, _, start, first, count) in enumerate(parts):
                for b in range(count):
                    target = target_of(distance, pl.ds((first + b) * rows, rows))
                    if target is not None:
                        source = own[number].at[start + b]
                        yield pltpu.make_async_copy(source, target, sems.at[number, b])

        def into_window(distance, span):
            if distance not in distances:
                return None
            return gv.at[span, pl.ds(distances.index(distance) * block, block)]

        early = list(window_copies(into_window, grad_sems))
        late = []
        if last:
            sums, slopes, strip, skips, sum_sems, skip_sems = refs[6:]
            late.append(pltpu.make_async_copy(begun_ref, sums, sum_sems.at[0]))
            late.append(pltpu.make_async_copy(slope_ref, slopes, sum_sems.at[1]))
            late += window_copies(lambda d, span: skips.at[me ^ d, span], skip_sems)
        for copy in early:
            copy.start()
        arriving = sorted([*kernel_copies(True), *kernel_copies(False)], key=lambda pair: pair[0])
        for _, copy in arriving:
            copy.start()
        for copy in late:
            copy.start()
        for copy in early:
            copy.wait()
        for k in range(taps):
            for tap, copy in arriving:
                if tap == k:
                    copy.wait()
            for part in range(2):
                kernel = wv[k, part * half : (part + 1) * half].reshape(2 * half * rows, depth)
                lanes = slice(part * 2 * half * rows, (part + 1) * 2 * half * rows)
                products[k, :, lanes] = lax.dot_general(
                    gv[EDGE : EDGE + used],
                    kernel,
                    (((1,), (1,)), ((), ())),
                    preferred_element_type=jnp.float32,
                )

        for copy in late:
            copy.wait()

        @pl.loop(0, coarse // STEP)
        def _(i):
            base = pl.multiple_of(i * STEP, STEP)
            spot, span = pl.ds(base, STEP), pl.ds(pl.multiple_of(2 * base, 2 * STEP), 2 * STEP)
            for c in range(width // LANES):
                lanes = slice(c * LANES, (c + 1) * LANES)
                if last:
                    left = c * LANES % block
                    skip = skips[c * LANES // block, pl.ds(base + HALO, STEP), left : left + LANES]
                    skip = 0.5 * skip.astype(jnp.float32)
                for parity in range(2):
                    total = shifted_total(products, base, lanes, parity)
                    if last:
                        total = (total + sums[parity, spot, lanes]) * slopes[parity, spot, lanes]
                        strip[c, pl.ds(parity, STEP, stride=2), :] = total + skip
                    else:
                        out_ref[parity, spot, lanes] = total
                if last:
                    out_ref[0, span, lanes] = strip[c].astype(jnp.bfloat16)

    out_shape = jax.ShapeDtypeStruct(shape if last else planar, jnp.bfloat16 if last else jnp.float32)
    scratch = [
        pltpu.VMEM((taps, planes, 2, rows, depth), jnp.bfloat16),
        pltpu.VMEM((window, depth), jnp.bfloat16),
        pltpu.VMEM((taps, used, width), jnp.float32),
        pltpu.SemaphoreType.DMA((taps, len(pieces), 2)),
        pltpu.SemaphoreType.DMA((len(parts), window // rows)),
    ]
    if last:
        scratch += [
            pltpu.VMEM(planar, jnp.float32),
            pltpu.VMEM(planar, jnp.float32),
            pltpu.VMEM((width // LANES, 2 * STEP, LANES), jnp.float32),
            pltpu.VMEM((seqs, window, block), jnp.bfloat16),
            pltpu.SemaphoreType.DMA((2,)),
            pltpu.SemaphoreType.DMA((len(parts), window // rows)),
        ]
    return pl.pallas_call(
        body,
        out_shape=out_shape,
        grid_spec=pltpu.PrefetchScalarGridSpec(
            num_scalar_prefetch=1,
            grid=(1,),
            in_specs=[ANYWHERE] * len(operands),
            out_specs=pl.BlockSpec(out_shape.shape, lambda i, place: (0, 0, 0)),
            scratch_shapes=scratch,
        ),
        compiler_params=pltpu.CompilerParams(vmem_limit_bytes=56 << 20),
        cost_estimate=SMALL,
        name="input_grad",
    )(place, *operands)

def stack_planes(place, line):
    count = len(line)

    def kernel(place, *refs):
        parts, out_ref = refs[:count], refs[count]
        for j in range(count):
            out_ref[place[1] // 2 ^ j] = parts[j][...]

    shape = line[0].shape
    return pl.pallas_call(
        kernel,
        out_shape=jax.ShapeDtypeStruct((count, *shape), line[0].dtype),
        grid_spec=pltpu.PrefetchScalarGridSpec(
            num_scalar_prefetch=1,
            grid=(1,),
            in_specs=[pl.BlockSpec(shape, lambda i, place: (0,) * len(shape))] * count,
            out_specs=pl.BlockSpec((count, *shape), lambda i, place: (0,) * (1 + len(shape))),
        ),
        compiler_params=pltpu.CompilerParams(vmem_limit_bytes=24 << 20),
        cost_estimate=SMALL,
        name="stack_planes",
    )(place, *line)

def on_device_square(inputs, trunk_grad, weights):
    seqs, reps = lax.axis_size("seq"), lax.axis_size("rep")
    me, rep = lax.axis_index("seq"), lax.axis_index("rep")
    place = jnp.stack([me, rep]).astype(jnp.int32)
    taps, rows, block = weights.shape
    fine = inputs.shape[1]
    coarse, planes = fine // 2, reps // 2
    half = coarse // 2

    last_taps = weights[SPLIT:]
    across = [last_taps] + [from_peer(last_taps, "seq", d) for d in range(1, seqs)]

    act = after(activate(inputs), *across[1:])
    beside, below = from_peer(act, "seq", 1), from_peer(act, "seq", 2)
    slope = half_slope(inputs)
    line = gather_line(weights[:SPLIT], "rep", planes, 2)
    line_across = gather_line(after(jnp.stack(across), act, *line[1:]), "rep", planes, 2)
    crossing = (line_across[1], line_across[planes - 1])
    trunk = trunk_grad[0]
    zeros = jnp.zeros((1, block), jnp.bfloat16)
    later = jnp.concatenate([trunk[1:], zeros])
    earlier = jnp.concatenate([zeros, trunk[:-1]])
    shifts = jnp.concatenate([later, trunk, earlier], axis=1)
    to_beside, to_below, own_window = kernel_messages(place, line, trunk_grad, coarse)
    ready = (slope, shifts, to_beside, *crossing)
    top, bottom = half_after(beside, 0, *ready), half_after(below, 1, *ready)
    far_top, far_bottom = from_peer(top, "seq", 2), from_peer(bottom, "seq", 1)

    scale = 0.5 * float(fine * seqs * reps) ** (-0.5)
    near_rows = [(d, 0, coarse, 0) for d in range(3)]
    far_rows = [(3, 0, half, 0), (3, half, half, 0)]
    early = early_terms(place, near_rows, [act, beside, below], shifts, coarse)
    line_across[2] = after(line_across[2], early)
    lines = stack_planes(place, line_across)
    far_top, far_bottom = after(far_top, early), after(far_bottom, early)

    to_beside, to_below = (
        after(message, far_top, far_bottom) for message in (to_beside, to_below)
    )
    kept_beside, kept_below = from_peer(to_beside, "seq", 1), from_peer(to_below, "seq", 2)
    other_column, other_lines = from_peer(to_below, "rep", 1), from_peer(lines, "rep", 1)

    mine, *theirs = late_terms(
        place,
        far_rows,
        [far_top, far_bottom],
        shifts,
        early,
        coarse,
        scale,
        planes,
        taps,
        rows,
        [line_across[2]],
    )
    arrived = [from_peer(part, "rep", 1) for part in theirs]
    pairs = []
    for j in range(planes):
        part = arrived[j // (planes // 2)][j % (planes // 2)]
        pairs.append(mine[j] + part.astype(jnp.float32))
    weight_grad, steps = reduce_line(pairs, "rep", planes, 2)

    window = (coarse + 2 * HALO) // rows
    count, side = planes * SPLIT, window // 2
    far_first = from_peer(kept_beside[: side + count // 2], "seq", 2)
    far_second = from_peer(kept_below[count // 2 : count + side], "seq", 1)

    windows = [
        [(own_window, 0, 0, window)],
        [(kept_beside, side + count, 0, window)],
        [(kept_below, count + side, 0, window)],
    ]
    stage = functools.partial(gradient_stage, place, taps=taps, slope=slope, shape=inputs.shape)
    soon = [(to_below, 0, 0, planes, 0, 0), (other_column, 0, 0, planes, 1, 0)]
    for part, start, distance in ((kept_beside, side, 1), (kept_below, 0, 2)):
        soon.append((part, start, 0, planes, 0, distance))
        soon.append((from_peer(part, "rep", 1), start, 0, planes, 1, distance))
    crossed = [
        (part, None, 0, planes, flip, d)
        for flip, part in enumerate((lines, other_lines))
        for d in range(seqs)
    ]
    near = [piece for piece in crossed if piece[-1] < 3]
    begun = stage(windows, pieces=soon + near, distances=[0, 1, 2], begun=None)
    far_first, far_second = after(far_first, begun, *steps[:1]), after(far_second, begun, *steps[:1])
    windows.append([(far_first, 0, 0, side), (far_second, count // 2, side, side)])
    rest = [piece for piece in crossed if piece[-1] == 3]
    for part, start, plane in ((far_first, side, 0), (far_second, 0, planes // 2)):
        rest.append((part, start, plane, planes // 2, 0, 3))
        rest.append((from_peer(part, "rep", 1), start, plane, planes // 2, 1, 3))
    input_grad = stage(windows, pieces=rest, distances=[3], begun=begun)
    weight_grad = weight_grad + after(steps[-1], input_grad)[0].astype(jnp.float32)
    return (input_grad, weight_grad)


def with_halo(value, sides, width):
    for axis, dim in sides:
        peers, length = (lax.axis_size(axis), value.shape[dim])
        up = [(i, (i + 1) % peers) for i in range(peers - 1)]
        down = [(j, i) for i, j in up]
        last = lax.slice_in_dim(value, length - width, length, axis=dim)
        leading = lax.slice_in_dim(value, 0, width, axis=dim)
        before = lax.ppermute(last, axis, up)
        after = lax.ppermute(leading, axis, down)
        value = jnp.concatenate([before, value, after], axis=dim)
    return value

def contract_last(left, right):
    return lax.dot_general(
        left, right, (((1,), (1,)), ((), ())), preferred_element_type=jnp.float32
    )

def contract_first(left, right):
    return lax.dot_general(
        left, right, (((0,), (0,)), ((), ())), preferred_element_type=jnp.float32
    )

def on_device_plain(inputs, trunk_grad, weights):
    taps = weights.shape[0]
    grad = lax.all_to_all(trunk_grad, "seq", split_axis=1, concat_axis=2, tiled=True)
    grad_up = jnp.repeat(grad.astype(jnp.float32) * 0.5, 2, axis=1).astype(jnp.bfloat16)
    rows = grad_up.shape[1]
    padded = with_halo(grad_up, (("seq", 1),), 2)
    shifts = [padded[0, 4 - k : 4 - k + rows] for k in range(taps)]
    inputs_f = inputs[0].astype(jnp.float32)
    act_vals, back = jax.vjp(jax.nn.gelu, inputs_f)
    slope = back(jnp.ones_like(inputs_f))[0]
    act = act_vals.astype(jnp.bfloat16)
    in_width = inputs.shape[2]
    columns = lax.all_gather(weights, "seq", axis=2, tiled=True)
    piece = lax.all_gather(columns, "rep", axis=1, tiled=True)
    result = contract_last(shifts[0], piece[0])
    for project_k in range(1, taps):
        result = result + contract_last(shifts[project_k], piece[project_k])
    input_grad = (result * slope + grad_up[0, :, :in_width].astype(jnp.float32)).astype(
        jnp.bfloat16
    )
    scale_factor = float(rows * lax.axis_size("seq") * lax.axis_size("rep")) ** (-0.5)
    terms = jnp.stack([contract_first(act, shifts[k]) for k in range(taps)]) * scale_factor
    partial_sum = lax.psum_scatter(terms, "rep", scatter_dimension=1, tiled=True)
    weight_grad = lax.psum_scatter(partial_sum, "seq", scatter_dimension=2, tiled=True)
    return (input_grad[None], weight_grad)

def on_device(inputs, trunk_grad, weights):
    square = lax.axis_size("seq") == 4 and lax.axis_size("rep") % 8 == 0
    if square and weights.shape[2] % LANES == 0 and inputs.shape[2] % LANES == 0:
        return on_device_square(inputs, trunk_grad, weights)
    return on_device_plain(inputs, trunk_grad, weights)

def solution(mesh):
    in_specs = (P("rep", "seq", None), P("rep", None, "seq"), P(None, "rep", "seq"))
    out_specs = (P("rep", "seq", None), P(None, "rep", "seq"))
    return jax.shard_map(
        on_device, mesh=mesh, in_specs=in_specs, out_specs=out_specs, check_vma=False
    )
```

```python
import functools
import math

import jax
import jax.numpy as jnp
from jax import lax
from jax.experimental import pallas as pl
from jax.experimental.pallas import tpu as pltpu
from jax.sharding import PartitionSpec as P

LANES = 128
HALO = 32
EDGE = 16
MARGIN = HALO - EDGE
STEP = 64
SPLIT = 3
ROOT = math.sqrt(2.0 / math.pi)
CUBIC = 0.044715
SMALL = pl.CostEstimate(flops=1 << 20, bytes_accessed=1 << 16, transcendentals=0)
ANYWHERE = pl.BlockSpec(memory_space=pl.ANY)
ROW_OFFSETS = ((1, 1), (0, 1), (0, 0), (-1, 0), (-1, -1))
GRAD_PARTS = ((0, 0), (1, 0), (1, 1), (2, 1), (2, 2))

def from_peer(value, axis, distance):
    peers = lax.axis_size(axis)
    return lax.ppermute(value, axis, [(i, i ^ distance) for i in range(peers)])

def after(value, *earlier):
    return pl.pallas_call(
        lambda *refs: None,
        out_shape=jax.ShapeDtypeStruct(value.shape, value.dtype),
        in_specs=[ANYWHERE] * (1 + len(earlier)),
        out_specs=ANYWHERE,
        input_output_aliases={0: 0},
        name="after",
    )(value, *earlier)

def reduce_line(blocks, axis, count, unit):
    held, masks = [[0]], []
    while count > 1:
        masks.append(count - 1)
        held.append(held[-1] + [d ^ masks[-1] for d in held[-1]])
        count //= 2
    blocks, steps = dict(enumerate(blocks)), []
    for mask, keep in reversed(list(zip(masks, held))):
        leaving = jnp.stack([blocks[d ^ mask].astype(jnp.bfloat16) for d in keep])
        steps.append(from_peer(leaving, axis, mask * unit))
        if mask != masks[0]:
            blocks = {d: blocks[d] + steps[-1][n].astype(jnp.float32) for n, d in enumerate(keep)}
    return blocks[0], steps


def gather_line(value, axis, count, unit):
    found, mask = {0: value}, count - 1
    while mask:
        for distance in list(found):
            found[distance ^ mask] = from_peer(found[distance], axis, mask * unit)
        mask //= 2
    return [found[distance] for distance in range(count)]

def gelu_slope(x):
    tanh = jnp.tanh(ROOT * (x + CUBIC * (x * x * x)))
    return 0.5 * (1.0 + tanh) + 0.5 * x * (1.0 - tanh * tanh) * (
        ROOT * (1.0 + 3.0 * CUBIC * (x * x))
    )

def act_kernel(x_ref, out_ref, strip):
    width = x_ref.shape[2]

    @pl.loop(0, out_ref.shape[0] // STEP)
    def _(step):
        start = pl.multiple_of(step * STEP, STEP)
        x = x_ref[0, pl.ds(pl.multiple_of(2 * start, 2 * STEP), 2 * STEP), :].astype(jnp.float32)
        act = x * (0.5 * (1.0 + jnp.tanh(ROOT * (x + CUBIC * (x * x * x)))))
        for c in range(width // LANES):
            strip[c] = act[:, c * LANES : (c + 1) * LANES]
        for parity in range(2):
            for c in range(width // LANES):
                picked = strip[c, pl.ds(parity, STEP, stride=2), :].astype(jnp.bfloat16)
                left = parity * width + c * LANES
                out_ref[pl.ds(start, STEP), left : left + LANES] = picked

def activate(inputs):
    fine, width = inputs.shape[1:]
    return pl.pallas_call(
        act_kernel,
        out_shape=jax.ShapeDtypeStruct((fine // 2, 2 * width), jnp.bfloat16),
        in_specs=[pl.BlockSpec(memory_space=pltpu.VMEM)],
        out_specs=pl.BlockSpec(memory_space=pltpu.VMEM),
        scratch_shapes=[pltpu.VMEM((width // LANES, 2 * STEP, LANES), jnp.float32)],
        compiler_params=pltpu.CompilerParams(vmem_limit_bytes=24 << 20),
        cost_estimate=SMALL,
        name="act",
    )(inputs)

def kernel_messages(place, line, trunk_grad, coarse):
    taps, rows, block = line[0].shape
    planes, length = len(line), trunk_grad.shape[1]
    window = (coarse + 2 * HALO) // rows
    half = planes // 2

    def kernel(place, *refs):
        parts, trunk_ref = refs[:planes], refs[planes]
        beside_ref, below_ref, own_ref, edged, sem = refs[planes + 1 :]
        copy = pltpu.make_async_copy(trunk_ref.at[0], edged.at[pl.ds(HALO, length)], sem)
        copy.start()
        edged[:HALO] = jnp.zeros((HALO, block), jnp.bfloat16)
        edged[HALO + length :] = jnp.zeros((HALO, block), jnp.bfloat16)
        for j in range(planes):
            plane = place[1] // 2 ^ j
            for k in range(taps):
                spot = (plane // half * taps + k) * half + plane % half
                beside_ref[window // 2 + spot] = parts[j][k]
                below_ref[spot] = parts[j][k]
        copy.wait()

        def cut(out_ref, spot, distance, first, last):
            base = (place[0] ^ distance) * coarse
            for b in range(first, last):
                out_ref[spot + b - first] = edged[pl.ds(pl.multiple_of(base + b * rows, 16), rows), :]

        cut(beside_ref, 0, 3, 0, window // 2)
        cut(beside_ref, window // 2 + planes * taps, 1, 0, window)
        cut(below_ref, planes * taps, 3, window // 2, window)
        cut(below_ref, planes * taps + window // 2, 2, 0, window)
        cut(own_ref, 0, 0, 0, window)

    count = window // 2 + planes * taps + window
    return pl.pallas_call(
        kernel,
        out_shape=[
            jax.ShapeDtypeStruct((n, rows, block), jnp.bfloat16) for n in (count, count, window)
        ],
        grid_spec=pltpu.PrefetchScalarGridSpec(
            num_scalar_prefetch=1,
            grid=(1,),
            in_specs=[pl.BlockSpec(line[0].shape, lambda i, place: (0, 0, 0))] * planes + [ANYWHERE],
            out_specs=[
                pl.BlockSpec((n, rows, block), lambda i, place: (0, 0, 0))
                for n in (count, count, window)
            ],
            scratch_shapes=[
                pltpu.VMEM((length + 2 * HALO, block), jnp.bfloat16),
                pltpu.SemaphoreType.DMA,
            ],
        ),
        compiler_params=pltpu.CompilerParams(vmem_limit_bytes=32 << 20),
        cost_estimate=SMALL,
        name="kernel_messages",
    )(place, *line, trunk_grad)

def slope_kernel(x_ref, out_ref, scratch):
    width = x_ref.shape[2]

    @pl.loop(0, out_ref.shape[1] // 64)
    def _(step):
        start = pl.multiple_of(step * 64, 64)
        span = pl.ds(pl.multiple_of(2 * start, 128), 128)
        for c in range(width // LANES):
            lanes = slice(c * LANES, (c + 1) * LANES)
            scratch[c] = 0.5 * gelu_slope(x_ref[0, span, lanes].astype(jnp.float32))
            for parity in range(2):
                out_ref[parity, pl.ds(start, 64), lanes] = scratch[c, pl.ds(parity, 64, stride=2), :]

def half_slope(inputs):
    fine, width = inputs.shape[1:]
    return pl.pallas_call(
        slope_kernel,
        out_shape=jax.ShapeDtypeStruct((2, fine // 2, width), jnp.float32),
        in_specs=[pl.BlockSpec(memory_space=pltpu.VMEM)],
        out_specs=pl.BlockSpec(memory_space=pltpu.VMEM),
        scratch_shapes=[pltpu.VMEM((width // LANES, 128, LANES), jnp.float32)],
        compiler_params=pltpu.CompilerParams(vmem_limit_bytes=24 << 20),
        name="half_slope",
    )(inputs)

def start_act(place, coarse, layout, pieces, shifts_ref, held, shifts, sems, shift_sems):
    copies, row = [], 0
    for i, (distance, first, size, offset) in enumerate(layout):
        start = pl.multiple_of((place[0] ^ distance) * coarse + first, 16)
        spot = pl.ds(row, size)
        source = pieces[i].at[pl.ds(offset, size)]
        copies.append(pltpu.make_async_copy(source, held.at[spot], sems.at[i]))
        copies.append(
            pltpu.make_async_copy(shifts_ref.at[pl.ds(start, size)], shifts.at[spot], shift_sems.at[i])
        )
        row += size
    for copy in copies:
        copy.start()
    return copies

def early_terms(place, layout, pieces, shifts, coarse):
    both, columns = pieces[0].shape[1], shifts.shape[1]
    rows = sum(size for _, _, size, _ in layout)
    tile = 256

    def kernel(place, shifts_ref, *refs):
        pieces, total = refs[: len(layout)], refs[len(layout)]
        held, shifts, sems, shift_sems = refs[len(layout) + 1 :]
        copies = start_act(
            place, coarse, layout, pieces, shifts_ref, held, shifts, sems, shift_sems
        )
        for copy in copies:
            copy.wait()

        @pl.loop(0, both // tile)
        def _(i):
            span = pl.ds(pl.multiple_of(i * tile, tile), tile)
            total[span, :] = lax.dot_general(
                held[:, span], shifts[...], (((0,), (0,)), ((), ())), preferred_element_type=jnp.float32
            )

    return pl.pallas_call(
        kernel,
        out_shape=jax.ShapeDtypeStruct((both, columns), jnp.float32),
        grid_spec=pltpu.PrefetchScalarGridSpec(
            num_scalar_prefetch=1,
            grid=(1,),
            in_specs=[ANYWHERE] * (1 + len(pieces)),
            out_specs=pl.BlockSpec((both, columns), lambda i, place: (0, 0)),
            scratch_shapes=[
                pltpu.VMEM((rows, both), jnp.bfloat16),
                pltpu.VMEM((rows, columns), jnp.bfloat16),
                pltpu.SemaphoreType.DMA((len(pieces),)),
                pltpu.SemaphoreType.DMA((len(pieces),)),
            ],
        ),
        compiler_params=pltpu.CompilerParams(vmem_limit_bytes=48 << 20),
        cost_estimate=SMALL,
        name="weight_grad_early",
    )(place, shifts, *pieces)

def late_terms(place, layout, pieces, shifts, early, coarse, scale, planes, taps, rows, earlier):
    both, columns = early.shape
    width, block = both // 2, columns // 3
    count = sum(size for _, _, size, _ in layout)
    tile = 256
    shape = (planes, taps, rows, block)

    def kernel(place, shifts_ref, early_ref, *refs):
        pieces, refs = refs[: len(layout)], refs[len(layout) + len(earlier) :]
        mine_ref, *theirs_refs = refs[:3]
        held, shifts, total, sems, shift_sems, early_sems = refs[3:]
        core, plane = place[1] % 2, place[1] // 2
        copies = start_act(
            place, coarse, layout, pieces, shifts_ref, held, shifts, sems, shift_sems
        )

        def fetch(i):
            span = pl.ds(pl.multiple_of(i * tile, tile), tile)
            return pltpu.make_async_copy(early_ref.at[span], total.at[span], early_sems.at[i])

        for i in range(both // tile):
            fetch(i).start()
        for copy in copies:
            copy.wait()

        @pl.loop(0, both // tile)
        def _(i):
            span = pl.ds(pl.multiple_of(i * tile, tile), tile)
            term = lax.dot_general(
                held[:, span], shifts[...], (((0,), (0,)), ((), ())), preferred_element_type=jnp.float32
            )
            fetch(i).wait()
            total[span, :] += term

        def finish(out_ref, at, j, parity, kind):
            start = ((plane ^ j) * 2 + parity) * rows
            even = pl.ds(pl.multiple_of(start, 16), rows)
            odd = pl.ds(pl.multiple_of(width + start, 16), rows)
            for k, (left, right) in enumerate(GRAD_PARTS):
                term = total[even, left * block : (left + 1) * block]
                term += total[odd, right * block : (right + 1) * block]
                out_ref[at, k] = (scale * term).astype(kind)

        for which, out_ref in enumerate(theirs_refs):

            @pl.loop(0, planes // 2)
            def _(at):
                finish(out_ref, at, at + which * (planes // 2), 1 - core, jnp.bfloat16)

        @pl.loop(0, planes)
        def _(j):
            finish(mine_ref, j, j, core, jnp.float32)

    half_shape = (planes // 2, *shape[1:])
    whole = pl.BlockSpec(shape, lambda i, place: (0, 0, 0, 0))
    half = pl.BlockSpec(half_shape, lambda i, place: (0, 0, 0, 0))
    return pl.pallas_call(
        kernel,
        out_shape=(
            jax.ShapeDtypeStruct(shape, jnp.float32),
            jax.ShapeDtypeStruct(half_shape, jnp.bfloat16),
            jax.ShapeDtypeStruct(half_shape, jnp.bfloat16),
        ),
        grid_spec=pltpu.PrefetchScalarGridSpec(
            num_scalar_prefetch=1,
            grid=(1,),
            in_specs=[ANYWHERE] * (2 + len(pieces) + len(earlier)),
            out_specs=[whole, half, half],
            scratch_shapes=[
                pltpu.VMEM((count, both), jnp.bfloat16),
                pltpu.VMEM((count, columns), jnp.bfloat16),
                pltpu.VMEM((both, columns), jnp.float32),
                pltpu.SemaphoreType.DMA((len(pieces),)),
                pltpu.SemaphoreType.DMA((len(pieces),)),
                pltpu.SemaphoreType.DMA((both // tile,)),
            ],
        ),
        compiler_params=pltpu.CompilerParams(vmem_limit_bytes=48 << 20),
        cost_estimate=SMALL,
        name="weight_grad_late",
    )(place, shifts, early, *pieces, *earlier)

def shifted_total(products, base, lanes, parity):
    total = None
    for by in (0, 1, -1):
        wanted = [k for k in range(products.shape[0]) if ROW_OFFSETS[k][parity] == by]
        if wanted:
            near = pl.ds(base + MARGIN - 8, STEP + 16)
            part = sum(products[k, near, lanes] for k in wanted)[8 + by : 8 + by + STEP]
            total = part if total is None else total + part
    return total

def gradient_stage(place, windows, taps, pieces, distances, slope, begun, shape):
    _, fine, width = shape
    coarse, seqs = fine // 2, lax.axis_size("seq")
    rows, block = pieces[0][0].shape[-2:]
    planes = width // (2 * rows)
    half = planes // 2
    window, used = coarse + 2 * HALO, coarse + 2 * MARGIN
    depth, planar = len(distances) * block, (2, coarse, width)
    last = begun is not None
    needed = list(range(seqs)) if last else distances
    parts = [(d, *part) for d in needed for part in windows[d]]
    operands = [part[1] for part in parts] + [piece[0] for piece in pieces]
    operands += [slope, begun] if last else []

    def body(place, *refs):
        own, refs = refs[: len(parts)], refs[len(parts) :]
        sources, refs = refs[: len(pieces)], refs[len(pieces) :]
        if last:
            (slope_ref, begun_ref), refs = refs[:2], refs[2:]
        out_ref, wv, gv, products, sems, grad_sems = refs[:6]
        me, core = place[0], place[1] % 2

        def kernel_copies(first):
            for number, (array, start, plane, count, flip, distance) in enumerate(pieces):
                spot = pl.ds(distances.index(distance) * block, block)
                if first != (start is not None):
                    continue
                for k in range(SPLIT if first else taps - SPLIT):
                    for h in range(count // half):
                        span = pl.ds(plane + h * half, half)
                        if first:
                            source = sources[number].at[pl.ds(start + (h * SPLIT + k) * half, half)]
                        else:
                            source = sources[number].at[span, distance, k]
                        tap = k if first else SPLIT + k
                        target = wv.at[tap, span, core ^ flip, :, spot]
                        sem = sems.at[tap, number, h]
                        yield tap, pltpu.make_async_copy(source, target, sem)

        def window_copies(target_of, sems):
            for number, (distance, _, start, first, count) in enumerate(parts):
                for b in range(count):
                    target = target_of(distance, pl.ds((first + b) * rows, rows))
                    if target is not None:
                        source = own[number].at[start + b]
                        yield pltpu.make_async_copy(source, target, sems.at[number, b])

        def into_window(distance, span):
            if distance not in distances:
                return None
            return gv.at[span, pl.ds(distances.index(distance) * block, block)]

        early = list(window_copies(into_window, grad_sems))
        late = []
        if last:
            sums, slopes, strip, skips, sum_sems, skip_sems = refs[6:]
            late.append(pltpu.make_async_copy(begun_ref, sums, sum_sems.at[0]))
            late.append(pltpu.make_async_copy(slope_ref, slopes, sum_sems.at[1]))
            late += window_copies(lambda d, span: skips.at[me ^ d, span], skip_sems)
        for copy in early:
            copy.start()
        arriving = sorted([*kernel_copies(True), *kernel_copies(False)], key=lambda pair: pair[0])
        for _, copy in arriving:
            copy.start()
        for copy in late:
            copy.start()
        for copy in early:
            copy.wait()
        for k in range(taps):
            for tap, copy in arriving:
                if tap == k:
                    copy.wait()
            for part in range(2):
                kernel = wv[k, part * half : (part + 1) * half].reshape(2 * half * rows, depth)
                lanes = slice(part * 2 * half * rows, (part + 1) * 2 * half * rows)
                products[k, :, lanes] = lax.dot_general(
                    gv[EDGE : EDGE + used],
                    kernel,
                    (((1,), (1,)), ((), ())),
                    preferred_element_type=jnp.float32,
                )

        for copy in late:
            copy.wait()

        @pl.loop(0, coarse // STEP)
        def _(i):
            base = pl.multiple_of(i * STEP, STEP)
            spot, span = pl.ds(base, STEP), pl.ds(pl.multiple_of(2 * base, 2 * STEP), 2 * STEP)
            for c in range(width // LANES):
                lanes = slice(c * LANES, (c + 1) * LANES)
                if last:
                    left = c * LANES % block
                    skip = skips[c * LANES // block, pl.ds(base + HALO, STEP), left : left + LANES]
                    skip = 0.5 * skip.astype(jnp.float32)
                for parity in range(2):
                    total = shifted_total(products, base, lanes, parity)
                    if last:
                        total = (total + sums[parity, spot, lanes]) * slopes[parity, spot, lanes]
                        strip[c, pl.ds(parity, STEP, stride=2), :] = total + skip
                    else:
                        out_ref[parity, spot, lanes] = total
                if last:
                    out_ref[0, span, lanes] = strip[c].astype(jnp.bfloat16)

    out_shape = jax.ShapeDtypeStruct(shape if last else planar, jnp.bfloat16 if last else jnp.float32)
    scratch = [
        pltpu.VMEM((taps, planes, 2, rows, depth), jnp.bfloat16),
        pltpu.VMEM((window, depth), jnp.bfloat16),
        pltpu.VMEM((taps, used, width), jnp.float32),
        pltpu.SemaphoreType.DMA((taps, len(pieces), 2)),
        pltpu.SemaphoreType.DMA((len(parts), window // rows)),
    ]
    if last:
        scratch += [
            pltpu.VMEM(planar, jnp.float32),
            pltpu.VMEM(planar, jnp.float32),
            pltpu.VMEM((width // LANES, 2 * STEP, LANES), jnp.float32),
            pltpu.VMEM((seqs, window, block), jnp.bfloat16),
            pltpu.SemaphoreType.DMA((2,)),
            pltpu.SemaphoreType.DMA((len(parts), window // rows)),
        ]
    return pl.pallas_call(
        body,
        out_shape=out_shape,
        grid_spec=pltpu.PrefetchScalarGridSpec(
            num_scalar_prefetch=1,
            grid=(1,),
            in_specs=[ANYWHERE] * len(operands),
            out_specs=pl.BlockSpec(out_shape.shape, lambda i, place: (0, 0, 0)),
            scratch_shapes=scratch,
        ),
        compiler_params=pltpu.CompilerParams(vmem_limit_bytes=56 << 20),
        cost_estimate=SMALL,
        name="input_grad",
    )(place, *operands)

def stack_planes(place, line):
    count = len(line)

    def kernel(place, *refs):
        parts, out_ref = refs[:count], refs[count]
        for j in range(count):
            out_ref[place[1] // 2 ^ j] = parts[j][...]

    shape = line[0].shape
    return pl.pallas_call(
        kernel,
        out_shape=jax.ShapeDtypeStruct((count, *shape), line[0].dtype),
        grid_spec=pltpu.PrefetchScalarGridSpec(
            num_scalar_prefetch=1,
            grid=(1,),
            in_specs=[pl.BlockSpec(shape, lambda i, place: (0,) * len(shape))] * count,
            out_specs=pl.BlockSpec((count, *shape), lambda i, place: (0,) * (1 + len(shape))),
        ),
        compiler_params=pltpu.CompilerParams(vmem_limit_bytes=24 << 20),
        cost_estimate=SMALL,
        name="stack_planes",
    )(place, *line)

def on_device_square(inputs, trunk_grad, weights):
    seqs, reps = lax.axis_size("seq"), lax.axis_size("rep")
    me, rep = lax.axis_index("seq"), lax.axis_index("rep")
    place = jnp.stack([me, rep]).astype(jnp.int32)
    taps, rows, block = weights.shape
    fine = inputs.shape[1]
    coarse, planes = fine // 2, reps // 2
    half = coarse // 2

    last_taps = weights[SPLIT:]
    across = [last_taps] + [from_peer(last_taps, "seq", d) for d in range(1, seqs)]

    act = after(activate(inputs), *across[1:])
    beside, below = from_peer(act, "seq", 1), from_peer(act, "seq", 2)
    slope = half_slope(inputs)
    line = gather_line(weights[:SPLIT], "rep", planes, 2)
    line_across = gather_line(after(jnp.stack(across), act, *line[1:]), "rep", planes, 2)
    crossing = (line_across[1], line_across[planes - 1])
    trunk = trunk_grad[0]
    zeros = jnp.zeros((1, block), jnp.bfloat16)
    later = jnp.concatenate([trunk[1:], zeros])
    earlier = jnp.concatenate([zeros, trunk[:-1]])
    shifts = jnp.concatenate([later, trunk, earlier], axis=1)
    to_beside, to_below, own_window = kernel_messages(place, line, trunk_grad, coarse)
    ready = (slope, shifts, to_beside, *crossing)
    top, bottom = after(beside[:half], *ready), after(below[half:], *ready)
    far_top, far_bottom = from_peer(top, "seq", 2), from_peer(bottom, "seq", 1)

    scale = 0.5 * float(fine * seqs * reps) ** (-0.5)
    near_rows = [(d, 0, coarse, 0) for d in range(3)]
    far_rows = [(3, 0, half, 0), (3, half, half, 0)]
    early = early_terms(place, near_rows, [act, beside, below], shifts, coarse)
    line_across[2] = after(line_across[2], early)
    lines = stack_planes(place, line_across)
    far_top, far_bottom = after(far_top, early), after(far_bottom, early)

    to_beside, to_below = (
        after(message, far_top, far_bottom) for message in (to_beside, to_below)
    )
    kept_beside, kept_below = from_peer(to_beside, "seq", 1), from_peer(to_below, "seq", 2)
    other_column, other_lines = from_peer(to_below, "rep", 1), from_peer(lines, "rep", 1)

    mine, *theirs = late_terms(
        place,
        far_rows,
        [far_top, far_bottom],
        shifts,
        early,
        coarse,
        scale,
        planes,
        taps,
        rows,
        [line_across[2]],
    )
    arrived = [from_peer(part, "rep", 1) for part in theirs]
    pairs = []
    for j in range(planes):
        part = arrived[j // (planes // 2)][j % (planes // 2)]
        pairs.append(mine[j] + part.astype(jnp.float32))
    weight_grad, steps = reduce_line(pairs, "rep", planes, 2)

    window = (coarse + 2 * HALO) // rows
    count, side = planes * SPLIT, window // 2
    far_first = from_peer(kept_beside[: side + count // 2], "seq", 2)
    far_second = from_peer(kept_below[count // 2 : count + side], "seq", 1)

    windows = [
        [(own_window, 0, 0, window)],
        [(kept_beside, side + count, 0, window)],
        [(kept_below, count + side, 0, window)],
    ]
    stage = functools.partial(gradient_stage, place, taps=taps, slope=slope, shape=inputs.shape)
    soon = [(to_below, 0, 0, planes, 0, 0), (other_column, 0, 0, planes, 1, 0)]
    for part, start, distance in ((kept_beside, side, 1), (kept_below, 0, 2)):
        soon.append((part, start, 0, planes, 0, distance))
        soon.append((from_peer(part, "rep", 1), start, 0, planes, 1, distance))
    crossed = [
        (part, None, 0, planes, flip, d)
        for flip, part in enumerate((lines, other_lines))
        for d in range(seqs)
    ]
    near = [piece for piece in crossed if piece[-1] < 3]
    begun = stage(windows, pieces=soon + near, distances=[0, 1, 2], begun=None)
    far_first, far_second = after(far_first, begun, *steps[:1]), after(far_second, begun, *steps[:1])
    windows.append([(far_first, 0, 0, side), (far_second, count // 2, side, side)])
    rest = [piece for piece in crossed if piece[-1] == 3]
    for part, start, plane in ((far_first, side, 0), (far_second, 0, planes // 2)):
        rest.append((part, start, plane, planes // 2, 0, 3))
        rest.append((from_peer(part, "rep", 1), start, plane, planes // 2, 1, 3))
    input_grad = stage(windows, pieces=rest, distances=[3], begun=begun)
    weight_grad = weight_grad + after(steps[-1], input_grad)[0].astype(jnp.float32)
    return (input_grad, weight_grad)


def with_halo(value, sides, width):
    for axis, dim in sides:
        peers, length = (lax.axis_size(axis), value.shape[dim])
        up = [(i, (i + 1) % peers) for i in range(peers - 1)]
        down = [(j, i) for i, j in up]
        last = lax.slice_in_dim(value, length - width, length, axis=dim)
        leading = lax.slice_in_dim(value, 0, width, axis=dim)
        before = lax.ppermute(last, axis, up)
        after = lax.ppermute(leading, axis, down)
        value = jnp.concatenate([before, value, after], axis=dim)
    return value

def contract_last(left, right):
    return lax.dot_general(
        left, right, (((1,), (1,)), ((), ())), preferred_element_type=jnp.float32
    )

def contract_first(left, right):
    return lax.dot_general(
        left, right, (((0,), (0,)), ((), ())), preferred_element_type=jnp.float32
    )

def on_device_plain(inputs, trunk_grad, weights):
    taps = weights.shape[0]
    grad = lax.all_to_all(trunk_grad, "seq", split_axis=1, concat_axis=2, tiled=True)
    grad_up = jnp.repeat(grad.astype(jnp.float32) * 0.5, 2, axis=1).astype(jnp.bfloat16)
    rows = grad_up.shape[1]
    padded = with_halo(grad_up, (("seq", 1),), 2)
    shifts = [padded[0, 4 - k : 4 - k + rows] for k in range(taps)]
    inputs_f = inputs[0].astype(jnp.float32)
    act_vals, back = jax.vjp(jax.nn.gelu, inputs_f)
    slope = back(jnp.ones_like(inputs_f))[0]
    act = act_vals.astype(jnp.bfloat16)
    in_width = inputs.shape[2]
    columns = lax.all_gather(weights, "seq", axis=2, tiled=True)
    piece = lax.all_gather(columns, "rep", axis=1, tiled=True)
    result = contract_last(shifts[0], piece[0])
    for project_k in range(1, taps):
        result = result + contract_last(shifts[project_k], piece[project_k])
    input_grad = (result * slope + grad_up[0, :, :in_width].astype(jnp.float32)).astype(
        jnp.bfloat16
    )
    scale_factor = float(rows * lax.axis_size("seq") * lax.axis_size("rep")) ** (-0.5)
    terms = jnp.stack([contract_first(act, shifts[k]) for k in range(taps)]) * scale_factor
    partial_sum = lax.psum_scatter(terms, "rep", scatter_dimension=1, tiled=True)
    weight_grad = lax.psum_scatter(partial_sum, "seq", scatter_dimension=2, tiled=True)
    return (input_grad[None], weight_grad)

def on_device(inputs, trunk_grad, weights):
    square = lax.axis_size("seq") == 4 and lax.axis_size("rep") % 8 == 0
    if square and weights.shape[2] % LANES == 0 and inputs.shape[2] % LANES == 0:
        return on_device_square(inputs, trunk_grad, weights)
    return on_device_plain(inputs, trunk_grad, weights)

def solution(mesh):
    in_specs = (P("rep", "seq", None), P("rep", None, "seq"), P(None, "rep", "seq"))
    out_specs = (P("rep", "seq", None), P(None, "rep", "seq"))
    return jax.shard_map(
        on_device, mesh=mesh, in_specs=in_specs, out_specs=out_specs, check_vma=False
    )
```

```python
import functools
import math

import jax
import jax.numpy as jnp
from jax import lax
from jax.experimental import pallas as pl
from jax.experimental.pallas import tpu as pltpu
from jax.sharding import PartitionSpec as P

LANES = 128
HALO = 32
EDGE = 16
MARGIN = HALO - EDGE
STEP = 64
SPLIT = 3
ROOT = math.sqrt(2.0 / math.pi)
CUBIC = 0.044715
SMALL = pl.CostEstimate(flops=1 << 20, bytes_accessed=1 << 16, transcendentals=0)
ANYWHERE = pl.BlockSpec(memory_space=pl.ANY)
ROW_OFFSETS = ((1, 1), (0, 1), (0, 0), (-1, 0), (-1, -1))
GRAD_PARTS = ((0, 0), (1, 0), (1, 1), (2, 1), (2, 2))

def from_peer(value, axis, distance):
    peers = lax.axis_size(axis)
    return lax.ppermute(value, axis, [(i, i ^ distance) for i in range(peers)])

def after(value, *earlier):
    return pl.pallas_call(
        lambda *refs: None,
        out_shape=jax.ShapeDtypeStruct(value.shape, value.dtype),
        in_specs=[ANYWHERE] * (1 + len(earlier)),
        out_specs=ANYWHERE,
        input_output_aliases={0: 0},
        name="after",
    )(value, *earlier)

def reduce_line(blocks, axis, count, unit):
    held, masks = [[0]], []
    while count > 1:
        masks.append(count - 1)
        held.append(held[-1] + [d ^ masks[-1] for d in held[-1]])
        count //= 2
    blocks, steps = dict(enumerate(blocks)), []
    for mask, keep in reversed(list(zip(masks, held))):
        leaving = jnp.stack([blocks[d ^ mask].astype(jnp.bfloat16) for d in keep])
        steps.append(from_peer(leaving, axis, mask * unit))
        if mask != masks[0]:
            blocks = {d: blocks[d] + steps[-1][n].astype(jnp.float32) for n, d in enumerate(keep)}
    return blocks[0], steps


def gather_line(value, axis, count, unit):
    found, mask = {0: value}, count - 1
    while mask:
        for distance in list(found):
            found[distance ^ mask] = from_peer(found[distance], axis, mask * unit)
        mask //= 2
    return [found[distance] for distance in range(count)]

def gelu_slope(x):
    tanh = jnp.tanh(ROOT * (x + CUBIC * (x * x * x)))
    return 0.5 * (1.0 + tanh) + 0.5 * x * (1.0 - tanh * tanh) * (
        ROOT * (1.0 + 3.0 * CUBIC * (x * x))
    )

def act_kernel(x_ref, out_ref, strip):
    width = x_ref.shape[2]

    @pl.loop(0, out_ref.shape[0] // STEP)
    def _(step):
        start = pl.multiple_of(step * STEP, STEP)
        x = x_ref[0, pl.ds(pl.multiple_of(2 * start, 2 * STEP), 2 * STEP), :].astype(jnp.float32)
        act = x * (0.5 * (1.0 + jnp.tanh(ROOT * (x + CUBIC * (x * x * x)))))
        for c in range(width // LANES):
            strip[c] = act[:, c * LANES : (c + 1) * LANES]
        for parity in range(2):
            for c in range(width // LANES):
                picked = strip[c, pl.ds(parity, STEP, stride=2), :].astype(jnp.bfloat16)
                left = parity * width + c * LANES
                out_ref[pl.ds(start, STEP), left : left + LANES] = picked

def activate(inputs):
    fine, width = inputs.shape[1:]
    return pl.pallas_call(
        act_kernel,
        out_shape=jax.ShapeDtypeStruct((fine // 2, 2 * width), jnp.bfloat16),
        in_specs=[pl.BlockSpec(memory_space=pltpu.VMEM)],
        out_specs=pl.BlockSpec(memory_space=pltpu.VMEM),
        scratch_shapes=[pltpu.VMEM((width // LANES, 2 * STEP, LANES), jnp.float32)],
        compiler_params=pltpu.CompilerParams(vmem_limit_bytes=24 << 20),
        cost_estimate=SMALL,
        name="act",
    )(inputs)

def kernel_messages(place, line, trunk_grad, coarse):
    taps, rows, block = line[0].shape
    planes, length = len(line), trunk_grad.shape[1]
    window = (coarse + 2 * HALO) // rows
    half = planes // 2

    def kernel(place, *refs):
        parts, trunk_ref = refs[:planes], refs[planes]
        beside_ref, below_ref, own_ref, edged, sem = refs[planes + 1 :]
        copy = pltpu.make_async_copy(trunk_ref.at[0], edged.at[pl.ds(HALO, length)], sem)
        copy.start()
        edged[:HALO] = jnp.zeros((HALO, block), jnp.bfloat16)
        edged[HALO + length :] = jnp.zeros((HALO, block), jnp.bfloat16)
        for j in range(planes):
            plane = place[1] // 2 ^ j
            for k in range(taps):
                spot = (plane // half * taps + k) * half + plane % half
                beside_ref[window // 2 + spot] = parts[j][k]
                below_ref[spot] = parts[j][k]
        copy.wait()

        def cut(out_ref, spot, distance, first, last):
            base = (place[0] ^ distance) * coarse
            for b in range(first, last):
                out_ref[spot + b - first] = edged[pl.ds(pl.multiple_of(base + b * rows, 16), rows), :]

        cut(beside_ref, 0, 3, 0, window // 2)
        cut(beside_ref, window // 2 + planes * taps, 1, 0, window)
        cut(below_ref, planes * taps, 3, window // 2, window)
        cut(below_ref, planes * taps + window // 2, 2, 0, window)
        cut(own_ref, 0, 0, 0, window)

    count = window // 2 + planes * taps + window
    return pl.pallas_call(
        kernel,
        out_shape=[
            jax.ShapeDtypeStruct((n, rows, block), jnp.bfloat16) for n in (count, count, window)
        ],
        grid_spec=pltpu.PrefetchScalarGridSpec(
            num_scalar_prefetch=1,
            grid=(1,),
            in_specs=[pl.BlockSpec(line[0].shape, lambda i, place: (0, 0, 0))] * planes + [ANYWHERE],
            out_specs=[
                pl.BlockSpec((n, rows, block), lambda i, place: (0, 0, 0))
                for n in (count, count, window)
            ],
            scratch_shapes=[
                pltpu.VMEM((length + 2 * HALO, block), jnp.bfloat16),
                pltpu.SemaphoreType.DMA,
            ],
        ),
        compiler_params=pltpu.CompilerParams(vmem_limit_bytes=32 << 20),
        cost_estimate=SMALL,
        name="kernel_messages",
    )(place, *line, trunk_grad)

def slope_kernel(x_ref, out_ref, scratch):
    width = x_ref.shape[2]

    @pl.loop(0, out_ref.shape[1] // 64)
    def _(step):
        start = pl.multiple_of(step * 64, 64)
        span = pl.ds(pl.multiple_of(2 * start, 128), 128)
        for c in range(width // LANES):
            lanes = slice(c * LANES, (c + 1) * LANES)
            scratch[c] = 0.5 * gelu_slope(x_ref[0, span, lanes].astype(jnp.float32))
            for parity in range(2):
                out_ref[parity, pl.ds(start, 64), lanes] = scratch[c, pl.ds(parity, 64, stride=2), :]

def half_slope(inputs):
    fine, width = inputs.shape[1:]
    return pl.pallas_call(
        slope_kernel,
        out_shape=jax.ShapeDtypeStruct((2, fine // 2, width), jnp.float32),
        in_specs=[pl.BlockSpec(memory_space=pltpu.VMEM)],
        out_specs=pl.BlockSpec(memory_space=pltpu.VMEM),
        scratch_shapes=[pltpu.VMEM((width // LANES, 128, LANES), jnp.float32)],
        compiler_params=pltpu.CompilerParams(vmem_limit_bytes=24 << 20),
        name="half_slope",
    )(inputs)

def start_act(place, coarse, layout, pieces, shifts_ref, held, shifts, sems, shift_sems):
    copies, row = [], 0
    for i, (distance, first, size, offset) in enumerate(layout):
        start = pl.multiple_of((place[0] ^ distance) * coarse + first, 16)
        spot = pl.ds(row, size)
        source = pieces[i].at[pl.ds(offset, size)]
        copies.append(pltpu.make_async_copy(source, held.at[spot], sems.at[i]))
        copies.append(
            pltpu.make_async_copy(shifts_ref.at[pl.ds(start, size)], shifts.at[spot], shift_sems.at[i])
        )
        row += size
    for copy in copies:
        copy.start()
    return copies

def early_terms(place, layout, pieces, shifts, coarse):
    both, columns = pieces[0].shape[1], shifts.shape[1]
    rows = sum(size for _, _, size, _ in layout)
    tile = 256

    def kernel(place, shifts_ref, *refs):
        pieces, total = refs[: len(layout)], refs[len(layout)]
        held, shifts, sems, shift_sems = refs[len(layout) + 1 :]
        copies = start_act(
            place, coarse, layout, pieces, shifts_ref, held, shifts, sems, shift_sems
        )
        for copy in copies:
            copy.wait()

        @pl.loop(0, both // tile)
        def _(i):
            span = pl.ds(pl.multiple_of(i * tile, tile), tile)
            total[span, :] = lax.dot_general(
                held[:, span], shifts[...], (((0,), (0,)), ((), ())), preferred_element_type=jnp.float32
            )

    return pl.pallas_call(
        kernel,
        out_shape=jax.ShapeDtypeStruct((both, columns), jnp.float32),
        grid_spec=pltpu.PrefetchScalarGridSpec(
            num_scalar_prefetch=1,
            grid=(1,),
            in_specs=[ANYWHERE] * (1 + len(pieces)),
            out_specs=pl.BlockSpec((both, columns), lambda i, place: (0, 0)),
            scratch_shapes=[
                pltpu.VMEM((rows, both), jnp.bfloat16),
                pltpu.VMEM((rows, columns), jnp.bfloat16),
                pltpu.SemaphoreType.DMA((len(pieces),)),
                pltpu.SemaphoreType.DMA((len(pieces),)),
            ],
        ),
        compiler_params=pltpu.CompilerParams(vmem_limit_bytes=48 << 20),
        cost_estimate=SMALL,
        name="weight_grad_early",
    )(place, shifts, *pieces)

def late_terms(place, layout, pieces, shifts, early, coarse, scale, planes, taps, rows, earlier):
    both, columns = early.shape
    width, block = both // 2, columns // 3
    count = sum(size for _, _, size, _ in layout)
    tile = 256
    shape = (planes, taps, rows, block)

    def kernel(place, shifts_ref, early_ref, *refs):
        pieces, refs = refs[: len(layout)], refs[len(layout) + len(earlier) :]
        mine_ref, *theirs_refs = refs[:3]
        held, shifts, total, sems, shift_sems, early_sems = refs[3:]
        core, plane = place[1] % 2, place[1] // 2
        copies = start_act(
            place, coarse, layout, pieces, shifts_ref, held, shifts, sems, shift_sems
        )

        def fetch(i):
            span = pl.ds(pl.multiple_of(i * tile, tile), tile)
            return pltpu.make_async_copy(early_ref.at[span], total.at[span], early_sems.at[i])

        for i in range(both // tile):
            fetch(i).start()
        for copy in copies:
            copy.wait()

        @pl.loop(0, both // tile)
        def _(i):
            span = pl.ds(pl.multiple_of(i * tile, tile), tile)
            term = lax.dot_general(
                held[:, span], shifts[...], (((0,), (0,)), ((), ())), preferred_element_type=jnp.float32
            )
            fetch(i).wait()
            total[span, :] += term

        def finish(out_ref, at, j, parity, kind):
            start = ((plane ^ j) * 2 + parity) * rows
            even = pl.ds(pl.multiple_of(start, 16), rows)
            odd = pl.ds(pl.multiple_of(width + start, 16), rows)
            for k, (left, right) in enumerate(GRAD_PARTS):
                term = total[even, left * block : (left + 1) * block]
                term += total[odd, right * block : (right + 1) * block]
                out_ref[at, k] = (scale * term).astype(kind)

        for which, out_ref in enumerate(theirs_refs):

            @pl.loop(0, planes // 2)
            def _(at):
                finish(out_ref, at, at + which * (planes // 2), 1 - core, jnp.bfloat16)

        @pl.loop(0, planes)
        def _(j):
            finish(mine_ref, j, j, core, jnp.float32)

    half_shape = (planes // 2, *shape[1:])
    whole = pl.BlockSpec(shape, lambda i, place: (0, 0, 0, 0))
    half = pl.BlockSpec(half_shape, lambda i, place: (0, 0, 0, 0))
    return pl.pallas_call(
        kernel,
        out_shape=(
            jax.ShapeDtypeStruct(shape, jnp.float32),
            jax.ShapeDtypeStruct(half_shape, jnp.bfloat16),
            jax.ShapeDtypeStruct(half_shape, jnp.bfloat16),
        ),
        grid_spec=pltpu.PrefetchScalarGridSpec(
            num_scalar_prefetch=1,
            grid=(1,),
            in_specs=[ANYWHERE] * (2 + len(pieces) + len(earlier)),
            out_specs=[whole, half, half],
            scratch_shapes=[
                pltpu.VMEM((count, both), jnp.bfloat16),
                pltpu.VMEM((count, columns), jnp.bfloat16),
                pltpu.VMEM((both, columns), jnp.float32),
                pltpu.SemaphoreType.DMA((len(pieces),)),
                pltpu.SemaphoreType.DMA((len(pieces),)),
                pltpu.SemaphoreType.DMA((both // tile,)),
            ],
        ),
        compiler_params=pltpu.CompilerParams(vmem_limit_bytes=48 << 20),
        cost_estimate=SMALL,
        name="weight_grad_late",
    )(place, shifts, early, *pieces, *earlier)

def shifted_total(products, base, lanes, parity):
    total = None
    for by in (0, 1, -1):
        wanted = [k for k in range(products.shape[0]) if ROW_OFFSETS[k][parity] == by]
        if wanted:
            near = pl.ds(base + MARGIN - 8, STEP + 16)
            part = sum(products[k, near, lanes] for k in wanted)[8 + by : 8 + by + STEP]
            total = part if total is None else total + part
    return total

def gradient_stage(place, windows, taps, pieces, distances, slope, begun, shape):
    _, fine, width = shape
    coarse, seqs = fine // 2, lax.axis_size("seq")
    rows, block = pieces[0][0].shape[-2:]
    planes = width // (2 * rows)
    half = planes // 2
    window, used = coarse + 2 * HALO, coarse + 2 * MARGIN
    depth, planar = len(distances) * block, (2, coarse, width)
    last = begun is not None
    needed = list(range(seqs)) if last else distances
    parts = [(d, *part) for d in needed for part in windows[d]]
    operands = [part[1] for part in parts] + [piece[0] for piece in pieces]
    operands += [slope, begun] if last else []

    def body(place, *refs):
        own, refs = refs[: len(parts)], refs[len(parts) :]
        sources, refs = refs[: len(pieces)], refs[len(pieces) :]
        if last:
            (slope_ref, begun_ref), refs = refs[:2], refs[2:]
        out_ref, wv, gv, products, sems, grad_sems = refs[:6]
        me, core = place[0], place[1] % 2

        def kernel_copies(first):
            for number, (array, start, plane, count, flip, distance) in enumerate(pieces):
                spot = pl.ds(distances.index(distance) * block, block)
                if first != (start is not None):
                    continue
                for k in range(SPLIT if first else taps - SPLIT):
                    for h in range(count // half):
                        span = pl.ds(plane + h * half, half)
                        if first:
                            source = sources[number].at[pl.ds(start + (h * SPLIT + k) * half, half)]
                        else:
                            source = sources[number].at[span, distance, k]
                        tap = k if first else SPLIT + k
                        target = wv.at[tap, span, core ^ flip, :, spot]
                        sem = sems.at[tap, number, h]
                        yield tap, pltpu.make_async_copy(source, target, sem)

        def window_copies(target_of, sems):
            for number, (distance, _, start, first, count) in enumerate(parts):
                for b in range(count):
                    target = target_of(distance, pl.ds((first + b) * rows, rows))
                    if target is not None:
                        source = own[number].at[start + b]
                        yield pltpu.make_async_copy(source, target, sems.at[number, b])

        def into_window(distance, span):
            if distance not in distances:
                return None
            return gv.at[span, pl.ds(distances.index(distance) * block, block)]

        early = list(window_copies(into_window, grad_sems))
        late = []
        if last:
            sums, slopes, strip, skips, sum_sems, skip_sems = refs[6:]

            def row_copies(n):
                span = pl.ds(pl.multiple_of(n * 2 * STEP, 2 * STEP), 2 * STEP)
                pairs = ((begun_ref, sums), (slope_ref, slopes))
                for number, (source, target) in enumerate(pairs):
                    sem = sum_sems.at[number, n]
                    yield pltpu.make_async_copy(source.at[:, span], target.at[:, span], sem)

            late += window_copies(lambda d, span: skips.at[me ^ d, span], skip_sems)
        for copy in early:
            copy.start()
        arriving = sorted([*kernel_copies(True), *kernel_copies(False)], key=lambda pair: pair[0])
        for _, copy in arriving:
            copy.start()
        for copy in late:
            copy.start()
        if last:
            for n in range(coarse // (2 * STEP)):
                for copy in row_copies(n):
                    copy.start()
        for copy in early:
            copy.wait()
        for k in range(taps):
            for tap, copy in arriving:
                if tap == k:
                    copy.wait()
            for part in range(2):
                kernel = wv[k, part * half : (part + 1) * half].reshape(2 * half * rows, depth)
                lanes = slice(part * 2 * half * rows, (part + 1) * 2 * half * rows)
                products[k, :, lanes] = lax.dot_general(
                    gv[EDGE : EDGE + used],
                    kernel,
                    (((1,), (1,)), ((), ())),
                    preferred_element_type=jnp.float32,
                )

        for copy in late:
            copy.wait()

        @pl.loop(0, coarse // STEP)
        def _(i):
            base = pl.multiple_of(i * STEP, STEP)
            spot, span = pl.ds(base, STEP), pl.ds(pl.multiple_of(2 * base, 2 * STEP), 2 * STEP)
            if last:

                @pl.when(i % 2 == 0)
                def _():
                    for copy in row_copies(i // 2):
                        copy.wait()

            for c in range(width // LANES):
                lanes = slice(c * LANES, (c + 1) * LANES)
                if last:
                    left = c * LANES % block
                    skip = skips[c * LANES // block, pl.ds(base + HALO, STEP), left : left + LANES]
                    skip = 0.5 * skip.astype(jnp.float32)
                for parity in range(2):
                    total = shifted_total(products, base, lanes, parity)
                    if last:
                        total = (total + sums[parity, spot, lanes]) * slopes[parity, spot, lanes]
                        strip[c, pl.ds(parity, STEP, stride=2), :] = total + skip
                    else:
                        out_ref[parity, spot, lanes] = total
                if last:
                    out_ref[0, span, lanes] = strip[c].astype(jnp.bfloat16)

    out_shape = jax.ShapeDtypeStruct(shape if last else planar, jnp.bfloat16 if last else jnp.float32)
    scratch = [
        pltpu.VMEM((taps, planes, 2, rows, depth), jnp.bfloat16),
        pltpu.VMEM((window, depth), jnp.bfloat16),
        pltpu.VMEM((taps, used, width), jnp.float32),
        pltpu.SemaphoreType.DMA((taps, len(pieces), 2)),
        pltpu.SemaphoreType.DMA((len(parts), window // rows)),
    ]
    if last:
        scratch += [
            pltpu.VMEM(planar, jnp.float32),
            pltpu.VMEM(planar, jnp.float32),
            pltpu.VMEM((width // LANES, 2 * STEP, LANES), jnp.float32),
            pltpu.VMEM((seqs, window, block), jnp.bfloat16),
            pltpu.SemaphoreType.DMA((2, coarse // (2 * STEP))),
            pltpu.SemaphoreType.DMA((len(parts), window // rows)),
        ]
    return pl.pallas_call(
        body,
        out_shape=out_shape,
        grid_spec=pltpu.PrefetchScalarGridSpec(
            num_scalar_prefetch=1,
            grid=(1,),
            in_specs=[ANYWHERE] * len(operands),
            out_specs=pl.BlockSpec(out_shape.shape, lambda i, place: (0, 0, 0)),
            scratch_shapes=scratch,
        ),
        compiler_params=pltpu.CompilerParams(vmem_limit_bytes=56 << 20),
        cost_estimate=SMALL,
        name="input_grad",
    )(place, *operands)

def stack_planes(place, line):
    count = len(line)

    def kernel(place, *refs):
        parts, out_ref = refs[:count], refs[count]
        for j in range(count):
            out_ref[place[1] // 2 ^ j] = parts[j][...]

    shape = line[0].shape
    return pl.pallas_call(
        kernel,
        out_shape=jax.ShapeDtypeStruct((count, *shape), line[0].dtype),
        grid_spec=pltpu.PrefetchScalarGridSpec(
            num_scalar_prefetch=1,
            grid=(1,),
            in_specs=[pl.BlockSpec(shape, lambda i, place: (0,) * len(shape))] * count,
            out_specs=pl.BlockSpec((count, *shape), lambda i, place: (0,) * (1 + len(shape))),
        ),
        compiler_params=pltpu.CompilerParams(vmem_limit_bytes=24 << 20),
        cost_estimate=SMALL,
        name="stack_planes",
    )(place, *line)

def on_device_square(inputs, trunk_grad, weights):
    seqs, reps = lax.axis_size("seq"), lax.axis_size("rep")
    me, rep = lax.axis_index("seq"), lax.axis_index("rep")
    place = jnp.stack([me, rep]).astype(jnp.int32)
    taps, rows, block = weights.shape
    fine = inputs.shape[1]
    coarse, planes = fine // 2, reps // 2
    half = coarse // 2

    last_taps = weights[SPLIT:]
    across = [last_taps] + [from_peer(last_taps, "seq", d) for d in range(1, seqs)]

    act = after(activate(inputs), *across[1:])
    beside, below = from_peer(act, "seq", 1), from_peer(act, "seq", 2)
    slope = half_slope(inputs)
    line = gather_line(weights[:SPLIT], "rep", planes, 2)
    line_across = gather_line(after(jnp.stack(across), act, *line[1:]), "rep", planes, 2)
    crossing = (line_across[1], line_across[planes - 1])
    trunk = trunk_grad[0]
    zeros = jnp.zeros((1, block), jnp.bfloat16)
    later = jnp.concatenate([trunk[1:], zeros])
    earlier = jnp.concatenate([zeros, trunk[:-1]])
    shifts = jnp.concatenate([later, trunk, earlier], axis=1)
    to_beside, to_below, own_window = kernel_messages(place, line, trunk_grad, coarse)
    ready = (slope, shifts, to_beside, *crossing)
    top, bottom = after(beside[:half], *ready), after(below[half:], *ready)
    far_top, far_bottom = from_peer(top, "seq", 2), from_peer(bottom, "seq", 1)

    scale = 0.5 * float(fine * seqs * reps) ** (-0.5)
    near_rows = [(d, 0, coarse, 0) for d in range(3)]
    far_rows = [(3, 0, half, 0), (3, half, half, 0)]
    early = early_terms(place, near_rows, [act, beside, below], shifts, coarse)
    line_across[2] = after(line_across[2], early)
    lines = stack_planes(place, line_across)
    far_top, far_bottom = after(far_top, early), after(far_bottom, early)

    to_beside, to_below = (
        after(message, far_top, far_bottom) for message in (to_beside, to_below)
    )
    kept_beside, kept_below = from_peer(to_beside, "seq", 1), from_peer(to_below, "seq", 2)
    other_column, other_lines = from_peer(to_below, "rep", 1), from_peer(lines, "rep", 1)

    mine, *theirs = late_terms(
        place,
        far_rows,
        [far_top, far_bottom],
        shifts,
        early,
        coarse,
        scale,
        planes,
        taps,
        rows,
        [line_across[2]],
    )
    arrived = [from_peer(part, "rep", 1) for part in theirs]
    pairs = []
    for j in range(planes):
        part = arrived[j // (planes // 2)][j % (planes // 2)]
        pairs.append(mine[j] + part.astype(jnp.float32))
    weight_grad, steps = reduce_line(pairs, "rep", planes, 2)

    window = (coarse + 2 * HALO) // rows
    count, side = planes * SPLIT, window // 2
    far_first = from_peer(kept_beside[: side + count // 2], "seq", 2)
    far_second = from_peer(kept_below[count // 2 : count + side], "seq", 1)

    windows = [
        [(own_window, 0, 0, window)],
        [(kept_beside, side + count, 0, window)],
        [(kept_below, count + side, 0, window)],
    ]
    stage = functools.partial(gradient_stage, place, taps=taps, slope=slope, shape=inputs.shape)
    soon = [(to_below, 0, 0, planes, 0, 0), (other_column, 0, 0, planes, 1, 0)]
    for part, start, distance in ((kept_beside, side, 1), (kept_below, 0, 2)):
        soon.append((part, start, 0, planes, 0, distance))
        soon.append((from_peer(part, "rep", 1), start, 0, planes, 1, distance))
    crossed = [
        (part, None, 0, planes, flip, d)
        for flip, part in enumerate((lines, other_lines))
        for d in range(seqs)
    ]
    near = [piece for piece in crossed if piece[-1] < 3]
    begun = stage(windows, pieces=soon + near, distances=[0, 1, 2], begun=None)
    far_first, far_second = after(far_first, begun, *steps[:1]), after(far_second, begun, *steps[:1])
    windows.append([(far_first, 0, 0, side), (far_second, count // 2, side, side)])
    rest = [piece for piece in crossed if piece[-1] == 3]
    for part, start, plane in ((far_first, side, 0), (far_second, 0, planes // 2)):
        rest.append((part, start, plane, planes // 2, 0, 3))
        rest.append((from_peer(part, "rep", 1), start, plane, planes // 2, 1, 3))
    input_grad = stage(windows, pieces=rest, distances=[3], begun=begun)
    weight_grad = weight_grad + after(steps[-1], input_grad)[0].astype(jnp.float32)
    return (input_grad, weight_grad)


def with_halo(value, sides, width):
    for axis, dim in sides:
        peers, length = (lax.axis_size(axis), value.shape[dim])
        up = [(i, (i + 1) % peers) for i in range(peers - 1)]
        down = [(j, i) for i, j in up]
        last = lax.slice_in_dim(value, length - width, length, axis=dim)
        leading = lax.slice_in_dim(value, 0, width, axis=dim)
        before = lax.ppermute(last, axis, up)
        after = lax.ppermute(leading, axis, down)
        value = jnp.concatenate([before, value, after], axis=dim)
    return value

def contract_last(left, right):
    return lax.dot_general(
        left, right, (((1,), (1,)), ((), ())), preferred_element_type=jnp.float32
    )

def contract_first(left, right):
    return lax.dot_general(
        left, right, (((0,), (0,)), ((), ())), preferred_element_type=jnp.float32
    )

def on_device_plain(inputs, trunk_grad, weights):
    taps = weights.shape[0]
    grad = lax.all_to_all(trunk_grad, "seq", split_axis=1, concat_axis=2, tiled=True)
    grad_up = jnp.repeat(grad.astype(jnp.float32) * 0.5, 2, axis=1).astype(jnp.bfloat16)
    rows = grad_up.shape[1]
    padded = with_halo(grad_up, (("seq", 1),), 2)
    shifts = [padded[0, 4 - k : 4 - k + rows] for k in range(taps)]
    inputs_f = inputs[0].astype(jnp.float32)
    act_vals, back = jax.vjp(jax.nn.gelu, inputs_f)
    slope = back(jnp.ones_like(inputs_f))[0]
    act = act_vals.astype(jnp.bfloat16)
    in_width = inputs.shape[2]
    columns = lax.all_gather(weights, "seq", axis=2, tiled=True)
    piece = lax.all_gather(columns, "rep", axis=1, tiled=True)
    result = contract_last(shifts[0], piece[0])
    for project_k in range(1, taps):
        result = result + contract_last(shifts[project_k], piece[project_k])
    input_grad = (result * slope + grad_up[0, :, :in_width].astype(jnp.float32)).astype(
        jnp.bfloat16
    )
    scale_factor = float(rows * lax.axis_size("seq") * lax.axis_size("rep")) ** (-0.5)
    terms = jnp.stack([contract_first(act, shifts[k]) for k in range(taps)]) * scale_factor
    partial_sum = lax.psum_scatter(terms, "rep", scatter_dimension=1, tiled=True)
    weight_grad = lax.psum_scatter(partial_sum, "seq", scatter_dimension=2, tiled=True)
    return (input_grad[None], weight_grad)

def on_device(inputs, trunk_grad, weights):
    square = lax.axis_size("seq") == 4 and lax.axis_size("rep") % 8 == 0
    if square and weights.shape[2] % LANES == 0 and inputs.shape[2] % LANES == 0:
        return on_device_square(inputs, trunk_grad, weights)
    return on_device_plain(inputs, trunk_grad, weights)

def solution(mesh):
    in_specs = (P("rep", "seq", None), P("rep", None, "seq"), P(None, "rep", "seq"))
    out_specs = (P("rep", "seq", None), P(None, "rep", "seq"))
    return jax.shard_map(
        on_device, mesh=mesh, in_specs=in_specs, out_specs=out_specs, check_vma=False
    )
```

```python
import functools
import math

import jax
import jax.numpy as jnp
from jax import lax
from jax.experimental import pallas as pl
from jax.experimental.pallas import tpu as pltpu
from jax.sharding import PartitionSpec as P

LANES = 128
HALO = 32
EDGE = 16
MARGIN = HALO - EDGE
STEP = 64
SPLIT = 3
ROOT = math.sqrt(2.0 / math.pi)
CUBIC = 0.044715
SMALL = pl.CostEstimate(flops=1 << 20, bytes_accessed=1 << 16, transcendentals=0)
ANYWHERE = pl.BlockSpec(memory_space=pl.ANY)
ROW_OFFSETS = ((1, 1), (0, 1), (0, 0), (-1, 0), (-1, -1))
GRAD_PARTS = ((0, 0), (1, 0), (1, 1), (2, 1), (2, 2))

def from_peer(value, axis, distance):
    peers = lax.axis_size(axis)
    return lax.ppermute(value, axis, [(i, i ^ distance) for i in range(peers)])

def after(value, *earlier):
    return pl.pallas_call(
        lambda *refs: None,
        out_shape=jax.ShapeDtypeStruct(value.shape, value.dtype),
        in_specs=[ANYWHERE] * (1 + len(earlier)),
        out_specs=ANYWHERE,
        input_output_aliases={0: 0},
        name="after",
    )(value, *earlier)

def reduce_line(blocks, axis, count, unit):
    held, masks = [[0]], []
    while count > 1:
        masks.append(count - 1)
        held.append(held[-1] + [d ^ masks[-1] for d in held[-1]])
        count //= 2
    blocks, steps = dict(enumerate(blocks)), []
    for mask, keep in reversed(list(zip(masks, held))):
        leaving = jnp.stack([blocks[d ^ mask].astype(jnp.bfloat16) for d in keep])
        steps.append(from_peer(leaving, axis, mask * unit))
        if mask != masks[0]:
            blocks = {d: blocks[d] + steps[-1][n].astype(jnp.float32) for n, d in enumerate(keep)}
    return blocks[0], steps


def gather_line(value, axis, count, unit):
    found, mask = {0: value}, count - 1
    while mask:
        for distance in list(found):
            found[distance ^ mask] = from_peer(found[distance], axis, mask * unit)
        mask //= 2
    return [found[distance] for distance in range(count)]

def gelu_slope(x):
    tanh = jnp.tanh(ROOT * (x + CUBIC * (x * x * x)))
    return 0.5 * (1.0 + tanh) + 0.5 * x * (1.0 - tanh * tanh) * (
        ROOT * (1.0 + 3.0 * CUBIC * (x * x))
    )

def act_kernel(x_ref, out_ref, strip):
    width = x_ref.shape[2]

    @pl.loop(0, out_ref.shape[0] // STEP)
    def _(step):
        start = pl.multiple_of(step * STEP, STEP)
        x = x_ref[0, pl.ds(pl.multiple_of(2 * start, 2 * STEP), 2 * STEP), :].astype(jnp.float32)
        act = x * (0.5 * (1.0 + jnp.tanh(ROOT * (x + CUBIC * (x * x * x)))))
        for c in range(width // LANES):
            strip[c] = act[:, c * LANES : (c + 1) * LANES]
        for parity in range(2):
            for c in range(width // LANES):
                picked = strip[c, pl.ds(parity, STEP, stride=2), :].astype(jnp.bfloat16)
                left = parity * width + c * LANES
                out_ref[pl.ds(start, STEP), left : left + LANES] = picked

def activate(inputs):
    fine, width = inputs.shape[1:]
    return pl.pallas_call(
        act_kernel,
        out_shape=jax.ShapeDtypeStruct((fine // 2, 2 * width), jnp.bfloat16),
        in_specs=[pl.BlockSpec(memory_space=pltpu.VMEM)],
        out_specs=pl.BlockSpec(memory_space=pltpu.VMEM),
        scratch_shapes=[pltpu.VMEM((width // LANES, 2 * STEP, LANES), jnp.float32)],
        compiler_params=pltpu.CompilerParams(vmem_limit_bytes=24 << 20),
        cost_estimate=SMALL,
        name="act",
    )(inputs)

def kernel_messages(place, line, trunk_grad, coarse):
    taps, rows, block = line[0].shape
    planes, length = len(line), trunk_grad.shape[1]
    window = (coarse + 2 * HALO) // rows
    half = planes // 2

    def kernel(place, *refs):
        parts, trunk_ref = refs[:planes], refs[planes]
        beside_ref, below_ref, own_ref, edged, sem = refs[planes + 1 :]
        copy = pltpu.make_async_copy(trunk_ref.at[0], edged.at[pl.ds(HALO, length)], sem)
        copy.start()
        edged[:HALO] = jnp.zeros((HALO, block), jnp.bfloat16)
        edged[HALO + length :] = jnp.zeros((HALO, block), jnp.bfloat16)
        for j in range(planes):
            plane = place[1] // 2 ^ j
            for k in range(taps):
                spot = (plane // half * taps + k) * half + plane % half
                beside_ref[window // 2 + spot] = parts[j][k]
                below_ref[spot] = parts[j][k]
        copy.wait()

        def cut(out_ref, spot, distance, first, last):
            base = (place[0] ^ distance) * coarse
            for b in range(first, last):
                out_ref[spot + b - first] = edged[pl.ds(pl.multiple_of(base + b * rows, 16), rows), :]

        cut(beside_ref, 0, 3, 0, window // 2)
        cut(beside_ref, window // 2 + planes * taps, 1, 0, window)
        cut(below_ref, planes * taps, 3, window // 2, window)
        cut(below_ref, planes * taps + window // 2, 2, 0, window)
        cut(own_ref, 0, 0, 0, window)

    count = window // 2 + planes * taps + window
    return pl.pallas_call(
        kernel,
        out_shape=[
            jax.ShapeDtypeStruct((n, rows, block), jnp.bfloat16) for n in (count, count, window)
        ],
        grid_spec=pltpu.PrefetchScalarGridSpec(
            num_scalar_prefetch=1,
            grid=(1,),
            in_specs=[pl.BlockSpec(line[0].shape, lambda i, place: (0, 0, 0))] * planes + [ANYWHERE],
            out_specs=[
                pl.BlockSpec((n, rows, block), lambda i, place: (0, 0, 0))
                for n in (count, count, window)
            ],
            scratch_shapes=[
                pltpu.VMEM((length + 2 * HALO, block), jnp.bfloat16),
                pltpu.SemaphoreType.DMA,
            ],
        ),
        compiler_params=pltpu.CompilerParams(vmem_limit_bytes=32 << 20),
        cost_estimate=SMALL,
        name="kernel_messages",
    )(place, *line, trunk_grad)

def slope_kernel(x_ref, out_ref, scratch):
    width = x_ref.shape[2]

    @pl.loop(0, out_ref.shape[1] // 64)
    def _(step):
        start = pl.multiple_of(step * 64, 64)
        span = pl.ds(pl.multiple_of(2 * start, 128), 128)
        for c in range(width // LANES):
            lanes = slice(c * LANES, (c + 1) * LANES)
            scratch[c] = 0.5 * gelu_slope(x_ref[0, span, lanes].astype(jnp.float32))
            for parity in range(2):
                out_ref[parity, pl.ds(start, 64), lanes] = scratch[c, pl.ds(parity, 64, stride=2), :]

def half_slope(inputs):
    fine, width = inputs.shape[1:]
    return pl.pallas_call(
        slope_kernel,
        out_shape=jax.ShapeDtypeStruct((2, fine // 2, width), jnp.float32),
        in_specs=[pl.BlockSpec(memory_space=pltpu.VMEM)],
        out_specs=pl.BlockSpec(memory_space=pltpu.VMEM),
        scratch_shapes=[pltpu.VMEM((width // LANES, 128, LANES), jnp.float32)],
        compiler_params=pltpu.CompilerParams(vmem_limit_bytes=24 << 20),
        name="half_slope",
    )(inputs)

def start_act(place, coarse, layout, pieces, shifts_ref, held, shifts, sems, shift_sems):
    copies, row = [], 0
    for i, (distance, first, size, offset) in enumerate(layout):
        start = pl.multiple_of((place[0] ^ distance) * coarse + first, 16)
        spot = pl.ds(row, size)
        source = pieces[i].at[pl.ds(offset, size)]
        copies.append(pltpu.make_async_copy(source, held.at[spot], sems.at[i]))
        copies.append(
            pltpu.make_async_copy(shifts_ref.at[pl.ds(start, size)], shifts.at[spot], shift_sems.at[i])
        )
        row += size
    for copy in copies:
        copy.start()
    return copies

def early_terms(place, layout, pieces, shifts, coarse):
    both, columns = pieces[0].shape[1], shifts.shape[1]
    rows = sum(size for _, _, size, _ in layout)
    tile = 256

    def kernel(place, shifts_ref, *refs):
        pieces, total = refs[: len(layout)], refs[len(layout)]
        held, shifts, sems, shift_sems = refs[len(layout) + 1 :]
        copies = start_act(
            place, coarse, layout, pieces, shifts_ref, held, shifts, sems, shift_sems
        )
        for copy in copies:
            copy.wait()

        @pl.loop(0, both // tile)
        def _(i):
            span = pl.ds(pl.multiple_of(i * tile, tile), tile)
            total[span, :] = lax.dot_general(
                held[:, span], shifts[...], (((0,), (0,)), ((), ())), preferred_element_type=jnp.float32
            )

    return pl.pallas_call(
        kernel,
        out_shape=jax.ShapeDtypeStruct((both, columns), jnp.float32),
        grid_spec=pltpu.PrefetchScalarGridSpec(
            num_scalar_prefetch=1,
            grid=(1,),
            in_specs=[ANYWHERE] * (1 + len(pieces)),
            out_specs=pl.BlockSpec((both, columns), lambda i, place: (0, 0)),
            scratch_shapes=[
                pltpu.VMEM((rows, both), jnp.bfloat16),
                pltpu.VMEM((rows, columns), jnp.bfloat16),
                pltpu.SemaphoreType.DMA((len(pieces),)),
                pltpu.SemaphoreType.DMA((len(pieces),)),
            ],
        ),
        compiler_params=pltpu.CompilerParams(vmem_limit_bytes=48 << 20),
        cost_estimate=SMALL,
        name="weight_grad_early",
    )(place, shifts, *pieces)

def late_terms(place, layout, pieces, shifts, early, coarse, scale, planes, taps, rows, earlier):
    both, columns = early.shape
    width, block = both // 2, columns // 3
    count = sum(size for _, _, size, _ in layout)
    tile = 256
    shape = (planes, taps, rows, block)

    def kernel(place, shifts_ref, early_ref, *refs):
        pieces, refs = refs[: len(layout)], refs[len(layout) + len(earlier) :]
        mine_ref, *theirs_refs = refs[:3]
        held, shifts, total, sems, shift_sems, early_sems = refs[3:]
        core, plane = place[1] % 2, place[1] // 2
        copies = start_act(
            place, coarse, layout, pieces, shifts_ref, held, shifts, sems, shift_sems
        )

        def fetch(i):
            span = pl.ds(pl.multiple_of(i * tile, tile), tile)
            return pltpu.make_async_copy(early_ref.at[span], total.at[span], early_sems.at[i])

        for i in range(both // tile):
            fetch(i).start()
        for copy in copies:
            copy.wait()

        @pl.loop(0, both // tile)
        def _(i):
            span = pl.ds(pl.multiple_of(i * tile, tile), tile)
            term = lax.dot_general(
                held[:, span], shifts[...], (((0,), (0,)), ((), ())), preferred_element_type=jnp.float32
            )
            fetch(i).wait()
            total[span, :] += term

        def finish(out_ref, at, j, parity, kind):
            start = ((plane ^ j) * 2 + parity) * rows
            even = pl.ds(pl.multiple_of(start, 16), rows)
            odd = pl.ds(pl.multiple_of(width + start, 16), rows)
            for k, (left, right) in enumerate(GRAD_PARTS):
                term = total[even, left * block : (left + 1) * block]
                term += total[odd, right * block : (right + 1) * block]
                out_ref[at, k] = (scale * term).astype(kind)

        for which, out_ref in enumerate(theirs_refs):

            @pl.loop(0, planes // 2)
            def _(at):
                finish(out_ref, at, at + which * (planes // 2), 1 - core, jnp.bfloat16)

        @pl.loop(0, planes)
        def _(j):
            finish(mine_ref, j, j, core, jnp.float32)

    half_shape = (planes // 2, *shape[1:])
    whole = pl.BlockSpec(shape, lambda i, place: (0, 0, 0, 0))
    half = pl.BlockSpec(half_shape, lambda i, place: (0, 0, 0, 0))
    return pl.pallas_call(
        kernel,
        out_shape=(
            jax.ShapeDtypeStruct(shape, jnp.float32),
            jax.ShapeDtypeStruct(half_shape, jnp.bfloat16),
            jax.ShapeDtypeStruct(half_shape, jnp.bfloat16),
        ),
        grid_spec=pltpu.PrefetchScalarGridSpec(
            num_scalar_prefetch=1,
            grid=(1,),
            in_specs=[ANYWHERE] * (2 + len(pieces) + len(earlier)),
            out_specs=[whole, half, half],
            scratch_shapes=[
                pltpu.VMEM((count, both), jnp.bfloat16),
                pltpu.VMEM((count, columns), jnp.bfloat16),
                pltpu.VMEM((both, columns), jnp.float32),
                pltpu.SemaphoreType.DMA((len(pieces),)),
                pltpu.SemaphoreType.DMA((len(pieces),)),
                pltpu.SemaphoreType.DMA((both // tile,)),
            ],
        ),
        compiler_params=pltpu.CompilerParams(vmem_limit_bytes=48 << 20),
        cost_estimate=SMALL,
        name="weight_grad_late",
    )(place, shifts, early, *pieces, *earlier)

def shifted_total(products, base, lanes, parity):
    total = None
    for by in (0, 1, -1):
        wanted = [k for k in range(products.shape[0]) if ROW_OFFSETS[k][parity] == by]
        if wanted:
            near = pl.ds(base + MARGIN - 8, STEP + 16)
            part = sum(products[k, near, lanes] for k in wanted)[8 + by : 8 + by + STEP]
            total = part if total is None else total + part
    return total

def gradient_stage(place, windows, taps, pieces, distances, slope, begun, shape):
    _, fine, width = shape
    coarse, seqs = fine // 2, lax.axis_size("seq")
    rows, block = pieces[0][0].shape[-2:]
    planes = width // (2 * rows)
    half = planes // 2
    window, used = coarse + 2 * HALO, coarse + 2 * MARGIN
    depth, planar = len(distances) * block, (2, coarse, width)
    last = begun is not None
    needed = list(range(seqs)) if last else distances
    parts = [(d, *part) for d in needed for part in windows[d]]
    operands = [part[1] for part in parts] + [piece[0] for piece in pieces]
    operands += [slope, begun] if last else []

    def body(place, *refs):
        own, refs = refs[: len(parts)], refs[len(parts) :]
        sources, refs = refs[: len(pieces)], refs[len(pieces) :]
        if last:
            (slope_ref, begun_ref), refs = refs[:2], refs[2:]
        out_ref, wv, gv, products, sems, grad_sems = refs[:6]
        me, core = place[0], place[1] % 2

        def kernel_copies(first):
            for number, (array, start, plane, count, flip, distance) in enumerate(pieces):
                spot = pl.ds(distances.index(distance) * block, block)
                if first != (start is not None):
                    continue
                for k in range(SPLIT if first else taps - SPLIT):
                    for h in range(count // half):
                        span = pl.ds(plane + h * half, half)
                        if first:
                            source = sources[number].at[pl.ds(start + (h * SPLIT + k) * half, half)]
                        else:
                            source = sources[number].at[span, distance, k]
                        tap = k if first else SPLIT + k
                        target = wv.at[tap, span, core ^ flip, :, spot]
                        sem = sems.at[tap, number, h]
                        yield tap, pltpu.make_async_copy(source, target, sem)

        def window_copies(target_of, sems):
            for number, (distance, _, start, first, count) in enumerate(parts):
                for b in range(count):
                    target = target_of(distance, pl.ds((first + b) * rows, rows))
                    if target is not None:
                        source = own[number].at[start + b]
                        yield pltpu.make_async_copy(source, target, sems.at[number, b])

        def into_window(distance, span):
            if distance not in distances:
                return None
            return gv.at[span, pl.ds(distances.index(distance) * block, block)]

        early = list(window_copies(into_window, grad_sems))
        late = []
        if last:
            sums, slopes, strip, skips, sum_sems, skip_sems = refs[6:]
            late.append(pltpu.make_async_copy(begun_ref, sums, sum_sems.at[0]))
            late.append(pltpu.make_async_copy(slope_ref, slopes, sum_sems.at[1]))
            late += window_copies(lambda d, span: skips.at[me ^ d, span], skip_sems)
        for copy in early:
            copy.start()
        arriving = sorted([*kernel_copies(True), *kernel_copies(False)], key=lambda pair: pair[0])
        for _, copy in arriving:
            copy.start()
        for copy in late:
            copy.start()
        for copy in early:
            copy.wait()
        for k in range(taps):
            for tap, copy in arriving:
                if tap == k:
                    copy.wait()
            for part in range(2):
                kernel = wv[k, part * half : (part + 1) * half].reshape(2 * half * rows, depth)
                lanes = slice(part * 2 * half * rows, (part + 1) * 2 * half * rows)
                products[k, :, lanes] = lax.dot_general(
                    gv[EDGE : EDGE + used],
                    kernel,
                    (((1,), (1,)), ((), ())),
                    preferred_element_type=jnp.float32,
                )

        for copy in late:
            copy.wait()

        @pl.loop(0, coarse // STEP)
        def _(i):
            base = pl.multiple_of(i * STEP, STEP)
            spot, span = pl.ds(base, STEP), pl.ds(pl.multiple_of(2 * base, 2 * STEP), 2 * STEP)
            for c in range(width // LANES):
                lanes = slice(c * LANES, (c + 1) * LANES)
                if last:
                    left = c * LANES % block
                    skip = skips[c * LANES // block, pl.ds(base + HALO, STEP), left : left + LANES]
                    skip = 0.5 * skip.astype(jnp.float32)
                for parity in range(2):
                    total = shifted_total(products, base, lanes, parity)
                    if last:
                        total = (total + sums[parity, spot, lanes]) * slopes[parity, spot, lanes]
                        strip[c, pl.ds(parity, STEP, stride=2), :] = total + skip
                    else:
                        out_ref[parity, spot, lanes] = total
                if last:
                    out_ref[0, span, lanes] = strip[c].astype(jnp.bfloat16)

    out_shape = jax.ShapeDtypeStruct(shape if last else planar, jnp.bfloat16 if last else jnp.float32)
    scratch = [
        pltpu.VMEM((taps, planes, 2, rows, depth), jnp.bfloat16),
        pltpu.VMEM((window, depth), jnp.bfloat16),
        pltpu.VMEM((taps, used, width), jnp.float32),
        pltpu.SemaphoreType.DMA((taps, len(pieces), 2)),
        pltpu.SemaphoreType.DMA((len(parts), window // rows)),
    ]
    if last:
        scratch += [
            pltpu.VMEM(planar, jnp.float32),
            pltpu.VMEM(planar, jnp.float32),
            pltpu.VMEM((width // LANES, 2 * STEP, LANES), jnp.float32),
            pltpu.VMEM((seqs, window, block), jnp.bfloat16),
            pltpu.SemaphoreType.DMA((2,)),
            pltpu.SemaphoreType.DMA((len(parts), window // rows)),
        ]
    return pl.pallas_call(
        body,
        out_shape=out_shape,
        grid_spec=pltpu.PrefetchScalarGridSpec(
            num_scalar_prefetch=1,
            grid=(1,),
            in_specs=[ANYWHERE] * len(operands),
            out_specs=pl.BlockSpec(out_shape.shape, lambda i, place: (0, 0, 0)),
            scratch_shapes=scratch,
        ),
        compiler_params=pltpu.CompilerParams(vmem_limit_bytes=56 << 20),
        cost_estimate=SMALL,
        name="input_grad",
    )(place, *operands)

def stack_planes(place, line):
    count = len(line)

    def kernel(place, *refs):
        parts, out_ref = refs[:count], refs[count]
        for j in range(count):
            out_ref[place[1] // 2 ^ j] = parts[j][...]

    shape = line[0].shape
    return pl.pallas_call(
        kernel,
        out_shape=jax.ShapeDtypeStruct((count, *shape), line[0].dtype),
        grid_spec=pltpu.PrefetchScalarGridSpec(
            num_scalar_prefetch=1,
            grid=(1,),
            in_specs=[pl.BlockSpec(shape, lambda i, place: (0,) * len(shape))] * count,
            out_specs=pl.BlockSpec((count, *shape), lambda i, place: (0,) * (1 + len(shape))),
        ),
        compiler_params=pltpu.CompilerParams(vmem_limit_bytes=24 << 20),
        cost_estimate=SMALL,
        name="stack_planes",
    )(place, *line)

def on_device_square(inputs, trunk_grad, weights):
    seqs, reps = lax.axis_size("seq"), lax.axis_size("rep")
    me, rep = lax.axis_index("seq"), lax.axis_index("rep")
    place = jnp.stack([me, rep]).astype(jnp.int32)
    taps, rows, block = weights.shape
    fine = inputs.shape[1]
    coarse, planes = fine // 2, reps // 2
    half = coarse // 2

    last_taps = weights[SPLIT:]
    across = [last_taps] + [from_peer(last_taps, "seq", d) for d in range(1, seqs)]

    act = after(activate(inputs), *across[1:])
    beside, below = from_peer(act, "seq", 1), from_peer(act, "seq", 2)
    slope = half_slope(inputs)
    line = gather_line(after(weights[:SPLIT], last_taps), "rep", planes, 2)
    line_across = gather_line(after(jnp.stack(across), act, *line[1:]), "rep", planes, 2)
    crossing = (line_across[1], line_across[planes - 1])
    trunk = trunk_grad[0]
    zeros = jnp.zeros((1, block), jnp.bfloat16)
    later = jnp.concatenate([trunk[1:], zeros])
    earlier = jnp.concatenate([zeros, trunk[:-1]])
    shifts = jnp.concatenate([later, trunk, earlier], axis=1)
    to_beside, to_below, own_window = kernel_messages(place, line, trunk_grad, coarse)
    ready = (slope, shifts, to_beside, *crossing)
    top, bottom = after(beside[:half], *ready), after(below[half:], *ready)
    far_top, far_bottom = from_peer(top, "seq", 2), from_peer(bottom, "seq", 1)

    scale = 0.5 * float(fine * seqs * reps) ** (-0.5)
    near_rows = [(d, 0, coarse, 0) for d in range(3)]
    far_rows = [(3, 0, half, 0), (3, half, half, 0)]
    early = early_terms(place, near_rows, [act, beside, below], shifts, coarse)
    line_across[2] = after(line_across[2], early)
    lines = stack_planes(place, line_across)
    far_top, far_bottom = after(far_top, early), after(far_bottom, early)

    to_beside, to_below = (
        after(message, far_top, far_bottom) for message in (to_beside, to_below)
    )
    kept_beside, kept_below = from_peer(to_beside, "seq", 1), from_peer(to_below, "seq", 2)
    other_column, other_lines = from_peer(to_below, "rep", 1), from_peer(lines, "rep", 1)

    mine, *theirs = late_terms(
        place,
        far_rows,
        [far_top, far_bottom],
        shifts,
        early,
        coarse,
        scale,
        planes,
        taps,
        rows,
        [line_across[2]],
    )
    arrived = [from_peer(part, "rep", 1) for part in theirs]
    pairs = []
    for j in range(planes):
        part = arrived[j // (planes // 2)][j % (planes // 2)]
        pairs.append(mine[j] + part.astype(jnp.float32))
    weight_grad, steps = reduce_line(pairs, "rep", planes, 2)

    window = (coarse + 2 * HALO) // rows
    count, side = planes * SPLIT, window // 2
    far_first = from_peer(kept_beside[: side + count // 2], "seq", 2)
    far_second = from_peer(kept_below[count // 2 : count + side], "seq", 1)

    windows = [
        [(own_window, 0, 0, window)],
        [(kept_beside, side + count, 0, window)],
        [(kept_below, count + side, 0, window)],
    ]
    stage = functools.partial(gradient_stage, place, taps=taps, slope=slope, shape=inputs.shape)
    soon = [(to_below, 0, 0, planes, 0, 0), (other_column, 0, 0, planes, 1, 0)]
    for part, start, distance in ((kept_beside, side, 1), (kept_below, 0, 2)):
        soon.append((part, start, 0, planes, 0, distance))
        soon.append((from_peer(part, "rep", 1), start, 0, planes, 1, distance))
    crossed = [
        (part, None, 0, planes, flip, d)
        for flip, part in enumerate((lines, other_lines))
        for d in range(seqs)
    ]
    near = [piece for piece in crossed if piece[-1] < 3]
    begun = stage(windows, pieces=soon + near, distances=[0, 1, 2], begun=None)
    far_first, far_second = after(far_first, begun, *steps[:1]), after(far_second, begun, *steps[:1])
    windows.append([(far_first, 0, 0, side), (far_second, count // 2, side, side)])
    rest = [piece for piece in crossed if piece[-1] == 3]
    for part, start, plane in ((far_first, side, 0), (far_second, 0, planes // 2)):
        rest.append((part, start, plane, planes // 2, 0, 3))
        rest.append((from_peer(part, "rep", 1), start, plane, planes // 2, 1, 3))
    input_grad = stage(windows, pieces=rest, distances=[3], begun=begun)
    weight_grad = weight_grad + after(steps[-1], input_grad)[0].astype(jnp.float32)
    return (input_grad, weight_grad)


def with_halo(value, sides, width):
    for axis, dim in sides:
        peers, length = (lax.axis_size(axis), value.shape[dim])
        up = [(i, (i + 1) % peers) for i in range(peers - 1)]
        down = [(j, i) for i, j in up]
        last = lax.slice_in_dim(value, length - width, length, axis=dim)
        leading = lax.slice_in_dim(value, 0, width, axis=dim)
        before = lax.ppermute(last, axis, up)
        after = lax.ppermute(leading, axis, down)
        value = jnp.concatenate([before, value, after], axis=dim)
    return value

def contract_last(left, right):
    return lax.dot_general(
        left, right, (((1,), (1,)), ((), ())), preferred_element_type=jnp.float32
    )

def contract_first(left, right):
    return lax.dot_general(
        left, right, (((0,), (0,)), ((), ())), preferred_element_type=jnp.float32
    )

def on_device_plain(inputs, trunk_grad, weights):
    taps = weights.shape[0]
    grad = lax.all_to_all(trunk_grad, "seq", split_axis=1, concat_axis=2, tiled=True)
    grad_up = jnp.repeat(grad.astype(jnp.float32) * 0.5, 2, axis=1).astype(jnp.bfloat16)
    rows = grad_up.shape[1]
    padded = with_halo(grad_up, (("seq", 1),), 2)
    shifts = [padded[0, 4 - k : 4 - k + rows] for k in range(taps)]
    inputs_f = inputs[0].astype(jnp.float32)
    act_vals, back = jax.vjp(jax.nn.gelu, inputs_f)
    slope = back(jnp.ones_like(inputs_f))[0]
    act = act_vals.astype(jnp.bfloat16)
    in_width = inputs.shape[2]
    columns = lax.all_gather(weights, "seq", axis=2, tiled=True)
    piece = lax.all_gather(columns, "rep", axis=1, tiled=True)
    result = contract_last(shifts[0], piece[0])
    for project_k in range(1, taps):
        result = result + contract_last(shifts[project_k], piece[project_k])
    input_grad = (result * slope + grad_up[0, :, :in_width].astype(jnp.float32)).astype(
        jnp.bfloat16
    )
    scale_factor = float(rows * lax.axis_size("seq") * lax.axis_size("rep")) ** (-0.5)
    terms = jnp.stack([contract_first(act, shifts[k]) for k in range(taps)]) * scale_factor
    partial_sum = lax.psum_scatter(terms, "rep", scatter_dimension=1, tiled=True)
    weight_grad = lax.psum_scatter(partial_sum, "seq", scatter_dimension=2, tiled=True)
    return (input_grad[None], weight_grad)

def on_device(inputs, trunk_grad, weights):
    square = lax.axis_size("seq") == 4 and lax.axis_size("rep") % 8 == 0
    if square and weights.shape[2] % LANES == 0 and inputs.shape[2] % LANES == 0:
        return on_device_square(inputs, trunk_grad, weights)
    return on_device_plain(inputs, trunk_grad, weights)

def solution(mesh):
    in_specs = (P("rep", "seq", None), P("rep", None, "seq"), P(None, "rep", "seq"))
    out_specs = (P("rep", "seq", None), P(None, "rep", "seq"))
    return jax.shard_map(
        on_device, mesh=mesh, in_specs=in_specs, out_specs=out_specs, check_vma=False
    )
```

```python
import functools
import math

import jax
import jax.numpy as jnp
from jax import lax
from jax.experimental import pallas as pl
from jax.experimental.pallas import tpu as pltpu
from jax.sharding import PartitionSpec as P

LANES = 128
HALO = 32
EDGE = 16
MARGIN = HALO - EDGE
STEP = 128
SPLIT = 3
ROOT = math.sqrt(2.0 / math.pi)
CUBIC = 0.044715
SMALL = pl.CostEstimate(flops=1 << 20, bytes_accessed=1 << 16, transcendentals=0)
ANYWHERE = pl.BlockSpec(memory_space=pl.ANY)
ROW_OFFSETS = ((1, 1), (0, 1), (0, 0), (-1, 0), (-1, -1))
GRAD_PARTS = ((0, 0), (1, 0), (1, 1), (2, 1), (2, 2))

def from_peer(value, axis, distance):
    peers = lax.axis_size(axis)
    return lax.ppermute(value, axis, [(i, i ^ distance) for i in range(peers)])

def after(value, *earlier):
    return pl.pallas_call(
        lambda *refs: None,
        out_shape=jax.ShapeDtypeStruct(value.shape, value.dtype),
        in_specs=[ANYWHERE] * (1 + len(earlier)),
        out_specs=ANYWHERE,
        input_output_aliases={0: 0},
        name="after",
    )(value, *earlier)

def reduce_line(blocks, axis, count, unit):
    held, masks = [[0]], []
    while count > 1:
        masks.append(count - 1)
        held.append(held[-1] + [d ^ masks[-1] for d in held[-1]])
        count //= 2
    blocks, steps = dict(enumerate(blocks)), []
    for mask, keep in reversed(list(zip(masks, held))):
        leaving = jnp.stack([blocks[d ^ mask].astype(jnp.bfloat16) for d in keep])
        steps.append(from_peer(leaving, axis, mask * unit))
        if mask != masks[0]:
            blocks = {d: blocks[d] + steps[-1][n].astype(jnp.float32) for n, d in enumerate(keep)}
    return blocks[0], steps


def gather_line(value, axis, count, unit):
    found, mask = {0: value}, count - 1
    while mask:
        for distance in list(found):
            found[distance ^ mask] = from_peer(found[distance], axis, mask * unit)
        mask //= 2
    return [found[distance] for distance in range(count)]

def gelu_slope(x):
    tanh = jnp.tanh(ROOT * (x + CUBIC * (x * x * x)))
    return 0.5 * (1.0 + tanh) + 0.5 * x * (1.0 - tanh * tanh) * (
        ROOT * (1.0 + 3.0 * CUBIC * (x * x))
    )

def act_kernel(x_ref, out_ref, strip):
    width = x_ref.shape[2]

    @pl.loop(0, out_ref.shape[0] // STEP)
    def _(step):
        start = pl.multiple_of(step * STEP, STEP)
        x = x_ref[0, pl.ds(pl.multiple_of(2 * start, 2 * STEP), 2 * STEP), :].astype(jnp.float32)
        act = x * (0.5 * (1.0 + jnp.tanh(ROOT * (x + CUBIC * (x * x * x)))))
        for c in range(width // LANES):
            strip[c] = act[:, c * LANES : (c + 1) * LANES]
        for parity in range(2):
            for c in range(width // LANES):
                picked = strip[c, pl.ds(parity, STEP, stride=2), :].astype(jnp.bfloat16)
                left = parity * width + c * LANES
                out_ref[pl.ds(start, STEP), left : left + LANES] = picked

def activate(inputs):
    fine, width = inputs.shape[1:]
    return pl.pallas_call(
        act_kernel,
        out_shape=jax.ShapeDtypeStruct((fine // 2, 2 * width), jnp.bfloat16),
        in_specs=[pl.BlockSpec(memory_space=pltpu.VMEM)],
        out_specs=pl.BlockSpec(memory_space=pltpu.VMEM),
        scratch_shapes=[pltpu.VMEM((width // LANES, 2 * STEP, LANES), jnp.float32)],
        compiler_params=pltpu.CompilerParams(vmem_limit_bytes=24 << 20),
        cost_estimate=SMALL,
        name="act",
    )(inputs)

def kernel_messages(place, line, trunk_grad, coarse):
    taps, rows, block = line[0].shape
    planes, length = len(line), trunk_grad.shape[1]
    window = (coarse + 2 * HALO) // rows
    half = planes // 2

    def kernel(place, *refs):
        parts, trunk_ref = refs[:planes], refs[planes]
        beside_ref, below_ref, own_ref, edged, sem = refs[planes + 1 :]
        copy = pltpu.make_async_copy(trunk_ref.at[0], edged.at[pl.ds(HALO, length)], sem)
        copy.start()
        edged[:HALO] = jnp.zeros((HALO, block), jnp.bfloat16)
        edged[HALO + length :] = jnp.zeros((HALO, block), jnp.bfloat16)
        for j in range(planes):
            plane = place[1] // 2 ^ j
            for k in range(taps):
                spot = (plane // half * taps + k) * half + plane % half
                beside_ref[window // 2 + spot] = parts[j][k]
                below_ref[spot] = parts[j][k]
        copy.wait()

        def cut(out_ref, spot, distance, first, last):
            base = (place[0] ^ distance) * coarse
            for b in range(first, last):
                out_ref[spot + b - first] = edged[pl.ds(pl.multiple_of(base + b * rows, 16), rows), :]

        cut(beside_ref, 0, 3, 0, window // 2)
        cut(beside_ref, window // 2 + planes * taps, 1, 0, window)
        cut(below_ref, planes * taps, 3, window // 2, window)
        cut(below_ref, planes * taps + window // 2, 2, 0, window)
        cut(own_ref, 0, 0, 0, window)

    count = window // 2 + planes * taps + window
    return pl.pallas_call(
        kernel,
        out_shape=[
            jax.ShapeDtypeStruct((n, rows, block), jnp.bfloat16) for n in (count, count, window)
        ],
        grid_spec=pltpu.PrefetchScalarGridSpec(
            num_scalar_prefetch=1,
            grid=(1,),
            in_specs=[pl.BlockSpec(line[0].shape, lambda i, place: (0, 0, 0))] * planes + [ANYWHERE],
            out_specs=[
                pl.BlockSpec((n, rows, block), lambda i, place: (0, 0, 0))
                for n in (count, count, window)
            ],
            scratch_shapes=[
                pltpu.VMEM((length + 2 * HALO, block), jnp.bfloat16),
                pltpu.SemaphoreType.DMA,
            ],
        ),
        compiler_params=pltpu.CompilerParams(vmem_limit_bytes=32 << 20),
        cost_estimate=SMALL,
        name="kernel_messages",
    )(place, *line, trunk_grad)

def slope_kernel(x_ref, out_ref, scratch):
    width = x_ref.shape[2]

    @pl.loop(0, out_ref.shape[1] // 64)
    def _(step):
        start = pl.multiple_of(step * 64, 64)
        span = pl.ds(pl.multiple_of(2 * start, 128), 128)
        for c in range(width // LANES):
            lanes = slice(c * LANES, (c + 1) * LANES)
            scratch[c] = 0.5 * gelu_slope(x_ref[0, span, lanes].astype(jnp.float32))
            for parity in range(2):
                out_ref[parity, pl.ds(start, 64), lanes] = scratch[c, pl.ds(parity, 64, stride=2), :]

def half_slope(inputs):
    fine, width = inputs.shape[1:]
    return pl.pallas_call(
        slope_kernel,
        out_shape=jax.ShapeDtypeStruct((2, fine // 2, width), jnp.float32),
        in_specs=[pl.BlockSpec(memory_space=pltpu.VMEM)],
        out_specs=pl.BlockSpec(memory_space=pltpu.VMEM),
        scratch_shapes=[pltpu.VMEM((width // LANES, 128, LANES), jnp.float32)],
        compiler_params=pltpu.CompilerParams(vmem_limit_bytes=24 << 20),
        name="half_slope",
    )(inputs)

def start_act(place, coarse, layout, pieces, shifts_ref, held, shifts, sems, shift_sems):
    copies, row = [], 0
    for i, (distance, first, size, offset) in enumerate(layout):
        start = pl.multiple_of((place[0] ^ distance) * coarse + first, 16)
        spot = pl.ds(row, size)
        source = pieces[i].at[pl.ds(offset, size)]
        copies.append(pltpu.make_async_copy(source, held.at[spot], sems.at[i]))
        copies.append(
            pltpu.make_async_copy(shifts_ref.at[pl.ds(start, size)], shifts.at[spot], shift_sems.at[i])
        )
        row += size
    for copy in copies:
        copy.start()
    return copies

def early_terms(place, layout, pieces, shifts, coarse):
    both, columns = pieces[0].shape[1], shifts.shape[1]
    rows = sum(size for _, _, size, _ in layout)
    tile = 256

    def kernel(place, shifts_ref, *refs):
        pieces, total = refs[: len(layout)], refs[len(layout)]
        held, shifts, sems, shift_sems = refs[len(layout) + 1 :]
        copies = start_act(
            place, coarse, layout, pieces, shifts_ref, held, shifts, sems, shift_sems
        )
        for copy in copies:
            copy.wait()

        @pl.loop(0, both // tile)
        def _(i):
            span = pl.ds(pl.multiple_of(i * tile, tile), tile)
            total[span, :] = lax.dot_general(
                held[:, span], shifts[...], (((0,), (0,)), ((), ())), preferred_element_type=jnp.float32
            )

    return pl.pallas_call(
        kernel,
        out_shape=jax.ShapeDtypeStruct((both, columns), jnp.float32),
        grid_spec=pltpu.PrefetchScalarGridSpec(
            num_scalar_prefetch=1,
            grid=(1,),
            in_specs=[ANYWHERE] * (1 + len(pieces)),
            out_specs=pl.BlockSpec((both, columns), lambda i, place: (0, 0)),
            scratch_shapes=[
                pltpu.VMEM((rows, both), jnp.bfloat16),
                pltpu.VMEM((rows, columns), jnp.bfloat16),
                pltpu.SemaphoreType.DMA((len(pieces),)),
                pltpu.SemaphoreType.DMA((len(pieces),)),
            ],
        ),
        compiler_params=pltpu.CompilerParams(vmem_limit_bytes=48 << 20),
        cost_estimate=SMALL,
        name="weight_grad_early",
    )(place, shifts, *pieces)

def late_terms(place, layout, pieces, shifts, early, coarse, scale, planes, taps, rows, earlier):
    both, columns = early.shape
    width, block = both // 2, columns // 3
    count = sum(size for _, _, size, _ in layout)
    tile = 256
    shape = (planes, taps, rows, block)

    def kernel(place, shifts_ref, early_ref, *refs):
        pieces, refs = refs[: len(layout)], refs[len(layout) + len(earlier) :]
        mine_ref, *theirs_refs = refs[:3]
        held, shifts, total, sems, shift_sems, early_sems = refs[3:]
        core, plane = place[1] % 2, place[1] // 2
        copies = start_act(
            place, coarse, layout, pieces, shifts_ref, held, shifts, sems, shift_sems
        )

        def fetch(i):
            span = pl.ds(pl.multiple_of(i * tile, tile), tile)
            return pltpu.make_async_copy(early_ref.at[span], total.at[span], early_sems.at[i])

        for i in range(both // tile):
            fetch(i).start()
        for copy in copies:
            copy.wait()

        @pl.loop(0, both // tile)
        def _(i):
            span = pl.ds(pl.multiple_of(i * tile, tile), tile)
            term = lax.dot_general(
                held[:, span], shifts[...], (((0,), (0,)), ((), ())), preferred_element_type=jnp.float32
            )
            fetch(i).wait()
            total[span, :] += term

        def finish(out_ref, at, j, parity, kind):
            start = ((plane ^ j) * 2 + parity) * rows
            even = pl.ds(pl.multiple_of(start, 16), rows)
            odd = pl.ds(pl.multiple_of(width + start, 16), rows)
            for k, (left, right) in enumerate(GRAD_PARTS):
                term = total[even, left * block : (left + 1) * block]
                term += total[odd, right * block : (right + 1) * block]
                out_ref[at, k] = (scale * term).astype(kind)

        for which, out_ref in enumerate(theirs_refs):

            @pl.loop(0, planes // 2)
            def _(at):
                finish(out_ref, at, at + which * (planes // 2), 1 - core, jnp.bfloat16)

        @pl.loop(0, planes)
        def _(j):
            finish(mine_ref, j, j, core, jnp.float32)

    half_shape = (planes // 2, *shape[1:])
    whole = pl.BlockSpec(shape, lambda i, place: (0, 0, 0, 0))
    half = pl.BlockSpec(half_shape, lambda i, place: (0, 0, 0, 0))
    return pl.pallas_call(
        kernel,
        out_shape=(
            jax.ShapeDtypeStruct(shape, jnp.float32),
            jax.ShapeDtypeStruct(half_shape, jnp.bfloat16),
            jax.ShapeDtypeStruct(half_shape, jnp.bfloat16),
        ),
        grid_spec=pltpu.PrefetchScalarGridSpec(
            num_scalar_prefetch=1,
            grid=(1,),
            in_specs=[ANYWHERE] * (2 + len(pieces) + len(earlier)),
            out_specs=[whole, half, half],
            scratch_shapes=[
                pltpu.VMEM((count, both), jnp.bfloat16),
                pltpu.VMEM((count, columns), jnp.bfloat16),
                pltpu.VMEM((both, columns), jnp.float32),
                pltpu.SemaphoreType.DMA((len(pieces),)),
                pltpu.SemaphoreType.DMA((len(pieces),)),
                pltpu.SemaphoreType.DMA((both // tile,)),
            ],
        ),
        compiler_params=pltpu.CompilerParams(vmem_limit_bytes=48 << 20),
        cost_estimate=SMALL,
        name="weight_grad_late",
    )(place, shifts, early, *pieces, *earlier)

def shifted_total(products, base, lanes, parity):
    total = None
    for by in (0, 1, -1):
        wanted = [k for k in range(products.shape[0]) if ROW_OFFSETS[k][parity] == by]
        if wanted:
            near = pl.ds(base + MARGIN - 8, STEP + 16)
            part = sum(products[k, near, lanes] for k in wanted)[8 + by : 8 + by + STEP]
            total = part if total is None else total + part
    return total

def gradient_stage(place, windows, taps, pieces, distances, slope, begun, shape):
    _, fine, width = shape
    coarse, seqs = fine // 2, lax.axis_size("seq")
    rows, block = pieces[0][0].shape[-2:]
    planes = width // (2 * rows)
    half = planes // 2
    window, used = coarse + 2 * HALO, coarse + 2 * MARGIN
    depth, planar = len(distances) * block, (2, coarse, width)
    last = begun is not None
    needed = list(range(seqs)) if last else distances
    parts = [(d, *part) for d in needed for part in windows[d]]
    operands = [part[1] for part in parts] + [piece[0] for piece in pieces]
    operands += [slope, begun] if last else []

    def body(place, *refs):
        own, refs = refs[: len(parts)], refs[len(parts) :]
        sources, refs = refs[: len(pieces)], refs[len(pieces) :]
        if last:
            (slope_ref, begun_ref), refs = refs[:2], refs[2:]
        out_ref, wv, gv, products, sems, grad_sems = refs[:6]
        me, core = place[0], place[1] % 2

        def kernel_copies(first):
            for number, (array, start, plane, count, flip, distance) in enumerate(pieces):
                spot = pl.ds(distances.index(distance) * block, block)
                if first != (start is not None):
                    continue
                for k in range(SPLIT if first else taps - SPLIT):
                    for h in range(count // half):
                        span = pl.ds(plane + h * half, half)
                        if first:
                            source = sources[number].at[pl.ds(start + (h * SPLIT + k) * half, half)]
                        else:
                            source = sources[number].at[span, distance, k]
                        tap = k if first else SPLIT + k
                        target = wv.at[tap, span, core ^ flip, :, spot]
                        sem = sems.at[tap, number, h]
                        yield tap, pltpu.make_async_copy(source, target, sem)

        def window_copies(target_of, sems):
            for number, (distance, _, start, first, count) in enumerate(parts):
                for b in range(count):
                    target = target_of(distance, pl.ds((first + b) * rows, rows))
                    if target is not None:
                        source = own[number].at[start + b]
                        yield pltpu.make_async_copy(source, target, sems.at[number, b])

        def into_window(distance, span):
            if distance not in distances:
                return None
            return gv.at[span, pl.ds(distances.index(distance) * block, block)]

        early = list(window_copies(into_window, grad_sems))
        late = []
        if last:
            sums, slopes, strip, skips, sum_sems, skip_sems = refs[6:]
            late.append(pltpu.make_async_copy(begun_ref, sums, sum_sems.at[0]))
            late.append(pltpu.make_async_copy(slope_ref, slopes, sum_sems.at[1]))
            late += window_copies(lambda d, span: skips.at[me ^ d, span], skip_sems)
        for copy in early:
            copy.start()
        arriving = sorted([*kernel_copies(True), *kernel_copies(False)], key=lambda pair: pair[0])
        for _, copy in arriving:
            copy.start()
        for copy in late:
            copy.start()
        for copy in early:
            copy.wait()
        for k in range(taps):
            for tap, copy in arriving:
                if tap == k:
                    copy.wait()
            for part in range(2):
                kernel = wv[k, part * half : (part + 1) * half].reshape(2 * half * rows, depth)
                lanes = slice(part * 2 * half * rows, (part + 1) * 2 * half * rows)
                products[k, :, lanes] = lax.dot_general(
                    gv[EDGE : EDGE + used],
                    kernel,
                    (((1,), (1,)), ((), ())),
                    preferred_element_type=jnp.float32,
                )

        for copy in late:
            copy.wait()

        @pl.loop(0, coarse // STEP)
        def _(i):
            base = pl.multiple_of(i * STEP, STEP)
            spot, span = pl.ds(base, STEP), pl.ds(pl.multiple_of(2 * base, 2 * STEP), 2 * STEP)
            for c in range(width // LANES):
                lanes = slice(c * LANES, (c + 1) * LANES)
                if last:
                    left = c * LANES % block
                    skip = skips[c * LANES // block, pl.ds(base + HALO, STEP), left : left + LANES]
                    skip = 0.5 * skip.astype(jnp.float32)
                for parity in range(2):
                    total = shifted_total(products, base, lanes, parity)
                    if last:
                        total = (total + sums[parity, spot, lanes]) * slopes[parity, spot, lanes]
                        strip[c, pl.ds(parity, STEP, stride=2), :] = total + skip
                    else:
                        out_ref[parity, spot, lanes] = total
                if last:
                    out_ref[0, span, lanes] = strip[c].astype(jnp.bfloat16)

    out_shape = jax.ShapeDtypeStruct(shape if last else planar, jnp.bfloat16 if last else jnp.float32)
    scratch = [
        pltpu.VMEM((taps, planes, 2, rows, depth), jnp.bfloat16),
        pltpu.VMEM((window, depth), jnp.bfloat16),
        pltpu.VMEM((taps, used, width), jnp.float32),
        pltpu.SemaphoreType.DMA((taps, len(pieces), 2)),
        pltpu.SemaphoreType.DMA((len(parts), window // rows)),
    ]
    if last:
        scratch += [
            pltpu.VMEM(planar, jnp.float32),
            pltpu.VMEM(planar, jnp.float32),
            pltpu.VMEM((width // LANES, 2 * STEP, LANES), jnp.float32),
            pltpu.VMEM((seqs, window, block), jnp.bfloat16),
            pltpu.SemaphoreType.DMA((2,)),
            pltpu.SemaphoreType.DMA((len(parts), window // rows)),
        ]
    return pl.pallas_call(
        body,
        out_shape=out_shape,
        grid_spec=pltpu.PrefetchScalarGridSpec(
            num_scalar_prefetch=1,
            grid=(1,),
            in_specs=[ANYWHERE] * len(operands),
            out_specs=pl.BlockSpec(out_shape.shape, lambda i, place: (0, 0, 0)),
            scratch_shapes=scratch,
        ),
        compiler_params=pltpu.CompilerParams(vmem_limit_bytes=56 << 20),
        cost_estimate=SMALL,
        name="input_grad",
    )(place, *operands)

def stack_planes(place, line):
    count = len(line)

    def kernel(place, *refs):
        parts, out_ref = refs[:count], refs[count]
        for j in range(count):
            out_ref[place[1] // 2 ^ j] = parts[j][...]

    shape = line[0].shape
    return pl.pallas_call(
        kernel,
        out_shape=jax.ShapeDtypeStruct((count, *shape), line[0].dtype),
        grid_spec=pltpu.PrefetchScalarGridSpec(
            num_scalar_prefetch=1,
            grid=(1,),
            in_specs=[pl.BlockSpec(shape, lambda i, place: (0,) * len(shape))] * count,
            out_specs=pl.BlockSpec((count, *shape), lambda i, place: (0,) * (1 + len(shape))),
        ),
        compiler_params=pltpu.CompilerParams(vmem_limit_bytes=24 << 20),
        cost_estimate=SMALL,
        name="stack_planes",
    )(place, *line)

def on_device_square(inputs, trunk_grad, weights):
    seqs, reps = lax.axis_size("seq"), lax.axis_size("rep")
    me, rep = lax.axis_index("seq"), lax.axis_index("rep")
    place = jnp.stack([me, rep]).astype(jnp.int32)
    taps, rows, block = weights.shape
    fine = inputs.shape[1]
    coarse, planes = fine // 2, reps // 2
    half = coarse // 2

    last_taps = weights[SPLIT:]
    across = [last_taps] + [from_peer(last_taps, "seq", d) for d in range(1, seqs)]

    act = after(activate(inputs), *across[1:])
    beside, below = from_peer(act, "seq", 1), from_peer(act, "seq", 2)
    slope = half_slope(inputs)
    line = gather_line(weights[:SPLIT], "rep", planes, 2)
    line_across = gather_line(after(jnp.stack(across), act, *line[1:]), "rep", planes, 2)
    crossing = (line_across[1], line_across[planes - 1])
    trunk = trunk_grad[0]
    zeros = jnp.zeros((1, block), jnp.bfloat16)
    later = jnp.concatenate([trunk[1:], zeros])
    earlier = jnp.concatenate([zeros, trunk[:-1]])
    shifts = jnp.concatenate([later, trunk, earlier], axis=1)
    to_beside, to_below, own_window = kernel_messages(place, line, trunk_grad, coarse)
    ready = (slope, shifts, to_beside, *crossing)
    top, bottom = after(beside[:half], *ready), after(below[half:], *ready)
    far_top, far_bottom = from_peer(top, "seq", 2), from_peer(bottom, "seq", 1)

    scale = 0.5 * float(fine * seqs * reps) ** (-0.5)
    near_rows = [(d, 0, coarse, 0) for d in range(3)]
    far_rows = [(3, 0, half, 0), (3, half, half, 0)]
    early = early_terms(place, near_rows, [act, beside, below], shifts, coarse)
    line_across[2] = after(line_across[2], early)
    lines = stack_planes(place, line_across)
    far_top, far_bottom = after(far_top, early), after(far_bottom, early)

    to_beside, to_below = (
        after(message, far_top, far_bottom) for message in (to_beside, to_below)
    )
    kept_beside, kept_below = from_peer(to_beside, "seq", 1), from_peer(to_below, "seq", 2)
    other_column, other_lines = from_peer(to_below, "rep", 1), from_peer(lines, "rep", 1)

    mine, *theirs = late_terms(
        place,
        far_rows,
        [far_top, far_bottom],
        shifts,
        early,
        coarse,
        scale,
        planes,
        taps,
        rows,
        [line_across[2]],
    )
    arrived = [from_peer(part, "rep", 1) for part in theirs]
    pairs = []
    for j in range(planes):
        part = arrived[j // (planes // 2)][j % (planes // 2)]
        pairs.append(mine[j] + part.astype(jnp.float32))
    weight_grad, steps = reduce_line(pairs, "rep", planes, 2)

    window = (coarse + 2 * HALO) // rows
    count, side = planes * SPLIT, window // 2
    far_first = from_peer(kept_beside[: side + count // 2], "seq", 2)
    far_second = from_peer(kept_below[count // 2 : count + side], "seq", 1)

    windows = [
        [(own_window, 0, 0, window)],
        [(kept_beside, side + count, 0, window)],
        [(kept_below, count + side, 0, window)],
    ]
    stage = functools.partial(gradient_stage, place, taps=taps, slope=slope, shape=inputs.shape)
    soon = [(to_below, 0, 0, planes, 0, 0), (other_column, 0, 0, planes, 1, 0)]
    for part, start, distance in ((kept_beside, side, 1), (kept_below, 0, 2)):
        soon.append((part, start, 0, planes, 0, distance))
        soon.append((from_peer(part, "rep", 1), start, 0, planes, 1, distance))
    crossed = [
        (part, None, 0, planes, flip, d)
        for flip, part in enumerate((lines, other_lines))
        for d in range(seqs)
    ]
    near = [piece for piece in crossed if piece[-1] < 3]
    begun = stage(windows, pieces=soon + near, distances=[0, 1, 2], begun=None)
    far_first, far_second = after(far_first, begun, *steps[:1]), after(far_second, begun, *steps[:1])
    windows.append([(far_first, 0, 0, side), (far_second, count // 2, side, side)])
    rest = [piece for piece in crossed if piece[-1] == 3]
    for part, start, plane in ((far_first, side, 0), (far_second, 0, planes // 2)):
        rest.append((part, start, plane, planes // 2, 0, 3))
        rest.append((from_peer(part, "rep", 1), start, plane, planes // 2, 1, 3))
    input_grad = stage(windows, pieces=rest, distances=[3], begun=begun)
    weight_grad = weight_grad + after(steps[-1], input_grad)[0].astype(jnp.float32)
    return (input_grad, weight_grad)


def with_halo(value, sides, width):
    for axis, dim in sides:
        peers, length = (lax.axis_size(axis), value.shape[dim])
        up = [(i, (i + 1) % peers) for i in range(peers - 1)]
        down = [(j, i) for i, j in up]
        last = lax.slice_in_dim(value, length - width, length, axis=dim)
        leading = lax.slice_in_dim(value, 0, width, axis=dim)
        before = lax.ppermute(last, axis, up)
        after = lax.ppermute(leading, axis, down)
        value = jnp.concatenate([before, value, after], axis=dim)
    return value

def contract_last(left, right):
    return lax.dot_general(
        left, right, (((1,), (1,)), ((), ())), preferred_element_type=jnp.float32
    )

def contract_first(left, right):
    return lax.dot_general(
        left, right, (((0,), (0,)), ((), ())), preferred_element_type=jnp.float32
    )

def on_device_plain(inputs, trunk_grad, weights):
    taps = weights.shape[0]
    grad = lax.all_to_all(trunk_grad, "seq", split_axis=1, concat_axis=2, tiled=True)
    grad_up = jnp.repeat(grad.astype(jnp.float32) * 0.5, 2, axis=1).astype(jnp.bfloat16)
    rows = grad_up.shape[1]
    padded = with_halo(grad_up, (("seq", 1),), 2)
    shifts = [padded[0, 4 - k : 4 - k + rows] for k in range(taps)]
    inputs_f = inputs[0].astype(jnp.float32)
    act_vals, back = jax.vjp(jax.nn.gelu, inputs_f)
    slope = back(jnp.ones_like(inputs_f))[0]
    act = act_vals.astype(jnp.bfloat16)
    in_width = inputs.shape[2]
    columns = lax.all_gather(weights, "seq", axis=2, tiled=True)
    piece = lax.all_gather(columns, "rep", axis=1, tiled=True)
    result = contract_last(shifts[0], piece[0])
    for project_k in range(1, taps):
        result = result + contract_last(shifts[project_k], piece[project_k])
    input_grad = (result * slope + grad_up[0, :, :in_width].astype(jnp.float32)).astype(
        jnp.bfloat16
    )
    scale_factor = float(rows * lax.axis_size("seq") * lax.axis_size("rep")) ** (-0.5)
    terms = jnp.stack([contract_first(act, shifts[k]) for k in range(taps)]) * scale_factor
    partial_sum = lax.psum_scatter(terms, "rep", scatter_dimension=1, tiled=True)
    weight_grad = lax.psum_scatter(partial_sum, "seq", scatter_dimension=2, tiled=True)
    return (input_grad[None], weight_grad)

def on_device(inputs, trunk_grad, weights):
    square = lax.axis_size("seq") == 4 and lax.axis_size("rep") % 8 == 0
    if square and weights.shape[2] % LANES == 0 and inputs.shape[2] % LANES == 0:
        return on_device_square(inputs, trunk_grad, weights)
    return on_device_plain(inputs, trunk_grad, weights)

def solution(mesh):
    in_specs = (P("rep", "seq", None), P("rep", None, "seq"), P(None, "rep", "seq"))
    out_specs = (P("rep", "seq", None), P(None, "rep", "seq"))
    return jax.shard_map(
        on_device, mesh=mesh, in_specs=in_specs, out_specs=out_specs, check_vma=False
    )
```
